32 devices in a mesh: grp: 4 (over y, x), seq: 4 (over z), rep: 2 (over core).
Axes of the slice: x: 2, y: 2, z: 4, core: 2. Of those that a mesh axis runs over, the one named last changes fastest.
Arguments:
- query_rows: bfloat16 [2, 4, 512, 2560], P('rep', 'grp', 'seq'), may hold values from -8 to 8
- key_rows: bfloat16 [2, 4, 512, 2560], P('rep', 'grp', 'seq'), may hold values from -8 to 8
- value_rows: bfloat16 [2, 4, 512, 2560], P('rep', 'grp', 'seq'), may hold values from -6 to 6
- view_frame: int32 [2, 4, 512], P('rep', 'grp', 'seq'), may hold values from 0 to 39, never falling along the last dimension, each value on 1 to 16 neighbouring positions
- control_row: int32 [2, 4, 512], P('rep', 'grp', 'seq'), may hold values from 0 to 511, as said below
- control_gate: float32 [2560], P('rep'), may hold values from 0.2 to 1.6
- out_grad: bfloat16 [2, 4, 512, 2560], P('rep', 'grp', 'seq'), may hold values from -6 to 6
Outputs:
- block_out: bfloat16 [2, 4, 512, 2560], P('rep', 'grp', 'seq')
- branch_grad: bfloat16 [2, 512, 2560], P('rep', 'seq')
The draws below stay inside these ranges and needn't reach their ends.
Inputs may be any that keep to these rules, and one draw needn't show every extreme that they name: `view_frame`: values never fall along a sequence; value // 20 is the camera and value % 20 the frame; one value holds at most 16 positions. `control_row`: position t of a sequence takes a row r with r // 128 == t // 128.
All inputs are finite; a program needn't handle non-finite values.
Results may differ from the reference program's by a relative error of at most 0.0057.
Values may be sent and summed in bfloat16 or wider, within the bound.
No kernel may reach another device: no remote copies, remote signals or barrier semaphores. Data moves between devices by JAX's collectives and lax.ppermute only.
A program may use at most 64 MiB of HBM per device.

```python
import math
import jax
import jax.numpy as jnp
import numpy as np
from jax import lax

HEADS = 32
DH = 80
TOK_DEV = 128
FRAMES = 20
SEGS = 40
L = 512
FRAME_MOST = 16
REACH = 32
BLOCK = 512
HD = 2560
CLIPS = 2
GROUPS = 4


def paired_rows(key):
    base = jax.random.fold_in(key, 7)
    first, second = jax.random.split(base, 2)
    shape = (CLIPS, GROUPS, L, HEADS * DH)
    queries = jnp.clip(jax.random.normal(first, shape, jnp.float32), -6.0, 6.0)
    keys_out = jnp.clip(jax.random.normal(second, shape, jnp.float32), -6.0, 6.0)
    return (queries, keys_out)


def draw_query_rows(key, part):
    return paired_rows(key)[0].astype(jnp.bfloat16)


def draw_key_rows(key, part):
    return paired_rows(key)[1].astype(jnp.bfloat16)


def draw_control_row(key, part):
    base = jax.random.fold_in(key, 11)
    first, second, third = jax.random.split(base, 3)
    blocks_count = L // TOK_DEV
    shape = (CLIPS, GROUPS, blocks_count, TOK_DEV)
    side_shape = (CLIPS, GROUPS, blocks_count, 1)
    rows_out = jax.random.randint(first, shape, 0, TOK_DEV)
    top_place = jax.random.randint(second, side_shape, 0, TOK_DEV)
    low_place = (top_place + 1 + jax.random.randint(third, side_shape, 0, TOK_DEV - 1)) % TOK_DEV
    places = jnp.arange(TOK_DEV, dtype=jnp.int32)
    rows_out = jnp.where(places == top_place, TOK_DEV - 1, rows_out)
    rows_out = jnp.where(places == low_place, 0, rows_out)
    offsets = (jnp.arange(blocks_count, dtype=jnp.int32) * TOK_DEV)[:, None]
    rows_out = rows_out + offsets
    return rows_out.reshape(CLIPS, GROUPS, L).astype(jnp.int32)


def block_levels(stream_key, extent, cuts, smallest, high):
    gain = 1.0
    for dim, blocks in cuts:
        heights = jax.random.uniform(jax.random.fold_in(jax.random.fold_in(stream_key, 6), dim), (blocks,), jnp.float32, smallest / len(cuts), high / len(cuts))
        gain = gain * jnp.repeat(jnp.exp(heights), extent[dim] // blocks).reshape((-1,) + (1,) * (len(extent) - 1 - dim))
    return gain


def split_up(number_of, total, bound, skew):
    portions = [(1 << 20) // math.isqrt(standing ** skew) + 1 for standing in range(2, number_of + 1)]
    rest, holding = total - bound - (number_of - 1), [1] * (number_of - 1)
    while rest > 0:
        movable = [i for i in range(number_of - 1) if holding[i] < bound]
        pool, remaining = sum([portions[i] for i in movable]), rest
        for i in movable:
            more = min(bound - holding[i], max(1, remaining * portions[i] // pool), rest)
            holding[i] = holding[i] + more
            rest = rest - more
    return np.array([bound] + holding)


def uneven(own_key, count, total, limit, skew):
    if count == 2:
        one = jax.random.randint(own_key, (), max(1, total - limit), min(limit, total - 1) + 1)
        return jnp.stack([one, total - one])
    lengths = jnp.asarray(split_up(count, total, limit, skew), jnp.int32)
    couples = (count - 1) // 2
    giver, taker = lengths[1:1 + 2 * couples:2], lengths[2:2 + 2 * couples:2]
    margin = jnp.minimum(giver - 1, limit - taker)
    shifted = jax.random.randint(jax.random.fold_in(own_key, 1), (couples,), 0, 1 << 20) % (margin + 1)
    lengths = lengths.at[1:1 + 2 * couples:2].set(giver - shifted).at[2:2 + 2 * couples:2].set(taker + shifted)
    return lengths[jax.random.permutation(jax.random.fold_in(own_key, 2), count)]


def noise(own_key, extent, spread, bound, cuts=(), kind=jnp.bfloat16):
    factor_of = block_levels(own_key, extent, cuts, -0.22, 0.18) if cuts else 1.0
    values = jax.random.normal(own_key, extent, jnp.float32) * spread * factor_of
    return jnp.minimum(jnp.maximum(values, -bound), bound).astype(kind)


def setup_inputs(seed: int = 0) -> dict:
    arg_keys = jax.random.split(jax.random.key(seed), 8)
    query_rows = draw_query_rows(jax.random.fold_in(arg_keys[7], 71), 0)
    key_rows = draw_key_rows(jax.random.fold_in(arg_keys[7], 71), 0)
    value_rows = noise(arg_keys[2], (CLIPS, GROUPS, L, HD), 1.0, 6.0, ((0, 2), (1, 4), (2, 4)))
    view_frame = jax.vmap(lambda own: jnp.searchsorted(jnp.cumsum(uneven(own, SEGS, L, FRAME_MOST, 1)), jnp.arange(L), side="right"))(jax.random.split(arg_keys[3], CLIPS * GROUPS)).reshape((CLIPS, GROUPS, L)).astype(jnp.int32)
    control_row = draw_control_row(jax.random.fold_in(arg_keys[7], 71), 0)
    control_gate = jnp.clip(0.2 + 1.4 * jax.random.uniform(arg_keys[5], (HD,), jnp.float32) ** block_levels(arg_keys[5], (HD,), ((0, 2),), -0.2, 0.2), 0.2, 1.6)
    out_grad = noise(arg_keys[6], (CLIPS, GROUPS, L, HD), 1.0, 6.0, ((0, 2), (1, 4), (2, 4)))
    return {"query_rows": query_rows, "key_rows": key_rows, "value_rows": value_rows, "view_frame": view_frame, "control_row": control_row, "control_gate": control_gate, "out_grad": out_grad}


def attend(queries, keys_pad, values_pad, query_tag, key_tag, reach_rows, frame_count, block_rows):
    length = queries.shape[-1]
    window = block_rows + 2 * reach_rows
    factor = 1.0 / math.sqrt(queries.shape[1])

    def one_block(block_index):
        first_row = block_index * block_rows
        query_block = lax.dynamic_slice_in_dim(queries, first_row, block_rows, 2).astype(jnp.float32)
        key_block = lax.dynamic_slice_in_dim(keys_pad, first_row, window, 2).astype(jnp.float32)
        value_block = lax.dynamic_slice_in_dim(values_pad, first_row, window, 2).astype(jnp.float32)
        query_seg = lax.dynamic_slice_in_dim(query_tag, first_row, block_rows, 0) - 1
        key_seg = lax.dynamic_slice_in_dim(key_tag, first_row, window, 0) - 1
        allowed = (key_seg[None, :] >= 0) & (query_seg[:, None] // frame_count == key_seg[None, :] // frame_count) & (jnp.abs(query_seg[:, None] - key_seg[None, :]) <= 1)
        scores = jnp.einsum('hdq,hdk->hqk', query_block, key_block) * factor
        scores = jnp.where(allowed[None], scores, -1e+30)
        largest = lax.optimization_barrier(jnp.max(scores, axis=-1, keepdims=True))
        powers = jnp.exp(scores - largest)
        totals = lax.optimization_barrier(jnp.sum(powers, axis=-1, keepdims=True))
        weights = (powers / totals).astype(jnp.bfloat16)
        mixed_rows = jnp.einsum('hqk,hdk->hdq', weights.astype(jnp.float32), value_block)
        return mixed_rows.astype(jnp.bfloat16)
    blocks = lax.map(one_block, jnp.arange(length // block_rows, dtype=jnp.int32))
    heads_count = queries.shape[0]
    return jnp.moveaxis(blocks, 0, 2).reshape(heads_count, queries.shape[1], length)

def reference(query_rows, key_rows, value_rows, view_frame, control_row, control_gate, out_grad):
    tags = (view_frame + 1).astype(jnp.int32)
    pad_rows = ((0, 0), (0, 0), (REACH, REACH))

    def head_major(rows_in):
        return rows_in.reshape(L, HEADS, DH).transpose(1, 2, 0)

    def one_sequence(packed):
        queries, keys_in, values_in, query_tag = packed
        keys_pad = jnp.pad(head_major(keys_in), pad_rows)
        values_pad = jnp.pad(head_major(values_in), pad_rows)
        key_tag = jnp.pad(query_tag, (REACH, REACH))
        result = attend(head_major(queries), keys_pad, values_pad, query_tag, key_tag, REACH, FRAMES, BLOCK)
        return result.transpose(2, 0, 1).reshape(L, HEADS * DH)

    def flatten_groups(array):
        return array.reshape((CLIPS * GROUPS,) + array.shape[2:])
    attended = lax.map(one_sequence, (flatten_groups(query_rows), flatten_groups(key_rows), flatten_groups(value_rows), flatten_groups(tags)))
    attended = attended.reshape(CLIPS, GROUPS, L, HEADS * DH)
    branch_rows = attended[:, 0]
    relayed = jax.vmap(lambda rows_in, picks: rows_in[picks])(branch_rows, control_row)
    block_out = (attended.astype(jnp.float32) + control_gate * relayed.astype(jnp.float32)).astype(jnp.bfloat16)

    def gathered_grad(grads, picks):
        flat_grads = grads.reshape(-1, HEADS * DH).astype(jnp.float32)
        return jax.ops.segment_sum(flat_grads, picks.reshape(-1), num_segments=L)
    summed = jax.vmap(gathered_grad)(out_grad, control_row)
    branch_grad = (out_grad[:, 0].astype(jnp.float32) + control_gate * summed).astype(jnp.bfloat16)
    return (block_out, branch_grad)
```

```python
import functools
import math

import jax
import jax.numpy as jnp
from jax import lax
from jax.experimental import pallas as pl
from jax.experimental.pallas import tpu as pltpu
from jax.sharding import PartitionSpec as P

HEADS = 32
DH = 80
FRAMES = 20
LANES = 128
VMEM_LIMIT = 48 * 1024 * 1024


def shifted(block, axis, distance):
    devices = range(lax.axis_size(axis))
    route = [(i - distance, i) for i in devices if i - distance in devices]
    return lax.ppermute(block, axis, route)


def lane_windows(heads):
    windows = []
    for head in range(heads):
        first, last = head * DH, (head + 1) * DH
        if windows and last <= windows[-1][0] + 2 * LANES:
            windows[-1][1].append(head)
        else:
            windows.append((first // LANES * LANES, [head]))
    out = []
    for start, members in windows:
        start = min(start, heads * DH - 2 * LANES)
        out.append((start, members))
    return out


def attend_kernel(hops, block_rows, reach, *refs):
    q_ref, k_ref, v_ref = refs[:3]
    lows = refs[3 : 3 + hops]
    highs = refs[3 + hops : 3 + 2 * hops]
    code_ref, window_code_ref, out_ref, keys, values, mask = refs[3 + 2 * hops :]
    tokens, width = q_ref.shape
    span = block_rows + 2 * reach
    blocks = tokens // block_rows
    factor = math.log2(math.e) / math.sqrt(DH)

    @pl.when(pl.program_id(0) == 0)
    def _():
        column = jnp.broadcast_to(code_ref[...], (tokens, tokens)).T
        for b in range(blocks):
            row = window_code_ref[:, pl.ds(b * block_rows, span)]
            mine = column[b * block_rows : (b + 1) * block_rows, :1]
            near = jnp.abs(mine - row) <= 1.5
            mask[b] = jnp.where(near, 0.0, -1e30)

    at = 0
    for piece in (*lows, None, *highs):
        if piece is None:
            keys[pl.ds(at, tokens), :] = k_ref[...]
            values[pl.ds(at, tokens), :] = v_ref[...]
            at += tokens
        else:
            rows = piece.shape[1]
            keys[pl.ds(at, rows), :] = piece[0]
            values[pl.ds(at, rows), :] = piece[1]
            at += rows

    for b in range(blocks):
        bias = mask[b]
        top = b * block_rows
        for start, members in lane_windows(width // DH):
            wide = slice(start, start + 2 * LANES)
            lane = lax.broadcasted_iota(jnp.int32, (block_rows, 2 * LANES), 1) + start
            inside = [(lane >= h * DH) & (lane < (h + 1) * DH) for h in members]
            query = q_ref[pl.ds(top, block_rows), wide]
            picked = [jnp.where(m, query, jnp.zeros_like(query)) for m in inside]
            key = keys[pl.ds(top, span), wide]
            value = values[pl.ds(top, span), wide]
            scores = lax.dot_general(
                jnp.concatenate(picked, axis=0),
                key,
                (((1,), (1,)), ((), ())),
                preferred_element_type=jnp.float32,
            )
            powers = []
            totals = []
            for n in range(len(members)):
                part = scores[n * block_rows : (n + 1) * block_rows] + bias
                largest = jnp.max(part, axis=-1, keepdims=True)
                power = jnp.exp2((part - largest) * factor)
                totals.append(jnp.sum(power, axis=-1, keepdims=True))
                powers.append(power.astype(jnp.bfloat16))
            mixed = jnp.dot(
                jnp.concatenate(powers, axis=0), value, preferred_element_type=jnp.float32
            )
            merged = mixed[:block_rows] / totals[0]
            for n in range(1, len(members)):
                merged = jnp.where(
                    inside[n], mixed[n * block_rows : (n + 1) * block_rows] / totals[n], merged
                )
            first, last = members[0] * DH, (members[-1] + 1) * DH
            for tile in range(2):
                low = start + tile * LANES
                lanes = slice(low, low + LANES)
                piece = merged[:, tile * LANES : (tile + 1) * LANES].astype(jnp.bfloat16)
                if first > low:
                    before = out_ref[pl.ds(top, block_rows), lanes]
                    piece = jnp.where(lane[:, tile * LANES : (tile + 1) * LANES] >= first, piece, before)
                out_ref[pl.ds(top, block_rows), lanes] = piece


def attend(queries, keys, values, lows, highs, code, window_code, reach):
    tokens, width = queries.shape
    period = math.lcm(DH, LANES)
    block_rows = tokens
    for rows in range(64, tokens, 16):
        if tokens % rows == 0 and (rows + 2 * reach) % LANES == 0:
            block_rows = rows
            break
    span = block_rows + 2 * reach
    window = tokens + 2 * reach
    rows_spec = pl.BlockSpec((tokens, period), lambda g: (0, g))
    pair_specs = [pl.BlockSpec((2, p.shape[1], period), lambda g: (0, 0, g)) for p in (*lows, *highs)]
    whole = lambda a: pl.BlockSpec(a.shape, lambda g: (0, 0))
    return pl.pallas_call(
        functools.partial(attend_kernel, len(lows), block_rows, reach),
        grid=(width // period,),
        in_specs=[rows_spec] * 3 + pair_specs + [whole(code), whole(window_code)],
        out_specs=rows_spec,
        out_shape=jax.ShapeDtypeStruct((tokens, width), jnp.bfloat16),
        scratch_shapes=[
            pltpu.VMEM((window, period), jnp.bfloat16),
            pltpu.VMEM((window, period), jnp.bfloat16),
            pltpu.VMEM((tokens // block_rows, block_rows, span), jnp.float32),
        ],
        compiler_params=pltpu.CompilerParams(vmem_limit_bytes=VMEM_LIMIT),
        cost_estimate=pl.CostEstimate(
            flops=HEADS * tokens * span * 2 * LANES * 4,
            bytes_accessed=12 * tokens * width,
            transcendentals=HEADS * tokens * span,
        ),
        name="attend",
    )(queries, keys, values, *lows, *highs, code, window_code)


def term_kernel(half, row_ref, root_ref, grad_ref, gate_ref, first_ref, second_ref):
    tokens = grad_ref.shape[0]
    wanted = lax.broadcasted_iota(jnp.int32, (tokens, tokens), 0)
    selector = jnp.where(wanted == row_ref[...], 1.0, 0.0).astype(jnp.bfloat16)
    grads = grad_ref[...]
    summed = jnp.dot(selector, grads, preferred_element_type=jnp.float32)
    term = gate_ref[...] * summed + root_ref[0] * grads.astype(jnp.float32)
    term = term.astype(jnp.bfloat16)
    first_ref[...] = term[:, :half]
    second_ref[...] = term[:, half:]


def grad_terms(local_rows, root, grads, gate):
    tokens, width = grads.shape
    half = width // 2
    vmem = pl.BlockSpec(memory_space=pltpu.VMEM)
    return pl.pallas_call(
        functools.partial(term_kernel, half),
        in_specs=[vmem, pl.BlockSpec(memory_space=pltpu.SMEM), vmem, vmem],
        out_specs=[vmem, vmem],
        out_shape=[jax.ShapeDtypeStruct((tokens, half), jnp.bfloat16)] * 2,
        compiler_params=pltpu.CompilerParams(vmem_limit_bytes=VMEM_LIMIT),
        cost_estimate=pl.CostEstimate(
            flops=2 * tokens * tokens * width, bytes_accessed=4 * tokens * width, transcendentals=0
        ),
        name="grad_terms",
    )(local_rows, root, grads, gate)


def add_kernel(a_ref, b_ref, c_ref, d_ref, first_ref, second_ref):
    first_ref[...] = (a_ref[...].astype(jnp.float32) + b_ref[...].astype(jnp.float32)).astype(
        jnp.bfloat16
    )
    second_ref[...] = (c_ref[...].astype(jnp.float32) + d_ref[...].astype(jnp.float32)).astype(
        jnp.bfloat16
    )


def add_pairs(a, b, c, d):
    vmem = pl.BlockSpec(memory_space=pltpu.VMEM)
    return pl.pallas_call(
        add_kernel,
        in_specs=[vmem] * 4,
        out_specs=[vmem] * 2,
        out_shape=[jax.ShapeDtypeStruct(a.shape, a.dtype), jax.ShapeDtypeStruct(c.shape, c.dtype)],
        compiler_params=pltpu.CompilerParams(vmem_limit_bytes=VMEM_LIMIT),
        cost_estimate=pl.CostEstimate(flops=2 * a.size, bytes_accessed=12 * a.size, transcendentals=0),
        name="add_pairs",
    )(a, b, c, d)


def join_kernel(a_ref, b_ref, c_ref, d_ref, out_ref):
    half = a_ref.shape[1]
    out_ref[:, :half] = (a_ref[...].astype(jnp.float32) + b_ref[...].astype(jnp.float32)).astype(
        jnp.bfloat16
    )
    out_ref[:, half:] = (c_ref[...].astype(jnp.float32) + d_ref[...].astype(jnp.float32)).astype(
        jnp.bfloat16
    )


def join_pairs(a, b, c, d):
    vmem = pl.BlockSpec(memory_space=pltpu.VMEM)
    return pl.pallas_call(
        join_kernel,
        in_specs=[vmem] * 4,
        out_specs=vmem,
        out_shape=jax.ShapeDtypeStruct((a.shape[0], 2 * a.shape[1]), a.dtype),
        compiler_params=pltpu.CompilerParams(vmem_limit_bytes=VMEM_LIMIT),
        cost_estimate=pl.CostEstimate(flops=2 * a.size, bytes_accessed=12 * a.size, transcendentals=0),
        name="join_pairs",
    )(a, b, c, d)


def relay_kernel(half, row_ref, own_ref, gate_ref, first_ref, second_ref, out_ref):
    tokens = own_ref.shape[0]
    wanted = lax.broadcasted_iota(jnp.int32, (tokens, tokens), 0)
    selector = jnp.where(wanted == row_ref[...], 1.0, 0.0).T.astype(jnp.bfloat16)
    for lanes, branch_ref in ((slice(0, half), first_ref), (slice(half, 2 * half), second_ref)):
        relayed = jnp.dot(selector, branch_ref[...], preferred_element_type=jnp.float32)
        out_ref[:, lanes] = (
            own_ref[:, lanes].astype(jnp.float32) + gate_ref[:, lanes] * relayed
        ).astype(jnp.bfloat16)


def relay(local_rows, own, gate, first, second):
    tokens, width = own.shape
    half = width // 2
    vmem = pl.BlockSpec(memory_space=pltpu.VMEM)
    return pl.pallas_call(
        functools.partial(relay_kernel, half),
        in_specs=[vmem] * 5,
        out_specs=vmem,
        out_shape=jax.ShapeDtypeStruct((tokens, width), jnp.bfloat16),
        compiler_params=pltpu.CompilerParams(vmem_limit_bytes=VMEM_LIMIT),
        cost_estimate=pl.CostEstimate(
            flops=2 * tokens * tokens * width, bytes_accessed=6 * tokens * width, transcendentals=0
        ),
        name="relay",
    )(local_rows, own, gate, first, second)


def whole_gate(gate):
    ranks = lax.axis_size("rep")
    if ranks != 2:
        return lax.all_gather(gate, "rep", axis=0, tiled=True)
    other = lax.ppermute(gate, "rep", [(0, 1), (1, 0)])
    first = lax.axis_index("rep") == 0
    return jnp.concatenate([jnp.where(first, gate, other), jnp.where(first, other, gate)])


def local(query_rows, key_rows, value_rows, view_frame, control_row, control_gate, out_grad):
    queries, keys, values = query_rows[0, 0], key_rows[0, 0], value_rows[0, 0]
    tokens, width = queries.shape
    length = tokens * lax.axis_size("seq")
    reach = 2 * (length // 32)
    hops = (reach + tokens - 1) // tokens
    half = width // 2
    group = lax.axis_index("grp")

    gate = whole_gate(control_gate)[None]
    tag = view_frame[0, 0]
    code = (tag + 8 * (tag // FRAMES) + 16).astype(jnp.float32)[None]
    lows, highs, low_codes, high_codes = [], [], [], []
    for hop in range(1, hops + 1):
        rows = min(tokens, reach - (hop - 1) * tokens)
        tail = jnp.stack((keys[tokens - rows :], values[tokens - rows :]))
        head = jnp.stack((keys[:rows], values[:rows]))
        lows.insert(0, shifted(tail, "seq", hop))
        highs.append(shifted(head, "seq", -hop))
        low_codes.insert(0, shifted(code[:, tokens - rows :], "seq", hop))
        high_codes.append(shifted(code[:, :rows], "seq", -hop))
    window_code = jnp.concatenate(low_codes + [code] + high_codes, axis=1)

    local_rows = (control_row[0] % tokens).astype(jnp.int32)
    root = (group == 0).astype(jnp.float32)[None]
    term_a, term_b = grad_terms(local_rows, root, out_grad[0, 0], gate)
    swap_x = [(0, 1), (1, 0), (2, 3), (3, 2)]
    swap_y = [(0, 2), (2, 0), (1, 3), (3, 1)]
    sum_a, sum_b = add_pairs(
        term_a, lax.ppermute(term_a, "grp", swap_x), term_b, lax.ppermute(term_b, "grp", swap_y)
    )
    branch_grad = join_pairs(
        sum_a, lax.ppermute(sum_a, "grp", swap_y), sum_b, lax.ppermute(sum_b, "grp", swap_x)
    )

    own = attend(queries, keys, values, lows, highs, code, window_code, reach)
    own_a, own_b = own[:, :half], own[:, half:]
    got_a = lax.ppermute(own_a, "grp", [(0, 1)])
    got_b = lax.ppermute(own_b, "grp", [(0, 2)])
    hold_a = jnp.where(group == 1, got_a, own_a)
    hold_b = jnp.where(group == 2, got_b, own_b)
    last_a = lax.ppermute(hold_a, "grp", [(0, 2), (1, 3)])
    last_b = lax.ppermute(hold_b, "grp", [(0, 1), (2, 3)])
    branch_a = jnp.where(group <= 1, hold_a, last_a)
    branch_b = jnp.where((group == 0) | (group == 2), hold_b, last_b)
    block_out = relay(local_rows, own, gate, branch_a, branch_b)
    return (block_out[None, None], branch_grad[None])


def solution(mesh):
    placed = (
        P("rep", "grp", "seq", None),
        P("rep", "grp", "seq", None),
        P("rep", "grp", "seq", None),
        P("rep", "grp", "seq"),
        P("rep", "grp", "seq"),
        P("rep"),
        P("rep", "grp", "seq", None),
    )
    return jax.shard_map(
        local,
        mesh=mesh,
        in_specs=placed,
        out_specs=(P("rep", "grp", "seq", None), P("rep", "seq", None)),
        check_vma=False,
    )
```

```python
import functools
import math

import jax
import jax.numpy as jnp
from jax import lax
from jax.experimental import pallas as pl
from jax.experimental.pallas import tpu as pltpu
from jax.sharding import PartitionSpec as P

HEADS = 32
DH = 80
FRAMES = 20
LANES = 128
VMEM_LIMIT = 48 * 1024 * 1024


def shifted(block, axis, distance):
    devices = range(lax.axis_size(axis))
    route = [(i - distance, i) for i in devices if i - distance in devices]
    return lax.ppermute(block, axis, route)


def lane_windows(heads):
    windows = []
    for head in range(heads):
        first, last = head * DH, (head + 1) * DH
        if windows and last <= windows[-1][0] + 2 * LANES:
            windows[-1][1].append(head)
        else:
            windows.append((first // LANES * LANES, [head]))
    out = []
    for start, members in windows:
        start = min(start, heads * DH - 2 * LANES)
        out.append((start, members))
    return out


def head_masks(rows, period):
    masks = {}
    for start, members in lane_windows(period // DH):
        lane = lax.broadcasted_iota(jnp.int32, (rows, 2 * LANES), 1) + start
        for h in members:
            inside = (lane >= h * DH) & (lane < (h + 1) * DH)
            masks[h] = jnp.where(inside, 1.0, 0.0).astype(jnp.bfloat16)
    return masks


def mixed_period(base, bias, query, key, value, masks, period):
    rows = bias.shape[0]
    factor = math.log2(math.e) / math.sqrt(DH)
    windows = lane_windows(period // DH)
    scores = []
    for start, members in windows:
        lanes = slice(base + start, base + start + 2 * LANES)
        part = query(lanes)
        stacked = jnp.concatenate([part * masks[h] for h in members], axis=0)
        scores.append(
            lax.dot_general(
                stacked, key(lanes), (((1,), (1,)), ((), ())), preferred_element_type=jnp.float32
            )
        )
    weights = []
    for part, (start, members) in zip(scores, windows):
        part = part.reshape(len(members), rows, -1) + bias[None]
        largest = jnp.max(part, axis=-1, keepdims=True)
        powers = jnp.exp2((part - largest) * factor)
        totals = jnp.sum(powers, axis=-1, keepdims=True)
        weight = (powers * (1.0 / totals)).astype(jnp.bfloat16)
        weights.append(weight.reshape(len(members) * rows, -1))
    tiles = {}
    for weight, (start, members) in zip(weights, windows):
        lanes = slice(base + start, base + start + 2 * LANES)
        mixed = jnp.dot(weight, value(lanes), preferred_element_type=jnp.float32)
        for n, h in enumerate(members):
            for t in range(2):
                low = start + t * LANES
                if h * DH >= low + LANES or (h + 1) * DH <= low:
                    continue
                piece = mixed[n * rows : (n + 1) * rows, t * LANES : (t + 1) * LANES]
                if low in tiles:
                    lane = lax.broadcasted_iota(jnp.int32, (rows, LANES), 1) + low
                    tiles[low] = jnp.where(lane >= h * DH, piece, tiles[low])
                else:
                    tiles[low] = piece
    return {low: tile.astype(jnp.bfloat16) for low, tile in tiles.items()}


def columns(code):
    return jnp.broadcast_to(code, (LANES, code.shape[1])).T


def attend_blocks(blocks, q_ref, keys, values, own_code, key_code, out_ref):
    width = q_ref.shape[1]
    period = math.lcm(DH, LANES)
    work = []
    masks = {}
    for top, first, rows, span, at in blocks:
        mine = own_code[top : top + rows, :1]
        theirs = key_code[first : first + span].T[:rows]
        bias = jnp.where(jnp.abs(mine - theirs) <= 1.5, 0.0, -1e30)
        if rows not in masks:
            masks[rows] = head_masks(rows, period)
        work.append((top, first, rows, span, at, bias))
    for base in range(0, width, period):
        for top, first, rows, span, at, bias in work:
            tiles = mixed_period(
                base,
                bias,
                lambda lanes: q_ref[top : top + rows, lanes],
                lambda lanes: keys[first : first + span, lanes],
                lambda lanes: values[first : first + span, lanes],
                masks[rows],
                period,
            )
            for low, tile in tiles.items():
                out_ref[at : at + rows, base + low : base + low + LANES] = tile


def middle_kernel(reach, q_ref, k_ref, v_ref, code_ref, out_ref):
    tokens = q_ref.shape[0]
    code = columns(code_ref[...])
    attend_blocks(
        [(reach, 0, tokens - 2 * reach, tokens, 0)], q_ref, k_ref, v_ref, code, code, out_ref
    )


def edge_kernel(hops, blocks, *refs):
    q_ref, k_ref, v_ref, code_ref = refs[:4]
    lows = refs[4 : 4 + hops]
    highs = refs[4 + hops : 4 + 2 * hops]
    out_ref, keys, values, codes = refs[4 + 2 * hops :]
    tokens, width = q_ref.shape
    code = columns(code_ref[...])
    at = 0
    for piece in (*lows, None, *highs):
        if piece is None:
            keys[at : at + tokens] = k_ref[...]
            values[at : at + tokens] = v_ref[...]
            codes[at : at + tokens] = code
            at += tokens
        else:
            rows = piece.shape[0]
            keys[at : at + rows] = piece[:, :width]
            values[at : at + rows] = piece[:, width : 2 * width]
            codes[at : at + rows] = piece[:, 2 * width :].astype(jnp.float32)
            at += rows
    attend_blocks(blocks, q_ref, keys, values, code, codes[...], out_ref)


def attend_cost(tokens, span, width):
    return pl.CostEstimate(
        flops=HEADS * tokens * span * 2 * LANES * 4,
        bytes_accessed=12 * tokens * width,
        transcendentals=HEADS * tokens * span,
    )


VMEM = pl.BlockSpec(memory_space=pltpu.VMEM)
PARAMS = pltpu.CompilerParams(vmem_limit_bytes=VMEM_LIMIT)


def attend_middle(queries, keys, values, code, reach):
    tokens, width = queries.shape
    return pl.pallas_call(
        functools.partial(middle_kernel, reach),
        in_specs=[VMEM] * 4,
        out_specs=VMEM,
        out_shape=jax.ShapeDtypeStruct((tokens - 2 * reach, width), jnp.bfloat16),
        compiler_params=PARAMS,
        cost_estimate=attend_cost(tokens - 2 * reach, tokens, width),
        name="attend_middle",
    )(queries, keys, values, code)


def attend_edges(queries, keys, values, code, lows, highs, reach):
    tokens, width = queries.shape
    window = tokens + 2 * reach
    if tokens > 2 * reach:
        span = min(tokens, -(-3 * reach // LANES) * LANES)
        blocks = [(0, 0, reach, span, 0), (tokens - reach, window - span, reach, span, reach)]
    else:
        blocks = [(0, 0, tokens, window, 0)]
    rows = sum(b[2] for b in blocks)
    return pl.pallas_call(
        functools.partial(edge_kernel, len(lows), blocks),
        in_specs=[VMEM] * (4 + 2 * len(lows)),
        out_specs=VMEM,
        out_shape=jax.ShapeDtypeStruct((rows, width), jnp.bfloat16),
        scratch_shapes=[
            pltpu.VMEM((window, width), jnp.bfloat16),
            pltpu.VMEM((window, width), jnp.bfloat16),
            pltpu.VMEM((window, LANES), jnp.float32),
        ],
        compiler_params=PARAMS,
        cost_estimate=attend_cost(rows, blocks[0][3], width),
        name="attend_edges",
    )(queries, keys, values, code, *lows, *highs)


def pack_kernel(rows, k_ref, v_ref, code_ref, tail_ref, head_ref):
    tokens, width = k_ref.shape
    code = columns(code_ref[...]).astype(jnp.bfloat16)
    for ref, part in ((tail_ref, slice(tokens - rows, tokens)), (head_ref, slice(0, rows))):
        ref[:, :width] = k_ref[part]
        ref[:, width : 2 * width] = v_ref[part]
        ref[:, 2 * width :] = code[part]


def pack_ends(keys, values, code, rows):
    width = keys.shape[1]
    return pl.pallas_call(
        functools.partial(pack_kernel, rows),
        in_specs=[VMEM] * 3,
        out_specs=[VMEM] * 2,
        out_shape=[jax.ShapeDtypeStruct((rows, 2 * width + LANES), jnp.bfloat16)] * 2,
        compiler_params=PARAMS,
        cost_estimate=pl.CostEstimate(flops=0, bytes_accessed=16 * rows * width, transcendentals=0),
        name="pack_ends",
    )(keys, values, code)


def term_kernel(row_ref, root_ref, grad_ref, gate_ref, out_ref):
    tokens = grad_ref.shape[0]
    wanted = lax.broadcasted_iota(jnp.int32, (tokens, tokens), 0)
    selector = jnp.where(wanted == row_ref[...], 1.0, 0.0).astype(jnp.bfloat16)
    grads = grad_ref[...]
    summed = jnp.dot(selector, grads, preferred_element_type=jnp.float32)
    term = gate_ref[...] * summed + root_ref[0] * grads.astype(jnp.float32)
    out_ref[...] = term.astype(jnp.bfloat16)


def grad_terms(local_rows, root, grads, gate):
    tokens, width = grads.shape
    return pl.pallas_call(
        term_kernel,
        in_specs=[VMEM, pl.BlockSpec(memory_space=pltpu.SMEM), VMEM, VMEM],
        out_specs=VMEM,
        out_shape=jax.ShapeDtypeStruct((tokens, width), jnp.bfloat16),
        compiler_params=PARAMS,
        cost_estimate=pl.CostEstimate(
            flops=2 * tokens * tokens * width, bytes_accessed=4 * tokens * width, transcendentals=0
        ),
        name="grad_terms",
    )(local_rows, root, grads, gate)


def relay_kernel(reach, row_ref, gate_ref, *refs):
    out_ref = refs[-1]
    count = (len(refs) - 1) // 2
    tokens = out_ref.shape[0]
    rows = row_ref[...]
    if count == 2:
        spots = [(reach, tokens - 2 * reach, 0, 0), (0, reach, 1, 0), (tokens - reach, reach, 1, reach)]
        low, high = rows < reach, rows >= tokens - reach
        place = jnp.where(low, rows + tokens - 2 * reach, jnp.where(high, rows, rows - reach))
    else:
        spots = [(0, tokens, 0, 0)]
        place = rows
    wanted = lax.broadcasted_iota(jnp.int32, (tokens, tokens), 0)
    selector = jnp.where(wanted == place, 1.0, 0.0).T.astype(jnp.bfloat16)
    branch = jnp.concatenate([ref[...] for ref in refs[count : 2 * count]], axis=0)
    relayed = gate_ref[...] * jnp.dot(selector, branch, preferred_element_type=jnp.float32)
    for top, size, piece, at in spots:
        own = refs[piece][at : at + size].astype(jnp.float32)
        out_ref[top : top + size] = (own + relayed[top : top + size]).astype(jnp.bfloat16)


def relay(local_rows, gate, own, branch, reach):
    tokens = sum(p.shape[0] for p in own)
    width = own[0].shape[1]
    return pl.pallas_call(
        functools.partial(relay_kernel, reach),
        in_specs=[VMEM] * (2 + 2 * len(own)),
        out_specs=VMEM,
        out_shape=jax.ShapeDtypeStruct((tokens, width), jnp.bfloat16),
        compiler_params=PARAMS,
        cost_estimate=pl.CostEstimate(
            flops=2 * tokens * tokens * width, bytes_accessed=6 * tokens * width, transcendentals=0
        ),
        name="relay",
    )(local_rows, gate, *own, *branch)


def whole_gate(gate):
    ranks = lax.axis_size("rep")
    if ranks != 2:
        return lax.all_gather(gate, "rep", axis=0, tiled=True)
    other = lax.ppermute(gate, "rep", [(0, 1), (1, 0)])
    first = lax.axis_index("rep") == 0
    return jnp.concatenate([jnp.where(first, gate, other), jnp.where(first, other, gate)])


def from_branch(rows, group):
    if lax.axis_size("grp") != 4:
        return lax.psum(jnp.where(group == 0, rows, jnp.zeros_like(rows)), "grp")
    got = lax.ppermute(rows, "grp", [(0, 1)])
    hold = jnp.where(group == 1, got, rows)
    last = lax.ppermute(hold, "grp", [(0, 2), (1, 3)])
    return jnp.where(group <= 1, hold, last)


def local(query_rows, key_rows, value_rows, view_frame, control_row, control_gate, out_grad):
    queries, keys, values = query_rows[0, 0], key_rows[0, 0], value_rows[0, 0]
    tokens, width = queries.shape
    length = tokens * lax.axis_size("seq")
    reach = 2 * (length // 32)
    hops = (reach + tokens - 1) // tokens
    group = lax.axis_index("grp")

    gate = whole_gate(control_gate)[None]
    tag = view_frame[0, 0]
    code = (tag + 8 * (tag // FRAMES) + 16).astype(jnp.float32)[None]
    most = min(tokens, reach)
    tail, head = pack_ends(keys, values, code, most)
    lows, highs = [], []
    for hop in range(1, hops + 1):
        rows = min(tokens, reach - (hop - 1) * tokens)
        lows.insert(0, shifted(tail[most - rows :], "seq", hop))
        highs.append(shifted(head[:rows], "seq", -hop))

    local_rows = (control_row[0] % tokens).astype(jnp.int32)
    root = (group == 0).astype(jnp.float32)[None]
    terms = grad_terms(local_rows, root, out_grad[0, 0], gate)
    branch_grad = lax.psum(terms, "grp")

    own = [attend_edges(queries, keys, values, code, lows, highs, reach)]
    if tokens > 2 * reach:
        own.insert(0, attend_middle(queries, keys, values, code, reach))
    branch = [from_branch(piece, group) for piece in own]
    block_out = relay(local_rows, gate, own, branch, reach)
    return (block_out[None, None], branch_grad[None])


def solution(mesh):
    placed = (
        P("rep", "grp", "seq", None),
        P("rep", "grp", "seq", None),
        P("rep", "grp", "seq", None),
        P("rep", "grp", "seq"),
        P("rep", "grp", "seq"),
        P("rep"),
        P("rep", "grp", "seq", None),
    )
    return jax.shard_map(
        local,
        mesh=mesh,
        in_specs=placed,
        out_specs=(P("rep", "grp", "seq", None), P("rep", "seq", None)),
        check_vma=False,
    )
```

```python
import functools
import math

import jax
import jax.numpy as jnp
from jax import lax
from jax.experimental import pallas as pl
from jax.experimental.pallas import tpu as pltpu
from jax.sharding import PartitionSpec as P

HEADS = 32
DH = 80
FRAMES = 20
LANES = 128
VMEM_LIMIT = 48 * 1024 * 1024


def shifted(block, axis, distance):
    devices = range(lax.axis_size(axis))
    route = [(i - distance, i) for i in devices if i - distance in devices]
    return lax.ppermute(block, axis, route)


def lane_windows(heads):
    windows = []
    for head in range(heads):
        first, last = head * DH, (head + 1) * DH
        if windows and last <= windows[-1][0] + 2 * LANES:
            windows[-1][1].append(head)
        else:
            windows.append((first // LANES * LANES, [head]))
    out = []
    for start, members in windows:
        start = min(start, heads * DH - 2 * LANES)
        out.append((start, members))
    return out


def head_masks(rows, period):
    masks = {}
    for start, members in lane_windows(period // DH):
        lane = lax.broadcasted_iota(jnp.int32, (rows, 2 * LANES), 1) + start
        for h in members:
            inside = (lane >= h * DH) & (lane < (h + 1) * DH)
            masks[h] = jnp.where(inside, 1.0, 0.0).astype(jnp.bfloat16)
    return masks


def mixed_period(base, bias, query, key, value, masks, period):
    rows = bias.shape[0]
    factor = math.log2(math.e) / math.sqrt(DH)
    windows = lane_windows(period // DH)
    scores = []
    for start, members in windows:
        lanes = slice(base + start, base + start + 2 * LANES)
        part = query(lanes)
        stacked = jnp.concatenate([part * masks[h] for h in members], axis=0)
        scores.append(
            lax.dot_general(
                stacked, key(lanes), (((1,), (1,)), ((), ())), preferred_element_type=jnp.float32
            )
        )
    weights = []
    for part, (start, members) in zip(scores, windows):
        part = part.reshape(len(members), rows, -1) + bias[None]
        largest = jnp.max(part, axis=-1, keepdims=True)
        powers = jnp.exp2((part - largest) * factor)
        totals = jnp.sum(powers, axis=-1, keepdims=True)
        weight = (powers * (1.0 / totals)).astype(jnp.bfloat16)
        weights.append(weight.reshape(len(members) * rows, -1))
    tiles = {}
    for weight, (start, members) in zip(weights, windows):
        lanes = slice(base + start, base + start + 2 * LANES)
        mixed = jnp.dot(weight, value(lanes), preferred_element_type=jnp.float32)
        for n, h in enumerate(members):
            for t in range(2):
                low = start + t * LANES
                if h * DH >= low + LANES or (h + 1) * DH <= low:
                    continue
                piece = mixed[n * rows : (n + 1) * rows, t * LANES : (t + 1) * LANES]
                if low in tiles:
                    lane = lax.broadcasted_iota(jnp.int32, (rows, LANES), 1) + low
                    tiles[low] = jnp.where(lane >= h * DH, piece, tiles[low])
                else:
                    tiles[low] = piece
    return {low: tile.astype(jnp.bfloat16) for low, tile in tiles.items()}


def frame_code(tag_ref):
    tag = tag_ref[...].astype(jnp.float32)
    return tag + 8.0 * jnp.floor((tag + 0.5) * (1.0 / FRAMES)) + 16.0


def columns(row):
    return jnp.broadcast_to(row, (LANES, row.shape[1])).T


def attend_blocks(blocks, q_ref, out_ref):
    width = q_ref.shape[1]
    period = math.lcm(DH, LANES)
    masks = {}
    work = []
    for top, rows, at, mine, theirs, key, value in blocks:
        if rows not in masks:
            masks[rows] = head_masks(rows, period)
        bias = jnp.where(jnp.abs(mine[:, :1] - theirs.T[:rows]) <= 1.5, 0.0, -1e30)
        work.append((top, rows, at, bias, key, value))
    for base in range(0, width, period):
        for top, rows, at, bias, key, value in work:
            tiles = mixed_period(
                base, bias, lambda lanes: q_ref[top : top + rows, lanes], key, value, masks[rows], period
            )
            for low, tile in tiles.items():
                out_ref[at : at + rows, base + low : base + low + LANES] = tile


def middle_kernel(reach, q_ref, k_ref, v_ref, tag_ref, out_ref):
    rows = q_ref.shape[0] - 2 * reach
    code = columns(frame_code(tag_ref))
    key = lambda lanes: k_ref[:, lanes]
    value = lambda lanes: v_ref[:, lanes]
    attend_blocks(
        [(reach, rows, 0, code[reach : reach + rows], code, key, value)], q_ref, out_ref
    )


def edge_kernel(hops, reach, *refs):
    q_ref, k_ref, v_ref, tag_ref = refs[:4]
    lows = refs[4 : 4 + hops]
    highs = refs[4 + hops : 4 + 2 * hops]
    out_ref = refs[-1]
    tokens, width = q_ref.shape
    code = columns(frame_code(tag_ref))

    def joined(before, first, last, after):
        def lanes_of(ref, own, shift):
            def take(lanes):
                moved = slice(lanes.start + shift, lanes.stop + shift)
                parts = [piece[:, moved] for piece in before]
                parts.append(own[first:last, lanes])
                parts.extend(piece[:, moved] for piece in after)
                return jnp.concatenate(parts, axis=0)

            return take

        parts = [piece[:, 2 * width :].astype(jnp.float32) for piece in before]
        parts.append(code[first:last])
        parts.extend(piece[:, 2 * width :].astype(jnp.float32) for piece in after)
        codes = jnp.concatenate(parts, axis=0)
        return codes, lanes_of(None, k_ref, 0), lanes_of(None, v_ref, width)

    if tokens > 2 * reach:
        last = tokens - reach
        blocks = [
            (0, reach, 0, code[:reach], *joined(lows, 0, 2 * reach, ())),
            (last, reach, reach, code[last:], *joined((), tokens - 2 * reach, tokens, highs)),
        ]
    else:
        blocks = [(0, tokens, 0, code, *joined(lows, 0, tokens, highs))]
    attend_blocks(blocks, q_ref, out_ref)


def attend_cost(tokens, span, width):
    return pl.CostEstimate(
        flops=HEADS * tokens * span * 2 * LANES * 4,
        bytes_accessed=12 * tokens * width,
        transcendentals=HEADS * tokens * span,
    )


VMEM = pl.BlockSpec(memory_space=pltpu.VMEM)
PARAMS = pltpu.CompilerParams(vmem_limit_bytes=VMEM_LIMIT)


def attend_middle(queries, keys, values, tags, reach):
    tokens, width = queries.shape
    return pl.pallas_call(
        functools.partial(middle_kernel, reach),
        in_specs=[VMEM] * 4,
        out_specs=VMEM,
        out_shape=jax.ShapeDtypeStruct((tokens - 2 * reach, width), jnp.bfloat16),
        compiler_params=PARAMS,
        cost_estimate=attend_cost(tokens - 2 * reach, tokens, width),
        name="attend_middle",
    )(queries, keys, values, tags)


def attend_edges(queries, keys, values, tags, lows, highs, reach):
    tokens, width = queries.shape
    rows = min(tokens, 2 * reach)
    return pl.pallas_call(
        functools.partial(edge_kernel, len(lows), reach),
        in_specs=[VMEM] * (4 + 2 * len(lows)),
        out_specs=VMEM,
        out_shape=jax.ShapeDtypeStruct((rows, width), jnp.bfloat16),
        compiler_params=PARAMS,
        cost_estimate=attend_cost(rows, LANES, width),
        name="attend_edges",
    )(queries, keys, values, tags, *lows, *highs)


def pack_kernel(most, k_ref, v_ref, grad_ref, tag_ref, row_ref, sent_ref, tail_ref, head_ref, sems):
    tokens, width = k_ref.shape
    ends = ((tail_ref, tokens - most), (head_ref, 0))
    copies = [pltpu.make_async_copy(grad_ref, sent_ref.at[:, pl.ds(0, width)], sems.at[0])]
    for n, (ref, first) in enumerate(ends):
        for m, source in enumerate((k_ref, v_ref)):
            copies.append(
                pltpu.make_async_copy(
                    source.at[pl.ds(first, most)],
                    ref.at[:, pl.ds(m * width, width)],
                    sems.at[1 + 2 * n + m],
                )
            )
    for copy in copies:
        copy.start()
    code = columns(frame_code(tag_ref)).astype(jnp.bfloat16)
    for ref, first in ends:
        ref[:, 2 * width :] = code[first : first + most]
    row = row_ref[...].astype(jnp.float32)
    place = row - tokens * jnp.floor((row + 0.5) * (1.0 / tokens))
    sent_ref[:, width:] = columns(place).astype(jnp.bfloat16)
    for copy in copies:
        copy.wait()


def pack(keys, values, grads, tags, rows, most):
    tokens, width = keys.shape
    anywhere = pl.BlockSpec(memory_space=pl.ANY)
    ends = jax.ShapeDtypeStruct((most, 2 * width + LANES), jnp.bfloat16)
    return pl.pallas_call(
        functools.partial(pack_kernel, most),
        in_specs=[anywhere] * 3 + [VMEM] * 2,
        out_specs=[VMEM] * 3,
        out_shape=[jax.ShapeDtypeStruct((tokens, width + LANES), jnp.bfloat16), ends, ends],
        scratch_shapes=[pltpu.SemaphoreType.DMA((5,))],
        compiler_params=PARAMS,
        cost_estimate=pl.CostEstimate(
            flops=0, bytes_accessed=4 * tokens * width + 16 * most * width, transcendentals=0
        ),
        name="pack",
    )(keys, values, grads, tags, rows)


def selector(row):
    tokens = row.shape[1]
    wanted = lax.broadcasted_iota(jnp.int32, (tokens, tokens), 0).astype(jnp.float32)
    return jnp.where(wanted == row, 1.0, 0.0)


def sums_kernel(sizes, flag_ref, mine_ref, theirs_ref, gate_ref, *out_refs):
    tokens = mine_ref.shape[0]
    width = gate_ref.shape[1]
    picks, rows = [], []
    for ref in (mine_ref, theirs_ref):
        place = ref[:, width : width + LANES].astype(jnp.float32).T[:1]
        picks.append(selector(place).astype(jnp.bfloat16))
        rows.append(ref[:, :width])
    summed = jnp.dot(
        jnp.concatenate(picks, axis=1),
        jnp.concatenate(rows, axis=0),
        preferred_element_type=jnp.float32,
    )
    term = gate_ref[...] * summed + flag_ref[0] * rows[1].astype(jnp.float32)
    term = term.astype(jnp.bfloat16)
    at = 0
    for ref, size in zip(out_refs, sizes):
        ref[...] = term[at : at + size]
        at += size


def pair_sums(flag, mine, theirs, gate, sizes):
    tokens, width = mine.shape[0], gate.shape[1]
    return pl.pallas_call(
        functools.partial(sums_kernel, sizes),
        in_specs=[pl.BlockSpec(memory_space=pltpu.SMEM)] + [VMEM] * 3,
        out_specs=[VMEM] * len(sizes),
        out_shape=[jax.ShapeDtypeStruct((size, width), jnp.bfloat16) for size in sizes],
        compiler_params=PARAMS,
        cost_estimate=pl.CostEstimate(
            flops=4 * tokens * tokens * width, bytes_accessed=6 * tokens * width, transcendentals=0
        ),
        name="pair_sums",
    )(flag, mine, theirs, gate)


def relay_kernel(reach, row_ref, gate_ref, *refs):
    out_ref = refs[-1]
    count = (len(refs) - 1) // 2
    tokens = out_ref.shape[0]
    row = row_ref[...].astype(jnp.float32)
    rows = row - tokens * jnp.floor((row + 0.5) * (1.0 / tokens))
    if count == 2:
        spots = [(reach, tokens - 2 * reach, 0, 0), (0, reach, 1, 0), (tokens - reach, reach, 1, reach)]
        low, high = rows < reach, rows >= tokens - reach
        place = jnp.where(low, rows + tokens - 2 * reach, jnp.where(high, rows, rows - reach))
    else:
        spots = [(0, tokens, 0, 0)]
        place = rows
    picks = selector(place).T.astype(jnp.bfloat16)
    branch = jnp.concatenate([ref[...] for ref in refs[count : 2 * count]], axis=0)
    relayed = gate_ref[...] * jnp.dot(picks, branch, preferred_element_type=jnp.float32)
    for top, size, piece, at in spots:
        own = refs[piece][at : at + size].astype(jnp.float32)
        out_ref[top : top + size] = (own + relayed[top : top + size]).astype(jnp.bfloat16)


def relay(rows, gate, own, branch, reach):
    tokens = sum(p.shape[0] for p in own)
    width = own[0].shape[1]
    return pl.pallas_call(
        functools.partial(relay_kernel, reach),
        in_specs=[VMEM] * (2 + 2 * len(own)),
        out_specs=VMEM,
        out_shape=jax.ShapeDtypeStruct((tokens, width), jnp.bfloat16),
        compiler_params=PARAMS,
        cost_estimate=pl.CostEstimate(
            flops=2 * tokens * tokens * width, bytes_accessed=6 * tokens * width, transcendentals=0
        ),
        name="relay",
    )(rows, gate, *own, *branch)


def whole_gate(gate):
    ranks = lax.axis_size("rep")
    if ranks != 2:
        return lax.all_gather(gate, "rep", axis=0, tiled=True)
    other = lax.ppermute(gate, "rep", [(0, 1), (1, 0)])
    first = lax.axis_index("rep") == 0
    return jnp.concatenate([jnp.where(first, gate, other), jnp.where(first, other, gate)])


def over_square(block, even, odd):
    ranks = lax.axis_size("rep")
    route = []
    for rank in range(ranks):
        for source, target in odd if rank % 2 else even:
            route.append((source * ranks + rank, target * ranks + rank))
    return lax.ppermute(block, ("grp", "rep"), route)


FIRST_EVEN = [(0, 2), (1, 3)]
FIRST_ODD = [(0, 1), (2, 3)]
SECOND_EVEN = [(0, 1), (2, 3), (3, 2)]
SECOND_ODD = [(0, 2), (1, 3), (3, 1)]
THIRD_EVEN = [(0, 2), (2, 0), (1, 3), (3, 1)]
THIRD_ODD = [(0, 1), (1, 0), (2, 3), (3, 2)]


def local(query_rows, key_rows, value_rows, view_frame, control_row, control_gate, out_grad):
    queries, keys, values = query_rows[0, 0], key_rows[0, 0], value_rows[0, 0]
    tags, rows = view_frame[0], control_row[0]
    tokens, width = queries.shape
    length = tokens * lax.axis_size("seq")
    reach = 2 * (length // 32)
    hops = (reach + tokens - 1) // tokens
    group = lax.axis_index("grp")
    odd = lax.axis_index("rep") % 2
    source = group == 0
    relaying = group == 1 + odd
    root_partner = group == 2 - odd

    gate = whole_gate(control_gate)[None]
    most = min(tokens, reach)
    sent, tail, head = pack(keys, values, out_grad[0, 0], tags, rows, most)
    got = over_square(sent, FIRST_EVEN, FIRST_ODD)
    lows, highs = [], []
    for hop in range(1, hops + 1):
        count = min(tokens, reach - (hop - 1) * tokens)
        lows.insert(0, shifted(tail[most - count :], "seq", hop))
        highs.append(shifted(head[:count], "seq", -hop))

    own = [attend_edges(queries, keys, values, tags, lows, highs, reach)]
    if tokens > 2 * reach:
        own.insert(0, attend_middle(queries, keys, values, tags, reach))
    sizes = [piece.shape[0] for piece in own]
    sums = pair_sums(root_partner.astype(jnp.float32)[None], sent, got, gate, sizes)
    branch, totals = [], []
    for piece, part in zip(own, sums):
        first = over_square(jnp.where(source, piece, part), SECOND_EVEN, SECOND_ODD)
        total = (part.astype(jnp.float32) + first.astype(jnp.float32)).astype(jnp.bfloat16)
        held = jnp.where(source, piece, first)
        last = over_square(jnp.where(source | relaying, held, total), THIRD_EVEN, THIRD_ODD)
        branch.append(jnp.where(source | relaying, held, last))
        totals.append(jnp.where(source | relaying, last, total))
    branch_grad = jnp.concatenate(totals, axis=0)
    block_out = relay(rows, gate, own, branch, reach)
    return (block_out[None, None], branch_grad[None])


def solution(mesh):
    placed = (
        P("rep", "grp", "seq", None),
        P("rep", "grp", "seq", None),
        P("rep", "grp", "seq", None),
        P("rep", "grp", "seq"),
        P("rep", "grp", "seq"),
        P("rep"),
        P("rep", "grp", "seq", None),
    )
    return jax.shard_map(
        local,
        mesh=mesh,
        in_specs=placed,
        out_specs=(P("rep", "grp", "seq", None), P("rep", "seq", None)),
        check_vma=False,
    )
```

```python
import functools
import math

import jax
import jax.numpy as jnp
from jax import lax
from jax.experimental import pallas as pl
from jax.experimental.pallas import tpu as pltpu
from jax.sharding import PartitionSpec as P

HEADS = 32
DH = 80
FRAMES = 20
LANES = 128
VMEM_LIMIT = 48 * 1024 * 1024
PACK_LIMIT = 62 * 1024 * 1024


def shifted(block, axis, distance):
    devices = range(lax.axis_size(axis))
    route = [(i - distance, i) for i in devices if i - distance in devices]
    return lax.ppermute(block, axis, route)


def lane_windows(heads):
    windows = []
    for head in range(heads):
        first, last = head * DH, (head + 1) * DH
        if windows and last <= windows[-1][0] + 2 * LANES:
            windows[-1][1].append(head)
        else:
            windows.append((first // LANES * LANES, [head]))
    out = []
    for start, members in windows:
        start = min(start, heads * DH - 2 * LANES)
        out.append((start, members))
    return out


def head_masks(rows, period):
    masks = {}
    for start, members in lane_windows(period // DH):
        lane = lax.broadcasted_iota(jnp.int32, (rows, 2 * LANES), 1) + start
        for h in members:
            inside = (lane >= h * DH) & (lane < (h + 1) * DH)
            masks[h] = jnp.where(inside, 1.0, 0.0).astype(jnp.bfloat16)
    return masks


def mixed_period(base, bias, query, key, value, masks, period):
    rows = bias.shape[0]
    factor = math.log2(math.e) / math.sqrt(DH)
    windows = lane_windows(period // DH)
    scores = []
    for start, members in windows:
        lanes = slice(base + start, base + start + 2 * LANES)
        part = query(lanes)
        stacked = jnp.concatenate([part * masks[h] for h in members], axis=0)
        scores.append(
            lax.dot_general(
                stacked, key(lanes), (((1,), (1,)), ((), ())), preferred_element_type=jnp.float32
            )
        )
    weights = []
    for part, (start, members) in zip(scores, windows):
        part = part.reshape(len(members), rows, -1) + bias[None]
        largest = jnp.max(part, axis=-1, keepdims=True)
        powers = jnp.exp2((part - largest) * factor)
        totals = jnp.sum(powers, axis=-1, keepdims=True)
        weight = (powers * (1.0 / totals)).astype(jnp.bfloat16)
        weights.append(weight.reshape(len(members) * rows, -1))
    tiles = {}
    for weight, (start, members) in zip(weights, windows):
        lanes = slice(base + start, base + start + 2 * LANES)
        mixed = jnp.dot(weight, value(lanes), preferred_element_type=jnp.float32)
        for n, h in enumerate(members):
            for t in range(2):
                low = start + t * LANES
                if h * DH >= low + LANES or (h + 1) * DH <= low:
                    continue
                piece = mixed[n * rows : (n + 1) * rows, t * LANES : (t + 1) * LANES]
                if low in tiles:
                    lane = lax.broadcasted_iota(jnp.int32, (rows, LANES), 1) + low
                    tiles[low] = jnp.where(lane >= h * DH, piece, tiles[low])
                else:
                    tiles[low] = piece
    return {low: tile.astype(jnp.bfloat16) for low, tile in tiles.items()}


def frame_code(tag_ref):
    tag = tag_ref[...].astype(jnp.float32)
    return tag + 8.0 * jnp.floor((tag + 0.5) * (1.0 / FRAMES)) + 16.0


def placed(row_ref):
    tokens = row_ref.shape[1]
    row = row_ref[...].astype(jnp.float32)
    return row - tokens * jnp.floor((row + 0.5) * (1.0 / tokens))


def columns(row):
    return jnp.broadcast_to(row, (LANES, row.shape[1])).T


def attend_blocks(blocks, q_ref, out_ref):
    width = q_ref.shape[1]
    period = math.lcm(DH, LANES)
    masks = {}
    work = []
    for top, rows, at, mine, theirs, key, value in blocks:
        if rows not in masks:
            masks[rows] = head_masks(rows, period)
        bias = jnp.where(jnp.abs(mine[:, :1] - theirs.T[:rows]) <= 1.5, 0.0, -1e30)
        work.append((top, rows, at, bias, key, value))
    for base in range(0, width, period):
        for top, rows, at, bias, key, value in work:
            tiles = mixed_period(
                base, bias, lambda lanes: q_ref[top : top + rows, lanes], key, value, masks[rows], period
            )
            for low, tile in tiles.items():
                out_ref[at : at + rows, base + low : base + low + LANES] = tile


def middle_kernel(reach, q_ref, k_ref, v_ref, tag_ref, out_ref):
    rows = q_ref.shape[0] - 2 * reach
    code = columns(frame_code(tag_ref))
    key = lambda lanes: k_ref[:, lanes]
    value = lambda lanes: v_ref[:, lanes]
    attend_blocks(
        [(reach, rows, 0, code[reach : reach + rows], code, key, value)], q_ref, out_ref
    )


def edge_kernel(hops, reach, *refs):
    q_ref, k_ref, v_ref, tag_ref = refs[:4]
    lows = refs[4 : 4 + hops]
    highs = refs[4 + hops : 4 + 2 * hops]
    out_ref = refs[-1]
    tokens, width = q_ref.shape
    code = columns(frame_code(tag_ref))

    def joined(before, first, last, after):
        def lanes_of(ref, own, shift):
            def take(lanes):
                moved = slice(lanes.start + shift, lanes.stop + shift)
                parts = [piece[:, moved] for piece in before]
                parts.append(own[first:last, lanes])
                parts.extend(piece[:, moved] for piece in after)
                return jnp.concatenate(parts, axis=0)

            return take

        parts = [piece[:, 2 * width :].astype(jnp.float32) for piece in before]
        parts.append(code[first:last])
        parts.extend(piece[:, 2 * width :].astype(jnp.float32) for piece in after)
        codes = jnp.concatenate(parts, axis=0)
        return codes, lanes_of(None, k_ref, 0), lanes_of(None, v_ref, width)

    if tokens > 2 * reach:
        last = tokens - reach
        held = min(tokens, -(-3 * reach // LANES) * LANES - reach)
        blocks = [
            (0, reach, 0, code[:reach], *joined(lows, 0, held, ())),
            (last, reach, reach, code[last:], *joined((), tokens - held, tokens, highs)),
        ]
    else:
        blocks = [(0, tokens, 0, code, *joined(lows, 0, tokens, highs))]
    attend_blocks(blocks, q_ref, out_ref)


def attend_cost(tokens, span, width):
    return pl.CostEstimate(
        flops=HEADS * tokens * span * 2 * LANES * 4,
        bytes_accessed=12 * tokens * width,
        transcendentals=HEADS * tokens * span,
    )


VMEM = pl.BlockSpec(memory_space=pltpu.VMEM)
PARAMS = pltpu.CompilerParams(vmem_limit_bytes=VMEM_LIMIT)


def attend_middle(queries, keys, values, tags, reach):
    tokens, width = queries.shape
    return pl.pallas_call(
        functools.partial(middle_kernel, reach),
        in_specs=[VMEM] * 4,
        out_specs=VMEM,
        out_shape=jax.ShapeDtypeStruct((tokens - 2 * reach, width), jnp.bfloat16),
        compiler_params=PARAMS,
        cost_estimate=attend_cost(tokens - 2 * reach, tokens, width),
        name="attend_middle",
    )(queries, keys, values, tags)


def attend_edges(queries, keys, values, tags, lows, highs, reach):
    tokens, width = queries.shape
    rows = min(tokens, 2 * reach)
    return pl.pallas_call(
        functools.partial(edge_kernel, len(lows), reach),
        in_specs=[VMEM] * (4 + 2 * len(lows)),
        out_specs=VMEM,
        out_shape=jax.ShapeDtypeStruct((rows, width), jnp.bfloat16),
        compiler_params=PARAMS,
        cost_estimate=attend_cost(rows, LANES, width),
        name="attend_edges",
    )(queries, keys, values, tags, *lows, *highs)


def pack_kernel(most, k_ref, v_ref, grad_ref, tag_ref, row_ref, *refs):
    first_ref, second_ref, tail_ref, head_ref, tags, rows, codes, places, sems, small_sems = refs
    tokens, width = k_ref.shape
    half = width // 2
    ends = ((tail_ref, tokens - most), (head_ref, 0))
    small = [
        pltpu.make_async_copy(tag_ref, tags, small_sems.at[0]),
        pltpu.make_async_copy(row_ref, rows, small_sems.at[1]),
    ]
    copies = []
    for n, (ref, first) in enumerate(ends):
        for m, source in enumerate((k_ref, v_ref)):
            copies.append(
                pltpu.make_async_copy(
                    source.at[pl.ds(first, most)],
                    ref.at[:, pl.ds(m * width, width)],
                    sems.at[2 * n + m],
                )
            )
    for n, ref in enumerate((first_ref, second_ref)):
        copies.append(
            pltpu.make_async_copy(
                grad_ref.at[:, pl.ds(n * half, half)], ref.at[:, pl.ds(0, half)], sems.at[4 + n]
            )
        )
    for copy in small + copies:
        copy.start()
    for copy in small:
        copy.wait()
    codes[...] = columns(frame_code(tags)).astype(jnp.bfloat16)
    places[...] = columns(placed(rows)).astype(jnp.bfloat16)
    marks = []
    for n, (ref, first) in enumerate(ends):
        marks.append(
            pltpu.make_async_copy(
                codes.at[pl.ds(first, most)], ref.at[:, pl.ds(2 * width, LANES)], sems.at[6 + n]
            )
        )
    for n, ref in enumerate((first_ref, second_ref)):
        marks.append(
            pltpu.make_async_copy(places, ref.at[:, pl.ds(half, LANES)], sems.at[8 + n])
        )
    for copy in marks:
        copy.start()
    for copy in copies + marks:
        copy.wait()


def pack(keys, values, grads, tags, rows, most):
    tokens, width = keys.shape
    ends = jax.ShapeDtypeStruct((most, 2 * width + LANES), jnp.bfloat16)
    halves = jax.ShapeDtypeStruct((tokens, width // 2 + LANES), jnp.bfloat16)
    return pl.pallas_call(
        functools.partial(pack_kernel, most),
        in_specs=[pl.BlockSpec(memory_space=pltpu.HBM)] * 5,
        out_specs=[pl.BlockSpec(memory_space=pltpu.HBM)] * 4,
        out_shape=[halves, halves, ends, ends],
        scratch_shapes=[
            pltpu.VMEM((1, tokens), jnp.int32),
            pltpu.VMEM((1, tokens), jnp.int32),
            pltpu.VMEM((tokens, LANES), jnp.bfloat16),
            pltpu.VMEM((tokens, LANES), jnp.bfloat16),
            pltpu.SemaphoreType.DMA((10,)),
            pltpu.SemaphoreType.DMA((2,)),
        ],
        compiler_params=pltpu.CompilerParams(vmem_limit_bytes=PACK_LIMIT),
        cost_estimate=pl.CostEstimate(
            flops=0, bytes_accessed=4 * tokens * width + 16 * most * width, transcendentals=0
        ),
        name="pack",
    )(keys, values, grads, tags, rows)


def selector(row):
    tokens = row.shape[1]
    wanted = lax.broadcasted_iota(jnp.int32, (tokens, tokens), 0).astype(jnp.float32)
    return jnp.where(wanted == row, 1.0, 0.0)


def sums_kernel(sizes, flag_ref, gate_ref, *refs):
    half = gate_ref.shape[1] // 2
    count = len(sizes)
    for n in range(2):
        mine_ref, theirs_ref = refs[2 * n : 2 * n + 2]
        picks, rows = [], []
        for ref in (mine_ref, theirs_ref):
            place = ref[:, half : half + LANES].astype(jnp.float32).T[:1]
            picks.append(selector(place).astype(jnp.bfloat16))
            rows.append(ref[:, :half])
        summed = jnp.dot(
            jnp.concatenate(picks, axis=1),
            jnp.concatenate(rows, axis=0),
            preferred_element_type=jnp.float32,
        )
        term = gate_ref[:, n * half : (n + 1) * half] * summed
        term = (term + flag_ref[n] * rows[1].astype(jnp.float32)).astype(jnp.bfloat16)
        at = 0
        for ref, size in zip(refs[4 + n * count : 4 + (n + 1) * count], sizes):
            ref[...] = term[at : at + size]
            at += size


def pair_sums(flags, gate, parts, sizes):
    tokens, width = parts[0].shape[0], gate.shape[1]
    outs = [jax.ShapeDtypeStruct((size, width // 2), jnp.bfloat16) for size in sizes] * 2
    return pl.pallas_call(
        functools.partial(sums_kernel, sizes),
        in_specs=[pl.BlockSpec(memory_space=pltpu.SMEM)] + [VMEM] * 5,
        out_specs=[VMEM] * len(outs),
        out_shape=outs,
        compiler_params=PARAMS,
        cost_estimate=pl.CostEstimate(
            flops=4 * tokens * tokens * width, bytes_accessed=6 * tokens * width, transcendentals=0
        ),
        name="pair_sums",
    )(flags, gate, *parts)


def piece_spots(tokens, reach, piece):
    if tokens <= 2 * reach:
        return [(0, tokens, 0)]
    if piece == 0:
        return [(reach, tokens - 2 * reach, 0)]
    return [(0, reach, 0), (tokens - reach, reach, reach)]


def relay_kernel(spots, row_ref, gate_ref, first_ref, second_ref, base_ref, out_ref):
    tokens, width = out_ref.shape
    half = width // 2
    picks = selector(placed(row_ref)).T.astype(jnp.bfloat16)
    picks = jnp.concatenate([picks[:, top : top + size] for top, size, at in spots], axis=1)
    for n, ref in enumerate((first_ref, second_ref)):
        lanes = slice(n * half, (n + 1) * half)
        relayed = jnp.dot(picks, ref[...], preferred_element_type=jnp.float32)
        total = base_ref[:, lanes].astype(jnp.float32) + gate_ref[:, lanes] * relayed
        out_ref[:, lanes] = total.astype(out_ref.dtype)


def relay(rows, gate, first, second, base, spots, dtype):
    tokens, width = base.shape
    return pl.pallas_call(
        functools.partial(relay_kernel, spots),
        in_specs=[VMEM] * 5,
        out_specs=VMEM,
        out_shape=jax.ShapeDtypeStruct((tokens, width), dtype),
        compiler_params=PARAMS,
        cost_estimate=pl.CostEstimate(
            flops=2 * tokens * tokens * width, bytes_accessed=24 * tokens * width, transcendentals=0
        ),
        name="relay",
    )(rows, gate, first, second, base)


def whole_gate(gate):
    ranks = lax.axis_size("rep")
    if ranks != 2:
        return lax.all_gather(gate, "rep", axis=0, tiled=True)
    other = lax.ppermute(gate, "rep", [(0, 1), (1, 0)])
    first = lax.axis_index("rep") == 0
    return jnp.concatenate([jnp.where(first, gate, other), jnp.where(first, other, gate)])


FIRST_A, FIRST_B = [(0, 1), (2, 3)], [(0, 2), (1, 3)]
SECOND_A, SECOND_B = [(0, 1), (1, 3), (3, 2)], [(0, 2), (2, 3), (3, 1)]
SWAP_X, SWAP_Y = [(0, 1), (1, 0), (2, 3), (3, 2)], [(0, 2), (2, 0), (1, 3), (3, 1)]


def added(a, b):
    return (a.astype(jnp.float32) + b.astype(jnp.float32)).astype(a.dtype)


def local(query_rows, key_rows, value_rows, view_frame, control_row, control_gate, out_grad):
    queries, keys, values = query_rows[0, 0], key_rows[0, 0], value_rows[0, 0]
    tags, rows = view_frame[0], control_row[0]
    tokens, width = queries.shape
    half = width // 2
    length = tokens * lax.axis_size("seq")
    reach = 2 * (length // 32)
    hops = (reach + tokens - 1) // tokens
    group = lax.axis_index("grp")
    send = lambda block, route: lax.ppermute(block, "grp", route)

    most = min(tokens, reach)
    sent_a, sent_b, tail, head = pack(keys, values, out_grad[0, 0], tags, rows, most)
    got_a, got_b = send(sent_a, FIRST_A), send(sent_b, FIRST_B)
    lows, highs = [], []
    for hop in range(1, hops + 1):
        count = min(tokens, reach - (hop - 1) * tokens)
        lows.insert(0, shifted(tail[most - count :], "seq", hop))
        highs.append(shifted(head[:count], "seq", -hop))
    gate = whole_gate(control_gate)[None]

    own = []
    sizes = [min(tokens, 2 * reach)]
    if tokens > 2 * reach:
        own.append(attend_middle(queries, keys, values, tags, reach))
        sizes.insert(0, tokens - 2 * reach)
    flags = jnp.stack([group == 1, group == 2]).astype(jnp.float32)
    sums = pair_sums(flags, gate, (sent_a, got_a, sent_b, got_b), sizes)
    tags, *sums = lax.optimization_barrier((tags, *sums))
    own.append(attend_edges(queries, keys, values, tags, lows, highs, reach))

    count = len(own)
    spots = [piece_spots(tokens, reach, n) for n in range(count)]
    order = [
        own[n][at : at + size] for top, size, n, at in sorted(
            (top, size, n, at) for n in range(count) for top, size, at in spots[n]
        )
    ]
    block_out = jnp.concatenate(order, axis=0)
    totals = []
    for n, (piece, sum_a, sum_b) in enumerate(zip(own, sums[:count], sums[count:])):
        piece_a, piece_b = piece[:, :half], piece[:, half:]
        one = send(jnp.where(group == 0, piece_a, jnp.where(group == 1, sum_a, sum_b)), SECOND_A)
        two = send(jnp.where(group == 0, piece_b, jnp.where(group == 2, sum_b, sum_a)), SECOND_B)
        total_a = added(sum_a, jnp.where(group == 1, two, one))
        total_b = added(sum_b, jnp.where(group == 2, one, two))
        held_a = jnp.where(group == 0, piece_a, one)
        held_b = jnp.where(group == 0, piece_b, two)
        across = send(jnp.where((group == 0) | (group == 2), held_b, total_a), SWAP_X)
        down = send(jnp.where(group <= 1, held_a, total_b), SWAP_Y)
        branch_a = jnp.where(group <= 1, held_a, down)
        branch_b = jnp.where((group == 0) | (group == 2), held_b, across)
        dtype = jnp.bfloat16 if n == count - 1 else jnp.float32
        block_out = relay(rows, gate, branch_a, branch_b, block_out, spots[n], dtype)
        totals.append(
            jnp.concatenate(
                (
                    jnp.where((group == 0) | (group == 2), across, total_a),
                    jnp.where(group <= 1, down, total_b),
                ),
                axis=1,
            )
        )
    branch_grad = jnp.concatenate(totals, axis=0)
    return (block_out[None, None], branch_grad[None])


def solution(mesh):
    placed = (
        P("rep", "grp", "seq", None),
        P("rep", "grp", "seq", None),
        P("rep", "grp", "seq", None),
        P("rep", "grp", "seq"),
        P("rep", "grp", "seq"),
        P("rep"),
        P("rep", "grp", "seq", None),
    )
    return jax.shard_map(
        local,
        mesh=mesh,
        in_specs=placed,
        out_specs=(P("rep", "grp", "seq", None), P("rep", "seq", None)),
        check_vma=False,
    )
```

```python
import functools
import math

import jax
import jax.numpy as jnp
from jax import lax
from jax.experimental import pallas as pl
from jax.experimental.pallas import tpu as pltpu
from jax.sharding import PartitionSpec as P

HEADS = 32
DH = 80
FRAMES = 20
LANES = 128
VMEM_LIMIT = 48 * 1024 * 1024
PACK_LIMIT = 52 * 1024 * 1024


def shifted(block, axis, distance):
    devices = range(lax.axis_size(axis))
    route = [(i - distance, i) for i in devices if i - distance in devices]
    return lax.ppermute(block, axis, route)


def paired(block, axis, first):
    size = lax.axis_size(axis)
    route = []
    for i in range(size):
        other = i + 1 if (i - first) % 2 == 0 else i - 1
        route.append((i, other if 0 <= other < size else i))
    return lax.ppermute(block, axis, route)


def lane_windows(heads):
    windows = []
    for head in range(heads):
        first, last = head * DH, (head + 1) * DH
        if windows and last <= windows[-1][0] + 2 * LANES:
            windows[-1][1].append(head)
        else:
            windows.append((first // LANES * LANES, [head]))
    out = []
    for start, members in windows:
        start = min(start, heads * DH - 2 * LANES)
        out.append((start, members))
    return out


def head_masks(rows, period):
    masks = {}
    for start, members in lane_windows(period // DH):
        lane = lax.broadcasted_iota(jnp.int32, (rows, 2 * LANES), 1) + start
        for h in members:
            inside = (lane >= h * DH) & (lane < (h + 1) * DH)
            masks[h] = jnp.where(inside, 1.0, 0.0).astype(jnp.bfloat16)
    return masks


def mixed_period(base, query, sets, masks, period):
    rows = sets[0][0].shape[0]
    factor = math.log2(math.e) / math.sqrt(DH)
    windows = lane_windows(period // DH)
    scores = []
    for start, members in windows:
        lanes = slice(base + start, base + start + 2 * LANES)
        part = query(lanes)
        stacked = jnp.concatenate([part * masks[h] for h in members], axis=0)
        scores.append(
            [
                lax.dot_general(
                    stacked, key(lanes), (((1,), (1,)), ((), ())), preferred_element_type=jnp.float32
                )
                for bias, key, value in sets
            ]
        )
    weights = []
    for parts, (start, members) in zip(scores, windows):
        parts = [
            part.reshape(len(members), rows, -1) + bias[None]
            for part, (bias, key, value) in zip(parts, sets)
        ]
        largest = row_reduce(jnp.maximum, jnp.max, parts)
        powers = [jnp.exp2((part - largest) * factor) for part in parts]
        scale = 1.0 / row_reduce(jnp.add, jnp.sum, powers)
        weights.append(
            [(p * scale).astype(jnp.bfloat16).reshape(len(members) * rows, -1) for p in powers]
        )
    tiles = {}
    for parts, (start, members) in zip(weights, windows):
        lanes = slice(base + start, base + start + 2 * LANES)
        mixed = sum(
            jnp.dot(part, value(lanes), preferred_element_type=jnp.float32)
            for part, (bias, key, value) in zip(parts, sets)
        )
        for n, h in enumerate(members):
            for t in range(2):
                low = start + t * LANES
                if h * DH >= low + LANES or (h + 1) * DH <= low:
                    continue
                piece = mixed[n * rows : (n + 1) * rows, t * LANES : (t + 1) * LANES]
                if low in tiles:
                    lane = lax.broadcasted_iota(jnp.int32, (rows, LANES), 1) + low
                    tiles[low] = jnp.where(lane >= h * DH, piece, tiles[low])
                else:
                    tiles[low] = piece
    return {low: tile.astype(jnp.bfloat16) for low, tile in tiles.items()}


def row_reduce(pair, reduce, parts):
    if all(part.shape == parts[0].shape for part in parts):
        return reduce(functools.reduce(pair, parts), axis=-1, keepdims=True)
    return functools.reduce(pair, [reduce(part, axis=-1, keepdims=True) for part in parts])


def columns(row):
    return jnp.broadcast_to(row, (LANES, row.shape[1])).T


def link_bias(mine, theirs):
    return jnp.where(jnp.abs(mine[:, :1] - theirs.T[: mine.shape[0]]) <= 1.5, 0.0, -1e30)


def attend_block(query, sets, out_ref):
    rows, width = out_ref.shape
    period = math.lcm(DH, LANES)
    masks = head_masks(rows, period)
    for base in range(0, width, period):
        tiles = mixed_period(base, query, sets, masks, period)
        for low, tile in tiles.items():
            out_ref[:, base + low : base + low + LANES] = tile


def middle_kernel(reach, q_ref, k_ref, v_ref, code_ref, out_ref):
    rows = out_ref.shape[0]
    code = columns(code_ref[...])
    bias = link_bias(code[reach : reach + rows], code)
    own = (bias, lambda lanes: k_ref[:, lanes], lambda lanes: v_ref[:, lanes])
    attend_block(lambda lanes: q_ref[reach : reach + rows, lanes], [own], out_ref)


def edge_kernel(reach, valid_ref, q_ref, k_ref, v_ref, code_ref, *refs):
    halos = refs[:-4]
    out_ref, keys, values, codes = refs[-4:]
    tokens, width = q_ref.shape
    code = columns(code_ref[...])
    at = 0
    for n, piece in enumerate(halos):
        rows = piece.shape[0]
        keys[at : at + rows] = piece[:, :width]
        values[at : at + rows] = piece[:, width : 2 * width]
        there = valid_ref[n] if n < 2 else 1.0
        codes[at : at + rows] = piece[:, 2 * width :].astype(jnp.float32) * there
        at += rows
    if at < keys.shape[0]:
        spare = keys.shape[0] - at
        keys[at:] = jnp.zeros((spare, width), keys.dtype)
        values[at:] = jnp.zeros((spare, width), values.dtype)
        codes[at:] = jnp.zeros((spare, LANES), codes.dtype)
    if tokens > 2 * reach:
        last = tokens - reach
        mine = jnp.concatenate((code[:reach], code[last:]), axis=0)
        query = lambda lanes: jnp.concatenate((q_ref[:reach, lanes], q_ref[last:, lanes]), axis=0)
    else:
        mine = code
        query = lambda lanes: q_ref[:, lanes]
    own = (link_bias(mine, code), lambda lanes: k_ref[:, lanes], lambda lanes: v_ref[:, lanes])
    halo = (
        link_bias(mine, codes[...]),
        lambda lanes: keys[:, lanes],
        lambda lanes: values[:, lanes],
    )
    attend_block(query, [own, halo], out_ref)


def attend_cost(tokens, span, width):
    return pl.CostEstimate(
        flops=HEADS * tokens * span * 2 * LANES * 4,
        bytes_accessed=12 * tokens * width,
        transcendentals=HEADS * tokens * span,
    )


VMEM = pl.BlockSpec(memory_space=pltpu.VMEM)
SMEM = pl.BlockSpec(memory_space=pltpu.SMEM)
PARAMS = pltpu.CompilerParams(vmem_limit_bytes=VMEM_LIMIT)


def attend_middle(queries, keys, values, code, reach):
    tokens, width = queries.shape
    return pl.pallas_call(
        functools.partial(middle_kernel, reach),
        in_specs=[VMEM] * 4,
        out_specs=VMEM,
        out_shape=jax.ShapeDtypeStruct((tokens - 2 * reach, width), jnp.bfloat16),
        compiler_params=PARAMS,
        cost_estimate=attend_cost(tokens - 2 * reach, tokens, width),
        name="attend_middle",
    )(queries, keys, values, code)


def attend_edges(valid, queries, keys, values, code, halos, reach):
    tokens, width = queries.shape
    rows = min(tokens, 2 * reach)
    held = -(-2 * reach // LANES) * LANES
    return pl.pallas_call(
        functools.partial(edge_kernel, reach),
        in_specs=[SMEM] + [VMEM] * (4 + len(halos)),
        out_specs=VMEM,
        out_shape=jax.ShapeDtypeStruct((rows, width), jnp.bfloat16),
        scratch_shapes=[
            pltpu.VMEM((held, width), jnp.bfloat16),
            pltpu.VMEM((held, width), jnp.bfloat16),
            pltpu.VMEM((held, LANES), jnp.float32),
        ],
        compiler_params=PARAMS,
        cost_estimate=attend_cost(rows, LANES, width),
        name="attend_edges",
    )(valid, queries, keys, values, code, *halos)


def pack_kernel(most, first_ref, k_ref, v_ref, grad_ref, mark_ref, *refs):
    half_refs, end_refs, sems = refs[:2], refs[2:4], refs[4]
    width = k_ref.shape[1]
    half = width // 2
    copies = []
    for n, ref in enumerate(half_refs):
        copies.append(
            pltpu.make_async_copy(
                grad_ref.at[:, pl.ds(n * half, half)], ref.at[:, pl.ds(0, half)], sems.at[n]
            )
        )
    for n, ref in enumerate(end_refs):
        first = pl.multiple_of(first_ref[n], most)
        for m, source in enumerate((k_ref, v_ref)):
            copies.append(
                pltpu.make_async_copy(
                    source.at[pl.ds(first, most)],
                    ref.at[:, pl.ds(m * width, width)],
                    sems.at[2 + 2 * n + m],
                )
            )
    for copy in copies:
        copy.start()
    tokens = grad_ref.shape[0]
    code = columns(mark_ref[:1])
    for n, ref in enumerate(end_refs):
        here = jnp.where(first_ref[n] == 0, code[:most], code[tokens - most :])
        ref[:, 2 * width :] = here.astype(jnp.bfloat16)
    place = columns(mark_ref[1:2]).astype(jnp.bfloat16)
    for ref in half_refs:
        ref[:, half:] = place
    for copy in copies:
        copy.wait()


def pack(firsts, keys, values, grads, marks, most):
    tokens, width = keys.shape
    ends = jax.ShapeDtypeStruct((most, 2 * width + LANES), jnp.bfloat16)
    halves = jax.ShapeDtypeStruct((tokens, width // 2 + LANES), jnp.bfloat16)
    return pl.pallas_call(
        functools.partial(pack_kernel, most),
        in_specs=[SMEM] + [pl.BlockSpec(memory_space=pltpu.HBM)] * 3 + [VMEM],
        out_specs=[VMEM] * 4,
        out_shape=[halves, halves, ends, ends],
        scratch_shapes=[pltpu.SemaphoreType.DMA((6,))],
        compiler_params=pltpu.CompilerParams(vmem_limit_bytes=PACK_LIMIT),
        cost_estimate=pl.CostEstimate(
            flops=0, bytes_accessed=4 * tokens * width + 16 * most * width, transcendentals=0
        ),
        name="pack",
    )(firsts, keys, values, grads, marks)


def selector(row):
    tokens = row.shape[1]
    wanted = lax.broadcasted_iota(jnp.int32, (tokens, tokens), 0).astype(jnp.float32)
    return jnp.where(wanted == row, 1.0, 0.0)


def sums_kernel(sizes, flag_ref, gate_ref, *refs):
    half = gate_ref.shape[1] // 2
    count = len(sizes)
    for n in range(2):
        mine_ref, theirs_ref = refs[2 * n : 2 * n + 2]
        picks, rows = [], []
        for ref in (mine_ref, theirs_ref):
            place = ref[:, half : half + LANES].astype(jnp.float32).T[:1]
            picks.append(selector(place).astype(jnp.bfloat16))
            rows.append(ref[:, :half])
        summed = jnp.dot(
            jnp.concatenate(picks, axis=1),
            jnp.concatenate(rows, axis=0),
            preferred_element_type=jnp.float32,
        )
        term = gate_ref[:, n * half : (n + 1) * half] * summed
        term = (term + flag_ref[n] * rows[1].astype(jnp.float32)).astype(jnp.bfloat16)
        at = 0
        for ref, size in zip(refs[4 + n * count : 4 + (n + 1) * count], sizes):
            ref[...] = term[at : at + size]
            at += size


def pair_sums(flags, gate, parts, sizes):
    tokens, width = parts[0].shape[0], gate.shape[1]
    outs = [jax.ShapeDtypeStruct((size, width // 2), jnp.bfloat16) for size in sizes] * 2
    return pl.pallas_call(
        functools.partial(sums_kernel, sizes),
        in_specs=[SMEM] + [VMEM] * 5,
        out_specs=[VMEM] * len(outs),
        out_shape=outs,
        compiler_params=PARAMS,
        cost_estimate=pl.CostEstimate(
            flops=4 * tokens * tokens * width, bytes_accessed=6 * tokens * width, transcendentals=0
        ),
        name="pair_sums",
    )(flags, gate, *parts)


def piece_spots(tokens, reach, piece):
    if tokens <= 2 * reach:
        return [(0, tokens, 0)]
    if piece == 0:
        return [(reach, tokens - 2 * reach, 0)]
    return [(0, reach, 0), (tokens - reach, reach, reach)]


def relay_kernel(spots, row_ref, gate_ref, first_ref, second_ref, base_ref, out_ref):
    tokens, width = out_ref.shape
    half = width // 2
    picks = selector(row_ref[...]).T.astype(jnp.bfloat16)
    picks = jnp.concatenate([picks[:, top : top + size] for top, size, at in spots], axis=1)
    for n, ref in enumerate((first_ref, second_ref)):
        lanes = slice(n * half, (n + 1) * half)
        relayed = jnp.dot(picks, ref[...], preferred_element_type=jnp.float32)
        total = base_ref[:, lanes].astype(jnp.float32) + gate_ref[:, lanes] * relayed
        out_ref[:, lanes] = total.astype(out_ref.dtype)


def relay(rows, gate, first, second, base, spots, dtype):
    tokens, width = base.shape
    return pl.pallas_call(
        functools.partial(relay_kernel, spots),
        in_specs=[VMEM] * 5,
        out_specs=VMEM,
        out_shape=jax.ShapeDtypeStruct((tokens, width), dtype),
        compiler_params=PARAMS,
        cost_estimate=pl.CostEstimate(
            flops=2 * tokens * tokens * width, bytes_accessed=24 * tokens * width, transcendentals=0
        ),
        name="relay",
    )(rows, gate, first, second, base)


def whole_gate(gate):
    ranks = lax.axis_size("rep")
    if ranks != 2:
        return lax.all_gather(gate, "rep", axis=0, tiled=True)
    other = lax.ppermute(gate, "rep", [(0, 1), (1, 0)])
    first = lax.axis_index("rep") == 0
    return jnp.concatenate([jnp.where(first, gate, other), jnp.where(first, other, gate)])


SWAP_X, SWAP_Y = [(0, 1), (1, 0), (2, 3), (3, 2)], [(0, 2), (2, 0), (1, 3), (3, 1)]
ROUND_A, ROUND_B = [(0, 1), (1, 3), (3, 2), (2, 0)], [(0, 2), (2, 3), (3, 1), (1, 0)]


def added(a, b):
    return (a.astype(jnp.float32) + b.astype(jnp.float32)).astype(a.dtype)


def local(query_rows, key_rows, value_rows, view_frame, control_row, control_gate, out_grad):
    queries, keys, values = query_rows[0, 0], key_rows[0, 0], value_rows[0, 0]
    tokens, width = queries.shape
    half = width // 2
    ranks = lax.axis_size("seq")
    reach = 2 * (tokens * ranks // 32)
    hops = (reach + tokens - 1) // tokens
    group, rank = lax.axis_index("grp"), lax.axis_index("seq")
    send = lambda block, route: lax.ppermute(block, "grp", route)

    tag = view_frame[0, 0]
    code = tag + 8 * (tag // FRAMES) + 16
    marks = jnp.stack((code, control_row[0, 0] % tokens)).astype(jnp.float32)
    code, rows = marks[:1], marks[1:]
    most = min(tokens, reach)
    even = rank % 2 == 0
    firsts = jnp.where(jnp.stack((even, ~even)), tokens - most, 0).astype(jnp.int32)
    sent_a, sent_b, end_one, end_two = pack(firsts, keys, values, out_grad[0, 0], marks, most)
    got_a, got_b = send(sent_a, SWAP_X), send(sent_b, SWAP_Y)
    halos = [paired(end_one, "seq", 0), paired(end_two, "seq", 1)]
    above, below = rank < ranks - 1, rank > 0
    valid = jnp.where(jnp.stack((even, ~even)), above, below).astype(jnp.float32)
    for hop in range(2, hops + 1):
        count = min(tokens, reach - (hop - 1) * tokens)
        tail, head = jnp.where(even, end_one, end_two), jnp.where(even, end_two, end_one)
        halos.append(shifted(tail[most - count :], "seq", hop))
        halos.append(shifted(head[:count], "seq", -hop))
    gate = whole_gate(control_gate)[None]

    own = []
    sizes = [min(tokens, 2 * reach)]
    if tokens > 2 * reach:
        own.append(attend_middle(queries, keys, values, code, reach))
        sizes.insert(0, tokens - 2 * reach)
    flags = jnp.stack([group == 1, group == 2]).astype(jnp.float32)
    sums = pair_sums(flags, gate, (sent_a, got_a, sent_b, got_b), sizes)
    valid, *sums = lax.optimization_barrier((valid, *sums))
    own.append(attend_edges(valid, queries, keys, values, code, halos, reach))

    count = len(own)
    spots = [piece_spots(tokens, reach, n) for n in range(count)]
    order = [
        own[n][at : at + size] for top, size, n, at in sorted(
            (top, size, n, at) for n in range(count) for top, size, at in spots[n]
        )
    ]
    block_out = jnp.concatenate(order, axis=0)
    totals = []
    for n, (piece, sum_a, sum_b) in enumerate(zip(own, sums[:count], sums[count:])):
        piece_a, piece_b = piece[:, :half], piece[:, half:]
        one = send(jnp.where(group == 0, piece_a, jnp.where(group == 1, sum_a, sum_b)), ROUND_A)
        two = send(jnp.where(group == 0, piece_b, jnp.where(group == 2, sum_b, sum_a)), ROUND_B)
        total_a = added(sum_a, jnp.where(group == 1, two, one))
        total_b = added(sum_b, jnp.where(group == 2, one, two))
        held_a = jnp.where(group == 0, piece_a, one)
        held_b = jnp.where(group == 0, piece_b, two)
        across = send(jnp.where((group == 0) | (group == 2), held_b, total_a), SWAP_X)
        down = send(jnp.where(group <= 1, held_a, total_b), SWAP_Y)
        branch_a = jnp.where(group <= 1, held_a, down)
        branch_b = jnp.where((group == 0) | (group == 2), held_b, across)
        dtype = jnp.bfloat16 if n == count - 1 else jnp.float32
        block_out = relay(rows, gate, branch_a, branch_b, block_out, spots[n], dtype)
        totals.append(
            jnp.concatenate(
                (
                    jnp.where((group == 0) | (group == 2), across, total_a),
                    jnp.where(group <= 1, down, total_b),
                ),
                axis=1,
            )
        )
    branch_grad = jnp.concatenate(totals, axis=0)
    return (block_out[None, None], branch_grad[None])


def solution(mesh):
    placed = (
        P("rep", "grp", "seq", None),
        P("rep", "grp", "seq", None),
        P("rep", "grp", "seq", None),
        P("rep", "grp", "seq"),
        P("rep", "grp", "seq"),
        P("rep"),
        P("rep", "grp", "seq", None),
    )
    return jax.shard_map(
        local,
        mesh=mesh,
        in_specs=placed,
        out_specs=(P("rep", "grp", "seq", None), P("rep", "seq", None)),
        check_vma=False,
    )
```

```python
import functools
import math

import jax
import jax.numpy as jnp
from jax import lax
from jax.experimental import pallas as pl
from jax.experimental.pallas import tpu as pltpu
from jax.sharding import PartitionSpec as P

HEADS = 32
DH = 80
FRAMES = 20
LANES = 128
VMEM_LIMIT = 48 * 1024 * 1024
PACK_LIMIT = 53 * 1024 * 1024
ENDS_LIMIT = 53 * 1024 * 1024


def shifted(block, axis, distance):
    devices = range(lax.axis_size(axis))
    route = [(i - distance, i) for i in devices if i - distance in devices]
    return lax.ppermute(block, axis, route)


def paired(block, axis, first):
    size = lax.axis_size(axis)
    route = []
    for i in range(size):
        other = i + 1 if (i - first) % 2 == 0 else i - 1
        route.append((i, other if 0 <= other < size else i))
    return lax.ppermute(block, axis, route)


def lane_windows(heads):
    windows = []
    for head in range(heads):
        first, last = head * DH, (head + 1) * DH
        if windows and last <= windows[-1][0] + 2 * LANES:
            windows[-1][1].append(head)
        else:
            windows.append((first // LANES * LANES, [head]))
    out = []
    for start, members in windows:
        start = min(start, heads * DH - 2 * LANES)
        out.append((start, members))
    return out


def head_masks(rows, period):
    masks = {}
    for start, members in lane_windows(period // DH):
        lane = lax.broadcasted_iota(jnp.int32, (rows, 2 * LANES), 1) + start
        for h in members:
            inside = (lane >= h * DH) & (lane < (h + 1) * DH)
            masks[h] = jnp.where(inside, 1.0, 0.0).astype(jnp.bfloat16)
    return masks


def mixed_period(base, query, sets, masks, period):
    rows = sets[0][0].shape[0]
    factor = math.log2(math.e) / math.sqrt(DH)
    windows = lane_windows(period // DH)
    scores = []
    for start, members in windows:
        lanes = slice(base + start, base + start + 2 * LANES)
        part = query(lanes)
        stacked = jnp.concatenate([part * masks[h] for h in members], axis=0)
        scores.append(
            [
                lax.dot_general(
                    stacked, key(lanes), (((1,), (1,)), ((), ())), preferred_element_type=jnp.float32
                )
                for bias, key, value in sets
            ]
        )
    weights = []
    for parts, (start, members) in zip(scores, windows):
        parts = [
            part.reshape(len(members), rows, -1) + bias[None]
            for part, (bias, key, value) in zip(parts, sets)
        ]
        largest = row_max(parts)
        weights.append(
            [
                jnp.exp2((part - largest) * factor).astype(jnp.bfloat16).reshape(len(members) * rows, -1)
                for part in parts
            ]
        )
    tiles = {}
    for parts, (start, members) in zip(weights, windows):
        lanes = slice(base + start, base + start + 2 * LANES)
        mixed = sum(
            jnp.dot(part, value(lanes), preferred_element_type=jnp.float32)
            for part, (bias, key, value) in zip(parts, sets)
        )
        totals = sum(
            jnp.dot(part, jnp.ones((part.shape[1], LANES), part.dtype), preferred_element_type=jnp.float32)
            for part in parts
        )
        scale = 1.0 / totals
        for n, h in enumerate(members):
            for t in range(2):
                low = start + t * LANES
                if h * DH >= low + LANES or (h + 1) * DH <= low:
                    continue
                mine = slice(n * rows, (n + 1) * rows)
                piece = mixed[mine, t * LANES : (t + 1) * LANES] * scale[mine]
                if low in tiles:
                    lane = lax.broadcasted_iota(jnp.int32, (rows, LANES), 1) + low
                    tiles[low] = jnp.where(lane >= h * DH, piece, tiles[low])
                else:
                    tiles[low] = piece
    return {low: tile.astype(jnp.bfloat16) for low, tile in tiles.items()}


def row_max(parts):
    if all(part.shape == parts[0].shape for part in parts):
        return jnp.max(functools.reduce(jnp.maximum, parts), axis=-1, keepdims=True)
    return functools.reduce(jnp.maximum, [jnp.max(part, axis=-1, keepdims=True) for part in parts])


def columns(row):
    return jnp.broadcast_to(row, (LANES, row.shape[1])).T


def link_bias(mine, theirs):
    return jnp.where(jnp.abs(mine[:, :1] - theirs.T[: mine.shape[0]]) <= 1.5, 0.0, -1e30)


def attend_block(query, sets, out_ref):
    rows, width = out_ref.shape
    period = math.lcm(DH, LANES)
    masks = head_masks(rows, period)
    for base in range(0, width, period):
        tiles = mixed_period(base, query, sets, masks, period)
        for low, tile in tiles.items():
            out_ref[:, base + low : base + low + LANES] = tile


def middle_kernel(reach, q_ref, k_ref, v_ref, code_ref, out_ref):
    rows = out_ref.shape[0]
    code = columns(code_ref[...])
    bias = link_bias(code[reach : reach + rows], code)
    own = (bias, lambda lanes: k_ref[:, lanes], lambda lanes: v_ref[:, lanes])
    attend_block(lambda lanes: q_ref[reach : reach + rows, lanes], [own], out_ref)


def edge_kernel(reach, valid_ref, q_ref, k_ref, v_ref, code_ref, *refs):
    halos = refs[:-4]
    out_ref, keys, values, codes = refs[-4:]
    tokens, width = q_ref.shape
    code = columns(code_ref[...])
    at = 0
    for n, piece in enumerate(halos):
        rows = piece.shape[0]
        keys[at : at + rows] = piece[:, :width]
        values[at : at + rows] = piece[:, width : 2 * width]
        there = valid_ref[n] if n < 2 else 1.0
        codes[at : at + rows] = piece[:, 2 * width :].astype(jnp.float32) * there
        at += rows
    if at < keys.shape[0]:
        spare = keys.shape[0] - at
        keys[at:] = jnp.zeros((spare, width), keys.dtype)
        values[at:] = jnp.zeros((spare, width), values.dtype)
        codes[at:] = jnp.zeros((spare, LANES), codes.dtype)
    if tokens > 2 * reach:
        last = tokens - reach
        mine = jnp.concatenate((code[:reach], code[last:]), axis=0)
        query = lambda lanes: jnp.concatenate((q_ref[:reach, lanes], q_ref[last:, lanes]), axis=0)
    else:
        mine = code
        query = lambda lanes: q_ref[:, lanes]
    own = (link_bias(mine, code), lambda lanes: k_ref[:, lanes], lambda lanes: v_ref[:, lanes])
    halo = (
        link_bias(mine, codes[...]),
        lambda lanes: keys[:, lanes],
        lambda lanes: values[:, lanes],
    )
    attend_block(query, [own, halo], out_ref)


def attend_cost(tokens, span, width):
    return pl.CostEstimate(
        flops=HEADS * tokens * span * 2 * LANES * 4,
        bytes_accessed=12 * tokens * width,
        transcendentals=HEADS * tokens * span,
    )


VMEM = pl.BlockSpec(memory_space=pltpu.VMEM)
SMEM = pl.BlockSpec(memory_space=pltpu.SMEM)
PARAMS = pltpu.CompilerParams(vmem_limit_bytes=VMEM_LIMIT)


def attend_middle(queries, keys, values, code, reach):
    tokens, width = queries.shape
    return pl.pallas_call(
        functools.partial(middle_kernel, reach),
        in_specs=[VMEM] * 4,
        out_specs=VMEM,
        out_shape=jax.ShapeDtypeStruct((tokens - 2 * reach, width), jnp.bfloat16),
        compiler_params=PARAMS,
        cost_estimate=attend_cost(tokens - 2 * reach, tokens, width),
        name="attend_middle",
    )(queries, keys, values, code)


def attend_edges(valid, queries, keys, values, code, halos, reach):
    tokens, width = queries.shape
    rows = min(tokens, 2 * reach)
    held = -(-2 * reach // LANES) * LANES
    return pl.pallas_call(
        functools.partial(edge_kernel, reach),
        in_specs=[SMEM] + [VMEM] * (4 + len(halos)),
        out_specs=VMEM,
        out_shape=jax.ShapeDtypeStruct((rows, width), jnp.bfloat16),
        scratch_shapes=[
            pltpu.VMEM((held, width), jnp.bfloat16),
            pltpu.VMEM((held, width), jnp.bfloat16),
            pltpu.VMEM((held, LANES), jnp.float32),
        ],
        compiler_params=PARAMS,
        cost_estimate=attend_cost(rows, LANES, width),
        name="attend_edges",
    )(valid, queries, keys, values, code, *halos)


def pack_grads_kernel(grad_ref, mark_ref, first_ref, second_ref, sems):
    half = grad_ref.shape[1] // 2
    copies = []
    for n, ref in enumerate((first_ref, second_ref)):
        copies.append(
            pltpu.make_async_copy(
                grad_ref.at[:, pl.ds(n * half, half)], ref.at[:, pl.ds(0, half)], sems.at[n]
            )
        )
    for copy in copies:
        copy.start()
    place = columns(mark_ref[1:2]).astype(jnp.bfloat16)
    for ref in (first_ref, second_ref):
        ref[:, half:] = place
    for copy in copies:
        copy.wait()


def pack_grads(grads, marks):
    tokens, width = grads.shape
    return pl.pallas_call(
        pack_grads_kernel,
        in_specs=[pl.BlockSpec(memory_space=pltpu.HBM), VMEM],
        out_specs=[VMEM] * 2,
        out_shape=[jax.ShapeDtypeStruct((tokens, width // 2 + LANES), jnp.bfloat16)] * 2,
        scratch_shapes=[pltpu.SemaphoreType.DMA((2,))],
        compiler_params=pltpu.CompilerParams(vmem_limit_bytes=PACK_LIMIT),
        cost_estimate=pl.CostEstimate(flops=0, bytes_accessed=4 * tokens * width, transcendentals=0),
        name="pack_grads",
    )(grads, marks)


def pack_ends_kernel(most, first_ref, k_ref, v_ref, mark_ref, gate_ref, *refs):
    end_refs, sems = refs[:2], refs[2]
    tokens, width = k_ref.shape
    copies = []
    for n, ref in enumerate(end_refs):
        first = pl.multiple_of(first_ref[n], most)
        for m, source in enumerate((k_ref, v_ref)):
            copies.append(
                pltpu.make_async_copy(
                    source.at[pl.ds(first, most)],
                    ref.at[:, pl.ds(m * width, width)],
                    sems.at[2 * n + m],
                )
            )
    for copy in copies:
        copy.start()
    code = columns(mark_ref[:1])
    for n, ref in enumerate(end_refs):
        here = jnp.where(first_ref[n] == 0, code[:most], code[tokens - most :])
        ref[:, 2 * width :] = here.astype(jnp.bfloat16)
    for copy in copies:
        copy.wait()


def pack_ends(firsts, keys, values, marks, gate, most):
    tokens, width = keys.shape
    ends = jax.ShapeDtypeStruct((most, 2 * width + LANES), jnp.bfloat16)
    return pl.pallas_call(
        functools.partial(pack_ends_kernel, most),
        in_specs=[SMEM] + [pl.BlockSpec(memory_space=pltpu.HBM)] * 2 + [VMEM] * 2,
        out_specs=[VMEM] * 2,
        out_shape=[ends, ends],
        scratch_shapes=[pltpu.SemaphoreType.DMA((4,))],
        compiler_params=pltpu.CompilerParams(vmem_limit_bytes=ENDS_LIMIT),
        cost_estimate=pl.CostEstimate(
            flops=0, bytes_accessed=16 * most * width, transcendentals=0
        ),
        name="pack_ends",
    )(firsts, keys, values, marks, gate)


def selector(row):
    tokens = row.shape[1]
    wanted = lax.broadcasted_iota(jnp.int32, (tokens, tokens), 0).astype(jnp.float32)
    return jnp.where(wanted == row, 1.0, 0.0)


def sums_kernel(sizes, flag_ref, gate_ref, *refs):
    half = gate_ref.shape[1] // 2
    count = len(sizes)
    for n in range(2):
        mine_ref, theirs_ref = refs[2 * n : 2 * n + 2]
        picks, rows = [], []
        for ref in (mine_ref, theirs_ref):
            place = ref[:, half : half + LANES].astype(jnp.float32).T[:1]
            picks.append(selector(place).astype(jnp.bfloat16))
            rows.append(ref[:, :half])
        summed = jnp.dot(
            jnp.concatenate(picks, axis=1),
            jnp.concatenate(rows, axis=0),
            preferred_element_type=jnp.float32,
        )
        term = gate_ref[:, n * half : (n + 1) * half] * summed
        term = (term + flag_ref[n] * rows[1].astype(jnp.float32)).astype(jnp.bfloat16)
        at = 0
        for ref, size in zip(refs[4 + n * count : 4 + (n + 1) * count], sizes):
            ref[...] = term[at : at + size]
            at += size


def pair_sums(flags, gate, parts, sizes):
    tokens, width = parts[0].shape[0], gate.shape[1]
    outs = [jax.ShapeDtypeStruct((size, width // 2), jnp.bfloat16) for size in sizes] * 2
    return pl.pallas_call(
        functools.partial(sums_kernel, sizes),
        in_specs=[SMEM] + [VMEM] * 5,
        out_specs=[VMEM] * len(outs),
        out_shape=outs,
        compiler_params=PARAMS,
        cost_estimate=pl.CostEstimate(
            flops=4 * tokens * tokens * width, bytes_accessed=6 * tokens * width, transcendentals=0
        ),
        name="pair_sums",
    )(flags, gate, *parts)


def piece_spots(tokens, reach, piece):
    if tokens <= 2 * reach:
        return [(0, tokens, 0)]
    if piece == 0:
        return [(reach, tokens - 2 * reach, 0)]
    return [(0, reach, 0), (tokens - reach, reach, reach)]


def relay_kernel(spots, first_row, chunks, row_ref, gate_ref, branch_refs, base_ref, total_refs, *refs):
    grad_ref, out_ref, staged, sems, grad_sems = refs[-5:]
    tokens, width = base_ref.shape
    half = width // 2
    copies = []
    for n, ref in enumerate(total_refs):
        copies.append(
            pltpu.make_async_copy(
                ref,
                grad_ref.at[pl.ds(first_row, ref.shape[0]), pl.ds(n * half, half)],
                grad_sems.at[n],
            )
        )
    for copy in copies:
        copy.start()
    picks = selector(row_ref[...]).T.astype(jnp.bfloat16)
    picks = jnp.concatenate([picks[:, top : top + size] for top, size, at in spots], axis=1)
    step = half // chunks
    for n, ref in enumerate(branch_refs):
        for c in range(chunks):
            lanes = slice(n * half + c * step, n * half + (c + 1) * step)
            relayed = jnp.dot(
                picks, ref[:, c * step : (c + 1) * step], preferred_element_type=jnp.float32
            )
            total = base_ref[:, lanes].astype(jnp.float32) + gate_ref[:, lanes] * relayed
            staged[:, lanes] = total.astype(staged.dtype)
            if sems is not None:
                part = pl.ds(n * half + c * step, step)
                copy = pltpu.make_async_copy(
                    staged.at[:, part], out_ref.at[:, part], sems.at[n * chunks + c]
                )
                copy.start()
                copies.append(copy)
    for copy in copies:
        copy.wait()


def relay(rows, gate, branch, base, totals, spots, first_row, grads, last):
    tokens, width = base.shape
    chunks = 2 if width // 2 % (2 * LANES) == 0 else 1
    far = pl.BlockSpec(memory_space=pltpu.HBM)
    whole = jax.ShapeDtypeStruct((tokens, width), jnp.bfloat16)

    def kernel(row_ref, gate_ref, a_ref, b_ref, base_ref, c_ref, d_ref, *refs):
        if grads is not None:
            refs = refs[1:]
        if last:
            grad_ref, out_ref, staged, sems, grad_sems = refs
        else:
            grad_ref, out_ref, grad_sems = refs
            staged, sems = out_ref, None
        relay_kernel(
            spots, first_row, chunks, row_ref, gate_ref, (a_ref, b_ref), base_ref, (c_ref, d_ref),
            grad_ref, out_ref, staged, sems, grad_sems,
        )

    out = whole if last else jax.ShapeDtypeStruct((tokens, width), jnp.float32)
    scratch = [pltpu.VMEM((tokens, width), jnp.bfloat16), pltpu.SemaphoreType.DMA((2 * chunks,))]
    operands = [rows, gate, *branch, base, *totals] + ([] if grads is None else [grads])
    return pl.pallas_call(
        kernel,
        in_specs=[VMEM] * 7 + ([] if grads is None else [far]),
        out_specs=[far, far if last else VMEM],
        out_shape=[whole, out],
        input_output_aliases={} if grads is None else {7: 0},
        scratch_shapes=(scratch if last else []) + [pltpu.SemaphoreType.DMA((2,))],
        compiler_params=PARAMS,
        cost_estimate=pl.CostEstimate(
            flops=2 * tokens * tokens * width,
            bytes_accessed=24 * tokens * width,
            transcendentals=0,
        ),
        name="relay",
    )(*operands)


def whole_gate(gate):
    ranks = lax.axis_size("rep")
    if ranks != 2:
        return lax.all_gather(gate, "rep", axis=0, tiled=True)
    other = lax.ppermute(gate, "rep", [(0, 1), (1, 0)])
    first = lax.axis_index("rep") == 0
    return jnp.concatenate([jnp.where(first, gate, other), jnp.where(first, other, gate)])


SWAP_X, SWAP_Y = [(0, 1), (1, 0), (2, 3), (3, 2)], [(0, 2), (2, 0), (1, 3), (3, 1)]
ROUND_A, ROUND_B = [(0, 1), (1, 3), (3, 2), (2, 0)], [(0, 2), (2, 3), (3, 1), (1, 0)]


def added(a, b):
    return (a.astype(jnp.float32) + b.astype(jnp.float32)).astype(a.dtype)


def local(query_rows, key_rows, value_rows, view_frame, control_row, control_gate, out_grad):
    queries, keys, values = query_rows[0, 0], key_rows[0, 0], value_rows[0, 0]
    tokens, width = queries.shape
    half = width // 2
    ranks = lax.axis_size("seq")
    reach = 2 * (tokens * ranks // 32)
    hops = (reach + tokens - 1) // tokens
    group, rank = lax.axis_index("grp"), lax.axis_index("seq")
    send = lambda block, route: lax.ppermute(block, "grp", route)

    tag = view_frame[0, 0]
    code = tag + 8 * (tag // FRAMES) + 16
    marks = jnp.stack((code, control_row[0, 0] % tokens)).astype(jnp.float32)
    code, rows = marks[:1], marks[1:]
    most = min(tokens, reach)
    even = rank % 2 == 0
    firsts = jnp.where(jnp.stack((even, ~even)), tokens - most, 0).astype(jnp.int32)
    sent_a, sent_b = pack_grads(out_grad[0, 0], marks)
    got_a, got_b = send(sent_a, SWAP_X), send(sent_b, SWAP_Y)
    gate = whole_gate(control_gate)[None]
    end_one, end_two = pack_ends(firsts, keys, values, marks, gate, most)
    halos = [paired(end_one, "seq", 0), paired(end_two, "seq", 1)]
    above, below = rank < ranks - 1, rank > 0
    valid = jnp.where(jnp.stack((even, ~even)), above, below).astype(jnp.float32)
    for hop in range(2, hops + 1):
        count = min(tokens, reach - (hop - 1) * tokens)
        tail, head = jnp.where(even, end_one, end_two), jnp.where(even, end_two, end_one)
        halos.append(shifted(tail[most - count :], "seq", hop))
        halos.append(shifted(head[:count], "seq", -hop))

    own = []
    sizes = [min(tokens, 2 * reach)]
    if tokens > 2 * reach:
        own.append(attend_middle(queries, keys, values, code, reach))
        sizes.insert(0, tokens - 2 * reach)
    flags = jnp.stack([group == 1, group == 2]).astype(jnp.float32)
    sums = pair_sums(flags, gate, (sent_a, got_a, sent_b, got_b), sizes)
    count = len(sizes)

    def outgoing(piece, sum_a, sum_b):
        to_a = jnp.where(group == 0, piece[:, :half], jnp.where(group == 1, sum_a, sum_b))
        to_b = jnp.where(group == 0, piece[:, half:], jnp.where(group == 2, sum_b, sum_a))
        return to_a, to_b

    going = [outgoing(own[0], sums[0], sums[count])] if own else []
    valid, *ready = lax.optimization_barrier((valid, *sums, *(going[0] if going else ())))
    sums = ready[: 2 * count]
    if going:
        going = [ready[2 * count :]]
    own.append(attend_edges(valid, queries, keys, values, code, halos, reach))

    going.append(outgoing(own[-1], sums[count - 1], sums[2 * count - 1]))
    spots = [piece_spots(tokens, reach, n) for n in range(count)]
    order = [
        own[n][at : at + size] for top, size, n, at in sorted(
            (top, size, n, at) for n in range(count) for top, size, at in spots[n]
        )
    ]
    block_out = jnp.concatenate(order, axis=0)
    branch_grad, first_row = None, 0
    for n, (piece, sum_a, sum_b) in enumerate(zip(own, sums[:count], sums[count:])):
        piece_a, piece_b = piece[:, :half], piece[:, half:]
        one, two = send(going[n][0], ROUND_A), send(going[n][1], ROUND_B)
        total_a = added(sum_a, jnp.where(group == 1, two, one))
        total_b = added(sum_b, jnp.where(group == 2, one, two))
        held_a = jnp.where(group == 0, piece_a, one)
        held_b = jnp.where(group == 0, piece_b, two)
        across = send(jnp.where((group == 0) | (group == 2), held_b, total_a), SWAP_X)
        down = send(jnp.where(group <= 1, held_a, total_b), SWAP_Y)
        branch_a = jnp.where(group <= 1, held_a, down)
        branch_b = jnp.where((group == 0) | (group == 2), held_b, across)
        totals = (
            jnp.where((group == 0) | (group == 2), across, total_a),
            jnp.where(group <= 1, down, total_b),
        )
        branch_grad, block_out = relay(
            rows, gate, (branch_a, branch_b), block_out, totals, spots[n], first_row, branch_grad,
            n == count - 1,
        )
        first_row += piece.shape[0]
    return (block_out[None, None], branch_grad[None])


def solution(mesh):
    placed = (
        P("rep", "grp", "seq", None),
        P("rep", "grp", "seq", None),
        P("rep", "grp", "seq", None),
        P("rep", "grp", "seq"),
        P("rep", "grp", "seq"),
        P("rep"),
        P("rep", "grp", "seq", None),
    )
    return jax.shard_map(
        local,
        mesh=mesh,
        in_specs=placed,
        out_specs=(P("rep", "grp", "seq", None), P("rep", "seq", None)),
        check_vma=False,
    )
```

```python
import functools
import math

import jax
import jax.numpy as jnp
from jax import lax
from jax.experimental import pallas as pl
from jax.experimental.pallas import tpu as pltpu
from jax.sharding import PartitionSpec as P

HEADS = 32
DH = 80
FRAMES = 20
LANES = 128
VMEM_LIMIT = 48 * 1024 * 1024
PACK_LIMIT = 53 * 1024 * 1024
ENDS_LIMIT = 53 * 1024 * 1024


def shifted(block, axis, distance):
    devices = range(lax.axis_size(axis))
    route = [(i - distance, i) for i in devices if i - distance in devices]
    return lax.ppermute(block, axis, route)


def paired(block, axis, first):
    size = lax.axis_size(axis)
    route = []
    for i in range(size):
        other = i + 1 if (i - first) % 2 == 0 else i - 1
        route.append((i, other if 0 <= other < size else i))
    return lax.ppermute(block, axis, route)


def lane_windows(heads):
    windows = []
    for head in range(heads):
        first, last = head * DH, (head + 1) * DH
        if windows and last <= windows[-1][0] + 2 * LANES:
            windows[-1][1].append(head)
        else:
            windows.append((first // LANES * LANES, [head]))
    out = []
    for start, members in windows:
        start = min(start, heads * DH - 2 * LANES)
        out.append((start, members))
    return out


def head_masks(rows, period):
    masks = {}
    for start, members in lane_windows(period // DH):
        lane = lax.broadcasted_iota(jnp.int32, (rows, 2 * LANES), 1) + start
        for h in members:
            inside = (lane >= h * DH) & (lane < (h + 1) * DH)
            masks[h] = jnp.where(inside, 1.0, 0.0).astype(jnp.bfloat16)
    return masks


def mixed_period(base, query, sets, masks, period):
    rows = sets[0][0].shape[0]
    factor = math.log2(math.e) / math.sqrt(DH)
    windows = lane_windows(period // DH)
    scores = []
    for start, members in windows:
        lanes = slice(base + start, base + start + 2 * LANES)
        part = query(lanes)
        stacked = jnp.concatenate([part * masks[h] for h in members], axis=0)
        scores.append(
            [
                lax.dot_general(
                    stacked, key(lanes), (((1,), (1,)), ((), ())), preferred_element_type=jnp.float32
                )
                for bias, key, value in sets
            ]
        )
    weights = []
    for parts, (start, members) in zip(scores, windows):
        parts = [
            part.reshape(len(members), rows, -1) + bias[None]
            for part, (bias, key, value) in zip(parts, sets)
        ]
        largest = row_max(parts)
        weights.append(
            [
                jnp.exp2((part - largest) * factor).astype(jnp.bfloat16).reshape(len(members) * rows, -1)
                for part in parts
            ]
        )
    tiles = {}
    for parts, (start, members) in zip(weights, windows):
        lanes = slice(base + start, base + start + 2 * LANES)
        mixed = sum(
            jnp.dot(part, value(lanes), preferred_element_type=jnp.float32)
            for part, (bias, key, value) in zip(parts, sets)
        )
        totals = sum(
            jnp.dot(part, jnp.ones((part.shape[1], LANES), part.dtype), preferred_element_type=jnp.float32)
            for part in parts
        )
        scale = 1.0 / totals
        for n, h in enumerate(members):
            for t in range(2):
                low = start + t * LANES
                if h * DH >= low + LANES or (h + 1) * DH <= low:
                    continue
                mine = slice(n * rows, (n + 1) * rows)
                piece = mixed[mine, t * LANES : (t + 1) * LANES] * scale[mine]
                if low in tiles:
                    lane = lax.broadcasted_iota(jnp.int32, (rows, LANES), 1) + low
                    tiles[low] = jnp.where(lane >= h * DH, piece, tiles[low])
                else:
                    tiles[low] = piece
    return {low: tile.astype(jnp.bfloat16) for low, tile in tiles.items()}


def row_max(parts):
    if all(part.shape == parts[0].shape for part in parts):
        return jnp.max(functools.reduce(jnp.maximum, parts), axis=-1, keepdims=True)
    return functools.reduce(jnp.maximum, [jnp.max(part, axis=-1, keepdims=True) for part in parts])


def columns(row):
    return jnp.broadcast_to(row, (LANES, row.shape[1])).T


def link_bias(mine, theirs):
    return jnp.where(jnp.abs(mine[:, :1] - theirs.T[: mine.shape[0]]) <= 1.5, 0.0, -1e30)


def attend_block(query, sets, out_ref):
    rows, width = out_ref.shape
    period = math.lcm(DH, LANES)
    masks = head_masks(rows, period)
    for base in range(0, width, period):
        tiles = mixed_period(base, query, sets, masks, period)
        for low, tile in tiles.items():
            out_ref[:, base + low : base + low + LANES] = tile


def middle_kernel(reach, q_ref, k_ref, v_ref, code_ref, out_ref):
    rows = out_ref.shape[0]
    code = columns(code_ref[...])
    bias = link_bias(code[reach : reach + rows], code)
    own = (bias, lambda lanes: k_ref[:, lanes], lambda lanes: v_ref[:, lanes])
    attend_block(lambda lanes: q_ref[reach : reach + rows, lanes], [own], out_ref)


def edge_kernel(reach, valid_ref, q_ref, k_ref, v_ref, code_ref, *refs):
    halos = refs[:-4]
    out_ref, keys, values, codes = refs[-4:]
    tokens, width = q_ref.shape
    code = columns(code_ref[...])
    at = 0
    for n, piece in enumerate(halos):
        rows = piece.shape[0]
        keys[at : at + rows] = piece[:, :width]
        values[at : at + rows] = piece[:, width : 2 * width]
        there = valid_ref[n] if n < 2 else 1.0
        codes[at : at + rows] = piece[:, 2 * width :].astype(jnp.float32) * there
        at += rows
    if at < keys.shape[0]:
        spare = keys.shape[0] - at
        keys[at:] = jnp.zeros((spare, width), keys.dtype)
        values[at:] = jnp.zeros((spare, width), values.dtype)
        codes[at:] = jnp.zeros((spare, LANES), codes.dtype)
    if tokens > 2 * reach:
        last = tokens - reach
        mine = jnp.concatenate((code[:reach], code[last:]), axis=0)
        query = lambda lanes: jnp.concatenate((q_ref[:reach, lanes], q_ref[last:, lanes]), axis=0)
    else:
        mine = code
        query = lambda lanes: q_ref[:, lanes]
    own = (link_bias(mine, code), lambda lanes: k_ref[:, lanes], lambda lanes: v_ref[:, lanes])
    halo = (
        link_bias(mine, codes[...]),
        lambda lanes: keys[:, lanes],
        lambda lanes: values[:, lanes],
    )
    attend_block(query, [own, halo], out_ref)


def attend_cost(tokens, span, width):
    return pl.CostEstimate(
        flops=HEADS * tokens * span * 2 * LANES * 4,
        bytes_accessed=12 * tokens * width,
        transcendentals=HEADS * tokens * span,
    )


VMEM = pl.BlockSpec(memory_space=pltpu.VMEM)
SMEM = pl.BlockSpec(memory_space=pltpu.SMEM)
PARAMS = pltpu.CompilerParams(vmem_limit_bytes=VMEM_LIMIT)


def attend_middle(queries, keys, values, code, reach):
    tokens, width = queries.shape
    return pl.pallas_call(
        functools.partial(middle_kernel, reach),
        in_specs=[VMEM] * 4,
        out_specs=VMEM,
        out_shape=jax.ShapeDtypeStruct((tokens - 2 * reach, width), jnp.bfloat16),
        compiler_params=PARAMS,
        cost_estimate=attend_cost(tokens - 2 * reach, tokens, width),
        name="attend_middle",
    )(queries, keys, values, code)


def attend_edges(valid, queries, keys, values, code, halos, reach):
    tokens, width = queries.shape
    rows = min(tokens, 2 * reach)
    held = -(-2 * reach // LANES) * LANES
    return pl.pallas_call(
        functools.partial(edge_kernel, reach),
        in_specs=[SMEM] + [VMEM] * (4 + len(halos)),
        out_specs=VMEM,
        out_shape=jax.ShapeDtypeStruct((rows, width), jnp.bfloat16),
        scratch_shapes=[
            pltpu.VMEM((held, width), jnp.bfloat16),
            pltpu.VMEM((held, width), jnp.bfloat16),
            pltpu.VMEM((held, LANES), jnp.float32),
        ],
        compiler_params=PARAMS,
        cost_estimate=attend_cost(rows, LANES, width),
        name="attend_edges",
    )(valid, queries, keys, values, code, *halos)


def pack_grads_kernel(grad_ref, mark_ref, first_ref, second_ref, sems):
    half = grad_ref.shape[1] // 2
    copies = []
    for n, ref in enumerate((first_ref, second_ref)):
        copies.append(
            pltpu.make_async_copy(
                grad_ref.at[:, pl.ds(n * half, half)], ref.at[:, pl.ds(0, half)], sems.at[n]
            )
        )
    for copy in copies:
        copy.start()
    place = columns(mark_ref[1:2]).astype(jnp.bfloat16)
    for ref in (first_ref, second_ref):
        ref[:, half:] = place
    for copy in copies:
        copy.wait()


def pack_grads(grads, marks):
    tokens, width = grads.shape
    return pl.pallas_call(
        pack_grads_kernel,
        in_specs=[pl.BlockSpec(memory_space=pltpu.HBM), VMEM],
        out_specs=[VMEM] * 2,
        out_shape=[jax.ShapeDtypeStruct((tokens, width // 2 + LANES), jnp.bfloat16)] * 2,
        scratch_shapes=[pltpu.SemaphoreType.DMA((2,))],
        compiler_params=pltpu.CompilerParams(vmem_limit_bytes=PACK_LIMIT),
        cost_estimate=pl.CostEstimate(flops=0, bytes_accessed=4 * tokens * width, transcendentals=0),
        name="pack_grads",
    )(grads, marks)


def pack_ends_kernel(most, first_ref, k_ref, v_ref, mark_ref, *refs):
    end_refs, sems = refs[:2], refs[2]
    tokens, width = k_ref.shape
    copies = []
    for n, ref in enumerate(end_refs):
        first = pl.multiple_of(first_ref[n], most)
        for m, source in enumerate((k_ref, v_ref)):
            copies.append(
                pltpu.make_async_copy(
                    source.at[pl.ds(first, most)],
                    ref.at[:, pl.ds(m * width, width)],
                    sems.at[2 * n + m],
                )
            )
    for copy in copies:
        copy.start()
    code = columns(mark_ref[:1])
    for n, ref in enumerate(end_refs):
        here = jnp.where(first_ref[n] == 0, code[:most], code[tokens - most :])
        ref[:, 2 * width :] = here.astype(jnp.bfloat16)
    for copy in copies:
        copy.wait()


def pack_ends(firsts, keys, values, marks, most):
    tokens, width = keys.shape
    ends = jax.ShapeDtypeStruct((most, 2 * width + LANES), jnp.bfloat16)
    return pl.pallas_call(
        functools.partial(pack_ends_kernel, most),
        in_specs=[SMEM] + [pl.BlockSpec(memory_space=pltpu.HBM)] * 2 + [VMEM],
        out_specs=[VMEM] * 2,
        out_shape=[ends, ends],
        scratch_shapes=[pltpu.SemaphoreType.DMA((4,))],
        compiler_params=pltpu.CompilerParams(vmem_limit_bytes=ENDS_LIMIT),
        cost_estimate=pl.CostEstimate(
            flops=0, bytes_accessed=16 * most * width, transcendentals=0
        ),
        name="pack_ends",
    )(firsts, keys, values, marks)


def selector(row):
    tokens = row.shape[1]
    wanted = lax.broadcasted_iota(jnp.int32, (tokens, tokens), 0).astype(jnp.float32)
    return jnp.where(wanted == row, 1.0, 0.0)


def sums_kernel(sizes, flag_ref, gate_ref, *refs):
    half = gate_ref.shape[1] // 2
    count = len(sizes)
    for n in range(2):
        mine_ref, theirs_ref = refs[2 * n : 2 * n + 2]
        picks, rows = [], []
        for ref in (mine_ref, theirs_ref):
            place = ref[:, half : half + LANES].astype(jnp.float32).T[:1]
            picks.append(selector(place).astype(jnp.bfloat16))
            rows.append(ref[:, :half])
        summed = jnp.dot(
            jnp.concatenate(picks, axis=1),
            jnp.concatenate(rows, axis=0),
            preferred_element_type=jnp.float32,
        )
        term = gate_ref[:, n * half : (n + 1) * half] * summed
        term = (term + flag_ref[n] * rows[1].astype(jnp.float32)).astype(jnp.bfloat16)
        at = 0
        for ref, size in zip(refs[4 + n * count : 4 + (n + 1) * count], sizes):
            ref[...] = term[at : at + size]
            at += size


def pair_sums(flags, gate, parts, sizes):
    tokens, width = parts[0].shape[0], gate.shape[1]
    outs = [jax.ShapeDtypeStruct((size, width // 2), jnp.bfloat16) for size in sizes] * 2
    return pl.pallas_call(
        functools.partial(sums_kernel, sizes),
        in_specs=[SMEM] + [VMEM] * 5,
        out_specs=[VMEM] * len(outs),
        out_shape=outs,
        compiler_params=PARAMS,
        cost_estimate=pl.CostEstimate(
            flops=4 * tokens * tokens * width, bytes_accessed=6 * tokens * width, transcendentals=0
        ),
        name="pair_sums",
    )(flags, gate, *parts)


def piece_spots(tokens, reach, piece):
    if tokens <= 2 * reach:
        return [(0, tokens, 0)]
    if piece == 0:
        return [(reach, tokens - 2 * reach, 0)]
    return [(0, reach, 0), (tokens - reach, reach, reach)]


def relay_kernel(spots, first_row, chunks, row_ref, gate_ref, branch_refs, base_ref, total_refs, *refs):
    grad_ref, out_ref, staged, sems, grad_sems = refs[-5:]
    tokens, width = base_ref.shape
    half = width // 2
    copies = []
    for n, ref in enumerate(total_refs):
        copies.append(
            pltpu.make_async_copy(
                ref,
                grad_ref.at[pl.ds(first_row, ref.shape[0]), pl.ds(n * half, half)],
                grad_sems.at[n],
            )
        )
    for copy in copies:
        copy.start()
    picks = selector(row_ref[...]).T.astype(jnp.bfloat16)
    picks = jnp.concatenate([picks[:, top : top + size] for top, size, at in spots], axis=1)
    step = half // chunks
    for n, ref in enumerate(branch_refs):
        for c in range(chunks):
            lanes = slice(n * half + c * step, n * half + (c + 1) * step)
            relayed = jnp.dot(
                picks, ref[:, c * step : (c + 1) * step], preferred_element_type=jnp.float32
            )
            total = base_ref[:, lanes].astype(jnp.float32) + gate_ref[:, lanes] * relayed
            staged[:, lanes] = total.astype(staged.dtype)
            if sems is not None:
                part = pl.ds(n * half + c * step, step)
                copy = pltpu.make_async_copy(
                    staged.at[:, part], out_ref.at[:, part], sems.at[n * chunks + c]
                )
                copy.start()
                copies.append(copy)
    for copy in copies:
        copy.wait()


def relay(rows, gate, branch, base, totals, spots, first_row, grads, last):
    tokens, width = base.shape
    chunks = 2 if width // 2 % (2 * LANES) == 0 else 1
    far = pl.BlockSpec(memory_space=pltpu.HBM)
    whole = jax.ShapeDtypeStruct((tokens, width), jnp.bfloat16)

    def kernel(row_ref, gate_ref, a_ref, b_ref, base_ref, c_ref, d_ref, *refs):
        if grads is not None:
            refs = refs[1:]
        if last:
            grad_ref, out_ref, staged, sems, grad_sems = refs
        else:
            grad_ref, out_ref, grad_sems = refs
            staged, sems = out_ref, None
        relay_kernel(
            spots, first_row, chunks, row_ref, gate_ref, (a_ref, b_ref), base_ref, (c_ref, d_ref),
            grad_ref, out_ref, staged, sems, grad_sems,
        )

    out = whole if last else jax.ShapeDtypeStruct((tokens, width), jnp.float32)
    scratch = [pltpu.VMEM((tokens, width), jnp.bfloat16), pltpu.SemaphoreType.DMA((2 * chunks,))]
    operands = [rows, gate, *branch, base, *totals] + ([] if grads is None else [grads])
    return pl.pallas_call(
        kernel,
        in_specs=[VMEM] * 7 + ([] if grads is None else [far]),
        out_specs=[far, far if last else VMEM],
        out_shape=[whole, out],
        input_output_aliases={} if grads is None else {7: 0},
        scratch_shapes=(scratch if last else []) + [pltpu.SemaphoreType.DMA((2,))],
        compiler_params=PARAMS,
        cost_estimate=pl.CostEstimate(
            flops=2 * tokens * tokens * width,
            bytes_accessed=24 * tokens * width,
            transcendentals=0,
        ),
        name="relay",
    )(*operands)


def whole_gate(gate):
    ranks = lax.axis_size("rep")
    if ranks != 2:
        return lax.all_gather(gate, "rep", axis=0, tiled=True)
    other = lax.ppermute(gate, "rep", [(0, 1), (1, 0)])
    first = lax.axis_index("rep") == 0
    return jnp.concatenate([jnp.where(first, gate, other), jnp.where(first, other, gate)])


SWAP_X, SWAP_Y = [(0, 1), (1, 0), (2, 3), (3, 2)], [(0, 2), (2, 0), (1, 3), (3, 1)]
ROUND_A, ROUND_B = [(0, 1), (1, 3), (3, 2), (2, 0)], [(0, 2), (2, 3), (3, 1), (1, 0)]


def added(a, b):
    return (a.astype(jnp.float32) + b.astype(jnp.float32)).astype(a.dtype)


def local(query_rows, key_rows, value_rows, view_frame, control_row, control_gate, out_grad):
    queries, keys, values = query_rows[0, 0], key_rows[0, 0], value_rows[0, 0]
    tokens, width = queries.shape
    half = width // 2
    ranks = lax.axis_size("seq")
    reach = 2 * (tokens * ranks // 32)
    hops = (reach + tokens - 1) // tokens
    group, rank = lax.axis_index("grp"), lax.axis_index("seq")
    send = lambda block, route: lax.ppermute(block, "grp", route)

    tag = view_frame[0, 0]
    code = tag + 8 * (tag // FRAMES) + 16
    marks = jnp.stack((code, control_row[0, 0] % tokens)).astype(jnp.float32)
    code, rows = marks[:1], marks[1:]
    most = min(tokens, reach)
    even = rank % 2 == 0
    firsts = jnp.where(jnp.stack((even, ~even)), tokens - most, 0).astype(jnp.int32)
    sent_a, sent_b = pack_grads(out_grad[0, 0], marks)
    marks, sent_a, sent_b = lax.optimization_barrier((marks, sent_a, sent_b))
    got_a, got_b = send(sent_a, SWAP_X), send(sent_b, SWAP_Y)
    end_one, end_two = pack_ends(firsts, keys, values, marks, most)
    code, end_one, end_two = lax.optimization_barrier((code, end_one, end_two))
    gate = whole_gate(control_gate)[None]
    halos = [paired(end_one, "seq", 0), paired(end_two, "seq", 1)]
    above, below = rank < ranks - 1, rank > 0
    valid = jnp.where(jnp.stack((even, ~even)), above, below).astype(jnp.float32)
    for hop in range(2, hops + 1):
        count = min(tokens, reach - (hop - 1) * tokens)
        tail, head = jnp.where(even, end_one, end_two), jnp.where(even, end_two, end_one)
        halos.append(shifted(tail[most - count :], "seq", hop))
        halos.append(shifted(head[:count], "seq", -hop))

    own = []
    sizes = [min(tokens, 2 * reach)]
    if tokens > 2 * reach:
        own.append(attend_middle(queries, keys, values, code, reach))
        sizes.insert(0, tokens - 2 * reach)
    flags = jnp.stack([group == 1, group == 2]).astype(jnp.float32)
    sums = pair_sums(flags, gate, (sent_a, got_a, sent_b, got_b), sizes)
    count = len(sizes)

    def outgoing(piece, sum_a, sum_b):
        to_a = jnp.where(group == 0, piece[:, :half], jnp.where(group == 1, sum_a, sum_b))
        to_b = jnp.where(group == 0, piece[:, half:], jnp.where(group == 2, sum_b, sum_a))
        return to_a, to_b

    going = [outgoing(own[0], sums[0], sums[count])] if own else []
    valid, *ready = lax.optimization_barrier((valid, *sums, *(going[0] if going else ())))
    sums = ready[: 2 * count]
    if going:
        going = [ready[2 * count :]]
    own.append(attend_edges(valid, queries, keys, values, code, halos, reach))

    going.append(outgoing(own[-1], sums[count - 1], sums[2 * count - 1]))
    spots = [piece_spots(tokens, reach, n) for n in range(count)]
    order = [
        own[n][at : at + size] for top, size, n, at in sorted(
            (top, size, n, at) for n in range(count) for top, size, at in spots[n]
        )
    ]
    block_out = jnp.concatenate(order, axis=0)
    branch_grad, first_row = None, 0
    for n, (piece, sum_a, sum_b) in enumerate(zip(own, sums[:count], sums[count:])):
        piece_a, piece_b = piece[:, :half], piece[:, half:]
        one, two = send(going[n][0], ROUND_A), send(going[n][1], ROUND_B)
        total_a = added(sum_a, jnp.where(group == 1, two, one))
        total_b = added(sum_b, jnp.where(group == 2, one, two))
        held_a = jnp.where(group == 0, piece_a, one)
        held_b = jnp.where(group == 0, piece_b, two)
        across = send(jnp.where((group == 0) | (group == 2), held_b, total_a), SWAP_X)
        down = send(jnp.where(group <= 1, held_a, total_b), SWAP_Y)
        branch_a = jnp.where(group <= 1, held_a, down)
        branch_b = jnp.where((group == 0) | (group == 2), held_b, across)
        totals = (
            jnp.where((group == 0) | (group == 2), across, total_a),
            jnp.where(group <= 1, down, total_b),
        )
        branch_grad, block_out = relay(
            rows, gate, (branch_a, branch_b), block_out, totals, spots[n], first_row, branch_grad,
            n == count - 1,
        )
        first_row += piece.shape[0]
    return (block_out[None, None], branch_grad[None])


def solution(mesh):
    placed = (
        P("rep", "grp", "seq", None),
        P("rep", "grp", "seq", None),
        P("rep", "grp", "seq", None),
        P("rep", "grp", "seq"),
        P("rep", "grp", "seq"),
        P("rep"),
        P("rep", "grp", "seq", None),
    )
    return jax.shard_map(
        local,
        mesh=mesh,
        in_specs=placed,
        out_specs=(P("rep", "grp", "seq", None), P("rep", "seq", None)),
        check_vma=False,
    )
```

```python
import functools
import math

import jax
import jax.numpy as jnp
from jax import lax
from jax.experimental import pallas as pl
from jax.experimental.pallas import tpu as pltpu
from jax.sharding import PartitionSpec as P

HEADS = 32
DH = 80
FRAMES = 20
LANES = 128
VMEM_LIMIT = 32 * 1024 * 1024
PACK_LIMIT = 53 * 1024 * 1024


def shifted(block, axis, distance):
    devices = range(lax.axis_size(axis))
    route = [(i - distance, i) for i in devices if i - distance in devices]
    return lax.ppermute(block, axis, route)


def paired(block, axis, first):
    size = lax.axis_size(axis)
    route = []
    for i in range(size):
        other = i + 1 if (i - first) % 2 == 0 else i - 1
        if 0 <= other < size:
            route.append((i, other))
    return lax.ppermute(block, axis, route)


def lane_windows(heads):
    windows = []
    for head in range(heads):
        first, last = head * DH, (head + 1) * DH
        if windows and last <= windows[-1][0] + 2 * LANES:
            windows[-1][1].append(head)
        else:
            windows.append((first // LANES * LANES, [head]))
    out = []
    for start, members in windows:
        start = min(start, heads * DH - 2 * LANES)
        out.append((start, members))
    return out


def head_masks(rows, period):
    masks = {}
    for start, members in lane_windows(period // DH):
        lane = lax.broadcasted_iota(jnp.int32, (rows, 2 * LANES), 1) + start
        for h in members:
            inside = (lane >= h * DH) & (lane < (h + 1) * DH)
            masks[h] = jnp.where(inside, 1.0, 0.0).astype(jnp.bfloat16)
    return masks


def mixed_period(base, query, sets, masks, period):
    rows = sets[0][0].shape[0]
    factor = math.log2(math.e) / math.sqrt(DH)
    windows = lane_windows(period // DH)
    scores = []
    for start, members in windows:
        lanes = slice(base + start, base + start + 2 * LANES)
        part = query(lanes)
        stacked = jnp.concatenate([part * masks[h] for h in members], axis=0)
        scores.append(
            [
                lax.dot_general(
                    stacked, key(lanes), (((1,), (1,)), ((), ())), preferred_element_type=jnp.float32
                )
                for bias, key, value in sets
            ]
        )
    weights = []
    for parts, (start, members) in zip(scores, windows):
        parts = [
            part.reshape(len(members), rows, -1) + bias[None]
            for part, (bias, key, value) in zip(parts, sets)
        ]
        largest = row_max(parts)
        weights.append(
            [
                jnp.exp2((part - largest) * factor).astype(jnp.bfloat16).reshape(len(members) * rows, -1)
                for part in parts
            ]
        )
    tiles = {}
    for parts, (start, members) in zip(weights, windows):
        lanes = slice(base + start, base + start + 2 * LANES)
        mixed = sum(
            jnp.dot(part, value(lanes), preferred_element_type=jnp.float32)
            for part, (bias, key, value) in zip(parts, sets)
        )
        totals = sum(
            jnp.dot(part, jnp.ones((part.shape[1], LANES), part.dtype), preferred_element_type=jnp.float32)
            for part in parts
        )
        scale = 1.0 / totals
        for n, h in enumerate(members):
            for t in range(2):
                low = start + t * LANES
                if h * DH >= low + LANES or (h + 1) * DH <= low:
                    continue
                mine = slice(n * rows, (n + 1) * rows)
                piece = mixed[mine, t * LANES : (t + 1) * LANES] * scale[mine]
                if low in tiles:
                    lane = lax.broadcasted_iota(jnp.int32, (rows, LANES), 1) + low
                    tiles[low] = jnp.where(lane >= h * DH, piece, tiles[low])
                else:
                    tiles[low] = piece
    return {low: tile.astype(jnp.bfloat16) for low, tile in tiles.items()}


def row_max(parts):
    if all(part.shape == parts[0].shape for part in parts):
        return jnp.max(functools.reduce(jnp.maximum, parts), axis=-1, keepdims=True)
    return functools.reduce(jnp.maximum, [jnp.max(part, axis=-1, keepdims=True) for part in parts])


def columns(row):
    return jnp.broadcast_to(row, (LANES, row.shape[1])).T


def link_bias(mine, theirs):
    return jnp.where(jnp.abs(mine[:, :1] - theirs.T[: mine.shape[0]]) <= 1.5, 0.0, -1e30)


def attend_block(query, sets, out_ref):
    rows, width = out_ref.shape
    period = math.lcm(DH, LANES)
    masks = head_masks(rows, period)
    for base in range(0, width, period):
        tiles = mixed_period(base, query, sets, masks, period)
        for low, tile in tiles.items():
            out_ref[:, base + low : base + low + LANES] = tile


def pack_ends(first_ref, k_ref, v_ref, code, end_refs):
    tokens, width = k_ref.shape
    for n, ref in enumerate(end_refs):
        most = ref.shape[0]
        first = pl.multiple_of(first_ref[n], most)
        ref[:, :width] = k_ref[pl.ds(first, most), :]
        ref[:, width : 2 * width] = v_ref[pl.ds(first, most), :]
        here = jnp.where(first == 0, code[:most], code[tokens - most :])
        ref[:, 2 * width :] = here.astype(jnp.bfloat16)


def middle_kernel(reach, first_ref, q_ref, k_ref, v_ref, code_ref, one_ref, two_ref, out_ref=None):
    code = columns(code_ref[...])
    pack_ends(first_ref, k_ref, v_ref, code, (one_ref, two_ref))
    if out_ref is None:
        return
    rows = out_ref.shape[0]
    bias = link_bias(code[reach : reach + rows], code)
    own = (bias, lambda lanes: k_ref[:, lanes], lambda lanes: v_ref[:, lanes])
    attend_block(lambda lanes: q_ref[reach : reach + rows, lanes], [own], out_ref)


def edge_kernel(reach, q_ref, k_ref, v_ref, code_ref, *refs):
    halos = refs[:-4]
    out_ref, keys, values, codes = refs[-4:]
    tokens, width = q_ref.shape
    code = columns(code_ref[...])
    at = 0
    for piece in halos:
        rows = piece.shape[0]
        keys[at : at + rows] = piece[:, :width]
        values[at : at + rows] = piece[:, width : 2 * width]
        codes[at : at + rows] = piece[:, 2 * width :].astype(jnp.float32)
        at += rows
    if at < keys.shape[0]:
        spare = keys.shape[0] - at
        keys[at:] = jnp.zeros((spare, width), keys.dtype)
        values[at:] = jnp.zeros((spare, width), values.dtype)
        codes[at:] = jnp.zeros((spare, LANES), codes.dtype)
    if tokens > 2 * reach:
        last = tokens - reach
        mine = jnp.concatenate((code[:reach], code[last:]), axis=0)
        query = lambda lanes: jnp.concatenate((q_ref[:reach, lanes], q_ref[last:, lanes]), axis=0)
    else:
        mine = code
        query = lambda lanes: q_ref[:, lanes]
    own = (link_bias(mine, code), lambda lanes: k_ref[:, lanes], lambda lanes: v_ref[:, lanes])
    halo = (
        link_bias(mine, codes[...]),
        lambda lanes: keys[:, lanes],
        lambda lanes: values[:, lanes],
    )
    attend_block(query, [own, halo], out_ref)


def attend_cost(tokens, span, width):
    return pl.CostEstimate(
        flops=HEADS * tokens * span * 2 * LANES * 4,
        bytes_accessed=12 * tokens * width,
        transcendentals=HEADS * tokens * span,
    )


VMEM = pl.BlockSpec(memory_space=pltpu.VMEM)
SMEM = pl.BlockSpec(memory_space=pltpu.SMEM)
PARAMS = pltpu.CompilerParams(vmem_limit_bytes=VMEM_LIMIT)


def attend_middle(firsts, queries, keys, values, code, reach):
    tokens, width = queries.shape
    ends = jax.ShapeDtypeStruct((min(tokens, reach), 2 * width + LANES), jnp.bfloat16)
    outs = [ends, ends]
    if tokens > 2 * reach:
        outs.append(jax.ShapeDtypeStruct((tokens - 2 * reach, width), jnp.bfloat16))
    return pl.pallas_call(
        functools.partial(middle_kernel, reach),
        in_specs=[SMEM] + [VMEM] * 4,
        out_specs=[VMEM] * len(outs),
        out_shape=outs,
        compiler_params=PARAMS,
        cost_estimate=attend_cost(tokens, tokens, width),
        name="attend_middle",
    )(firsts, queries, keys, values, code)


def attend_edges(queries, keys, values, code, halos, reach):
    tokens, width = queries.shape
    rows = min(tokens, 2 * reach)
    held = -(-2 * reach // LANES) * LANES
    return pl.pallas_call(
        functools.partial(edge_kernel, reach),
        in_specs=[VMEM] * (4 + len(halos)),
        out_specs=VMEM,
        out_shape=jax.ShapeDtypeStruct((rows, width), jnp.bfloat16),
        scratch_shapes=[
            pltpu.VMEM((held, width), jnp.bfloat16),
            pltpu.VMEM((held, width), jnp.bfloat16),
            pltpu.VMEM((held, LANES), jnp.float32),
        ],
        compiler_params=PARAMS,
        cost_estimate=attend_cost(rows, LANES, width),
        name="attend_edges",
    )(queries, keys, values, code, *halos)


def pack_grads_kernel(grad_ref, mark_ref, *refs):
    first_ref, second_ref, sems = refs[-3:]
    half = grad_ref.shape[1] // 2
    copies = []
    for n, ref in enumerate((first_ref, second_ref)):
        copies.append(
            pltpu.make_async_copy(
                grad_ref.at[:, pl.ds(n * half, half)], ref.at[:, pl.ds(0, half)], sems.at[n]
            )
        )
    for copy in copies:
        copy.start()
    place = columns(mark_ref[1:2]).astype(jnp.bfloat16)
    for ref in (first_ref, second_ref):
        ref[:, half:] = place
    for copy in copies:
        copy.wait()


def pack_grads(grads, marks, *others):
    tokens, width = grads.shape
    far = pl.BlockSpec(memory_space=pltpu.HBM)
    return pl.pallas_call(
        pack_grads_kernel,
        in_specs=[far, VMEM] + [far] * len(others),
        out_specs=[VMEM] * 2,
        out_shape=[jax.ShapeDtypeStruct((tokens, width // 2 + LANES), jnp.bfloat16)] * 2,
        scratch_shapes=[pltpu.SemaphoreType.DMA((2,))],
        compiler_params=pltpu.CompilerParams(vmem_limit_bytes=PACK_LIMIT),
        cost_estimate=pl.CostEstimate(flops=0, bytes_accessed=4 * tokens * width, transcendentals=0),
        name="pack_grads",
    )(grads, marks, *others)


def selector(row):
    tokens = row.shape[1]
    wanted = lax.broadcasted_iota(jnp.int32, (tokens, tokens), 0).astype(jnp.float32)
    return jnp.where(wanted == row, 1.0, 0.0)


def sums_kernel(sizes, flag_ref, gate_ref, *refs):
    half = gate_ref.shape[1] // 2
    count = len(sizes)
    for n in range(2):
        mine_ref, theirs_ref = refs[2 * n : 2 * n + 2]
        picks, rows = [], []
        for ref in (mine_ref, theirs_ref):
            place = ref[:, half : half + LANES].astype(jnp.float32).T[:1]
            picks.append(selector(place).astype(jnp.bfloat16))
            rows.append(ref[:, :half])
        summed = jnp.dot(
            jnp.concatenate(picks, axis=1),
            jnp.concatenate(rows, axis=0),
            preferred_element_type=jnp.float32,
        )
        term = gate_ref[:, n * half : (n + 1) * half] * summed
        term = (term + flag_ref[n] * rows[1].astype(jnp.float32)).astype(jnp.bfloat16)
        at = 0
        for ref, size in zip(refs[4 + n * count : 4 + (n + 1) * count], sizes):
            ref[...] = term[at : at + size]
            at += size


def pair_sums(flags, gate, parts, sizes):
    tokens, width = parts[0].shape[0], gate.shape[1]
    outs = [jax.ShapeDtypeStruct((size, width // 2), jnp.bfloat16) for size in sizes] * 2
    return pl.pallas_call(
        functools.partial(sums_kernel, sizes),
        in_specs=[SMEM] + [VMEM] * 5,
        out_specs=[VMEM] * len(outs),
        out_shape=outs,
        compiler_params=PARAMS,
        cost_estimate=pl.CostEstimate(
            flops=4 * tokens * tokens * width, bytes_accessed=6 * tokens * width, transcendentals=0
        ),
        name="pair_sums",
    )(flags, gate, *parts)


def piece_spots(tokens, reach, piece):
    if tokens <= 2 * reach:
        return [(0, tokens, 0)]
    if piece == 0:
        return [(reach, tokens - 2 * reach, 0)]
    return [(0, reach, 0), (tokens - reach, reach, reach)]


def relay_kernel(spots, first_row, chunks, row_ref, gate_ref, branch_refs, base_ref, total_refs, *refs):
    grad_ref, out_ref, staged, sems, grad_sems = refs[-5:]
    tokens, width = base_ref.shape
    half = width // 2
    copies = []
    for n, ref in enumerate(total_refs):
        copies.append(
            pltpu.make_async_copy(
                ref,
                grad_ref.at[pl.ds(first_row, ref.shape[0]), pl.ds(n * half, half)],
                grad_sems.at[n],
            )
        )
    for copy in copies:
        copy.start()
    picks = selector(row_ref[...]).T.astype(jnp.bfloat16)
    picks = jnp.concatenate([picks[:, top : top + size] for top, size, at in spots], axis=1)
    step = half // chunks
    for n, ref in enumerate(branch_refs):
        for c in range(chunks):
            lanes = slice(n * half + c * step, n * half + (c + 1) * step)
            relayed = jnp.dot(
                picks, ref[:, c * step : (c + 1) * step], preferred_element_type=jnp.float32
            )
            total = base_ref[:, lanes].astype(jnp.float32) + gate_ref[:, lanes] * relayed
            staged[:, lanes] = total.astype(staged.dtype)
            if sems is not None:
                part = pl.ds(n * half + c * step, step)
                copy = pltpu.make_async_copy(
                    staged.at[:, part], out_ref.at[:, part], sems.at[n * chunks + c]
                )
                copy.start()
                copies.append(copy)
    for copy in copies:
        copy.wait()


def relay(rows, gate, branch, base, totals, spots, first_row, grads, last):
    tokens, width = base.shape
    chunks = 2 if width // 2 % (2 * LANES) == 0 else 1
    far = pl.BlockSpec(memory_space=pltpu.HBM)
    whole = jax.ShapeDtypeStruct((tokens, width), jnp.bfloat16)

    def kernel(row_ref, gate_ref, a_ref, b_ref, base_ref, c_ref, d_ref, *refs):
        if grads is not None:
            refs = refs[1:]
        if last:
            grad_ref, out_ref, staged, sems, grad_sems = refs
        else:
            grad_ref, out_ref, grad_sems = refs
            staged, sems = out_ref, None
        relay_kernel(
            spots, first_row, chunks, row_ref, gate_ref, (a_ref, b_ref), base_ref, (c_ref, d_ref),
            grad_ref, out_ref, staged, sems, grad_sems,
        )

    out = whole if last else jax.ShapeDtypeStruct((tokens, width), jnp.float32)
    scratch = [pltpu.VMEM((tokens, width), jnp.bfloat16), pltpu.SemaphoreType.DMA((2 * chunks,))]
    operands = [rows, gate, *branch, base, *totals] + ([] if grads is None else [grads])
    return pl.pallas_call(
        kernel,
        in_specs=[VMEM] * 7 + ([] if grads is None else [far]),
        out_specs=[far, far if last else VMEM],
        out_shape=[whole, out],
        input_output_aliases={} if grads is None else {7: 0},
        scratch_shapes=(scratch if last else []) + [pltpu.SemaphoreType.DMA((2,))],
        compiler_params=PARAMS,
        cost_estimate=pl.CostEstimate(
            flops=2 * tokens * tokens * width,
            bytes_accessed=24 * tokens * width,
            transcendentals=0,
        ),
        name="relay",
    )(*operands)


def whole_gate(gate):
    ranks = lax.axis_size("rep")
    if ranks != 2:
        return lax.all_gather(gate, "rep", axis=0, tiled=True)
    other = lax.ppermute(gate, "rep", [(0, 1), (1, 0)])
    first = lax.axis_index("rep") == 0
    return jnp.concatenate([jnp.where(first, gate, other), jnp.where(first, other, gate)])


SWAP_X, SWAP_Y = [(0, 1), (1, 0), (2, 3), (3, 2)], [(0, 2), (2, 0), (1, 3), (3, 1)]
ROUND_A, ROUND_B = [(0, 1), (1, 3), (3, 2), (2, 0)], [(0, 2), (2, 3), (3, 1), (1, 0)]


def added(a, b):
    return (a.astype(jnp.float32) + b.astype(jnp.float32)).astype(a.dtype)


def local(query_rows, key_rows, value_rows, view_frame, control_row, control_gate, out_grad):
    queries, keys, values = query_rows[0, 0], key_rows[0, 0], value_rows[0, 0]
    tokens, width = queries.shape
    half = width // 2
    ranks = lax.axis_size("seq")
    reach = 2 * (tokens * ranks // 32)
    hops = (reach + tokens - 1) // tokens
    group, rank = lax.axis_index("grp"), lax.axis_index("seq")
    send = lambda block, route: lax.ppermute(block, "grp", route)

    tag = view_frame[0, 0]
    code = tag + 8 * (tag // FRAMES) + 16
    marks = jnp.stack((code, control_row[0, 0] % tokens)).astype(jnp.float32)
    code, rows = marks[:1], marks[1:]
    most = min(tokens, reach)
    even = rank % 2 == 0
    firsts = jnp.where(jnp.stack((even, ~even)), tokens - most, 0).astype(jnp.int32)
    sent_a, sent_b = pack_grads(out_grad[0, 0], marks, queries, keys, values)
    code, sent_a, sent_b = lax.optimization_barrier((code, sent_a, sent_b))
    got_a, got_b = send(sent_a, SWAP_X), send(sent_b, SWAP_Y)
    end_one, end_two, *own = attend_middle(firsts, queries, keys, values, code, reach)
    gate = whole_gate(control_gate)[None]
    halos = [paired(end_one, "seq", 0), paired(end_two, "seq", 1)]
    for hop in range(2, hops + 1):
        count = min(tokens, reach - (hop - 1) * tokens)
        tail, head = jnp.where(even, end_one, end_two), jnp.where(even, end_two, end_one)
        halos.append(shifted(tail[most - count :], "seq", hop))
        halos.append(shifted(head[:count], "seq", -hop))
    sizes = [piece.shape[0] for piece in own] + [min(tokens, 2 * reach)]
    flags = jnp.stack([group == 1, group == 2]).astype(jnp.float32)
    sums = pair_sums(flags, gate, (sent_a, got_a, sent_b, got_b), sizes)
    count = len(sizes)

    def outgoing(piece, sum_a, sum_b):
        to_a = jnp.where(group == 0, piece[:, :half], jnp.where(group == 1, sum_a, sum_b))
        to_b = jnp.where(group == 0, piece[:, half:], jnp.where(group == 2, sum_b, sum_a))
        return to_a, to_b

    going = [outgoing(own[0], sums[0], sums[count])] if own else []
    code, *ready = lax.optimization_barrier((code, *sums, *(going[0] if going else ())))
    sums = ready[: 2 * count]
    if going:
        going = [ready[2 * count :]]
    own.append(attend_edges(queries, keys, values, code, halos, reach))

    going.append(outgoing(own[-1], sums[count - 1], sums[2 * count - 1]))
    spots = [piece_spots(tokens, reach, n) for n in range(count)]
    order = [
        own[n][at : at + size] for top, size, n, at in sorted(
            (top, size, n, at) for n in range(count) for top, size, at in spots[n]
        )
    ]
    block_out = jnp.concatenate(order, axis=0)
    branch_grad, first_row = None, 0
    for n, (piece, sum_a, sum_b) in enumerate(zip(own, sums[:count], sums[count:])):
        piece_a, piece_b = piece[:, :half], piece[:, half:]
        one, two = send(going[n][0], ROUND_A), send(going[n][1], ROUND_B)
        total_a = added(sum_a, jnp.where(group == 1, two, one))
        total_b = added(sum_b, jnp.where(group == 2, one, two))
        held_a = jnp.where(group == 0, piece_a, one)
        held_b = jnp.where(group == 0, piece_b, two)
        across = send(jnp.where((group == 0) | (group == 2), held_b, total_a), SWAP_X)
        down = send(jnp.where(group <= 1, held_a, total_b), SWAP_Y)
        branch_a = jnp.where(group <= 1, held_a, down)
        branch_b = jnp.where((group == 0) | (group == 2), held_b, across)
        totals = (
            jnp.where((group == 0) | (group == 2), across, total_a),
            jnp.where(group <= 1, down, total_b),
        )
        branch_grad, block_out = relay(
            rows, gate, (branch_a, branch_b), block_out, totals, spots[n], first_row, branch_grad,
            n == count - 1,
        )
        first_row += piece.shape[0]
    return (block_out[None, None], branch_grad[None])


def solution(mesh):
    placed = (
        P("rep", "grp", "seq", None),
        P("rep", "grp", "seq", None),
        P("rep", "grp", "seq", None),
        P("rep", "grp", "seq"),
        P("rep", "grp", "seq"),
        P("rep"),
        P("rep", "grp", "seq", None),
    )
    return jax.shard_map(
        local,
        mesh=mesh,
        in_specs=placed,
        out_specs=(P("rep", "grp", "seq", None), P("rep", "seq", None)),
        check_vma=False,
    )
```

```python
import functools
import math

import jax
import jax.numpy as jnp
from jax import lax
from jax.experimental import pallas as pl
from jax.experimental.pallas import tpu as pltpu
from jax.sharding import PartitionSpec as P

HEADS = 32
DH = 80
FRAMES = 20
LANES = 128
VMEM_LIMIT = 32 * 1024 * 1024
PACK_LIMIT = 52 * 1024 * 1024


def shifted(block, axis, distance):
    devices = range(lax.axis_size(axis))
    route = [(i - distance, i) for i in devices if i - distance in devices]
    return lax.ppermute(block, axis, route)


def paired(block, axis, first):
    size = lax.axis_size(axis)
    route = []
    for i in range(size):
        other = i + 1 if (i - first) % 2 == 0 else i - 1
        if 0 <= other < size:
            route.append((i, other))
    return lax.ppermute(block, axis, route)


def lane_windows(heads):
    windows = []
    for head in range(heads):
        first, last = head * DH, (head + 1) * DH
        if windows and last <= windows[-1][0] + 2 * LANES:
            windows[-1][1].append(head)
        else:
            windows.append((first // LANES * LANES, [head]))
    out = []
    for start, members in windows:
        start = min(start, heads * DH - 2 * LANES)
        out.append((start, members))
    return out


def head_masks(rows, period):
    masks = {}
    for start, members in lane_windows(period // DH):
        lane = lax.broadcasted_iota(jnp.int32, (rows, 2 * LANES), 1) + start
        for h in members:
            inside = (lane >= h * DH) & (lane < (h + 1) * DH)
            masks[h] = jnp.where(inside, 1.0, 0.0).astype(jnp.bfloat16)
    return masks


def mixed_period(base, query, sets, masks, period):
    rows = sets[0][0].shape[0]
    factor = math.log2(math.e) / math.sqrt(DH)
    windows = lane_windows(period // DH)
    scores = []
    for start, members in windows:
        lanes = slice(base + start, base + start + 2 * LANES)
        part = query(lanes)
        stacked = jnp.concatenate([part * masks[h] for h in members], axis=0)
        scores.append(
            [
                lax.dot_general(
                    stacked, key(lanes), (((1,), (1,)), ((), ())), preferred_element_type=jnp.float32
                )
                for bias, key, value in sets
            ]
        )
    weights = []
    for parts, (start, members) in zip(scores, windows):
        parts = [
            part.reshape(len(members), rows, -1) + bias[None]
            for part, (bias, key, value) in zip(parts, sets)
        ]
        largest = row_max(parts)
        weights.append(
            [
                jnp.exp2((part - largest) * factor).astype(jnp.bfloat16).reshape(len(members) * rows, -1)
                for part in parts
            ]
        )
    tiles = {}
    for parts, (start, members) in zip(weights, windows):
        lanes = slice(base + start, base + start + 2 * LANES)
        mixed = sum(
            jnp.dot(part, value(lanes), preferred_element_type=jnp.float32)
            for part, (bias, key, value) in zip(parts, sets)
        )
        totals = sum(
            jnp.dot(part, jnp.ones((part.shape[1], LANES), part.dtype), preferred_element_type=jnp.float32)
            for part in parts
        )
        scale = 1.0 / totals
        for n, h in enumerate(members):
            for t in range(2):
                low = start + t * LANES
                if h * DH >= low + LANES or (h + 1) * DH <= low:
                    continue
                mine = slice(n * rows, (n + 1) * rows)
                piece = mixed[mine, t * LANES : (t + 1) * LANES] * scale[mine]
                if low in tiles:
                    lane = lax.broadcasted_iota(jnp.int32, (rows, LANES), 1) + low
                    tiles[low] = jnp.where(lane >= h * DH, piece, tiles[low])
                else:
                    tiles[low] = piece
    return {low: tile.astype(jnp.bfloat16) for low, tile in tiles.items()}


def row_max(parts):
    if all(part.shape == parts[0].shape for part in parts):
        return jnp.max(functools.reduce(jnp.maximum, parts), axis=-1, keepdims=True)
    return functools.reduce(jnp.maximum, [jnp.max(part, axis=-1, keepdims=True) for part in parts])


def columns(row):
    return jnp.broadcast_to(row, (LANES, row.shape[1])).T


def link_bias(mine, theirs):
    return jnp.where(jnp.abs(mine[:, :1] - theirs.T[: mine.shape[0]]) <= 1.5, 0.0, -1e30)


def attend_block(query, sets, out_ref):
    rows, width = out_ref.shape
    period = math.lcm(DH, LANES)
    masks = head_masks(rows, period)
    for base in range(0, width, period):
        tiles = mixed_period(base, query, sets, masks, period)
        for low, tile in tiles.items():
            out_ref[:, base + low : base + low + LANES] = tile


def pack_ends(first_ref, k_ref, v_ref, code, end_refs):
    tokens, width = k_ref.shape
    for n, ref in enumerate(end_refs):
        most = ref.shape[0]
        first = pl.multiple_of(first_ref[n], most)
        ref[:, :width] = k_ref[pl.ds(first, most), :]
        ref[:, width : 2 * width] = v_ref[pl.ds(first, most), :]
        here = jnp.where(first == 0, code[:most], code[tokens - most :])
        ref[:, 2 * width :] = here.astype(jnp.bfloat16)


def middle_kernel(reach, first_ref, q_ref, k_ref, v_ref, code_ref, one_ref, two_ref, out_ref=None):
    code = columns(code_ref[...])
    pack_ends(first_ref, k_ref, v_ref, code, (one_ref, two_ref))
    if out_ref is None:
        return
    rows = out_ref.shape[0]
    bias = link_bias(code[reach : reach + rows], code)
    own = (bias, lambda lanes: k_ref[:, lanes], lambda lanes: v_ref[:, lanes])
    attend_block(lambda lanes: q_ref[reach : reach + rows, lanes], [own], out_ref)


def edge_kernel(reach, q_ref, k_ref, v_ref, code_ref, *refs):
    halos = refs[:-4]
    out_ref, keys, values, codes = refs[-4:]
    tokens, width = q_ref.shape
    code = columns(code_ref[...])
    at = 0
    for piece in halos:
        rows = piece.shape[0]
        keys[at : at + rows] = piece[:, :width]
        values[at : at + rows] = piece[:, width : 2 * width]
        codes[at : at + rows] = piece[:, 2 * width :].astype(jnp.float32)
        at += rows
    if at < keys.shape[0]:
        spare = keys.shape[0] - at
        keys[at:] = jnp.zeros((spare, width), keys.dtype)
        values[at:] = jnp.zeros((spare, width), values.dtype)
        codes[at:] = jnp.zeros((spare, LANES), codes.dtype)
    if tokens > 2 * reach:
        last = tokens - reach
        mine = jnp.concatenate((code[:reach], code[last:]), axis=0)
        query = lambda lanes: jnp.concatenate((q_ref[:reach, lanes], q_ref[last:, lanes]), axis=0)
    else:
        mine = code
        query = lambda lanes: q_ref[:, lanes]
    own = (link_bias(mine, code), lambda lanes: k_ref[:, lanes], lambda lanes: v_ref[:, lanes])
    halo = (
        link_bias(mine, codes[...]),
        lambda lanes: keys[:, lanes],
        lambda lanes: values[:, lanes],
    )
    attend_block(query, [own, halo], out_ref)


def attend_cost(tokens, span, width):
    return pl.CostEstimate(
        flops=HEADS * tokens * span * 2 * LANES * 4,
        bytes_accessed=12 * tokens * width,
        transcendentals=HEADS * tokens * span,
    )


VMEM = pl.BlockSpec(memory_space=pltpu.VMEM)
SMEM = pl.BlockSpec(memory_space=pltpu.SMEM)
PARAMS = pltpu.CompilerParams(vmem_limit_bytes=VMEM_LIMIT)


def attend_middle(firsts, queries, keys, values, code, reach):
    tokens, width = queries.shape
    ends = jax.ShapeDtypeStruct((min(tokens, reach), 2 * width + LANES), jnp.bfloat16)
    outs = [ends, ends]
    if tokens > 2 * reach:
        outs.append(jax.ShapeDtypeStruct((tokens - 2 * reach, width), jnp.bfloat16))
    return pl.pallas_call(
        functools.partial(middle_kernel, reach),
        in_specs=[SMEM] + [VMEM] * 4,
        out_specs=[VMEM] * len(outs),
        out_shape=outs,
        compiler_params=PARAMS,
        cost_estimate=attend_cost(tokens, tokens, width),
        name="attend_middle",
    )(firsts, queries, keys, values, code)


def attend_edges(queries, keys, values, code, halos, reach):
    tokens, width = queries.shape
    rows = min(tokens, 2 * reach)
    held = -(-2 * reach // LANES) * LANES
    return pl.pallas_call(
        functools.partial(edge_kernel, reach),
        in_specs=[VMEM] * (4 + len(halos)),
        out_specs=VMEM,
        out_shape=jax.ShapeDtypeStruct((rows, width), jnp.bfloat16),
        scratch_shapes=[
            pltpu.VMEM((held, width), jnp.bfloat16),
            pltpu.VMEM((held, width), jnp.bfloat16),
            pltpu.VMEM((held, LANES), jnp.float32),
        ],
        compiler_params=PARAMS,
        cost_estimate=attend_cost(rows, LANES, width),
        name="attend_edges",
    )(queries, keys, values, code, *halos)


def pack_grads_kernel(grad_ref, mark_ref, *refs):
    first_ref, second_ref, sems = refs[-3:]
    half = grad_ref.shape[1] // 2
    copies = []
    for n, ref in enumerate((first_ref, second_ref)):
        copies.append(
            pltpu.make_async_copy(
                grad_ref.at[:, pl.ds(n * half, half)], ref.at[:, pl.ds(0, half)], sems.at[n]
            )
        )
    for copy in copies:
        copy.start()
    place = columns(mark_ref[1:2]).astype(jnp.bfloat16)
    for ref in (first_ref, second_ref):
        ref[:, half:] = place
    for copy in copies:
        copy.wait()


def pack_grads(grads, marks, *others):
    tokens, width = grads.shape
    far = pl.BlockSpec(memory_space=pltpu.HBM)
    return pl.pallas_call(
        pack_grads_kernel,
        in_specs=[far, VMEM] + [far] * len(others),
        out_specs=[VMEM] * 2,
        out_shape=[jax.ShapeDtypeStruct((tokens, width // 2 + LANES), jnp.bfloat16)] * 2,
        scratch_shapes=[pltpu.SemaphoreType.DMA((2,))],
        compiler_params=pltpu.CompilerParams(vmem_limit_bytes=PACK_LIMIT),
        cost_estimate=pl.CostEstimate(flops=0, bytes_accessed=4 * tokens * width, transcendentals=0),
        name="pack_grads",
    )(grads, marks, *others)


def selector(row):
    tokens = row.shape[1]
    wanted = lax.broadcasted_iota(jnp.int32, (tokens, tokens), 0).astype(jnp.float32)
    return jnp.where(wanted == row, 1.0, 0.0)


def sums_kernel(sizes, flag_ref, gate_ref, *refs):
    half = gate_ref.shape[1] // 2
    count = len(sizes)
    for n in range(2):
        mine_ref, theirs_ref = refs[2 * n : 2 * n + 2]
        picks, rows = [], []
        for ref in (mine_ref, theirs_ref):
            place = ref[:, half : half + LANES].astype(jnp.float32).T[:1]
            picks.append(selector(place).astype(jnp.bfloat16))
            rows.append(ref[:, :half])
        summed = jnp.dot(
            jnp.concatenate(picks, axis=1),
            jnp.concatenate(rows, axis=0),
            preferred_element_type=jnp.float32,
        )
        term = gate_ref[:, n * half : (n + 1) * half] * summed
        term = (term + flag_ref[n] * rows[1].astype(jnp.float32)).astype(jnp.bfloat16)
        at = 0
        for ref, size in zip(refs[4 + n * count : 4 + (n + 1) * count], sizes):
            ref[...] = term[at : at + size]
            at += size


def pair_sums(flags, gate, parts, sizes):
    tokens, width = parts[0].shape[0], gate.shape[1]
    outs = [jax.ShapeDtypeStruct((size, width // 2), jnp.bfloat16) for size in sizes] * 2
    return pl.pallas_call(
        functools.partial(sums_kernel, sizes),
        in_specs=[SMEM] + [VMEM] * 5,
        out_specs=[VMEM] * len(outs),
        out_shape=outs,
        compiler_params=PARAMS,
        cost_estimate=pl.CostEstimate(
            flops=4 * tokens * tokens * width, bytes_accessed=6 * tokens * width, transcendentals=0
        ),
        name="pair_sums",
    )(flags, gate, *parts)


def piece_spots(tokens, reach, piece):
    if tokens <= 2 * reach:
        return [(0, tokens, 0)]
    if piece == 0:
        return [(reach, tokens - 2 * reach, 0)]
    return [(0, reach, 0), (tokens - reach, reach, reach)]


def relay_kernel(spots, first_row, chunks, row_ref, gate_ref, branch_refs, base_ref, total_refs, *refs):
    grad_ref, out_ref, staged, sems, grad_sems = refs[-5:]
    tokens, width = base_ref.shape
    half = width // 2
    copies = []
    for n, ref in enumerate(total_refs):
        copies.append(
            pltpu.make_async_copy(
                ref,
                grad_ref.at[pl.ds(first_row, ref.shape[0]), pl.ds(n * half, half)],
                grad_sems.at[n],
            )
        )
    for copy in copies:
        copy.start()
    picks = selector(row_ref[...]).T.astype(jnp.bfloat16)
    picks = jnp.concatenate([picks[:, top : top + size] for top, size, at in spots], axis=1)
    step = half // chunks
    for n, ref in enumerate(branch_refs):
        for c in range(chunks):
            lanes = slice(n * half + c * step, n * half + (c + 1) * step)
            relayed = jnp.dot(
                picks, ref[:, c * step : (c + 1) * step], preferred_element_type=jnp.float32
            )
            total = base_ref[:, lanes].astype(jnp.float32) + gate_ref[:, lanes] * relayed
            staged[:, lanes] = total.astype(staged.dtype)
            if sems is not None:
                part = pl.ds(n * half + c * step, step)
                copy = pltpu.make_async_copy(
                    staged.at[:, part], out_ref.at[:, part], sems.at[n * chunks + c]
                )
                copy.start()
                copies.append(copy)
    for copy in copies:
        copy.wait()


def relay(rows, gate, branch, base, totals, spots, first_row, grads, last):
    tokens, width = base.shape
    chunks = 2 if width // 2 % (2 * LANES) == 0 else 1
    far = pl.BlockSpec(memory_space=pltpu.HBM)
    whole = jax.ShapeDtypeStruct((tokens, width), jnp.bfloat16)

    def kernel(row_ref, gate_ref, a_ref, b_ref, base_ref, c_ref, d_ref, *refs):
        if grads is not None:
            refs = refs[1:]
        if last:
            grad_ref, out_ref, staged, sems, grad_sems = refs
        else:
            grad_ref, out_ref, grad_sems = refs
            staged, sems = out_ref, None
        relay_kernel(
            spots, first_row, chunks, row_ref, gate_ref, (a_ref, b_ref), base_ref, (c_ref, d_ref),
            grad_ref, out_ref, staged, sems, grad_sems,
        )

    out = whole if last else jax.ShapeDtypeStruct((tokens, width), jnp.float32)
    scratch = [pltpu.VMEM((tokens, width), jnp.bfloat16), pltpu.SemaphoreType.DMA((2 * chunks,))]
    operands = [rows, gate, *branch, base, *totals] + ([] if grads is None else [grads])
    return pl.pallas_call(
        kernel,
        in_specs=[VMEM] * 7 + ([] if grads is None else [far]),
        out_specs=[far, far if last else VMEM],
        out_shape=[whole, out],
        input_output_aliases={} if grads is None else {7: 0},
        scratch_shapes=(scratch if last else []) + [pltpu.SemaphoreType.DMA((2,))],
        compiler_params=PARAMS,
        cost_estimate=pl.CostEstimate(
            flops=2 * tokens * tokens * width,
            bytes_accessed=24 * tokens * width,
            transcendentals=0,
        ),
        name="relay",
    )(*operands)


def whole_gate(gate):
    ranks = lax.axis_size("rep")
    if ranks != 2:
        return lax.all_gather(gate, "rep", axis=0, tiled=True)
    other = lax.ppermute(gate, "rep", [(0, 1), (1, 0)])
    first = lax.axis_index("rep") == 0
    return jnp.concatenate([jnp.where(first, gate, other), jnp.where(first, other, gate)])


SWAP_X, SWAP_Y = [(0, 1), (1, 0), (2, 3), (3, 2)], [(0, 2), (2, 0), (1, 3), (3, 1)]
ROUND_A, ROUND_B = [(0, 1), (1, 3), (3, 2), (2, 0)], [(0, 2), (2, 3), (3, 1), (1, 0)]


def added(a, b):
    return (a.astype(jnp.float32) + b.astype(jnp.float32)).astype(a.dtype)


def local(query_rows, key_rows, value_rows, view_frame, control_row, control_gate, out_grad):
    queries, keys, values = query_rows[0, 0], key_rows[0, 0], value_rows[0, 0]
    tokens, width = queries.shape
    half = width // 2
    ranks = lax.axis_size("seq")
    reach = 2 * (tokens * ranks // 32)
    hops = (reach + tokens - 1) // tokens
    group, rank = lax.axis_index("grp"), lax.axis_index("seq")
    send = lambda block, route: lax.ppermute(block, "grp", route)

    tag = view_frame[0, 0]
    code = tag + 8 * (tag // FRAMES) + 16
    marks = jnp.stack((code, control_row[0, 0] % tokens)).astype(jnp.float32)
    code, rows = marks[:1], marks[1:]
    most = min(tokens, reach)
    even = rank % 2 == 0
    firsts = jnp.where(jnp.stack((even, ~even)), tokens - most, 0).astype(jnp.int32)
    sent_a, sent_b = pack_grads(out_grad[0, 0], marks, queries, keys, values)
    code, sent_a, sent_b = lax.optimization_barrier((code, sent_a, sent_b))
    got_a, got_b = send(sent_a, SWAP_X), send(sent_b, SWAP_Y)
    end_one, end_two, *own = attend_middle(firsts, queries, keys, values, code, reach)
    gate = whole_gate(control_gate)[None]
    halos = [paired(end_one, "seq", 0), paired(end_two, "seq", 1)]
    for hop in range(2, hops + 1):
        count = min(tokens, reach - (hop - 1) * tokens)
        tail, head = jnp.where(even, end_one, end_two), jnp.where(even, end_two, end_one)
        halos.append(shifted(tail[most - count :], "seq", hop))
        halos.append(shifted(head[:count], "seq", -hop))
    sizes = [piece.shape[0] for piece in own] + [min(tokens, 2 * reach)]
    flags = jnp.stack([group == 1, group == 2]).astype(jnp.float32)
    sums = pair_sums(flags, gate, (sent_a, got_a, sent_b, got_b), sizes)
    count = len(sizes)

    def outgoing(piece, sum_a, sum_b):
        to_a = jnp.where(group == 0, piece[:, :half], jnp.where(group == 1, sum_a, sum_b))
        to_b = jnp.where(group == 0, piece[:, half:], jnp.where(group == 2, sum_b, sum_a))
        return to_a, to_b

    going = [outgoing(own[0], sums[0], sums[count])] if own else []
    code, *ready = lax.optimization_barrier((code, *sums, *(going[0] if going else ())))
    sums = ready[: 2 * count]
    if going:
        going = [ready[2 * count :]]
    own.append(attend_edges(queries, keys, values, code, halos, reach))

    going.append(outgoing(own[-1], sums[count - 1], sums[2 * count - 1]))
    spots = [piece_spots(tokens, reach, n) for n in range(count)]
    order = [
        own[n][at : at + size] for top, size, n, at in sorted(
            (top, size, n, at) for n in range(count) for top, size, at in spots[n]
        )
    ]
    block_out = jnp.concatenate(order, axis=0)
    branch_grad, first_row = None, 0
    for n, (piece, sum_a, sum_b) in enumerate(zip(own, sums[:count], sums[count:])):
        piece_a, piece_b = piece[:, :half], piece[:, half:]
        one, two = send(going[n][0], ROUND_A), send(going[n][1], ROUND_B)
        total_a = added(sum_a, jnp.where(group == 1, two, one))
        total_b = added(sum_b, jnp.where(group == 2, one, two))
        held_a = jnp.where(group == 0, piece_a, one)
        held_b = jnp.where(group == 0, piece_b, two)
        across = send(jnp.where((group == 0) | (group == 2), held_b, total_a), SWAP_X)
        down = send(jnp.where(group <= 1, held_a, total_b), SWAP_Y)
        branch_a = jnp.where(group <= 1, held_a, down)
        branch_b = jnp.where((group == 0) | (group == 2), held_b, across)
        totals = (
            jnp.where((group == 0) | (group == 2), across, total_a),
            jnp.where(group <= 1, down, total_b),
        )
        branch_grad, block_out = relay(
            rows, gate, (branch_a, branch_b), block_out, totals, spots[n], first_row, branch_grad,
            n == count - 1,
        )
        first_row += piece.shape[0]
    return (block_out[None, None], branch_grad[None])


def solution(mesh):
    placed = (
        P("rep", "grp", "seq", None),
        P("rep", "grp", "seq", None),
        P("rep", "grp", "seq", None),
        P("rep", "grp", "seq"),
        P("rep", "grp", "seq"),
        P("rep"),
        P("rep", "grp", "seq", None),
    )
    return jax.shard_map(
        local,
        mesh=mesh,
        in_specs=placed,
        out_specs=(P("rep", "grp", "seq", None), P("rep", "seq", None)),
        check_vma=False,
    )
```

```python
import functools
import math

import jax
import jax.numpy as jnp
from jax import lax
from jax.experimental import pallas as pl
from jax.experimental.pallas import tpu as pltpu
from jax.sharding import PartitionSpec as P

HEADS = 32
DH = 80
FRAMES = 20
LANES = 128
VMEM_LIMIT = 32 * 1024 * 1024
PACK_LIMIT = 53 * 1024 * 1024


def shifted(block, axis, distance):
    devices = range(lax.axis_size(axis))
    route = [(i - distance, i) for i in devices if i - distance in devices]
    return lax.ppermute(block, axis, route)


def paired(block, axis, first):
    size = lax.axis_size(axis)
    route = []
    for i in range(size):
        other = i + 1 if (i - first) % 2 == 0 else i - 1
        if 0 <= other < size:
            route.append((i, other))
    return lax.ppermute(block, axis, route)


def lane_windows(heads):
    windows = []
    for head in range(heads):
        first, last = head * DH, (head + 1) * DH
        if windows and last <= windows[-1][0] + 2 * LANES:
            windows[-1][1].append(head)
        else:
            windows.append((first // LANES * LANES, [head]))
    out = []
    for start, members in windows:
        start = min(start, heads * DH - 2 * LANES)
        out.append((start, members))
    return out


def head_masks(rows, period):
    masks = {}
    for start, members in lane_windows(period // DH):
        lane = lax.broadcasted_iota(jnp.int32, (rows, 2 * LANES), 1) + start
        for h in members:
            inside = (lane >= h * DH) & (lane < (h + 1) * DH)
            masks[h] = jnp.where(inside, 1.0, 0.0).astype(jnp.bfloat16)
    return masks


def period_scores(base, query, keys, masks, period):
    scores = []
    for start, members in lane_windows(period // DH):
        lanes = slice(base + start, base + start + 2 * LANES)
        part = query(lanes)
        stacked = jnp.concatenate([part * masks[h] for h in members], axis=0)
        scores.append(
            [
                lax.dot_general(
                    stacked, key(lanes), (((1,), (1,)), ((), ())), preferred_element_type=jnp.float32
                )
                for key in keys
            ]
        )
    return scores


def mixed_period(base, scores, sets, period):
    rows = sets[0][0].shape[0]
    factor = math.log2(math.e) / math.sqrt(DH)
    windows = lane_windows(period // DH)
    weights = []
    for parts, (start, members) in zip(scores, windows):
        parts = [
            part.reshape(len(members), rows, -1) + bias[None]
            for part, (bias, value) in zip(parts, sets)
        ]
        largest = row_max(parts)
        weights.append(
            [
                jnp.exp2((part - largest) * factor).astype(jnp.bfloat16).reshape(len(members) * rows, -1)
                for part in parts
            ]
        )
    tiles = {}
    for parts, (start, members) in zip(weights, windows):
        lanes = slice(base + start, base + start + 2 * LANES)
        mixed = sum(
            jnp.dot(part, value(lanes), preferred_element_type=jnp.float32)
            for part, (bias, value) in zip(parts, sets)
        )
        totals = sum(
            jnp.dot(part, jnp.ones((part.shape[1], LANES), part.dtype), preferred_element_type=jnp.float32)
            for part in parts
        )
        scale = 1.0 / totals
        for n, h in enumerate(members):
            for t in range(2):
                low = start + t * LANES
                if h * DH >= low + LANES or (h + 1) * DH <= low:
                    continue
                mine = slice(n * rows, (n + 1) * rows)
                piece = mixed[mine, t * LANES : (t + 1) * LANES] * scale[mine]
                if low in tiles:
                    lane = lax.broadcasted_iota(jnp.int32, (rows, LANES), 1) + low
                    tiles[low] = jnp.where(lane >= h * DH, piece, tiles[low])
                else:
                    tiles[low] = piece
    return {low: tile.astype(jnp.bfloat16) for low, tile in tiles.items()}


def row_max(parts):
    if all(part.shape == parts[0].shape for part in parts):
        return jnp.max(functools.reduce(jnp.maximum, parts), axis=-1, keepdims=True)
    return functools.reduce(jnp.maximum, [jnp.max(part, axis=-1, keepdims=True) for part in parts])


def columns(row):
    return jnp.broadcast_to(row, (LANES, row.shape[1])).T


def link_bias(mine, theirs):
    return jnp.where(jnp.abs(mine[:, :1] - theirs.T[: mine.shape[0]]) <= 1.5, 0.0, -1e30)


def store_period(base, tiles, out_ref):
    for low, tile in tiles.items():
        out_ref[:, base + low : base + low + LANES] = tile


def ends_kernel(first_ref, k_ref, v_ref, code_ref, *end_refs):
    tokens, width = k_ref.shape
    code = columns(code_ref[...])
    for n, ref in enumerate(end_refs):
        most = ref.shape[0]
        first = pl.multiple_of(first_ref[n], most)
        ref[:, :width] = k_ref[pl.ds(first, most), :]
        ref[:, width : 2 * width] = v_ref[pl.ds(first, most), :]
        here = jnp.where(first == 0, code[:most], code[tokens - most :])
        ref[:, 2 * width :] = here.astype(jnp.bfloat16)


def middle_kernel(reach, q_ref, k_ref, v_ref, code_ref, out_ref):
    rows = out_ref.shape[0]
    code = columns(code_ref[...])
    bias = link_bias(code[reach : reach + rows], code)
    period = math.lcm(DH, LANES)
    masks = head_masks(rows, period)
    query = lambda lanes: q_ref[reach : reach + rows, lanes]
    for base in range(0, out_ref.shape[1], period):
        scores = period_scores(base, query, [lambda lanes: k_ref[:, lanes]], masks, period)
        sets = [(bias, lambda lanes: v_ref[:, lanes])]
        store_period(base, mixed_period(base, scores, sets, period), out_ref)


def edge_kernel(reach, q_ref, k_ref, v_ref, code_ref, *refs):
    halos = refs[:-6]
    out_ref, keys, values, codes, near, sems = refs[-6:]
    tokens, width = q_ref.shape
    copies = []
    at = 0
    for n, piece in enumerate(halos):
        rows = piece.shape[0]
        for m, (ref, size) in enumerate(((keys, width), (values, width), (codes, LANES))):
            copies.append(
                pltpu.make_async_copy(
                    piece.at[:, pl.ds(m * width, size)], ref.at[pl.ds(at, rows)], sems.at[n, m]
                )
            )
        at += rows
    for copy in copies:
        copy.start()
    if at < keys.shape[0]:
        for ref in (keys, values, codes):
            ref[at:] = jnp.zeros((ref.shape[0] - at, ref.shape[1]), ref.dtype)
    code = columns(code_ref[...])
    if tokens > 2 * reach:
        last = tokens - reach
        mine = jnp.concatenate((code[:reach], code[last:]), axis=0)
        query = lambda lanes: jnp.concatenate((q_ref[:reach, lanes], q_ref[last:, lanes]), axis=0)
    else:
        mine = code
        query = lambda lanes: q_ref[:, lanes]
    period = math.lcm(DH, LANES)
    rows = out_ref.shape[0]
    masks = head_masks(rows, period)
    place = {}
    at = 0
    for base in range(0, width, period):
        scores = period_scores(base, query, [lambda lanes: k_ref[:, lanes]], masks, period)
        place[base] = []
        for (part,) in scores:
            near[at : at + part.shape[0]] = part
            place[base].append((at, part.shape[0]))
            at += part.shape[0]
    own_bias = link_bias(mine, code)
    for copy in copies:
        copy.wait()
    sets = [
        (own_bias, lambda lanes: v_ref[:, lanes]),
        (link_bias(mine, codes[...].astype(jnp.float32)), lambda lanes: values[:, lanes]),
    ]
    for base in range(0, width, period):
        scores = period_scores(base, query, [lambda lanes: keys[:, lanes]], masks, period)
        scores = [
            [near[first : first + size], *parts]
            for (first, size), parts in zip(place[base], scores)
        ]
        store_period(base, mixed_period(base, scores, sets, period), out_ref)


def attend_cost(tokens, span, width):
    return pl.CostEstimate(
        flops=HEADS * tokens * span * 2 * LANES * 4,
        bytes_accessed=12 * tokens * width,
        transcendentals=HEADS * tokens * span,
    )


VMEM = pl.BlockSpec(memory_space=pltpu.VMEM)
SMEM = pl.BlockSpec(memory_space=pltpu.SMEM)
PARAMS = pltpu.CompilerParams(vmem_limit_bytes=VMEM_LIMIT)


def pack_ends(firsts, keys, values, code, most):
    width = keys.shape[1]
    ends = jax.ShapeDtypeStruct((most, 2 * width + LANES), jnp.bfloat16)
    return pl.pallas_call(
        ends_kernel,
        in_specs=[SMEM] + [VMEM] * 3,
        out_specs=[VMEM] * 2,
        out_shape=[ends, ends],
        compiler_params=PARAMS,
        cost_estimate=pl.CostEstimate(flops=0, bytes_accessed=16 * most * width, transcendentals=0),
        name="pack_ends",
    )(firsts, keys, values, code)


def attend_middle(queries, keys, values, code, reach):
    tokens, width = queries.shape
    return pl.pallas_call(
        functools.partial(middle_kernel, reach),
        in_specs=[VMEM] * 4,
        out_specs=VMEM,
        out_shape=jax.ShapeDtypeStruct((tokens - 2 * reach, width), jnp.bfloat16),
        compiler_params=PARAMS,
        cost_estimate=attend_cost(tokens - 2 * reach, tokens, width),
        name="attend_middle",
    )(queries, keys, values, code)


def attend_edges(queries, keys, values, code, halos, reach):
    tokens, width = queries.shape
    rows = min(tokens, 2 * reach)
    held = -(-2 * reach // LANES) * LANES
    return pl.pallas_call(
        functools.partial(edge_kernel, reach),
        in_specs=[VMEM] * 4 + [pl.BlockSpec(memory_space=pltpu.HBM)] * len(halos),
        out_specs=VMEM,
        out_shape=jax.ShapeDtypeStruct((rows, width), jnp.bfloat16),
        scratch_shapes=[
            pltpu.VMEM((held, width), jnp.bfloat16),
            pltpu.VMEM((held, width), jnp.bfloat16),
            pltpu.VMEM((held, LANES), jnp.bfloat16),
            pltpu.VMEM((rows * (width // DH), tokens), jnp.float32),
            pltpu.SemaphoreType.DMA((len(halos), 3)),
        ],
        compiler_params=PARAMS,
        cost_estimate=attend_cost(rows, LANES, width),
        name="attend_edges",
    )(queries, keys, values, code, *halos)


def pack_grads_kernel(grad_ref, mark_ref, *refs):
    first_ref, second_ref, sems = refs[-3:]
    half = grad_ref.shape[1] // 2
    copies = []
    for n, ref in enumerate((first_ref, second_ref)):
        copies.append(
            pltpu.make_async_copy(
                grad_ref.at[:, pl.ds(n * half, half)], ref.at[:, pl.ds(0, half)], sems.at[n]
            )
        )
    for copy in copies:
        copy.start()
    place = columns(mark_ref[1:2]).astype(jnp.bfloat16)
    for ref in (first_ref, second_ref):
        ref[:, half:] = place
    for copy in copies:
        copy.wait()


def pack_grads(grads, marks, *others):
    tokens, width = grads.shape
    far = pl.BlockSpec(memory_space=pltpu.HBM)
    return pl.pallas_call(
        pack_grads_kernel,
        in_specs=[far, VMEM] + [far] * len(others),
        out_specs=[VMEM] * 2,
        out_shape=[jax.ShapeDtypeStruct((tokens, width // 2 + LANES), jnp.bfloat16)] * 2,
        scratch_shapes=[pltpu.SemaphoreType.DMA((2,))],
        compiler_params=pltpu.CompilerParams(vmem_limit_bytes=PACK_LIMIT),
        cost_estimate=pl.CostEstimate(flops=0, bytes_accessed=4 * tokens * width, transcendentals=0),
        name="pack_grads",
    )(grads, marks, *others)


def selector(row):
    tokens = row.shape[1]
    wanted = lax.broadcasted_iota(jnp.int32, (tokens, tokens), 0).astype(jnp.float32)
    return jnp.where(wanted == row, 1.0, 0.0)


def sums_kernel(sizes, flag_ref, gate_ref, *refs):
    half = gate_ref.shape[1] // 2
    count = len(sizes)
    for n in range(2):
        mine_ref, theirs_ref = refs[2 * n : 2 * n + 2]
        picks, rows = [], []
        for ref in (mine_ref, theirs_ref):
            place = ref[:, half : half + LANES].astype(jnp.float32).T[:1]
            picks.append(selector(place).astype(jnp.bfloat16))
            rows.append(ref[:, :half])
        summed = jnp.dot(
            jnp.concatenate(picks, axis=1),
            jnp.concatenate(rows, axis=0),
            preferred_element_type=jnp.float32,
        )
        term = gate_ref[:, n * half : (n + 1) * half] * summed
        term = (term + flag_ref[n] * rows[1].astype(jnp.float32)).astype(jnp.bfloat16)
        at = 0
        for ref, size in zip(refs[4 + n * count : 4 + (n + 1) * count], sizes):
            ref[...] = term[at : at + size]
            at += size


def pair_sums(flags, gate, parts, sizes):
    tokens, width = parts[0].shape[0], gate.shape[1]
    outs = [jax.ShapeDtypeStruct((size, width // 2), jnp.bfloat16) for size in sizes] * 2
    return pl.pallas_call(
        functools.partial(sums_kernel, sizes),
        in_specs=[SMEM] + [VMEM] * 5,
        out_specs=[VMEM] * len(outs),
        out_shape=outs,
        compiler_params=PARAMS,
        cost_estimate=pl.CostEstimate(
            flops=4 * tokens * tokens * width, bytes_accessed=6 * tokens * width, transcendentals=0
        ),
        name="pair_sums",
    )(flags, gate, *parts)


def piece_spots(tokens, reach, piece):
    if tokens <= 2 * reach:
        return [(0, tokens, 0)]
    if piece == 0:
        return [(reach, tokens - 2 * reach, 0)]
    return [(0, reach, 0), (tokens - reach, reach, reach)]


def relay_kernel(spots, first_row, chunks, row_ref, gate_ref, branch_refs, base_ref, total_refs, *refs):
    grad_ref, out_ref, staged, sems, grad_sems = refs[-5:]
    tokens, width = base_ref.shape
    half = width // 2
    copies = []
    for n, ref in enumerate(total_refs):
        copies.append(
            pltpu.make_async_copy(
                ref,
                grad_ref.at[pl.ds(first_row, ref.shape[0]), pl.ds(n * half, half)],
                grad_sems.at[n],
            )
        )
    for copy in copies:
        copy.start()
    picks = selector(row_ref[...]).T.astype(jnp.bfloat16)
    picks = jnp.concatenate([picks[:, top : top + size] for top, size, at in spots], axis=1)
    step = half // chunks
    for n, ref in enumerate(branch_refs):
        for c in range(chunks):
            lanes = slice(n * half + c * step, n * half + (c + 1) * step)
            relayed = jnp.dot(
                picks, ref[:, c * step : (c + 1) * step], preferred_element_type=jnp.float32
            )
            total = base_ref[:, lanes].astype(jnp.float32) + gate_ref[:, lanes] * relayed
            staged[:, lanes] = total.astype(staged.dtype)
            if sems is not None:
                part = pl.ds(n * half + c * step, step)
                copy = pltpu.make_async_copy(
                    staged.at[:, part], out_ref.at[:, part], sems.at[n * chunks + c]
                )
                copy.start()
                copies.append(copy)
    for copy in copies:
        copy.wait()


def relay(rows, gate, branch, base, totals, spots, first_row, grads, last):
    tokens, width = base.shape
    chunks = width // 2 // (2 * LANES) if width // 2 % (2 * LANES) == 0 else 1
    far = pl.BlockSpec(memory_space=pltpu.HBM)
    whole = jax.ShapeDtypeStruct((tokens, width), jnp.bfloat16)

    def kernel(row_ref, gate_ref, a_ref, b_ref, base_ref, c_ref, d_ref, *refs):
        if grads is not None:
            refs = refs[1:]
        if last:
            grad_ref, out_ref, staged, sems, grad_sems = refs
        else:
            grad_ref, out_ref, grad_sems = refs
            staged, sems = out_ref, None
        relay_kernel(
            spots, first_row, chunks, row_ref, gate_ref, (a_ref, b_ref), base_ref, (c_ref, d_ref),
            grad_ref, out_ref, staged, sems, grad_sems,
        )

    out = whole if last else jax.ShapeDtypeStruct((tokens, width), jnp.float32)
    scratch = [pltpu.VMEM((tokens, width), jnp.bfloat16), pltpu.SemaphoreType.DMA((2 * chunks,))]
    operands = [rows, gate, *branch, base, *totals] + ([] if grads is None else [grads])
    return pl.pallas_call(
        kernel,
        in_specs=[VMEM] * 7 + ([] if grads is None else [far]),
        out_specs=[far, far if last else VMEM],
        out_shape=[whole, out],
        input_output_aliases={} if grads is None else {7: 0},
        scratch_shapes=(scratch if last else []) + [pltpu.SemaphoreType.DMA((2,))],
        compiler_params=PARAMS,
        cost_estimate=pl.CostEstimate(
            flops=2 * tokens * tokens * width,
            bytes_accessed=24 * tokens * width,
            transcendentals=0,
        ),
        name="relay",
    )(*operands)


def whole_gate(gate):
    ranks = lax.axis_size("rep")
    if ranks != 2:
        return lax.all_gather(gate, "rep", axis=0, tiled=True)
    other = lax.ppermute(gate, "rep", [(0, 1), (1, 0)])
    first = lax.axis_index("rep") == 0
    return jnp.concatenate([jnp.where(first, gate, other), jnp.where(first, other, gate)])


SWAP_X, SWAP_Y = [(0, 1), (1, 0), (2, 3), (3, 2)], [(0, 2), (2, 0), (1, 3), (3, 1)]
ROUND_A, ROUND_B = [(0, 1), (1, 3), (3, 2), (2, 0)], [(0, 2), (2, 3), (3, 1), (1, 0)]


def added(a, b):
    return (a.astype(jnp.float32) + b.astype(jnp.float32)).astype(a.dtype)


def local(query_rows, key_rows, value_rows, view_frame, control_row, control_gate, out_grad):
    queries, keys, values = query_rows[0, 0], key_rows[0, 0], value_rows[0, 0]
    tokens, width = queries.shape
    half = width // 2
    ranks = lax.axis_size("seq")
    reach = 2 * (tokens * ranks // 32)
    hops = (reach + tokens - 1) // tokens
    group, rank = lax.axis_index("grp"), lax.axis_index("seq")
    send = lambda block, route: lax.ppermute(block, "grp", route)

    tag = view_frame[0, 0]
    code = tag + 8 * (tag // FRAMES) + 16
    marks = jnp.stack((code, control_row[0, 0] % tokens)).astype(jnp.float32)
    code, rows = marks[:1], marks[1:]
    most = min(tokens, reach)
    even = rank % 2 == 0
    firsts = jnp.where(jnp.stack((even, ~even)), tokens - most, 0).astype(jnp.int32)
    sent_a, sent_b = pack_grads(out_grad[0, 0], marks, queries, keys, values)
    code, sent_a, sent_b = lax.optimization_barrier((code, sent_a, sent_b))
    got_a, got_b = send(sent_a, SWAP_X), send(sent_b, SWAP_Y)
    end_one, end_two = pack_ends(firsts, keys, values, code, most)
    code, end_one, end_two = lax.optimization_barrier((code, end_one, end_two))
    own = [attend_middle(queries, keys, values, code, reach)] if tokens > 2 * reach else []
    gate = whole_gate(control_gate)[None]
    halos = [paired(end_one, "seq", 0), paired(end_two, "seq", 1)]
    for hop in range(2, hops + 1):
        count = min(tokens, reach - (hop - 1) * tokens)
        tail, head = jnp.where(even, end_one, end_two), jnp.where(even, end_two, end_one)
        halos.append(shifted(tail[most - count :], "seq", hop))
        halos.append(shifted(head[:count], "seq", -hop))
    sizes = [piece.shape[0] for piece in own] + [min(tokens, 2 * reach)]
    flags = jnp.stack([group == 1, group == 2]).astype(jnp.float32)
    sums = pair_sums(flags, gate, (sent_a, got_a, sent_b, got_b), sizes)
    count = len(sizes)

    def outgoing(piece, sum_a, sum_b):
        to_a = jnp.where(group == 0, piece[:, :half], jnp.where(group == 1, sum_a, sum_b))
        to_b = jnp.where(group == 0, piece[:, half:], jnp.where(group == 2, sum_b, sum_a))
        return to_a, to_b

    going = [outgoing(own[0], sums[0], sums[count])] if own else []
    code, *ready = lax.optimization_barrier((code, *sums, *(going[0] if going else ())))
    sums = ready[: 2 * count]
    if going:
        going = [ready[2 * count :]]
    own.append(attend_edges(queries, keys, values, code, halos, reach))

    going.append(outgoing(own[-1], sums[count - 1], sums[2 * count - 1]))
    spots = [piece_spots(tokens, reach, n) for n in range(count)]
    order = [
        own[n][at : at + size] for top, size, n, at in sorted(
            (top, size, n, at) for n in range(count) for top, size, at in spots[n]
        )
    ]
    block_out = jnp.concatenate(order, axis=0)
    branch_grad, first_row = None, 0
    for n, (piece, sum_a, sum_b) in enumerate(zip(own, sums[:count], sums[count:])):
        piece_a, piece_b = piece[:, :half], piece[:, half:]
        one, two = send(going[n][0], ROUND_A), send(going[n][1], ROUND_B)
        total_a = added(sum_a, jnp.where(group == 1, two, one))
        total_b = added(sum_b, jnp.where(group == 2, one, two))
        held_a = jnp.where(group == 0, piece_a, one)
        held_b = jnp.where(group == 0, piece_b, two)
        across = send(jnp.where((group == 0) | (group == 2), held_b, total_a), SWAP_X)
        down = send(jnp.where(group <= 1, held_a, total_b), SWAP_Y)
        branch_a = jnp.where(group <= 1, held_a, down)
        branch_b = jnp.where((group == 0) | (group == 2), held_b, across)
        totals = (
            jnp.where((group == 0) | (group == 2), across, total_a),
            jnp.where(group <= 1, down, total_b),
        )
        branch_grad, block_out = relay(
            rows, gate, (branch_a, branch_b), block_out, totals, spots[n], first_row, branch_grad,
            n == count - 1,
        )
        first_row += piece.shape[0]
    return (block_out[None, None], branch_grad[None])


def solution(mesh):
    placed = (
        P("rep", "grp", "seq", None),
        P("rep", "grp", "seq", None),
        P("rep", "grp", "seq", None),
        P("rep", "grp", "seq"),
        P("rep", "grp", "seq"),
        P("rep"),
        P("rep", "grp", "seq", None),
    )
    return jax.shard_map(
        local,
        mesh=mesh,
        in_specs=placed,
        out_specs=(P("rep", "grp", "seq", None), P("rep", "seq", None)),
        check_vma=False,
    )
```

```python
import functools
import math

import jax
import jax.numpy as jnp
from jax import lax
from jax.experimental import pallas as pl
from jax.experimental.pallas import tpu as pltpu
from jax.sharding import PartitionSpec as P

HEADS = 32
DH = 80
FRAMES = 20
LANES = 128
VMEM_LIMIT = 32 * 1024 * 1024
PACK_LIMIT = 53 * 1024 * 1024


def shifted(block, axis, distance):
    devices = range(lax.axis_size(axis))
    route = [(i - distance, i) for i in devices if i - distance in devices]
    return lax.ppermute(block, axis, route)


def paired(block, axis, first):
    size = lax.axis_size(axis)
    route = []
    for i in range(size):
        other = i + 1 if (i - first) % 2 == 0 else i - 1
        if 0 <= other < size:
            route.append((i, other))
    return lax.ppermute(block, axis, route)


def lane_windows(heads):
    windows = []
    for head in range(heads):
        first, last = head * DH, (head + 1) * DH
        if windows and last <= windows[-1][0] + 2 * LANES:
            windows[-1][1].append(head)
        else:
            windows.append((first // LANES * LANES, [head]))
    out = []
    for start, members in windows:
        start = min(start, heads * DH - 2 * LANES)
        out.append((start, members))
    return out


def head_masks(rows, period):
    masks = {}
    for start, members in lane_windows(period // DH):
        lane = lax.broadcasted_iota(jnp.int32, (rows, 2 * LANES), 1) + start
        for h in members:
            inside = (lane >= h * DH) & (lane < (h + 1) * DH)
            masks[h] = jnp.where(inside, 1.0, 0.0).astype(jnp.bfloat16)
    return masks


def period_scores(base, query, keys, masks, period):
    scores = []
    for start, members in lane_windows(period // DH):
        lanes = slice(base + start, base + start + 2 * LANES)
        part = query(lanes)
        stacked = jnp.concatenate([part * masks[h] for h in members], axis=0)
        scores.append(
            [
                lax.dot_general(
                    stacked, key(lanes), (((1,), (1,)), ((), ())), preferred_element_type=jnp.float32
                )
                for key in keys
            ]
        )
    return scores


def mixed_period(base, scores, sets, period):
    rows = sets[0][0].shape[0]
    factor = math.log2(math.e) / math.sqrt(DH)
    windows = lane_windows(period // DH)
    weights = []
    for parts, (start, members) in zip(scores, windows):
        parts = [
            part.reshape(len(members), rows, -1) + bias[None]
            for part, (bias, value) in zip(parts, sets)
        ]
        largest = row_max(parts)
        weights.append(
            [
                jnp.exp2((part - largest) * factor).astype(jnp.bfloat16).reshape(len(members) * rows, -1)
                for part in parts
            ]
        )
    tiles = {}
    for parts, (start, members) in zip(weights, windows):
        lanes = slice(base + start, base + start + 2 * LANES)
        mixed = sum(
            jnp.dot(part, value(lanes), preferred_element_type=jnp.float32)
            for part, (bias, value) in zip(parts, sets)
        )
        totals = sum(
            jnp.dot(part, jnp.ones((part.shape[1], LANES), part.dtype), preferred_element_type=jnp.float32)
            for part in parts
        )
        scale = 1.0 / totals
        for n, h in enumerate(members):
            for t in range(2):
                low = start + t * LANES
                if h * DH >= low + LANES or (h + 1) * DH <= low:
                    continue
                mine = slice(n * rows, (n + 1) * rows)
                piece = mixed[mine, t * LANES : (t + 1) * LANES] * scale[mine]
                if low in tiles:
                    lane = lax.broadcasted_iota(jnp.int32, (rows, LANES), 1) + low
                    tiles[low] = jnp.where(lane >= h * DH, piece, tiles[low])
                else:
                    tiles[low] = piece
    return {low: tile.astype(jnp.bfloat16) for low, tile in tiles.items()}


def row_max(parts):
    if all(part.shape == parts[0].shape for part in parts):
        return jnp.max(functools.reduce(jnp.maximum, parts), axis=-1, keepdims=True)
    return functools.reduce(jnp.maximum, [jnp.max(part, axis=-1, keepdims=True) for part in parts])


def columns(row):
    return jnp.broadcast_to(row, (LANES, row.shape[1])).T


def link_bias(mine, theirs):
    return jnp.where(jnp.abs(mine[:, :1] - theirs.T[: mine.shape[0]]) <= 1.5, 0.0, -1e30)


def store_period(base, tiles, out_ref):
    for low, tile in tiles.items():
        out_ref[:, base + low : base + low + LANES] = tile


def ends_kernel(first_ref, k_ref, v_ref, code_ref, *end_refs):
    tokens, width = k_ref.shape
    code = columns(code_ref[...])
    for n, ref in enumerate(end_refs):
        most = ref.shape[0]
        first = pl.multiple_of(first_ref[n], most)
        ref[:, :width] = k_ref[pl.ds(first, most), :]
        ref[:, width : 2 * width] = v_ref[pl.ds(first, most), :]
        here = jnp.where(first == 0, code[:most], code[tokens - most :])
        ref[:, 2 * width :] = here.astype(jnp.bfloat16)


def middle_kernel(reach, q_ref, k_ref, v_ref, code_ref, out_ref):
    rows = out_ref.shape[0]
    code = columns(code_ref[...])
    bias = link_bias(code[reach : reach + rows], code)
    period = math.lcm(DH, LANES)
    masks = head_masks(rows, period)
    query = lambda lanes: q_ref[reach : reach + rows, lanes]
    for base in range(0, out_ref.shape[1], period):
        scores = period_scores(base, query, [lambda lanes: k_ref[:, lanes]], masks, period)
        sets = [(bias, lambda lanes: v_ref[:, lanes])]
        store_period(base, mixed_period(base, scores, sets, period), out_ref)


def edge_kernel(reach, q_ref, k_ref, v_ref, code_ref, *refs):
    halos = refs[:-5]
    out_ref, keys, values, codes, sems = refs[-5:]
    tokens, width = q_ref.shape
    period = math.lcm(DH, LANES)
    bases = list(range(0, width, period))
    waits = {base: [] for base in bases}
    code_waits = []
    at = 0
    for n, piece in enumerate(halos):
        rows = pl.ds(at, piece.shape[0])
        code_waits.append(
            pltpu.make_async_copy(
                piece.at[:, pl.ds(2 * width, LANES)], codes.at[rows], sems.at[n, 2 * len(bases)]
            )
        )
        at += piece.shape[0]
    for c, base in enumerate(bases):
        at = 0
        for n, piece in enumerate(halos):
            rows = pl.ds(at, piece.shape[0])
            for m, ref in enumerate((keys, values)):
                waits[base].append(
                    pltpu.make_async_copy(
                        piece.at[:, pl.ds(m * width + base, period)],
                        ref.at[rows, pl.ds(base, period)],
                        sems.at[n, 2 * c + m],
                    )
                )
            at += piece.shape[0]
    for copy in code_waits + [copy for base in bases for copy in waits[base]]:
        copy.start()
    if at < keys.shape[0]:
        for ref in (keys, values, codes):
            ref[at:] = jnp.zeros((ref.shape[0] - at, ref.shape[1]), ref.dtype)
    code = columns(code_ref[...])
    if tokens > 2 * reach:
        last = tokens - reach
        mine = jnp.concatenate((code[:reach], code[last:]), axis=0)
        query = lambda lanes: jnp.concatenate((q_ref[:reach, lanes], q_ref[last:, lanes]), axis=0)
    else:
        mine = code
        query = lambda lanes: q_ref[:, lanes]
    masks = head_masks(out_ref.shape[0], period)
    own_bias = link_bias(mine, code)
    own_key, halo_key = lambda lanes: k_ref[:, lanes], lambda lanes: keys[:, lanes]
    own_value, halo_value = lambda lanes: v_ref[:, lanes], lambda lanes: values[:, lanes]
    halo_bias = None
    for base in bases:
        if halo_bias is None:
            early = period_scores(base, query, [own_key], masks, period)
            for copy in code_waits + waits[base]:
                copy.wait()
            halo_bias = link_bias(mine, codes[...].astype(jnp.float32))
            late = period_scores(base, query, [halo_key], masks, period)
            scores = [first + second for first, second in zip(early, late)]
        else:
            for copy in waits[base]:
                copy.wait()
            scores = period_scores(base, query, [own_key, halo_key], masks, period)
        sets = [(own_bias, own_value), (halo_bias, halo_value)]
        store_period(base, mixed_period(base, scores, sets, period), out_ref)


def attend_cost(tokens, span, width):
    return pl.CostEstimate(
        flops=HEADS * tokens * span * 2 * LANES * 4,
        bytes_accessed=12 * tokens * width,
        transcendentals=HEADS * tokens * span,
    )


VMEM = pl.BlockSpec(memory_space=pltpu.VMEM)
SMEM = pl.BlockSpec(memory_space=pltpu.SMEM)
PARAMS = pltpu.CompilerParams(vmem_limit_bytes=VMEM_LIMIT)


def pack_ends(firsts, keys, values, code, most):
    width = keys.shape[1]
    ends = jax.ShapeDtypeStruct((most, 2 * width + LANES), jnp.bfloat16)
    return pl.pallas_call(
        ends_kernel,
        in_specs=[SMEM] + [VMEM] * 3,
        out_specs=[VMEM] * 2,
        out_shape=[ends, ends],
        compiler_params=PARAMS,
        cost_estimate=pl.CostEstimate(flops=0, bytes_accessed=16 * most * width, transcendentals=0),
        name="pack_ends",
    )(firsts, keys, values, code)


def attend_middle(queries, keys, values, code, reach):
    tokens, width = queries.shape
    return pl.pallas_call(
        functools.partial(middle_kernel, reach),
        in_specs=[VMEM] * 4,
        out_specs=VMEM,
        out_shape=jax.ShapeDtypeStruct((tokens - 2 * reach, width), jnp.bfloat16),
        compiler_params=PARAMS,
        cost_estimate=attend_cost(tokens - 2 * reach, tokens, width),
        name="attend_middle",
    )(queries, keys, values, code)


def attend_edges(queries, keys, values, code, halos, reach):
    tokens, width = queries.shape
    rows = min(tokens, 2 * reach)
    held = -(-2 * reach // LANES) * LANES
    return pl.pallas_call(
        functools.partial(edge_kernel, reach),
        in_specs=[VMEM] * 4 + [pl.BlockSpec(memory_space=pltpu.HBM)] * len(halos),
        out_specs=VMEM,
        out_shape=jax.ShapeDtypeStruct((rows, width), jnp.bfloat16),
        scratch_shapes=[
            pltpu.VMEM((held, width), jnp.bfloat16),
            pltpu.VMEM((held, width), jnp.bfloat16),
            pltpu.VMEM((held, LANES), jnp.bfloat16),
            pltpu.SemaphoreType.DMA((len(halos), 2 * width // math.lcm(DH, LANES) + 1)),
        ],
        compiler_params=PARAMS,
        cost_estimate=attend_cost(rows, LANES, width),
        name="attend_edges",
    )(queries, keys, values, code, *halos)


def pack_grads_kernel(grad_ref, mark_ref, *refs):
    first_ref, second_ref, sems = refs[-3:]
    half = grad_ref.shape[1] // 2
    copies = []
    for n, ref in enumerate((first_ref, second_ref)):
        copies.append(
            pltpu.make_async_copy(
                grad_ref.at[:, pl.ds(n * half, half)], ref.at[:, pl.ds(0, half)], sems.at[n]
            )
        )
    for copy in copies:
        copy.start()
    place = columns(mark_ref[1:2]).astype(jnp.bfloat16)
    for ref in (first_ref, second_ref):
        ref[:, half:] = place
    for copy in copies:
        copy.wait()


def pack_grads(grads, marks, *others):
    tokens, width = grads.shape
    far = pl.BlockSpec(memory_space=pltpu.HBM)
    return pl.pallas_call(
        pack_grads_kernel,
        in_specs=[far, VMEM] + [far] * len(others),
        out_specs=[VMEM] * 2,
        out_shape=[jax.ShapeDtypeStruct((tokens, width // 2 + LANES), jnp.bfloat16)] * 2,
        scratch_shapes=[pltpu.SemaphoreType.DMA((2,))],
        compiler_params=pltpu.CompilerParams(vmem_limit_bytes=PACK_LIMIT),
        cost_estimate=pl.CostEstimate(flops=0, bytes_accessed=4 * tokens * width, transcendentals=0),
        name="pack_grads",
    )(grads, marks, *others)


def selector(row):
    tokens = row.shape[1]
    wanted = lax.broadcasted_iota(jnp.int32, (tokens, tokens), 0).astype(jnp.float32)
    return jnp.where(wanted == row, 1.0, 0.0)


def sums_kernel(sizes, flag_ref, gate_ref, *refs):
    half = gate_ref.shape[1] // 2
    count = len(sizes)
    second, sem = refs[-2:]
    copy = pltpu.make_async_copy(refs[3], second, sem)
    copy.start()
    for n in range(2):
        mine_ref, theirs_ref = refs[2 * n : 2 * n + 2]
        if n == 1:
            theirs_ref = second
            copy.wait()
        picks, rows = [], []
        for ref in (mine_ref, theirs_ref):
            place = ref[:, half : half + LANES].astype(jnp.float32).T[:1]
            picks.append(selector(place).astype(jnp.bfloat16))
            rows.append(ref[:, :half])
        summed = jnp.dot(
            jnp.concatenate(picks, axis=1),
            jnp.concatenate(rows, axis=0),
            preferred_element_type=jnp.float32,
        )
        term = gate_ref[:, n * half : (n + 1) * half] * summed
        term = (term + flag_ref[n] * rows[1].astype(jnp.float32)).astype(jnp.bfloat16)
        at = 0
        for ref, size in zip(refs[4 + n * count : 4 + (n + 1) * count], sizes):
            ref[...] = term[at : at + size]
            at += size


def pair_sums(flags, gate, parts, sizes):
    tokens, width = parts[0].shape[0], gate.shape[1]
    outs = [jax.ShapeDtypeStruct((size, width // 2), jnp.bfloat16) for size in sizes] * 2
    return pl.pallas_call(
        functools.partial(sums_kernel, sizes),
        in_specs=[SMEM] + [VMEM] * 4 + [pl.BlockSpec(memory_space=pltpu.HBM)],
        scratch_shapes=[pltpu.VMEM(parts[3].shape, jnp.bfloat16), pltpu.SemaphoreType.DMA],
        out_specs=[VMEM] * len(outs),
        out_shape=outs,
        compiler_params=PARAMS,
        cost_estimate=pl.CostEstimate(
            flops=4 * tokens * tokens * width, bytes_accessed=6 * tokens * width, transcendentals=0
        ),
        name="pair_sums",
    )(flags, gate, *parts)


def piece_spots(tokens, reach, piece):
    if tokens <= 2 * reach:
        return [(0, tokens, 0)]
    if piece == 0:
        return [(reach, tokens - 2 * reach, 0)]
    return [(0, reach, 0), (tokens - reach, reach, reach)]


def relay_kernel(spots, first_row, chunks, row_ref, gate_ref, branch_refs, base_ref, total_refs, *refs):
    grad_ref, out_ref, staged, sems, grad_sems = refs[-5:]
    tokens, width = base_ref.shape
    half = width // 2
    copies = []
    for n, ref in enumerate(total_refs):
        copies.append(
            pltpu.make_async_copy(
                ref,
                grad_ref.at[pl.ds(first_row, ref.shape[0]), pl.ds(n * half, half)],
                grad_sems.at[n],
            )
        )
    for copy in copies:
        copy.start()
    picks = selector(row_ref[...]).T.astype(jnp.bfloat16)
    picks = jnp.concatenate([picks[:, top : top + size] for top, size, at in spots], axis=1)
    step = half // chunks
    for n, ref in enumerate(branch_refs):
        for c in range(chunks):
            lanes = slice(n * half + c * step, n * half + (c + 1) * step)
            relayed = jnp.dot(
                picks, ref[:, c * step : (c + 1) * step], preferred_element_type=jnp.float32
            )
            total = base_ref[:, lanes].astype(jnp.float32) + gate_ref[:, lanes] * relayed
            staged[:, lanes] = total.astype(staged.dtype)
            if sems is not None:
                part = pl.ds(n * half + c * step, step)
                copy = pltpu.make_async_copy(
                    staged.at[:, part], out_ref.at[:, part], sems.at[n * chunks + c]
                )
                copy.start()
                copies.append(copy)
    for copy in copies:
        copy.wait()


def relay(rows, gate, branch, base, totals, spots, first_row, grads, last):
    tokens, width = base.shape
    chunks = 2 if width // 2 % (2 * LANES) == 0 else 1
    far = pl.BlockSpec(memory_space=pltpu.HBM)
    whole = jax.ShapeDtypeStruct((tokens, width), jnp.bfloat16)

    def kernel(row_ref, gate_ref, a_ref, b_ref, base_ref, c_ref, d_ref, *refs):
        if grads is not None:
            refs = refs[1:]
        if last:
            grad_ref, out_ref, staged, sems, grad_sems = refs
        else:
            grad_ref, out_ref, grad_sems = refs
            staged, sems = out_ref, None
        relay_kernel(
            spots, first_row, chunks, row_ref, gate_ref, (a_ref, b_ref), base_ref, (c_ref, d_ref),
            grad_ref, out_ref, staged, sems, grad_sems,
        )

    out = whole if last else jax.ShapeDtypeStruct((tokens, width), jnp.float32)
    scratch = [pltpu.VMEM((tokens, width), jnp.bfloat16), pltpu.SemaphoreType.DMA((2 * chunks,))]
    operands = [rows, gate, *branch, base, *totals] + ([] if grads is None else [grads])
    return pl.pallas_call(
        kernel,
        in_specs=[VMEM] * 7 + ([] if grads is None else [far]),
        out_specs=[far, far if last else VMEM],
        out_shape=[whole, out],
        input_output_aliases={} if grads is None else {7: 0},
        scratch_shapes=(scratch if last else []) + [pltpu.SemaphoreType.DMA((2,))],
        compiler_params=PARAMS,
        cost_estimate=pl.CostEstimate(
            flops=2 * tokens * tokens * width,
            bytes_accessed=24 * tokens * width,
            transcendentals=0,
        ),
        name="relay",
    )(*operands)


def whole_gate(gate):
    ranks = lax.axis_size("rep")
    if ranks != 2:
        return lax.all_gather(gate, "rep", axis=0, tiled=True)
    other = lax.ppermute(gate, "rep", [(0, 1), (1, 0)])
    first = lax.axis_index("rep") == 0
    return jnp.concatenate([jnp.where(first, gate, other), jnp.where(first, other, gate)])


SWAP_X, SWAP_Y = [(0, 1), (1, 0), (2, 3), (3, 2)], [(0, 2), (2, 0), (1, 3), (3, 1)]
ROUND_A, ROUND_B = [(0, 1), (1, 3), (3, 2), (2, 0)], [(0, 2), (2, 3), (3, 1), (1, 0)]


def added(a, b):
    return (a.astype(jnp.float32) + b.astype(jnp.float32)).astype(a.dtype)


def local(query_rows, key_rows, value_rows, view_frame, control_row, control_gate, out_grad):
    queries, keys, values = query_rows[0, 0], key_rows[0, 0], value_rows[0, 0]
    tokens, width = queries.shape
    half = width // 2
    ranks = lax.axis_size("seq")
    reach = 2 * (tokens * ranks // 32)
    hops = (reach + tokens - 1) // tokens
    group, rank = lax.axis_index("grp"), lax.axis_index("seq")
    send = lambda block, route: lax.ppermute(block, "grp", route)

    tag = view_frame[0, 0]
    code = tag + 8 * (tag // FRAMES) + 16
    marks = jnp.stack((code, control_row[0, 0] % tokens)).astype(jnp.float32)
    code, rows = marks[:1], marks[1:]
    most = min(tokens, reach)
    even = rank % 2 == 0
    firsts = jnp.where(jnp.stack((even, ~even)), tokens - most, 0).astype(jnp.int32)
    sent_a, sent_b = pack_grads(out_grad[0, 0], marks, queries, keys, values)
    code, sent_a, sent_b = lax.optimization_barrier((code, sent_a, sent_b))
    got_a, got_b = send(sent_a, SWAP_X), send(sent_b, SWAP_Y)
    end_one, end_two = pack_ends(firsts, keys, values, code, most)
    code, end_one, end_two = lax.optimization_barrier((code, end_one, end_two))
    own = [attend_middle(queries, keys, values, code, reach)] if tokens > 2 * reach else []
    gate = whole_gate(control_gate)[None]
    halos = [paired(end_one, "seq", 0), paired(end_two, "seq", 1)]
    for hop in range(2, hops + 1):
        count = min(tokens, reach - (hop - 1) * tokens)
        tail, head = jnp.where(even, end_one, end_two), jnp.where(even, end_two, end_one)
        halos.append(shifted(tail[most - count :], "seq", hop))
        halos.append(shifted(head[:count], "seq", -hop))
    sizes = [piece.shape[0] for piece in own] + [min(tokens, 2 * reach)]
    flags = jnp.stack([group == 1, group == 2]).astype(jnp.float32)
    sums = pair_sums(flags, gate, (sent_a, got_a, sent_b, got_b), sizes)
    count = len(sizes)

    def outgoing(piece, sum_a, sum_b):
        to_a = jnp.where(group == 0, piece[:, :half], jnp.where(group == 1, sum_a, sum_b))
        to_b = jnp.where(group == 0, piece[:, half:], jnp.where(group == 2, sum_b, sum_a))
        return to_a, to_b

    going = [outgoing(own[0], sums[0], sums[count])] if own else []
    code, *ready = lax.optimization_barrier((code, *sums, *(going[0] if going else ())))
    sums = ready[: 2 * count]
    if going:
        going = [ready[2 * count :]]
    own.append(attend_edges(queries, keys, values, code, halos, reach))

    going.append(outgoing(own[-1], sums[count - 1], sums[2 * count - 1]))
    spots = [piece_spots(tokens, reach, n) for n in range(count)]
    order = [
        own[n][at : at + size] for top, size, n, at in sorted(
            (top, size, n, at) for n in range(count) for top, size, at in spots[n]
        )
    ]
    block_out = jnp.concatenate(order, axis=0)
    branch_grad, first_row = None, 0
    for n, (piece, sum_a, sum_b) in enumerate(zip(own, sums[:count], sums[count:])):
        piece_a, piece_b = piece[:, :half], piece[:, half:]
        one, two = send(going[n][0], ROUND_A), send(going[n][1], ROUND_B)
        total_a = added(sum_a, jnp.where(group == 1, two, one))
        total_b = added(sum_b, jnp.where(group == 2, one, two))
        held_a = jnp.where(group == 0, piece_a, one)
        held_b = jnp.where(group == 0, piece_b, two)
        across = send(jnp.where((group == 0) | (group == 2), held_b, total_a), SWAP_X)
        down = send(jnp.where(group <= 1, held_a, total_b), SWAP_Y)
        branch_a = jnp.where(group <= 1, held_a, down)
        branch_b = jnp.where((group == 0) | (group == 2), held_b, across)
        totals = (
            jnp.where((group == 0) | (group == 2), across, total_a),
            jnp.where(group <= 1, down, total_b),
        )
        branch_grad, block_out = relay(
            rows, gate, (branch_a, branch_b), block_out, totals, spots[n], first_row, branch_grad,
            n == count - 1,
        )
        first_row += piece.shape[0]
    return (block_out[None, None], branch_grad[None])


def solution(mesh):
    placed = (
        P("rep", "grp", "seq", None),
        P("rep", "grp", "seq", None),
        P("rep", "grp", "seq", None),
        P("rep", "grp", "seq"),
        P("rep", "grp", "seq"),
        P("rep"),
        P("rep", "grp", "seq", None),
    )
    return jax.shard_map(
        local,
        mesh=mesh,
        in_specs=placed,
        out_specs=(P("rep", "grp", "seq", None), P("rep", "seq", None)),
        check_vma=False,
    )
```

```python
import functools
import math

import jax
import jax.numpy as jnp
from jax import lax
from jax.experimental import pallas as pl
from jax.experimental.pallas import tpu as pltpu
from jax.sharding import PartitionSpec as P

HEADS = 32
DH = 80
FRAMES = 20
LANES = 128
VMEM_LIMIT = 32 * 1024 * 1024
PACK_LIMIT = 53 * 1024 * 1024


def shifted(block, axis, distance):
    devices = range(lax.axis_size(axis))
    route = [(i - distance, i) for i in devices if i - distance in devices]
    return lax.ppermute(block, axis, route)


def paired(block, axis, first):
    size = lax.axis_size(axis)
    route = []
    for i in range(size):
        other = i + 1 if (i - first) % 2 == 0 else i - 1
        if 0 <= other < size:
            route.append((i, other))
    return lax.ppermute(block, axis, route)


def lane_windows(heads):
    windows = []
    for head in range(heads):
        first, last = head * DH, (head + 1) * DH
        if windows and last <= windows[-1][0] + 2 * LANES:
            windows[-1][1].append(head)
        else:
            windows.append((first // LANES * LANES, [head]))
    out = []
    for start, members in windows:
        start = min(start, heads * DH - 2 * LANES)
        out.append((start, members))
    return out


def head_masks(rows, period):
    masks = {}
    for start, members in lane_windows(period // DH):
        lane = lax.broadcasted_iota(jnp.int32, (rows, 2 * LANES), 1) + start
        for h in members:
            inside = (lane >= h * DH) & (lane < (h + 1) * DH)
            masks[h] = jnp.where(inside, 1.0, 0.0).astype(jnp.bfloat16)
    return masks


def period_scores(base, query, keys, masks, period):
    scores = []
    for start, members in lane_windows(period // DH):
        lanes = slice(base + start, base + start + 2 * LANES)
        part = query(lanes)
        stacked = jnp.concatenate([part * masks[h] for h in members], axis=0)
        scores.append(
            [
                lax.dot_general(
                    stacked, key(lanes), (((1,), (1,)), ((), ())), preferred_element_type=jnp.float32
                )
                for key in keys
            ]
        )
    return scores


def mixed_period(base, scores, sets, period):
    rows = sets[0][0].shape[0]
    factor = math.log2(math.e) / math.sqrt(DH)
    windows = lane_windows(period // DH)
    weights = []
    for parts, (start, members) in zip(scores, windows):
        parts = [
            part.reshape(len(members), rows, -1) + bias[None]
            for part, (bias, value) in zip(parts, sets)
        ]
        largest = row_max(parts)
        weights.append(
            [
                jnp.exp2((part - largest) * factor).astype(jnp.bfloat16).reshape(len(members) * rows, -1)
                for part in parts
            ]
        )
    tiles = {}
    for parts, (start, members) in zip(weights, windows):
        lanes = slice(base + start, base + start + 2 * LANES)
        mixed = sum(
            jnp.dot(part, value(lanes), preferred_element_type=jnp.float32)
            for part, (bias, value) in zip(parts, sets)
        )
        totals = sum(
            jnp.dot(part, jnp.ones((part.shape[1], LANES), part.dtype), preferred_element_type=jnp.float32)
            for part in parts
        )
        scale = 1.0 / totals
        for n, h in enumerate(members):
            for t in range(2):
                low = start + t * LANES
                if h * DH >= low + LANES or (h + 1) * DH <= low:
                    continue
                mine = slice(n * rows, (n + 1) * rows)
                piece = mixed[mine, t * LANES : (t + 1) * LANES] * scale[mine]
                if low in tiles:
                    lane = lax.broadcasted_iota(jnp.int32, (rows, LANES), 1) + low
                    tiles[low] = jnp.where(lane >= h * DH, piece, tiles[low])
                else:
                    tiles[low] = piece
    return {low: tile.astype(jnp.bfloat16) for low, tile in tiles.items()}


def row_max(parts):
    if all(part.shape == parts[0].shape for part in parts):
        return jnp.max(functools.reduce(jnp.maximum, parts), axis=-1, keepdims=True)
    return functools.reduce(jnp.maximum, [jnp.max(part, axis=-1, keepdims=True) for part in parts])


def columns(row):
    return jnp.broadcast_to(row, (LANES, row.shape[1])).T


def link_bias(mine, theirs):
    return jnp.where(jnp.abs(mine[:, :1] - theirs.T[: mine.shape[0]]) <= 1.5, 0.0, -1e30)


def store_period(base, tiles, out_ref):
    for low, tile in tiles.items():
        out_ref[:, base + low : base + low + LANES] = tile


def ends_kernel(first_ref, k_ref, v_ref, code_ref, *end_refs):
    tokens, width = k_ref.shape
    code = columns(code_ref[...])
    for n, ref in enumerate(end_refs):
        most = ref.shape[0]
        first = pl.multiple_of(first_ref[n], most)
        ref[:, :width] = k_ref[pl.ds(first, most), :]
        ref[:, width : 2 * width] = v_ref[pl.ds(first, most), :]
        here = jnp.where(first == 0, code[:most], code[tokens - most :])
        ref[:, 2 * width :] = here.astype(jnp.bfloat16)


def middle_kernel(reach, q_ref, k_ref, v_ref, code_ref, out_ref):
    rows = out_ref.shape[0]
    code = columns(code_ref[...])
    bias = link_bias(code[reach : reach + rows], code)
    period = math.lcm(DH, LANES)
    masks = head_masks(rows, period)
    query = lambda lanes: q_ref[reach : reach + rows, lanes]
    for base in range(0, out_ref.shape[1], period):
        scores = period_scores(base, query, [lambda lanes: k_ref[:, lanes]], masks, period)
        sets = [(bias, lambda lanes: v_ref[:, lanes])]
        store_period(base, mixed_period(base, scores, sets, period), out_ref)


def sides_kernel(reach, even_ref, q_ref, k_ref, v_ref, code_ref, one_ref, two_ref, *refs):
    out_ref, keys, values, codes = refs
    tokens, width = q_ref.shape
    near = 2 * reach
    code = columns(code_ref[...])
    even = even_ref[0] == 1
    period = math.lcm(DH, LANES)
    masks = head_masks(reach, period)
    blocks = []
    for side, first in ((0, 0), (1, tokens - near)):
        own = slice(first, first + near)
        use_two = even if side == 0 else jnp.logical_not(even)
        halo = jnp.where(use_two, two_ref[...], one_ref[...])
        keys[side, :near] = k_ref[own]
        values[side, :near] = v_ref[own]
        codes[side, :near] = code[own]
        keys[side, near : near + reach] = halo[:, :width]
        values[side, near : near + reach] = halo[:, width : 2 * width]
        codes[side, near : near + reach] = halo[:, 2 * width :].astype(jnp.float32)
        spare = keys.shape[1] - near - reach
        if spare:
            for ref in (keys, values, codes):
                ref[side, near + reach :] = jnp.zeros((spare, ref.shape[2]), ref.dtype)
        top = side * (tokens - reach)
        blocks.append((side, top, link_bias(code[top : top + reach], codes[side])))
    for base in range(0, width, period):
        scores = []
        for side, top, bias in blocks:
            query = lambda lanes: q_ref[top : top + reach, lanes]
            key = lambda lanes: keys[side, :, lanes]
            scores.append(period_scores(base, query, [key], masks, period))
        for (side, top, bias), part in zip(blocks, scores):
            sets = [(bias, lambda lanes: values[side, :, lanes])]
            tiles = mixed_period(base, part, sets, period)
            store_period(base, tiles, out_ref.at[side * reach : (side + 1) * reach])


def edge_kernel(reach, q_ref, k_ref, v_ref, code_ref, *refs):
    halos = refs[:-4]
    out_ref, keys, values, codes = refs[-4:]
    width = q_ref.shape[1]
    code = columns(code_ref[...])
    at = 0
    for piece in halos:
        rows = piece.shape[0]
        keys[at : at + rows] = piece[:, :width]
        values[at : at + rows] = piece[:, width : 2 * width]
        codes[at : at + rows] = piece[:, 2 * width :].astype(jnp.float32)
        at += rows
    if at < keys.shape[0]:
        for ref in (keys, values, codes):
            ref[at:] = jnp.zeros((ref.shape[0] - at, ref.shape[1]), ref.dtype)
    period = math.lcm(DH, LANES)
    masks = head_masks(q_ref.shape[0], period)
    query = lambda lanes: q_ref[:, lanes]
    pair = [lambda lanes: k_ref[:, lanes], lambda lanes: keys[:, lanes]]
    sets = [
        (link_bias(code, code), lambda lanes: v_ref[:, lanes]),
        (link_bias(code, codes[...]), lambda lanes: values[:, lanes]),
    ]
    for base in range(0, width, period):
        scores = period_scores(base, query, pair, masks, period)
        store_period(base, mixed_period(base, scores, sets, period), out_ref)


def attend_cost(tokens, span, width):
    return pl.CostEstimate(
        flops=HEADS * tokens * span * 2 * LANES * 4,
        bytes_accessed=12 * tokens * width,
        transcendentals=HEADS * tokens * span,
    )


VMEM = pl.BlockSpec(memory_space=pltpu.VMEM)
SMEM = pl.BlockSpec(memory_space=pltpu.SMEM)
PARAMS = pltpu.CompilerParams(vmem_limit_bytes=VMEM_LIMIT)


def pack_ends(firsts, keys, values, code, most):
    width = keys.shape[1]
    ends = jax.ShapeDtypeStruct((most, 2 * width + LANES), jnp.bfloat16)
    return pl.pallas_call(
        ends_kernel,
        in_specs=[SMEM] + [VMEM] * 3,
        out_specs=[VMEM] * 2,
        out_shape=[ends, ends],
        compiler_params=PARAMS,
        cost_estimate=pl.CostEstimate(flops=0, bytes_accessed=16 * most * width, transcendentals=0),
        name="pack_ends",
    )(firsts, keys, values, code)


def attend_middle(queries, keys, values, code, reach):
    tokens, width = queries.shape
    return pl.pallas_call(
        functools.partial(middle_kernel, reach),
        in_specs=[VMEM] * 4,
        out_specs=VMEM,
        out_shape=jax.ShapeDtypeStruct((tokens - 2 * reach, width), jnp.bfloat16),
        compiler_params=PARAMS,
        cost_estimate=attend_cost(tokens - 2 * reach, tokens, width),
        name="attend_middle",
    )(queries, keys, values, code)


def attend_edges(even, queries, keys, values, code, halos, reach):
    tokens, width = queries.shape
    rows = min(tokens, 2 * reach)
    if tokens > 2 * reach:
        kernel, operands = sides_kernel, [even, queries, keys, values, code, *halos]
        held = (2, -(-3 * reach // LANES) * LANES)
    else:
        kernel, operands = edge_kernel, [queries, keys, values, code, *halos]
        held = (-(-2 * reach // LANES) * LANES,)
    return pl.pallas_call(
        functools.partial(kernel, reach),
        in_specs=[SMEM if operand is even else VMEM for operand in operands],
        out_specs=VMEM,
        out_shape=jax.ShapeDtypeStruct((rows, width), jnp.bfloat16),
        scratch_shapes=[
            pltpu.VMEM((*held, width), jnp.bfloat16),
            pltpu.VMEM((*held, width), jnp.bfloat16),
            pltpu.VMEM((*held, LANES), jnp.float32),
        ],
        compiler_params=PARAMS,
        cost_estimate=attend_cost(rows, LANES, width),
        name="attend_edges",
    )(*operands)


def pack_grads_kernel(grad_ref, mark_ref, *refs):
    first_ref, second_ref, sems = refs[-3:]
    half = grad_ref.shape[1] // 2
    copies = []
    for n, ref in enumerate((first_ref, second_ref)):
        copies.append(
            pltpu.make_async_copy(
                grad_ref.at[:, pl.ds(n * half, half)], ref.at[:, pl.ds(0, half)], sems.at[n]
            )
        )
    for copy in copies:
        copy.start()
    place = columns(mark_ref[1:2]).astype(jnp.bfloat16)
    for ref in (first_ref, second_ref):
        ref[:, half:] = place
    for copy in copies:
        copy.wait()


def pack_grads(grads, marks, *others):
    tokens, width = grads.shape
    far = pl.BlockSpec(memory_space=pltpu.HBM)
    return pl.pallas_call(
        pack_grads_kernel,
        in_specs=[far, VMEM] + [far] * len(others),
        out_specs=[VMEM] * 2,
        out_shape=[jax.ShapeDtypeStruct((tokens, width // 2 + LANES), jnp.bfloat16)] * 2,
        scratch_shapes=[pltpu.SemaphoreType.DMA((2,))],
        compiler_params=pltpu.CompilerParams(vmem_limit_bytes=PACK_LIMIT),
        cost_estimate=pl.CostEstimate(flops=0, bytes_accessed=4 * tokens * width, transcendentals=0),
        name="pack_grads",
    )(grads, marks, *others)


def selector(row):
    tokens = row.shape[1]
    wanted = lax.broadcasted_iota(jnp.int32, (tokens, tokens), 0).astype(jnp.float32)
    return jnp.where(wanted == row, 1.0, 0.0)


def sums_kernel(sizes, flag_ref, gate_ref, *refs):
    half = gate_ref.shape[1] // 2
    count = len(sizes)
    for n in range(2):
        mine_ref, theirs_ref = refs[2 * n : 2 * n + 2]
        picks, rows = [], []
        for ref in (mine_ref, theirs_ref):
            place = ref[:, half : half + LANES].astype(jnp.float32).T[:1]
            picks.append(selector(place).astype(jnp.bfloat16))
            rows.append(ref[:, :half])
        summed = jnp.dot(
            jnp.concatenate(picks, axis=1),
            jnp.concatenate(rows, axis=0),
            preferred_element_type=jnp.float32,
        )
        term = gate_ref[:, n * half : (n + 1) * half] * summed
        term = (term + flag_ref[n] * rows[1].astype(jnp.float32)).astype(jnp.bfloat16)
        at = 0
        for ref, size in zip(refs[4 + n * count : 4 + (n + 1) * count], sizes):
            ref[...] = term[at : at + size]
            at += size


def pair_sums(flags, gate, parts, sizes):
    tokens, width = parts[0].shape[0], gate.shape[1]
    outs = [jax.ShapeDtypeStruct((size, width // 2), jnp.bfloat16) for size in sizes] * 2
    return pl.pallas_call(
        functools.partial(sums_kernel, sizes),
        in_specs=[SMEM] + [VMEM] * 5,
        out_specs=[VMEM] * len(outs),
        out_shape=outs,
        compiler_params=PARAMS,
        cost_estimate=pl.CostEstimate(
            flops=4 * tokens * tokens * width, bytes_accessed=6 * tokens * width, transcendentals=0
        ),
        name="pair_sums",
    )(flags, gate, *parts)


def piece_spots(tokens, reach, piece):
    if tokens <= 2 * reach:
        return [(0, tokens, 0)]
    if piece == 0:
        return [(reach, tokens - 2 * reach, 0)]
    return [(0, reach, 0), (tokens - reach, reach, reach)]


def relay_kernel(spots, first_row, chunks, row_ref, gate_ref, branch_refs, base_ref, total_refs, *refs):
    grad_ref, out_ref, staged, sems, grad_sems = refs[-5:]
    tokens, width = base_ref.shape
    half = width // 2
    copies = []
    for n, ref in enumerate(total_refs):
        copies.append(
            pltpu.make_async_copy(
                ref,
                grad_ref.at[pl.ds(first_row, ref.shape[0]), pl.ds(n * half, half)],
                grad_sems.at[n],
            )
        )
    for copy in copies:
        copy.start()
    picks = selector(row_ref[...]).T.astype(jnp.bfloat16)
    picks = jnp.concatenate([picks[:, top : top + size] for top, size, at in spots], axis=1)
    step = half // chunks
    for n, ref in enumerate(branch_refs):
        for c in range(chunks):
            lanes = slice(n * half + c * step, n * half + (c + 1) * step)
            relayed = jnp.dot(
                picks, ref[:, c * step : (c + 1) * step], preferred_element_type=jnp.float32
            )
            total = base_ref[:, lanes].astype(jnp.float32) + gate_ref[:, lanes] * relayed
            staged[:, lanes] = total.astype(staged.dtype)
            if sems is not None:
                part = pl.ds(n * half + c * step, step)
                copy = pltpu.make_async_copy(
                    staged.at[:, part], out_ref.at[:, part], sems.at[n * chunks + c]
                )
                copy.start()
                copies.append(copy)
    for copy in copies:
        copy.wait()


def relay(rows, gate, branch, base, totals, spots, first_row, grads, last):
    tokens, width = base.shape
    chunks = 2 if width // 2 % (2 * LANES) == 0 else 1
    far = pl.BlockSpec(memory_space=pltpu.HBM)
    whole = jax.ShapeDtypeStruct((tokens, width), jnp.bfloat16)

    def kernel(row_ref, gate_ref, a_ref, b_ref, base_ref, c_ref, d_ref, *refs):
        if grads is not None:
            refs = refs[1:]
        if last:
            grad_ref, out_ref, staged, sems, grad_sems = refs
        else:
            grad_ref, out_ref, grad_sems = refs
            staged, sems = out_ref, None
        relay_kernel(
            spots, first_row, chunks, row_ref, gate_ref, (a_ref, b_ref), base_ref, (c_ref, d_ref),
            grad_ref, out_ref, staged, sems, grad_sems,
        )

    out = whole if last else jax.ShapeDtypeStruct((tokens, width), jnp.float32)
    scratch = [pltpu.VMEM((tokens, width), jnp.bfloat16), pltpu.SemaphoreType.DMA((2 * chunks,))]
    operands = [rows, gate, *branch, base, *totals] + ([] if grads is None else [grads])
    return pl.pallas_call(
        kernel,
        in_specs=[VMEM] * 7 + ([] if grads is None else [far]),
        out_specs=[far, far if last else VMEM],
        out_shape=[whole, out],
        input_output_aliases={} if grads is None else {7: 0},
        scratch_shapes=(scratch if last else []) + [pltpu.SemaphoreType.DMA((2,))],
        compiler_params=PARAMS,
        cost_estimate=pl.CostEstimate(
            flops=2 * tokens * tokens * width,
            bytes_accessed=24 * tokens * width,
            transcendentals=0,
        ),
        name="relay",
    )(*operands)


def whole_gate(gate):
    ranks = lax.axis_size("rep")
    if ranks != 2:
        return lax.all_gather(gate, "rep", axis=0, tiled=True)
    other = lax.ppermute(gate, "rep", [(0, 1), (1, 0)])
    first = lax.axis_index("rep") == 0
    return jnp.concatenate([jnp.where(first, gate, other), jnp.where(first, other, gate)])


SWAP_X, SWAP_Y = [(0, 1), (1, 0), (2, 3), (3, 2)], [(0, 2), (2, 0), (1, 3), (3, 1)]
ROUND_A, ROUND_B = [(0, 1), (1, 3), (3, 2), (2, 0)], [(0, 2), (2, 3), (3, 1), (1, 0)]


def added(a, b):
    return (a.astype(jnp.float32) + b.astype(jnp.float32)).astype(a.dtype)


def local(query_rows, key_rows, value_rows, view_frame, control_row, control_gate, out_grad):
    queries, keys, values = query_rows[0, 0], key_rows[0, 0], value_rows[0, 0]
    tokens, width = queries.shape
    half = width // 2
    ranks = lax.axis_size("seq")
    reach = 2 * (tokens * ranks // 32)
    hops = (reach + tokens - 1) // tokens
    group, rank = lax.axis_index("grp"), lax.axis_index("seq")
    send = lambda block, route: lax.ppermute(block, "grp", route)

    tag = view_frame[0, 0]
    code = tag + 8 * (tag // FRAMES) + 16
    marks = jnp.stack((code, control_row[0, 0] % tokens)).astype(jnp.float32)
    code, rows = marks[:1], marks[1:]
    most = min(tokens, reach)
    even = rank % 2 == 0
    firsts = jnp.where(jnp.stack((even, ~even)), tokens - most, 0).astype(jnp.int32)
    sent_a, sent_b = pack_grads(out_grad[0, 0], marks, queries, keys, values)
    code, sent_a, sent_b = lax.optimization_barrier((code, sent_a, sent_b))
    got_a, got_b = send(sent_a, SWAP_X), send(sent_b, SWAP_Y)
    end_one, end_two = pack_ends(firsts, keys, values, code, most)
    code, end_one, end_two = lax.optimization_barrier((code, end_one, end_two))
    own = [attend_middle(queries, keys, values, code, reach)] if tokens > 2 * reach else []
    gate = whole_gate(control_gate)[None]
    halos = [paired(end_one, "seq", 0), paired(end_two, "seq", 1)]
    for hop in range(2, hops + 1):
        count = min(tokens, reach - (hop - 1) * tokens)
        tail, head = jnp.where(even, end_one, end_two), jnp.where(even, end_two, end_one)
        halos.append(shifted(tail[most - count :], "seq", hop))
        halos.append(shifted(head[:count], "seq", -hop))
    sizes = [piece.shape[0] for piece in own] + [min(tokens, 2 * reach)]
    flags = jnp.stack([group == 1, group == 2]).astype(jnp.float32)
    sums = pair_sums(flags, gate, (sent_a, got_a, sent_b, got_b), sizes)
    count = len(sizes)

    def outgoing(piece, sum_a, sum_b):
        to_a = jnp.where(group == 0, piece[:, :half], jnp.where(group == 1, sum_a, sum_b))
        to_b = jnp.where(group == 0, piece[:, half:], jnp.where(group == 2, sum_b, sum_a))
        return to_a, to_b

    going = [outgoing(own[0], sums[0], sums[count])] if own else []
    code, *ready = lax.optimization_barrier((code, *sums, *(going[0] if going else ())))
    sums = ready[: 2 * count]
    if going:
        going = [ready[2 * count :]]
    own.append(attend_edges(even.astype(jnp.int32)[None], queries, keys, values, code, halos, reach))

    going.append(outgoing(own[-1], sums[count - 1], sums[2 * count - 1]))
    spots = [piece_spots(tokens, reach, n) for n in range(count)]
    order = [
        own[n][at : at + size] for top, size, n, at in sorted(
            (top, size, n, at) for n in range(count) for top, size, at in spots[n]
        )
    ]
    block_out = jnp.concatenate(order, axis=0)
    branch_grad, first_row = None, 0
    for n, (piece, sum_a, sum_b) in enumerate(zip(own, sums[:count], sums[count:])):
        piece_a, piece_b = piece[:, :half], piece[:, half:]
        one, two = send(going[n][0], ROUND_A), send(going[n][1], ROUND_B)
        total_a = added(sum_a, jnp.where(group == 1, two, one))
        total_b = added(sum_b, jnp.where(group == 2, one, two))
        held_a = jnp.where(group == 0, piece_a, one)
        held_b = jnp.where(group == 0, piece_b, two)
        across = send(jnp.where((group == 0) | (group == 2), held_b, total_a), SWAP_X)
        down = send(jnp.where(group <= 1, held_a, total_b), SWAP_Y)
        branch_a = jnp.where(group <= 1, held_a, down)
        branch_b = jnp.where((group == 0) | (group == 2), held_b, across)
        totals = (
            jnp.where((group == 0) | (group == 2), across, total_a),
            jnp.where(group <= 1, down, total_b),
        )
        branch_grad, block_out = relay(
            rows, gate, (branch_a, branch_b), block_out, totals, spots[n], first_row, branch_grad,
            n == count - 1,
        )
        first_row += piece.shape[0]
    return (block_out[None, None], branch_grad[None])


def solution(mesh):
    placed = (
        P("rep", "grp", "seq", None),
        P("rep", "grp", "seq", None),
        P("rep", "grp", "seq", None),
        P("rep", "grp", "seq"),
        P("rep", "grp", "seq"),
        P("rep"),
        P("rep", "grp", "seq", None),
    )
    return jax.shard_map(
        local,
        mesh=mesh,
        in_specs=placed,
        out_specs=(P("rep", "grp", "seq", None), P("rep", "seq", None)),
        check_vma=False,
    )
```

```python
import functools
import math

import jax
import jax.numpy as jnp
from jax import lax
from jax.experimental import pallas as pl
from jax.experimental.pallas import tpu as pltpu
from jax.sharding import PartitionSpec as P

HEADS = 32
DH = 80
FRAMES = 20
LANES = 128
VMEM_LIMIT = 32 * 1024 * 1024
PACK_LIMIT = 53 * 1024 * 1024


def shifted(block, axis, distance):
    devices = range(lax.axis_size(axis))
    route = [(i - distance, i) for i in devices if i - distance in devices]
    return lax.ppermute(block, axis, route)


def paired(block, axis, first):
    size = lax.axis_size(axis)
    route = []
    for i in range(size):
        other = i + 1 if (i - first) % 2 == 0 else i - 1
        if 0 <= other < size:
            route.append((i, other))
    return lax.ppermute(block, axis, route)


def lane_windows(heads):
    windows = []
    for head in range(heads):
        first, last = head * DH, (head + 1) * DH
        if windows and last <= windows[-1][0] + 2 * LANES:
            windows[-1][1].append(head)
        else:
            windows.append((first // LANES * LANES, [head]))
    out = []
    for start, members in windows:
        start = min(start, heads * DH - 2 * LANES)
        out.append((start, members))
    return out


def head_masks(rows, period):
    masks = {}
    for start, members in lane_windows(period // DH):
        lane = lax.broadcasted_iota(jnp.int32, (rows, 2 * LANES), 1) + start
        for h in members:
            inside = (lane >= h * DH) & (lane < (h + 1) * DH)
            masks[h] = jnp.where(inside, 1.0, 0.0).astype(jnp.bfloat16)
    return masks


def period_scores(base, query, keys, masks, period):
    scores = []
    for start, members in lane_windows(period // DH):
        lanes = slice(base + start, base + start + 2 * LANES)
        part = query(lanes)
        stacked = jnp.concatenate([part * masks[h] for h in members], axis=0)
        scores.append(
            [
                lax.dot_general(
                    stacked, key(lanes), (((1,), (1,)), ((), ())), preferred_element_type=jnp.float32
                )
                for key in keys
            ]
        )
    return scores


def mixed_period(base, scores, sets, period):
    rows = sets[0][0].shape[0]
    factor = math.log2(math.e) / math.sqrt(DH)
    windows = lane_windows(period // DH)
    weights = []
    for parts, (start, members) in zip(scores, windows):
        parts = [
            part.reshape(len(members), rows, -1) + bias[None]
            for part, (bias, value) in zip(parts, sets)
        ]
        largest = row_max(parts)
        weights.append(
            [
                jnp.exp2((part - largest) * factor).astype(jnp.bfloat16).reshape(len(members) * rows, -1)
                for part in parts
            ]
        )
    tiles = {}
    for parts, (start, members) in zip(weights, windows):
        lanes = slice(base + start, base + start + 2 * LANES)
        mixed = sum(
            jnp.dot(part, value(lanes), preferred_element_type=jnp.float32)
            for part, (bias, value) in zip(parts, sets)
        )
        totals = sum(
            jnp.dot(part, jnp.ones((part.shape[1], LANES), part.dtype), preferred_element_type=jnp.float32)
            for part in parts
        )
        scale = 1.0 / totals
        for n, h in enumerate(members):
            for t in range(2):
                low = start + t * LANES
                if h * DH >= low + LANES or (h + 1) * DH <= low:
                    continue
                mine = slice(n * rows, (n + 1) * rows)
                piece = mixed[mine, t * LANES : (t + 1) * LANES] * scale[mine]
                if low in tiles:
                    lane = lax.broadcasted_iota(jnp.int32, (rows, LANES), 1) + low
                    tiles[low] = jnp.where(lane >= h * DH, piece, tiles[low])
                else:
                    tiles[low] = piece
    return {low: tile.astype(jnp.bfloat16) for low, tile in tiles.items()}


def row_max(parts):
    if all(part.shape == parts[0].shape for part in parts):
        return jnp.max(functools.reduce(jnp.maximum, parts), axis=-1, keepdims=True)
    return functools.reduce(jnp.maximum, [jnp.max(part, axis=-1, keepdims=True) for part in parts])


def columns(row):
    return jnp.broadcast_to(row, (LANES, row.shape[1])).T


def link_bias(mine, theirs):
    return jnp.where(jnp.abs(mine[:, :1] - theirs.T[: mine.shape[0]]) <= 1.5, 0.0, -1e30)


def store_period(base, tiles, out_ref):
    for low, tile in tiles.items():
        out_ref[:, base + low : base + low + LANES] = tile


def ends_kernel(first_ref, k_ref, v_ref, code_ref, *end_refs):
    tokens, width = k_ref.shape
    code = columns(code_ref[...])
    for n, ref in enumerate(end_refs):
        most = ref.shape[0]
        first = pl.multiple_of(first_ref[n], most)
        ref[:, :width] = k_ref[pl.ds(first, most), :]
        ref[:, width : 2 * width] = v_ref[pl.ds(first, most), :]
        here = jnp.where(first == 0, code[:most], code[tokens - most :])
        ref[:, 2 * width :] = here.astype(jnp.bfloat16)


def middle_kernel(reach, q_ref, k_ref, v_ref, code_ref, out_ref):
    rows = out_ref.shape[0]
    code = columns(code_ref[...])
    bias = link_bias(code[reach : reach + rows], code)
    period = math.lcm(DH, LANES)
    masks = head_masks(rows, period)
    query = lambda lanes: q_ref[reach : reach + rows, lanes]
    for base in range(0, out_ref.shape[1], period):
        scores = period_scores(base, query, [lambda lanes: k_ref[:, lanes]], masks, period)
        sets = [(bias, lambda lanes: v_ref[:, lanes])]
        store_period(base, mixed_period(base, scores, sets, period), out_ref)


def sides_kernel(reach, even_ref, q_ref, k_ref, v_ref, code_ref, one_ref, two_ref, *refs):
    out_ref, keys, values, codes = refs
    tokens, width = q_ref.shape
    near = 2 * reach
    code = columns(code_ref[...])
    even = even_ref[0] == 1
    period = math.lcm(DH, LANES)
    masks = head_masks(reach, period)
    blocks = []
    for side, first in ((0, 0), (1, tokens - near)):
        own = slice(first, first + near)
        use_two = even if side == 0 else jnp.logical_not(even)
        halo = jnp.where(use_two, two_ref[...], one_ref[...])
        keys[side, :near] = k_ref[own]
        values[side, :near] = v_ref[own]
        codes[side, :near] = code[own]
        keys[side, near : near + reach] = halo[:, :width]
        values[side, near : near + reach] = halo[:, width : 2 * width]
        codes[side, near : near + reach] = halo[:, 2 * width :].astype(jnp.float32)
        spare = keys.shape[1] - near - reach
        if spare:
            for ref in (keys, values, codes):
                ref[side, near + reach :] = jnp.zeros((spare, ref.shape[2]), ref.dtype)
        top = side * (tokens - reach)
        blocks.append((side, top, link_bias(code[top : top + reach], codes[side])))
    for base in range(0, width, period):
        scores = []
        for side, top, bias in blocks:
            query = lambda lanes: q_ref[top : top + reach, lanes]
            key = lambda lanes: keys[side, :, lanes]
            scores.append(period_scores(base, query, [key], masks, period))
        for (side, top, bias), part in zip(blocks, scores):
            sets = [(bias, lambda lanes: values[side, :, lanes])]
            tiles = mixed_period(base, part, sets, period)
            store_period(base, tiles, out_ref.at[side * reach : (side + 1) * reach])


def edge_kernel(reach, q_ref, k_ref, v_ref, code_ref, *refs):
    halos = refs[:-4]
    out_ref, keys, values, codes = refs[-4:]
    width = q_ref.shape[1]
    code = columns(code_ref[...])
    at = 0
    for piece in halos:
        rows = piece.shape[0]
        keys[at : at + rows] = piece[:, :width]
        values[at : at + rows] = piece[:, width : 2 * width]
        codes[at : at + rows] = piece[:, 2 * width :].astype(jnp.float32)
        at += rows
    if at < keys.shape[0]:
        for ref in (keys, values, codes):
            ref[at:] = jnp.zeros((ref.shape[0] - at, ref.shape[1]), ref.dtype)
    period = math.lcm(DH, LANES)
    masks = head_masks(q_ref.shape[0], period)
    query = lambda lanes: q_ref[:, lanes]
    pair = [lambda lanes: k_ref[:, lanes], lambda lanes: keys[:, lanes]]
    sets = [
        (link_bias(code, code), lambda lanes: v_ref[:, lanes]),
        (link_bias(code, codes[...]), lambda lanes: values[:, lanes]),
    ]
    for base in range(0, width, period):
        scores = period_scores(base, query, pair, masks, period)
        store_period(base, mixed_period(base, scores, sets, period), out_ref)


def attend_cost(tokens, span, width):
    return pl.CostEstimate(
        flops=HEADS * tokens * span * 2 * LANES * 4,
        bytes_accessed=12 * tokens * width,
        transcendentals=HEADS * tokens * span,
    )


VMEM = pl.BlockSpec(memory_space=pltpu.VMEM)
SMEM = pl.BlockSpec(memory_space=pltpu.SMEM)
PARAMS = pltpu.CompilerParams(vmem_limit_bytes=VMEM_LIMIT)


def pack_ends(firsts, keys, values, code, most):
    width = keys.shape[1]
    ends = jax.ShapeDtypeStruct((most, 2 * width + LANES), jnp.bfloat16)
    return pl.pallas_call(
        ends_kernel,
        in_specs=[SMEM] + [VMEM] * 3,
        out_specs=[VMEM] * 2,
        out_shape=[ends, ends],
        compiler_params=PARAMS,
        cost_estimate=pl.CostEstimate(flops=0, bytes_accessed=16 * most * width, transcendentals=0),
        name="pack_ends",
    )(firsts, keys, values, code)


def attend_middle(queries, keys, values, code, reach):
    tokens, width = queries.shape
    return pl.pallas_call(
        functools.partial(middle_kernel, reach),
        in_specs=[VMEM] * 4,
        out_specs=VMEM,
        out_shape=jax.ShapeDtypeStruct((tokens - 2 * reach, width), jnp.bfloat16),
        compiler_params=PARAMS,
        cost_estimate=attend_cost(tokens - 2 * reach, tokens, width),
        name="attend_middle",
    )(queries, keys, values, code)


def attend_edges(even, queries, keys, values, code, halos, reach):
    tokens, width = queries.shape
    rows = min(tokens, 2 * reach)
    if tokens > 2 * reach:
        kernel, operands = sides_kernel, [even, queries, keys, values, code, *halos]
        held = (2, -(-3 * reach // LANES) * LANES)
    else:
        kernel, operands = edge_kernel, [queries, keys, values, code, *halos]
        held = (-(-2 * reach // LANES) * LANES,)
    return pl.pallas_call(
        functools.partial(kernel, reach),
        in_specs=[SMEM if operand is even else VMEM for operand in operands],
        out_specs=VMEM,
        out_shape=jax.ShapeDtypeStruct((rows, width), jnp.bfloat16),
        scratch_shapes=[
            pltpu.VMEM((*held, width), jnp.bfloat16),
            pltpu.VMEM((*held, width), jnp.bfloat16),
            pltpu.VMEM((*held, LANES), jnp.float32),
        ],
        compiler_params=PARAMS,
        cost_estimate=attend_cost(rows, LANES, width),
        name="attend_edges",
    )(*operands)


def pack_grads_kernel(grad_ref, mark_ref, *refs):
    first_ref, second_ref, sems = refs[-3:]
    half = grad_ref.shape[1] // 2
    copies = []
    for n, ref in enumerate((first_ref, second_ref)):
        copies.append(
            pltpu.make_async_copy(
                grad_ref.at[:, pl.ds(n * half, half)], ref.at[:, pl.ds(0, half)], sems.at[n]
            )
        )
    for copy in copies:
        copy.start()
    place = columns(mark_ref[1:2]).astype(jnp.bfloat16)
    for ref in (first_ref, second_ref):
        ref[:, half:] = place
    for copy in copies:
        copy.wait()


def pack_grads(grads, marks, *others):
    tokens, width = grads.shape
    far = pl.BlockSpec(memory_space=pltpu.HBM)
    return pl.pallas_call(
        pack_grads_kernel,
        in_specs=[far, VMEM] + [far] * len(others),
        out_specs=[VMEM] * 2,
        out_shape=[jax.ShapeDtypeStruct((tokens, width // 2 + LANES), jnp.bfloat16)] * 2,
        scratch_shapes=[pltpu.SemaphoreType.DMA((2,))],
        compiler_params=pltpu.CompilerParams(vmem_limit_bytes=PACK_LIMIT),
        cost_estimate=pl.CostEstimate(flops=0, bytes_accessed=4 * tokens * width, transcendentals=0),
        name="pack_grads",
    )(grads, marks, *others)


def selector(row):
    tokens = row.shape[1]
    wanted = lax.broadcasted_iota(jnp.int32, (tokens, tokens), 0).astype(jnp.float32)
    return jnp.where(wanted == row, 1.0, 0.0)


def sums_kernel(sizes, flag_ref, gate_ref, *refs):
    half = gate_ref.shape[1] // 2
    count = len(sizes)
    for n in range(2):
        mine_ref, theirs_ref = refs[2 * n : 2 * n + 2]
        picks, rows = [], []
        for ref in (mine_ref, theirs_ref):
            place = ref[:, half : half + LANES].astype(jnp.float32).T[:1]
            picks.append(selector(place).astype(jnp.bfloat16))
            rows.append(ref[:, :half])
        summed = jnp.dot(
            jnp.concatenate(picks, axis=1),
            jnp.concatenate(rows, axis=0),
            preferred_element_type=jnp.float32,
        )
        term = gate_ref[:, n * half : (n + 1) * half] * summed
        term = (term + flag_ref[n] * rows[1].astype(jnp.float32)).astype(jnp.bfloat16)
        at = 0
        for ref, size in zip(refs[4 + n * count : 4 + (n + 1) * count], sizes):
            ref[...] = term[at : at + size]
            at += size


def pair_sums(flags, gate, parts, sizes):
    tokens, width = parts[0].shape[0], gate.shape[1]
    outs = [jax.ShapeDtypeStruct((size, width // 2), jnp.bfloat16) for size in sizes] * 2
    return pl.pallas_call(
        functools.partial(sums_kernel, sizes),
        in_specs=[SMEM] + [VMEM] * 5,
        out_specs=[VMEM] * len(outs),
        out_shape=outs,
        compiler_params=PARAMS,
        cost_estimate=pl.CostEstimate(
            flops=4 * tokens * tokens * width, bytes_accessed=6 * tokens * width, transcendentals=0
        ),
        name="pair_sums",
    )(flags, gate, *parts)


def piece_spots(tokens, reach, piece):
    if tokens <= 2 * reach:
        return [(0, tokens, 0)]
    if piece == 0:
        return [(reach, tokens - 2 * reach, 0)]
    return [(0, reach, 0), (tokens - reach, reach, reach)]


def relayed_rows(spots, row_ref, branch):
    picks = selector(row_ref[...]).T.astype(jnp.bfloat16)
    picks = jnp.concatenate([picks[:, top : top + size] for top, size, at in spots], axis=1)
    return jnp.dot(picks, branch, preferred_element_type=jnp.float32)


def relay_first_kernel(spots, row_ref, gate_ref, a_ref, b_ref, base_ref, c_ref, d_ref, grad_ref, out_ref, sems):
    half = a_ref.shape[1]
    copies = []
    for n, ref in enumerate((c_ref, d_ref)):
        to = grad_ref.at[pl.ds(0, ref.shape[0]), pl.ds(n * half, half)]
        copies.append(pltpu.make_async_copy(ref, to, sems.at[n]))
    for copy in copies:
        copy.start()
    for n, ref in enumerate((a_ref, b_ref)):
        lanes = slice(n * half, (n + 1) * half)
        relayed = relayed_rows(spots, row_ref, ref[...])
        out_ref[:, lanes] = base_ref[:, lanes].astype(jnp.float32) + gate_ref[:, lanes] * relayed
    for copy in copies:
        copy.wait()


def relay_first(rows, gate, branch, base, totals, spots):
    tokens, width = base.shape
    return pl.pallas_call(
        functools.partial(relay_first_kernel, spots),
        in_specs=[VMEM] * 7,
        out_specs=[pl.BlockSpec(memory_space=pltpu.HBM), VMEM],
        out_shape=[
            jax.ShapeDtypeStruct((tokens, width), jnp.bfloat16),
            jax.ShapeDtypeStruct((tokens, width), jnp.float32),
        ],
        scratch_shapes=[pltpu.SemaphoreType.DMA((2,))],
        compiler_params=PARAMS,
        cost_estimate=pl.CostEstimate(
            flops=2 * tokens * tokens * width, bytes_accessed=24 * tokens * width, transcendentals=0
        ),
        name="relay_first",
    )(rows, gate, *branch, base, *totals)


def relay_last_kernel(
    spots, part, chunks, first_row, holds_ref, row_ref, gate_ref, held_ref, got_ref, base_ref, total_ref, *refs
):
    grad_ref, out_ref, staged, summed, sems, grad_sem = refs[-6:]
    half = held_ref.shape[1]
    other = 1 - part
    holds = holds_ref[0] == 1
    summed[...] = jnp.where(holds, got_ref[...], total_ref[...])
    to = grad_ref.at[pl.ds(first_row, total_ref.shape[0]), pl.ds(other * half, half)]
    copies = [pltpu.make_async_copy(summed, to, grad_sem)]
    copies[0].start()
    step = half // chunks
    for c in range(chunks):
        mine = slice(c * step, (c + 1) * step)
        lanes = slice(part * half + c * step, part * half + (c + 1) * step)
        branch = jnp.where(holds, held_ref[:, mine], got_ref[:, mine])
        relayed = relayed_rows(spots, row_ref, branch)
        total = base_ref[:, lanes].astype(jnp.float32) + gate_ref[:, lanes] * relayed
        staged[:, mine] = total.astype(staged.dtype)
        copies.append(
            pltpu.make_async_copy(
                staged.at[:, pl.ds(c * step, step)],
                out_ref.at[:, pl.ds(part * half + c * step, step)],
                sems.at[c],
            )
        )
        copies[-1].start()
    for copy in copies:
        copy.wait()


def relay_last(holds, rows, gate, held, got, base, total, spots, part, first_row, grads, out):
    tokens, width = base.shape
    chunks = 2 if width // 2 % (2 * LANES) == 0 else 1
    far = pl.BlockSpec(memory_space=pltpu.HBM)
    operands = [holds, rows, gate, held, got, base, total]
    aliases = {}
    for n, buffer in enumerate((grads, out)):
        if buffer is not None:
            aliases[len(operands)] = n
            operands.append(buffer)
    return pl.pallas_call(
        functools.partial(relay_last_kernel, spots, part, chunks, first_row),
        in_specs=[SMEM] + [VMEM] * 6 + [far] * len(aliases),
        out_specs=[far] * 2,
        out_shape=[jax.ShapeDtypeStruct((tokens, width), jnp.bfloat16)] * 2,
        input_output_aliases=aliases,
        scratch_shapes=[
            pltpu.VMEM((tokens, width // 2), jnp.bfloat16),
            pltpu.VMEM(total.shape, jnp.bfloat16),
            pltpu.SemaphoreType.DMA((chunks,)),
            pltpu.SemaphoreType.DMA,
        ],
        compiler_params=PARAMS,
        cost_estimate=pl.CostEstimate(
            flops=tokens * tokens * width, bytes_accessed=6 * tokens * width, transcendentals=0
        ),
        name="relay_last",
    )(*operands)


def whole_gate(gate):
    ranks = lax.axis_size("rep")
    if ranks != 2:
        return lax.all_gather(gate, "rep", axis=0, tiled=True)
    other = lax.ppermute(gate, "rep", [(0, 1), (1, 0)])
    first = lax.axis_index("rep") == 0
    return jnp.concatenate([jnp.where(first, gate, other), jnp.where(first, other, gate)])


SWAP_X, SWAP_Y = [(0, 1), (1, 0), (2, 3), (3, 2)], [(0, 2), (2, 0), (1, 3), (3, 1)]
ROUND_A, ROUND_B = [(0, 1), (1, 3), (3, 2), (2, 0)], [(0, 2), (2, 3), (3, 1), (1, 0)]


def added(a, b):
    return (a.astype(jnp.float32) + b.astype(jnp.float32)).astype(a.dtype)


def local(query_rows, key_rows, value_rows, view_frame, control_row, control_gate, out_grad):
    queries, keys, values = query_rows[0, 0], key_rows[0, 0], value_rows[0, 0]
    tokens, width = queries.shape
    half = width // 2
    ranks = lax.axis_size("seq")
    reach = 2 * (tokens * ranks // 32)
    hops = (reach + tokens - 1) // tokens
    group, rank = lax.axis_index("grp"), lax.axis_index("seq")
    send = lambda block, route: lax.ppermute(block, "grp", route)

    tag = view_frame[0, 0]
    code = tag + 8 * (tag // FRAMES) + 16
    marks = jnp.stack((code, control_row[0, 0] % tokens)).astype(jnp.float32)
    code, rows = marks[:1], marks[1:]
    most = min(tokens, reach)
    even = rank % 2 == 0
    firsts = jnp.where(jnp.stack((even, ~even)), tokens - most, 0).astype(jnp.int32)
    sent_a, sent_b = pack_grads(out_grad[0, 0], marks, queries, keys, values)
    code, sent_a, sent_b = lax.optimization_barrier((code, sent_a, sent_b))
    got_a, got_b = send(sent_a, SWAP_X), send(sent_b, SWAP_Y)
    end_one, end_two = pack_ends(firsts, keys, values, code, most)
    code, end_one, end_two = lax.optimization_barrier((code, end_one, end_two))
    own = [attend_middle(queries, keys, values, code, reach)] if tokens > 2 * reach else []
    gate = whole_gate(control_gate)[None]
    halos = [paired(end_one, "seq", 0), paired(end_two, "seq", 1)]
    for hop in range(2, hops + 1):
        count = min(tokens, reach - (hop - 1) * tokens)
        tail, head = jnp.where(even, end_one, end_two), jnp.where(even, end_two, end_one)
        halos.append(shifted(tail[most - count :], "seq", hop))
        halos.append(shifted(head[:count], "seq", -hop))
    sizes = [piece.shape[0] for piece in own] + [min(tokens, 2 * reach)]
    flags = jnp.stack([group == 1, group == 2]).astype(jnp.float32)
    sums = pair_sums(flags, gate, (sent_a, got_a, sent_b, got_b), sizes)
    count = len(sizes)

    def outgoing(piece, sum_a, sum_b):
        to_a = jnp.where(group == 0, piece[:, :half], jnp.where(group == 1, sum_a, sum_b))
        to_b = jnp.where(group == 0, piece[:, half:], jnp.where(group == 2, sum_b, sum_a))
        return to_a, to_b

    going = [outgoing(own[0], sums[0], sums[count])] if own else []
    code, *ready = lax.optimization_barrier((code, *sums, *(going[0] if going else ())))
    sums = ready[: 2 * count]
    if going:
        going = [ready[2 * count :]]
    own.append(attend_edges(even.astype(jnp.int32)[None], queries, keys, values, code, halos, reach))

    going.append(outgoing(own[-1], sums[count - 1], sums[2 * count - 1]))
    spots = [piece_spots(tokens, reach, n) for n in range(count)]
    order = [
        own[n][at : at + size] for top, size, n, at in sorted(
            (top, size, n, at) for n in range(count) for top, size, at in spots[n]
        )
    ]
    block_out = jnp.concatenate(order, axis=0)
    branch_grad, first_row = None, 0
    for n, (piece, sum_a, sum_b) in enumerate(zip(own, sums[:count], sums[count:])):
        piece_a, piece_b = piece[:, :half], piece[:, half:]
        one, two = send(going[n][0], ROUND_A), send(going[n][1], ROUND_B)
        total_a = added(sum_a, jnp.where(group == 1, two, one))
        total_b = added(sum_b, jnp.where(group == 2, one, two))
        held_a = jnp.where(group == 0, piece_a, one)
        held_b = jnp.where(group == 0, piece_b, two)
        across = send(jnp.where((group == 0) | (group == 2), held_b, total_a), SWAP_X)
        down = send(jnp.where(group <= 1, held_a, total_b), SWAP_Y)
        branch_a = jnp.where(group <= 1, held_a, down)
        branch_b = jnp.where((group == 0) | (group == 2), held_b, across)
        totals = (
            jnp.where((group == 0) | (group == 2), across, total_a),
            jnp.where(group <= 1, down, total_b),
        )
        if n < count - 1:
            branch_grad, block_out = relay_first(
                rows, gate, (branch_a, branch_b), block_out, totals, spots[n]
            )
            first_row = piece.shape[0]
            continue
        base, block_out = block_out, None
        ends = ((group <= 1, held_a, down, total_b), ((group == 0) | (group == 2), held_b, across, total_a))
        for part in (1, 0):
            holds, held, got, total = ends[part]
            branch_grad, block_out = relay_last(
                holds.astype(jnp.int32)[None], rows, gate, held, got, base, total, spots[n], part,
                first_row, branch_grad, block_out,
            )
    return (block_out[None, None], branch_grad[None])


def solution(mesh):
    placed = (
        P("rep", "grp", "seq", None),
        P("rep", "grp", "seq", None),
        P("rep", "grp", "seq", None),
        P("rep", "grp", "seq"),
        P("rep", "grp", "seq"),
        P("rep"),
        P("rep", "grp", "seq", None),
    )
    return jax.shard_map(
        local,
        mesh=mesh,
        in_specs=placed,
        out_specs=(P("rep", "grp", "seq", None), P("rep", "seq", None)),
        check_vma=False,
    )
```

```python
import functools
import math

import jax
import jax.numpy as jnp
from jax import lax
from jax.experimental import pallas as pl
from jax.experimental.pallas import tpu as pltpu
from jax.sharding import PartitionSpec as P

HEADS = 32
DH = 80
FRAMES = 20
LANES = 128
VMEM_LIMIT = 32 * 1024 * 1024
PACK_LIMIT = 53 * 1024 * 1024


def shifted(block, axis, distance):
    devices = range(lax.axis_size(axis))
    route = [(i - distance, i) for i in devices if i - distance in devices]
    return lax.ppermute(block, axis, route)


def paired(block, axis, first):
    size = lax.axis_size(axis)
    route = []
    for i in range(size):
        other = i + 1 if (i - first) % 2 == 0 else i - 1
        if 0 <= other < size:
            route.append((i, other))
    return lax.ppermute(block, axis, route)


def lane_windows(heads):
    windows = []
    for head in range(heads):
        first, last = head * DH, (head + 1) * DH
        if windows and last <= windows[-1][0] + 2 * LANES:
            windows[-1][1].append(head)
        else:
            windows.append((first // LANES * LANES, [head]))
    out = []
    for start, members in windows:
        start = min(start, heads * DH - 2 * LANES)
        out.append((start, members))
    return out


def head_masks(rows, period):
    masks = {}
    for start, members in lane_windows(period // DH):
        lane = lax.broadcasted_iota(jnp.int32, (rows, 2 * LANES), 1) + start
        for h in members:
            inside = (lane >= h * DH) & (lane < (h + 1) * DH)
            masks[h] = jnp.where(inside, 1.0, 0.0).astype(jnp.bfloat16)
    return masks


def period_scores(base, query, keys, masks, period):
    scores = []
    for start, members in lane_windows(period // DH):
        lanes = slice(base + start, base + start + 2 * LANES)
        part = query(lanes)
        stacked = jnp.concatenate([part * masks[h] for h in members], axis=0)
        scores.append(
            [
                lax.dot_general(
                    stacked, key(lanes), (((1,), (1,)), ((), ())), preferred_element_type=jnp.float32
                )
                for key in keys
            ]
        )
    return scores


def mixed_period(base, scores, sets, period):
    rows = sets[0][0].shape[0]
    factor = math.log2(math.e) / math.sqrt(DH)
    windows = lane_windows(period // DH)
    weights = []
    for parts, (start, members) in zip(scores, windows):
        parts = [
            part.reshape(len(members), rows, -1) + bias[None]
            for part, (bias, value) in zip(parts, sets)
        ]
        largest = row_max(parts)
        weights.append(
            [
                jnp.exp2((part - largest) * factor).astype(jnp.bfloat16).reshape(len(members) * rows, -1)
                for part in parts
            ]
        )
    tiles = {}
    for parts, (start, members) in zip(weights, windows):
        lanes = slice(base + start, base + start + 2 * LANES)
        mixed = sum(
            jnp.dot(part, value(lanes), preferred_element_type=jnp.float32)
            for part, (bias, value) in zip(parts, sets)
        )
        totals = sum(
            jnp.dot(part, jnp.ones((part.shape[1], LANES), part.dtype), preferred_element_type=jnp.float32)
            for part in parts
        )
        scale = 1.0 / totals
        for n, h in enumerate(members):
            for t in range(2):
                low = start + t * LANES
                if h * DH >= low + LANES or (h + 1) * DH <= low:
                    continue
                mine = slice(n * rows, (n + 1) * rows)
                piece = mixed[mine, t * LANES : (t + 1) * LANES] * scale[mine]
                if low in tiles:
                    lane = lax.broadcasted_iota(jnp.int32, (rows, LANES), 1) + low
                    tiles[low] = jnp.where(lane >= h * DH, piece, tiles[low])
                else:
                    tiles[low] = piece
    return {low: tile.astype(jnp.bfloat16) for low, tile in tiles.items()}


def row_max(parts):
    if all(part.shape == parts[0].shape for part in parts):
        return jnp.max(functools.reduce(jnp.maximum, parts), axis=-1, keepdims=True)
    return functools.reduce(jnp.maximum, [jnp.max(part, axis=-1, keepdims=True) for part in parts])


def columns(row):
    return jnp.broadcast_to(row, (LANES, row.shape[1])).T


def link_bias(mine, theirs):
    return jnp.where(jnp.abs(mine[:, :1] - theirs.T[: mine.shape[0]]) <= 1.5, 0.0, -1e30)


def store_period(base, tiles, out_ref):
    for low, tile in tiles.items():
        out_ref[:, base + low : base + low + LANES] = tile


def ends_kernel(k_ref, v_ref, code_ref, *end_refs):
    even = lax.axis_index("seq") % 2 == 0
    tokens, width = k_ref.shape
    code = columns(code_ref[...])
    for n, ref in enumerate(end_refs):
        most = ref.shape[0]
        tail = even if n == 0 else jnp.logical_not(even)
        first = pl.multiple_of(jnp.where(tail, tokens - most, 0), most)
        ref[:, :width] = k_ref[pl.ds(first, most), :]
        ref[:, width : 2 * width] = v_ref[pl.ds(first, most), :]
        here = jnp.where(tail, code[tokens - most :], code[:most])
        ref[:, 2 * width :] = here.astype(jnp.bfloat16)


def middle_kernel(reach, q_ref, k_ref, v_ref, code_ref, out_ref):
    rows = out_ref.shape[0]
    code = columns(code_ref[...])
    bias = link_bias(code[reach : reach + rows], code)
    period = math.lcm(DH, LANES)
    masks = head_masks(rows, period)
    query = lambda lanes: q_ref[reach : reach + rows, lanes]
    for base in range(0, out_ref.shape[1], period):
        scores = period_scores(base, query, [lambda lanes: k_ref[:, lanes]], masks, period)
        sets = [(bias, lambda lanes: v_ref[:, lanes])]
        store_period(base, mixed_period(base, scores, sets, period), out_ref)


def sides_kernel(reach, q_ref, k_ref, v_ref, code_ref, one_ref, two_ref, *refs):
    out_ref, keys, values, codes = refs
    tokens, width = q_ref.shape
    near = 2 * reach
    code = columns(code_ref[...])
    even = lax.axis_index("seq") % 2 == 0
    period = math.lcm(DH, LANES)
    masks = head_masks(reach, period)
    blocks = []
    for side, first in ((0, 0), (1, tokens - near)):
        own = slice(first, first + near)
        use_two = even if side == 0 else jnp.logical_not(even)
        halo = jnp.where(use_two, two_ref[...], one_ref[...])
        keys[side, :near] = k_ref[own]
        values[side, :near] = v_ref[own]
        codes[side, :near] = code[own]
        keys[side, near : near + reach] = halo[:, :width]
        values[side, near : near + reach] = halo[:, width : 2 * width]
        codes[side, near : near + reach] = halo[:, 2 * width :].astype(jnp.float32)
        spare = keys.shape[1] - near - reach
        if spare:
            for ref in (keys, values, codes):
                ref[side, near + reach :] = jnp.zeros((spare, ref.shape[2]), ref.dtype)
        top = side * (tokens - reach)
        blocks.append((side, top, link_bias(code[top : top + reach], codes[side])))
    for base in range(0, width, period):
        scores = []
        for side, top, bias in blocks:
            query = lambda lanes: q_ref[top : top + reach, lanes]
            key = lambda lanes: keys[side, :, lanes]
            scores.append(period_scores(base, query, [key], masks, period))
        for (side, top, bias), part in zip(blocks, scores):
            sets = [(bias, lambda lanes: values[side, :, lanes])]
            tiles = mixed_period(base, part, sets, period)
            store_period(base, tiles, out_ref.at[side * reach : (side + 1) * reach])


def edge_kernel(reach, q_ref, k_ref, v_ref, code_ref, *refs):
    halos = refs[:-4]
    out_ref, keys, values, codes = refs[-4:]
    width = q_ref.shape[1]
    code = columns(code_ref[...])
    at = 0
    for piece in halos:
        rows = piece.shape[0]
        keys[at : at + rows] = piece[:, :width]
        values[at : at + rows] = piece[:, width : 2 * width]
        codes[at : at + rows] = piece[:, 2 * width :].astype(jnp.float32)
        at += rows
    if at < keys.shape[0]:
        for ref in (keys, values, codes):
            ref[at:] = jnp.zeros((ref.shape[0] - at, ref.shape[1]), ref.dtype)
    period = math.lcm(DH, LANES)
    masks = head_masks(q_ref.shape[0], period)
    query = lambda lanes: q_ref[:, lanes]
    pair = [lambda lanes: k_ref[:, lanes], lambda lanes: keys[:, lanes]]
    sets = [
        (link_bias(code, code), lambda lanes: v_ref[:, lanes]),
        (link_bias(code, codes[...]), lambda lanes: values[:, lanes]),
    ]
    for base in range(0, width, period):
        scores = period_scores(base, query, pair, masks, period)
        store_period(base, mixed_period(base, scores, sets, period), out_ref)


def attend_cost(tokens, span, width):
    return pl.CostEstimate(
        flops=HEADS * tokens * span * 2 * LANES * 4,
        bytes_accessed=12 * tokens * width,
        transcendentals=HEADS * tokens * span,
    )


VMEM = pl.BlockSpec(memory_space=pltpu.VMEM)
PARAMS = pltpu.CompilerParams(vmem_limit_bytes=VMEM_LIMIT)


def pack_ends(keys, values, code, most):
    width = keys.shape[1]
    ends = jax.ShapeDtypeStruct((most, 2 * width + LANES), jnp.bfloat16)
    return pl.pallas_call(
        ends_kernel,
        in_specs=[VMEM] * 3,
        out_specs=[VMEM] * 2,
        out_shape=[ends, ends],
        compiler_params=PARAMS,
        cost_estimate=pl.CostEstimate(flops=0, bytes_accessed=16 * most * width, transcendentals=0),
        name="pack_ends",
    )(keys, values, code)


def attend_middle(queries, keys, values, code, reach):
    tokens, width = queries.shape
    return pl.pallas_call(
        functools.partial(middle_kernel, reach),
        in_specs=[VMEM] * 4,
        out_specs=VMEM,
        out_shape=jax.ShapeDtypeStruct((tokens - 2 * reach, width), jnp.bfloat16),
        compiler_params=PARAMS,
        cost_estimate=attend_cost(tokens - 2 * reach, tokens, width),
        name="attend_middle",
    )(queries, keys, values, code)


def attend_edges(queries, keys, values, code, halos, reach):
    tokens, width = queries.shape
    rows = min(tokens, 2 * reach)
    if tokens > 2 * reach:
        kernel = sides_kernel
        held = (2, -(-3 * reach // LANES) * LANES)
    else:
        kernel = edge_kernel
        held = (-(-2 * reach // LANES) * LANES,)
    operands = [queries, keys, values, code, *halos]
    return pl.pallas_call(
        functools.partial(kernel, reach),
        in_specs=[VMEM] * len(operands),
        out_specs=VMEM,
        out_shape=jax.ShapeDtypeStruct((rows, width), jnp.bfloat16),
        scratch_shapes=[
            pltpu.VMEM((*held, width), jnp.bfloat16),
            pltpu.VMEM((*held, width), jnp.bfloat16),
            pltpu.VMEM((*held, LANES), jnp.float32),
        ],
        compiler_params=PARAMS,
        cost_estimate=attend_cost(rows, LANES, width),
        name="attend_edges",
    )(*operands)


def pack_grads_kernel(grad_ref, mark_ref, *refs):
    first_ref, second_ref, sems = refs[-3:]
    half = grad_ref.shape[1] // 2
    copies = []
    for n, ref in enumerate((first_ref, second_ref)):
        copies.append(
            pltpu.make_async_copy(
                grad_ref.at[:, pl.ds(n * half, half)], ref.at[:, pl.ds(0, half)], sems.at[n]
            )
        )
    for copy in copies:
        copy.start()
    place = columns(mark_ref[1:2]).astype(jnp.bfloat16)
    for ref in (first_ref, second_ref):
        ref[:, half:] = place
    for copy in copies:
        copy.wait()


def pack_grads(grads, marks, *others):
    tokens, width = grads.shape
    far = pl.BlockSpec(memory_space=pltpu.HBM)
    return pl.pallas_call(
        pack_grads_kernel,
        in_specs=[far, VMEM] + [far] * len(others),
        out_specs=[VMEM] * 2,
        out_shape=[jax.ShapeDtypeStruct((tokens, width // 2 + LANES), jnp.bfloat16)] * 2,
        scratch_shapes=[pltpu.SemaphoreType.DMA((2,))],
        compiler_params=pltpu.CompilerParams(vmem_limit_bytes=PACK_LIMIT),
        cost_estimate=pl.CostEstimate(flops=0, bytes_accessed=4 * tokens * width, transcendentals=0),
        name="pack_grads",
    )(grads, marks, *others)


def selector(row):
    tokens = row.shape[1]
    wanted = lax.broadcasted_iota(jnp.int32, (tokens, tokens), 0).astype(jnp.float32)
    return jnp.where(wanted == row, 1.0, 0.0)


def sums_kernel(sizes, gate_ref, *refs):
    group = lax.axis_index("grp")
    half = gate_ref.shape[1] // 2
    count = len(sizes)
    for n in range(2):
        mine_ref, theirs_ref = refs[2 * n : 2 * n + 2]
        picks, rows = [], []
        for ref in (mine_ref, theirs_ref):
            place = ref[:, half : half + LANES].astype(jnp.float32).T[:1]
            picks.append(selector(place).astype(jnp.bfloat16))
            rows.append(ref[:, :half])
        summed = jnp.dot(
            jnp.concatenate(picks, axis=1),
            jnp.concatenate(rows, axis=0),
            preferred_element_type=jnp.float32,
        )
        term = gate_ref[:, n * half : (n + 1) * half] * summed
        own = jnp.where(group == n + 1, 1.0, 0.0)
        term = (term + own * rows[1].astype(jnp.float32)).astype(jnp.bfloat16)
        at = 0
        for ref, size in zip(refs[4 + n * count : 4 + (n + 1) * count], sizes):
            ref[...] = term[at : at + size]
            at += size


def pair_sums(gate, parts, sizes):
    tokens, width = parts[0].shape[0], gate.shape[1]
    outs = [jax.ShapeDtypeStruct((size, width // 2), jnp.bfloat16) for size in sizes] * 2
    return pl.pallas_call(
        functools.partial(sums_kernel, sizes),
        in_specs=[VMEM] * 5,
        out_specs=[VMEM] * len(outs),
        out_shape=outs,
        compiler_params=PARAMS,
        cost_estimate=pl.CostEstimate(
            flops=4 * tokens * tokens * width, bytes_accessed=6 * tokens * width, transcendentals=0
        ),
        name="pair_sums",
    )(gate, *parts)


def piece_spots(tokens, reach, piece):
    if tokens <= 2 * reach:
        return [(0, tokens, 0)]
    if piece == 0:
        return [(reach, tokens - 2 * reach, 0)]
    return [(0, reach, 0), (tokens - reach, reach, reach)]


def picked(spots, row_ref):
    picks = selector(row_ref[...]).T.astype(jnp.bfloat16)
    return jnp.concatenate([picks[:, top : top + size] for top, size, at in spots], axis=1)


def relay_first_kernel(
    spots, later, row_ref, gate_ref, a_ref, b_ref, base_ref, c_ref, d_ref, grad_ref, out_ref, picks_ref, sems
):
    half = a_ref.shape[1]
    copies = []
    for n, ref in enumerate((c_ref, d_ref)):
        to = grad_ref.at[pl.ds(0, ref.shape[0]), pl.ds(n * half, half)]
        copies.append(pltpu.make_async_copy(ref, to, sems.at[n]))
    for copy in copies:
        copy.start()
    picks = picked(spots, row_ref)
    for n, ref in enumerate((a_ref, b_ref)):
        lanes = slice(n * half, (n + 1) * half)
        relayed = jnp.dot(picks, ref[...], preferred_element_type=jnp.float32)
        out_ref[:, lanes] = base_ref[:, lanes].astype(jnp.float32) + gate_ref[:, lanes] * relayed
    picks_ref[...] = picked(later, row_ref)
    for copy in copies:
        copy.wait()


def relay_first(rows, gate, branch, base, totals, spots, later):
    tokens, width = base.shape
    return pl.pallas_call(
        functools.partial(relay_first_kernel, spots, later),
        in_specs=[VMEM] * 7,
        out_specs=[pl.BlockSpec(memory_space=pltpu.HBM), VMEM, VMEM],
        out_shape=[
            jax.ShapeDtypeStruct((tokens, width), jnp.bfloat16),
            jax.ShapeDtypeStruct((tokens, width), jnp.float32),
            jax.ShapeDtypeStruct((tokens, sum(size for top, size, at in later)), jnp.bfloat16),
        ],
        scratch_shapes=[pltpu.SemaphoreType.DMA((2,))],
        compiler_params=PARAMS,
        cost_estimate=pl.CostEstimate(
            flops=2 * tokens * tokens * width, bytes_accessed=24 * tokens * width, transcendentals=0
        ),
        name="relay_first",
    )(rows, gate, *branch, base, *totals)


def relay_last_kernel(
    part, chunks, first_row, picks_ref, gate_ref, held_ref, got_ref, base_ref, total_ref, *refs
):
    grad_ref, out_ref, staged, summed, sems, grad_sem = refs[-6:]
    half = held_ref.shape[1]
    other = 1 - part
    group = lax.axis_index("grp")
    holds = group <= 1 if part == 0 else group % 2 == 0
    summed[...] = jnp.where(holds, got_ref[...], total_ref[...])
    to = grad_ref.at[pl.ds(first_row, total_ref.shape[0]), pl.ds(other * half, half)]
    copies = [pltpu.make_async_copy(summed, to, grad_sem)]
    copies[0].start()
    step = half // chunks
    for c in range(chunks):
        mine = slice(c * step, (c + 1) * step)
        lanes = slice(part * half + c * step, part * half + (c + 1) * step)
        branch = jnp.where(holds, held_ref[:, mine], got_ref[:, mine])
        relayed = jnp.dot(picks_ref[...], branch, preferred_element_type=jnp.float32)
        total = base_ref[:, lanes].astype(jnp.float32) + gate_ref[:, lanes] * relayed
        staged[:, mine] = total.astype(staged.dtype)
        copies.append(
            pltpu.make_async_copy(
                staged.at[:, pl.ds(c * step, step)],
                out_ref.at[:, pl.ds(part * half + c * step, step)],
                sems.at[c],
            )
        )
        copies[-1].start()
    for copy in copies:
        copy.wait()


def relay_last(picks, gate, held, got, base, total, part, first_row, grads, out):
    tokens, width = base.shape
    chunks = 2 if width // 2 % (2 * LANES) == 0 else 1
    far = pl.BlockSpec(memory_space=pltpu.HBM)
    operands = [picks, gate, held, got, base, total]
    aliases = {}
    for n, buffer in enumerate((grads, out)):
        if buffer is not None:
            aliases[len(operands)] = n
            operands.append(buffer)
    return pl.pallas_call(
        functools.partial(relay_last_kernel, part, chunks, first_row),
        in_specs=[VMEM] * 6 + [far] * len(aliases),
        out_specs=[far] * 2,
        out_shape=[jax.ShapeDtypeStruct((tokens, width), jnp.bfloat16)] * 2,
        input_output_aliases=aliases,
        scratch_shapes=[
            pltpu.VMEM((tokens, width // 2), jnp.bfloat16),
            pltpu.VMEM(total.shape, jnp.bfloat16),
            pltpu.SemaphoreType.DMA((chunks,)),
            pltpu.SemaphoreType.DMA,
        ],
        compiler_params=PARAMS,
        cost_estimate=pl.CostEstimate(
            flops=tokens * tokens * width, bytes_accessed=6 * tokens * width, transcendentals=0
        ),
        name="relay_last",
    )(*operands)


def whole_gate(gate):
    ranks = lax.axis_size("rep")
    if ranks != 2:
        return lax.all_gather(gate, "rep", axis=0, tiled=True)
    other = lax.ppermute(gate, "rep", [(0, 1), (1, 0)])
    first = lax.axis_index("rep") == 0
    return jnp.concatenate([jnp.where(first, gate, other), jnp.where(first, other, gate)])


SWAP_X, SWAP_Y = [(0, 1), (1, 0), (2, 3), (3, 2)], [(0, 2), (2, 0), (1, 3), (3, 1)]
ROUND_A, ROUND_B = [(0, 1), (1, 3), (3, 2), (2, 0)], [(0, 2), (2, 3), (3, 1), (1, 0)]


def added(a, b):
    return (a.astype(jnp.float32) + b.astype(jnp.float32)).astype(a.dtype)


def local(query_rows, key_rows, value_rows, view_frame, control_row, control_gate, out_grad):
    queries, keys, values = query_rows[0, 0], key_rows[0, 0], value_rows[0, 0]
    tokens, width = queries.shape
    half = width // 2
    ranks = lax.axis_size("seq")
    reach = 2 * (tokens * ranks // 32)
    hops = (reach + tokens - 1) // tokens
    group, rank = lax.axis_index("grp"), lax.axis_index("seq")
    send = lambda block, route: lax.ppermute(block, "grp", route)

    tag = view_frame[0, 0]
    code = tag + 8 * (tag // FRAMES) + 16
    marks = jnp.stack((code, control_row[0, 0] % tokens)).astype(jnp.float32)
    code, rows = marks[:1], marks[1:]
    most = min(tokens, reach)
    even = rank % 2 == 0
    sent_a, sent_b = pack_grads(out_grad[0, 0], marks, queries, keys, values)
    code, sent_a, sent_b = lax.optimization_barrier((code, sent_a, sent_b))
    got_a, got_b = send(sent_a, SWAP_X), send(sent_b, SWAP_Y)
    end_one, end_two = pack_ends(keys, values, code, most)
    code, end_one, end_two = lax.optimization_barrier((code, end_one, end_two))
    own = [attend_middle(queries, keys, values, code, reach)] if tokens > 2 * reach else []
    gate = whole_gate(control_gate)[None]
    halos = [paired(end_one, "seq", 0), paired(end_two, "seq", 1)]
    for hop in range(2, hops + 1):
        count = min(tokens, reach - (hop - 1) * tokens)
        tail, head = jnp.where(even, end_one, end_two), jnp.where(even, end_two, end_one)
        halos.append(shifted(tail[most - count :], "seq", hop))
        halos.append(shifted(head[:count], "seq", -hop))
    sizes = [piece.shape[0] for piece in own] + [min(tokens, 2 * reach)]
    sums = pair_sums(gate, (sent_a, got_a, sent_b, got_b), sizes)
    count = len(sizes)

    def outgoing(piece, sum_a, sum_b):
        to_a = jnp.where(group == 0, piece[:, :half], jnp.where(group == 1, sum_a, sum_b))
        to_b = jnp.where(group == 0, piece[:, half:], jnp.where(group == 2, sum_b, sum_a))
        return to_a, to_b

    going = [outgoing(own[0], sums[0], sums[count])] if own else []
    code, *ready = lax.optimization_barrier((code, *sums, *(going[0] if going else ())))
    sums = ready[: 2 * count]
    if going:
        going = [ready[2 * count :]]
    own.append(attend_edges(queries, keys, values, code, halos, reach))

    going.append(outgoing(own[-1], sums[count - 1], sums[2 * count - 1]))
    spots = [piece_spots(tokens, reach, n) for n in range(count)]
    order = [
        own[n][at : at + size] for top, size, n, at in sorted(
            (top, size, n, at) for n in range(count) for top, size, at in spots[n]
        )
    ]
    block_out = jnp.concatenate(order, axis=0)
    branch_grad, first_row = None, 0
    picks = (rows[0][:, None] == jnp.arange(tokens)).astype(jnp.bfloat16) if count == 1 else None
    for n, (piece, sum_a, sum_b) in enumerate(zip(own, sums[:count], sums[count:])):
        piece_a, piece_b = piece[:, :half], piece[:, half:]
        one, two = send(going[n][0], ROUND_A), send(going[n][1], ROUND_B)
        total_a = added(sum_a, jnp.where(group == 1, two, one))
        total_b = added(sum_b, jnp.where(group == 2, one, two))
        held_a = jnp.where(group == 0, piece_a, one)
        held_b = jnp.where(group == 0, piece_b, two)
        across = send(jnp.where((group == 0) | (group == 2), held_b, total_a), SWAP_X)
        down = send(jnp.where(group <= 1, held_a, total_b), SWAP_Y)
        branch_a = jnp.where(group <= 1, held_a, down)
        branch_b = jnp.where((group == 0) | (group == 2), held_b, across)
        totals = (
            jnp.where((group == 0) | (group == 2), across, total_a),
            jnp.where(group <= 1, down, total_b),
        )
        if n < count - 1:
            branch_grad, block_out, picks = relay_first(
                rows, gate, (branch_a, branch_b), block_out, totals, spots[n], spots[n + 1]
            )
            first_row = piece.shape[0]
            continue
        base, block_out = block_out, None
        ends = ((held_a, down, total_b), (held_b, across, total_a))
        for part in (1, 0):
            held, got, total = ends[part]
            branch_grad, block_out = relay_last(
                picks, gate, held, got, base, total, part, first_row, branch_grad, block_out
            )
    return (block_out[None, None], branch_grad[None])


def solution(mesh):
    placed = (
        P("rep", "grp", "seq", None),
        P("rep", "grp", "seq", None),
        P("rep", "grp", "seq", None),
        P("rep", "grp", "seq"),
        P("rep", "grp", "seq"),
        P("rep"),
        P("rep", "grp", "seq", None),
    )
    return jax.shard_map(
        local,
        mesh=mesh,
        in_specs=placed,
        out_specs=(P("rep", "grp", "seq", None), P("rep", "seq", None)),
        check_vma=False,
    )
```

```python
import functools
import math

import jax
import jax.numpy as jnp
from jax import lax
from jax.experimental import pallas as pl
from jax.experimental.pallas import tpu as pltpu
from jax.sharding import PartitionSpec as P

HEADS = 32
DH = 80
FRAMES = 20
LANES = 128
VMEM_LIMIT = 32 * 1024 * 1024
PACK_LIMIT = 53 * 1024 * 1024


def shifted(block, axis, distance):
    devices = range(lax.axis_size(axis))
    route = [(i - distance, i) for i in devices if i - distance in devices]
    return lax.ppermute(block, axis, route)


def paired(block, axis, first):
    size = lax.axis_size(axis)
    route = []
    for i in range(size):
        other = i + 1 if (i - first) % 2 == 0 else i - 1
        if 0 <= other < size:
            route.append((i, other))
    return lax.ppermute(block, axis, route)


def lane_windows(heads):
    windows = []
    for head in range(heads):
        first, last = head * DH, (head + 1) * DH
        if windows and last <= windows[-1][0] + 2 * LANES:
            windows[-1][1].append(head)
        else:
            windows.append((first // LANES * LANES, [head]))
    out = []
    for start, members in windows:
        start = min(start, heads * DH - 2 * LANES)
        out.append((start, members))
    return out


def head_masks(rows, period):
    masks = {}
    for start, members in lane_windows(period // DH):
        lane = lax.broadcasted_iota(jnp.int32, (rows, 2 * LANES), 1) + start
        for h in members:
            inside = (lane >= h * DH) & (lane < (h + 1) * DH)
            masks[h] = jnp.where(inside, 1.0, 0.0).astype(jnp.bfloat16)
    return masks


def period_scores(base, query, keys, masks, period):
    scores = []
    for start, members in lane_windows(period // DH):
        lanes = slice(base + start, base + start + 2 * LANES)
        part = query(lanes)
        stacked = jnp.concatenate([part * masks[h] for h in members], axis=0)
        scores.append(
            [
                lax.dot_general(
                    stacked, key(lanes), (((1,), (1,)), ((), ())), preferred_element_type=jnp.float32
                )
                for key in keys
            ]
        )
    return scores


def mixed_period(base, scores, sets, period):
    rows = sets[0][0].shape[0]
    factor = math.log2(math.e) / math.sqrt(DH)
    windows = lane_windows(period // DH)
    weights = []
    for parts, (start, members) in zip(scores, windows):
        parts = [
            part.reshape(len(members), rows, -1) + bias[None]
            for part, (bias, value) in zip(parts, sets)
        ]
        largest = row_max(parts)
        weights.append(
            [
                jnp.exp2((part - largest) * factor).astype(jnp.bfloat16).reshape(len(members) * rows, -1)
                for part in parts
            ]
        )
    tiles = {}
    for parts, (start, members) in zip(weights, windows):
        lanes = slice(base + start, base + start + 2 * LANES)
        mixed = sum(
            jnp.dot(part, value(lanes), preferred_element_type=jnp.float32)
            for part, (bias, value) in zip(parts, sets)
        )
        totals = sum(
            jnp.dot(part, jnp.ones((part.shape[1], LANES), part.dtype), preferred_element_type=jnp.float32)
            for part in parts
        )
        scale = 1.0 / totals
        for n, h in enumerate(members):
            for t in range(2):
                low = start + t * LANES
                if h * DH >= low + LANES or (h + 1) * DH <= low:
                    continue
                mine = slice(n * rows, (n + 1) * rows)
                piece = mixed[mine, t * LANES : (t + 1) * LANES] * scale[mine]
                if low in tiles:
                    lane = lax.broadcasted_iota(jnp.int32, (rows, LANES), 1) + low
                    tiles[low] = jnp.where(lane >= h * DH, piece, tiles[low])
                else:
                    tiles[low] = piece
    return {low: tile.astype(jnp.bfloat16) for low, tile in tiles.items()}


def row_max(parts):
    if all(part.shape == parts[0].shape for part in parts):
        return jnp.max(functools.reduce(jnp.maximum, parts), axis=-1, keepdims=True)
    return functools.reduce(jnp.maximum, [jnp.max(part, axis=-1, keepdims=True) for part in parts])


def columns(row):
    return jnp.broadcast_to(row, (LANES, row.shape[1])).T


def link_bias(mine, theirs):
    return jnp.where(jnp.abs(mine[:, :1] - theirs.T[: mine.shape[0]]) <= 1.5, 0.0, -1e30)


def store_period(base, tiles, out_ref):
    for low, tile in tiles.items():
        out_ref[:, base + low : base + low + LANES] = tile


def ends_kernel(k_ref, v_ref, code_ref, *end_refs):
    even = lax.axis_index("seq") % 2 == 0
    tokens, width = k_ref.shape
    code = columns(code_ref[...])
    for n, ref in enumerate(end_refs):
        most = ref.shape[0]
        tail = even if n == 0 else jnp.logical_not(even)
        first = pl.multiple_of(jnp.where(tail, tokens - most, 0), most)
        ref[:, :width] = k_ref[pl.ds(first, most), :]
        ref[:, width : 2 * width] = v_ref[pl.ds(first, most), :]
        here = jnp.where(tail, code[tokens - most :], code[:most])
        ref[:, 2 * width :] = here.astype(jnp.bfloat16)


def middle_kernel(reach, q_ref, k_ref, v_ref, code_ref, out_ref):
    rows = out_ref.shape[0]
    code = columns(code_ref[...])
    bias = link_bias(code[reach : reach + rows], code)
    period = math.lcm(DH, LANES)
    masks = head_masks(rows, period)
    query = lambda lanes: q_ref[reach : reach + rows, lanes]
    for base in range(0, out_ref.shape[1], period):
        scores = period_scores(base, query, [lambda lanes: k_ref[:, lanes]], masks, period)
        sets = [(bias, lambda lanes: v_ref[:, lanes])]
        store_period(base, mixed_period(base, scores, sets, period), out_ref)


def sides_kernel(reach, q_ref, k_ref, v_ref, code_ref, one_ref, two_ref, *refs):
    out_ref, keys, values, codes = refs
    tokens, width = q_ref.shape
    near = 2 * reach
    code = columns(code_ref[...])
    even = lax.axis_index("seq") % 2 == 0
    period = math.lcm(DH, LANES)
    masks = head_masks(reach, period)
    blocks = []
    for side, first in ((0, 0), (1, tokens - near)):
        own = slice(first, first + near)
        use_two = even if side == 0 else jnp.logical_not(even)
        halo = jnp.where(use_two, two_ref[...], one_ref[...])
        keys[side, :near] = k_ref[own]
        values[side, :near] = v_ref[own]
        codes[side, :near] = code[own]
        keys[side, near : near + reach] = halo[:, :width]
        values[side, near : near + reach] = halo[:, width : 2 * width]
        codes[side, near : near + reach] = halo[:, 2 * width :].astype(jnp.float32)
        spare = keys.shape[1] - near - reach
        if spare:
            for ref in (keys, values, codes):
                ref[side, near + reach :] = jnp.zeros((spare, ref.shape[2]), ref.dtype)
        top = side * (tokens - reach)
        blocks.append((side, top, link_bias(code[top : top + reach], codes[side])))
    for base in range(0, width, period):
        scores = []
        for side, top, bias in blocks:
            query = lambda lanes: q_ref[top : top + reach, lanes]
            key = lambda lanes: keys[side, :, lanes]
            scores.append(period_scores(base, query, [key], masks, period))
        for (side, top, bias), part in zip(blocks, scores):
            sets = [(bias, lambda lanes: values[side, :, lanes])]
            tiles = mixed_period(base, part, sets, period)
            store_period(base, tiles, out_ref.at[side * reach : (side + 1) * reach])


def edge_kernel(reach, q_ref, k_ref, v_ref, code_ref, *refs):
    halos = refs[:-4]
    out_ref, keys, values, codes = refs[-4:]
    width = q_ref.shape[1]
    code = columns(code_ref[...])
    at = 0
    for piece in halos:
        rows = piece.shape[0]
        keys[at : at + rows] = piece[:, :width]
        values[at : at + rows] = piece[:, width : 2 * width]
        codes[at : at + rows] = piece[:, 2 * width :].astype(jnp.float32)
        at += rows
    if at < keys.shape[0]:
        for ref in (keys, values, codes):
            ref[at:] = jnp.zeros((ref.shape[0] - at, ref.shape[1]), ref.dtype)
    period = math.lcm(DH, LANES)
    masks = head_masks(q_ref.shape[0], period)
    query = lambda lanes: q_ref[:, lanes]
    pair = [lambda lanes: k_ref[:, lanes], lambda lanes: keys[:, lanes]]
    sets = [
        (link_bias(code, code), lambda lanes: v_ref[:, lanes]),
        (link_bias(code, codes[...]), lambda lanes: values[:, lanes]),
    ]
    for base in range(0, width, period):
        scores = period_scores(base, query, pair, masks, period)
        store_period(base, mixed_period(base, scores, sets, period), out_ref)


def attend_cost(tokens, span, width):
    return pl.CostEstimate(
        flops=HEADS * tokens * span * 2 * LANES * 4,
        bytes_accessed=12 * tokens * width,
        transcendentals=HEADS * tokens * span,
    )


VMEM = pl.BlockSpec(memory_space=pltpu.VMEM)
PARAMS = pltpu.CompilerParams(vmem_limit_bytes=VMEM_LIMIT)


def pack_ends(keys, values, code, most):
    width = keys.shape[1]
    ends = jax.ShapeDtypeStruct((most, 2 * width + LANES), jnp.bfloat16)
    return pl.pallas_call(
        ends_kernel,
        in_specs=[VMEM] * 3,
        out_specs=[VMEM] * 2,
        out_shape=[ends, ends],
        compiler_params=PARAMS,
        cost_estimate=pl.CostEstimate(flops=0, bytes_accessed=16 * most * width, transcendentals=0),
        name="pack_ends",
    )(keys, values, code)


def attend_middle(queries, keys, values, code, reach):
    tokens, width = queries.shape
    return pl.pallas_call(
        functools.partial(middle_kernel, reach),
        in_specs=[VMEM] * 4,
        out_specs=VMEM,
        out_shape=jax.ShapeDtypeStruct((tokens - 2 * reach, width), jnp.bfloat16),
        compiler_params=PARAMS,
        cost_estimate=attend_cost(tokens - 2 * reach, tokens, width),
        name="attend_middle",
    )(queries, keys, values, code)


def attend_edges(queries, keys, values, code, halos, reach):
    tokens, width = queries.shape
    rows = min(tokens, 2 * reach)
    if tokens > 2 * reach:
        kernel = sides_kernel
        held = (2, -(-3 * reach // LANES) * LANES)
    else:
        kernel = edge_kernel
        held = (-(-2 * reach // LANES) * LANES,)
    operands = [queries, keys, values, code, *halos]
    return pl.pallas_call(
        functools.partial(kernel, reach),
        in_specs=[VMEM] * len(operands),
        out_specs=VMEM,
        out_shape=jax.ShapeDtypeStruct((rows, width), jnp.bfloat16),
        scratch_shapes=[
            pltpu.VMEM((*held, width), jnp.bfloat16),
            pltpu.VMEM((*held, width), jnp.bfloat16),
            pltpu.VMEM((*held, LANES), jnp.float32),
        ],
        compiler_params=PARAMS,
        cost_estimate=attend_cost(rows, LANES, width),
        name="attend_edges",
    )(*operands)


def pack_grads_kernel(grad_ref, mark_ref, *refs):
    first_ref, second_ref, sems = refs[-3:]
    half = grad_ref.shape[1] // 2
    copies = []
    for n, ref in enumerate((first_ref, second_ref)):
        copies.append(
            pltpu.make_async_copy(
                grad_ref.at[:, pl.ds(n * half, half)], ref.at[:, pl.ds(0, half)], sems.at[n]
            )
        )
    for copy in copies:
        copy.start()
    place = columns(mark_ref[1:2]).astype(jnp.bfloat16)
    for ref in (first_ref, second_ref):
        ref[:, half:] = place
    for copy in copies:
        copy.wait()


def pack_grads(grads, marks, *others):
    tokens, width = grads.shape
    far = pl.BlockSpec(memory_space=pltpu.HBM)
    return pl.pallas_call(
        pack_grads_kernel,
        in_specs=[far, VMEM] + [far] * len(others),
        out_specs=[VMEM] * 2,
        out_shape=[jax.ShapeDtypeStruct((tokens, width // 2 + LANES), jnp.bfloat16)] * 2,
        scratch_shapes=[pltpu.SemaphoreType.DMA((2,))],
        compiler_params=pltpu.CompilerParams(vmem_limit_bytes=PACK_LIMIT),
        cost_estimate=pl.CostEstimate(flops=0, bytes_accessed=4 * tokens * width, transcendentals=0),
        name="pack_grads",
    )(grads, marks, *others)


def selector(row):
    tokens = row.shape[1]
    wanted = lax.broadcasted_iota(jnp.int32, (tokens, tokens), 0).astype(jnp.float32)
    return jnp.where(wanted == row, 1.0, 0.0)


def sums_kernel(part, sizes, gate_ref, row_ref, mine_ref, theirs_ref, *out_refs):
    half = gate_ref.shape[1] // 2
    place = theirs_ref[:, half:].astype(jnp.float32).T[:1]
    picks = [selector(row).astype(jnp.bfloat16) for row in (row_ref[...], place)]
    theirs = theirs_ref[:, :half]
    summed = jnp.dot(
        jnp.concatenate(picks, axis=1),
        jnp.concatenate((mine_ref[:, :half], theirs), axis=0),
        preferred_element_type=jnp.float32,
    )
    own = jnp.where(lax.axis_index("grp") == part + 1, 1.0, 0.0)
    term = gate_ref[:, part * half : (part + 1) * half] * summed + own * theirs.astype(jnp.float32)
    term = term.astype(jnp.bfloat16)
    at = 0
    for ref, size in zip(out_refs, sizes):
        ref[...] = term[at : at + size]
        at += size


def pair_sums(part, gate, rows, mine, theirs, sizes):
    tokens, half = mine.shape[0], gate.shape[1] // 2
    return pl.pallas_call(
        functools.partial(sums_kernel, part, sizes),
        in_specs=[VMEM] * 4,
        out_specs=[VMEM] * len(sizes),
        out_shape=[jax.ShapeDtypeStruct((size, half), jnp.bfloat16) for size in sizes],
        compiler_params=PARAMS,
        cost_estimate=pl.CostEstimate(
            flops=4 * tokens * tokens * half, bytes_accessed=6 * tokens * half, transcendentals=0
        ),
        name="pair_sums",
    )(gate, rows, mine, theirs)


def piece_spots(tokens, reach, piece):
    if tokens <= 2 * reach:
        return [(0, tokens, 0)]
    if piece == 0:
        return [(reach, tokens - 2 * reach, 0)]
    return [(0, reach, 0), (tokens - reach, reach, reach)]


def picked(spots, row_ref):
    picks = selector(row_ref[...]).T.astype(jnp.bfloat16)
    return jnp.concatenate([picks[:, top : top + size] for top, size, at in spots], axis=1)


def relay_first_kernel(
    spots, later, row_ref, gate_ref, a_ref, b_ref, base_ref, c_ref, d_ref, grad_ref, out_ref, picks_ref, sems
):
    half = a_ref.shape[1]
    copies = []
    for n, ref in enumerate((c_ref, d_ref)):
        to = grad_ref.at[pl.ds(0, ref.shape[0]), pl.ds(n * half, half)]
        copies.append(pltpu.make_async_copy(ref, to, sems.at[n]))
    for copy in copies:
        copy.start()
    picks = picked(spots, row_ref)
    for n, ref in enumerate((a_ref, b_ref)):
        lanes = slice(n * half, (n + 1) * half)
        relayed = jnp.dot(picks, ref[...], preferred_element_type=jnp.float32)
        out_ref[:, lanes] = base_ref[:, lanes].astype(jnp.float32) + gate_ref[:, lanes] * relayed
    picks_ref[...] = picked(later, row_ref)
    for copy in copies:
        copy.wait()


def relay_first(rows, gate, branch, base, totals, spots, later):
    tokens, width = base.shape
    return pl.pallas_call(
        functools.partial(relay_first_kernel, spots, later),
        in_specs=[VMEM] * 7,
        out_specs=[pl.BlockSpec(memory_space=pltpu.HBM), VMEM, VMEM],
        out_shape=[
            jax.ShapeDtypeStruct((tokens, width), jnp.bfloat16),
            jax.ShapeDtypeStruct((tokens, width), jnp.float32),
            jax.ShapeDtypeStruct((tokens, sum(size for top, size, at in later)), jnp.bfloat16),
        ],
        scratch_shapes=[pltpu.SemaphoreType.DMA((2,))],
        compiler_params=PARAMS,
        cost_estimate=pl.CostEstimate(
            flops=2 * tokens * tokens * width, bytes_accessed=24 * tokens * width, transcendentals=0
        ),
        name="relay_first",
    )(rows, gate, *branch, base, *totals)


def relay_last_kernel(
    part, chunks, first_row, picks_ref, gate_ref, held_ref, got_ref, base_ref, total_ref, *refs
):
    grad_ref, out_ref, staged, summed, sems, grad_sem = refs[-6:]
    half = held_ref.shape[1]
    other = 1 - part
    group = lax.axis_index("grp")
    holds = group <= 1 if part == 0 else group % 2 == 0
    summed[...] = jnp.where(holds, got_ref[...], total_ref[...])
    to = grad_ref.at[pl.ds(first_row, total_ref.shape[0]), pl.ds(other * half, half)]
    copies = [pltpu.make_async_copy(summed, to, grad_sem)]
    copies[0].start()
    step = half // chunks
    for c in range(chunks):
        mine = slice(c * step, (c + 1) * step)
        lanes = slice(part * half + c * step, part * half + (c + 1) * step)
        branch = jnp.where(holds, held_ref[:, mine], got_ref[:, mine])
        relayed = jnp.dot(picks_ref[...], branch, preferred_element_type=jnp.float32)
        total = base_ref[:, lanes].astype(jnp.float32) + gate_ref[:, lanes] * relayed
        staged[:, mine] = total.astype(staged.dtype)
        copies.append(
            pltpu.make_async_copy(
                staged.at[:, pl.ds(c * step, step)],
                out_ref.at[:, pl.ds(part * half + c * step, step)],
                sems.at[c],
            )
        )
        copies[-1].start()
    for copy in copies:
        copy.wait()


def relay_last(picks, gate, held, got, base, total, part, first_row, grads, out):
    tokens, width = base.shape
    chunks = 2 if width // 2 % (2 * LANES) == 0 else 1
    far = pl.BlockSpec(memory_space=pltpu.HBM)
    operands = [picks, gate, held, got, base, total]
    aliases = {}
    for n, buffer in enumerate((grads, out)):
        if buffer is not None:
            aliases[len(operands)] = n
            operands.append(buffer)
    return pl.pallas_call(
        functools.partial(relay_last_kernel, part, chunks, first_row),
        in_specs=[VMEM] * 6 + [far] * len(aliases),
        out_specs=[far] * 2,
        out_shape=[jax.ShapeDtypeStruct((tokens, width), jnp.bfloat16)] * 2,
        input_output_aliases=aliases,
        scratch_shapes=[
            pltpu.VMEM((tokens, width // 2), jnp.bfloat16),
            pltpu.VMEM(total.shape, jnp.bfloat16),
            pltpu.SemaphoreType.DMA((chunks,)),
            pltpu.SemaphoreType.DMA,
        ],
        compiler_params=PARAMS,
        cost_estimate=pl.CostEstimate(
            flops=tokens * tokens * width, bytes_accessed=6 * tokens * width, transcendentals=0
        ),
        name="relay_last",
    )(*operands)


def whole_gate(gate):
    ranks = lax.axis_size("rep")
    if ranks != 2:
        return lax.all_gather(gate, "rep", axis=0, tiled=True)
    other = lax.ppermute(gate, "rep", [(0, 1), (1, 0)])
    first = lax.axis_index("rep") == 0
    return jnp.concatenate([jnp.where(first, gate, other), jnp.where(first, other, gate)])


SWAP_X, SWAP_Y = [(0, 1), (1, 0), (2, 3), (3, 2)], [(0, 2), (2, 0), (1, 3), (3, 1)]
ROUND_A, ROUND_B = [(0, 1), (1, 3), (3, 2), (2, 0)], [(0, 2), (2, 3), (3, 1), (1, 0)]


def added(a, b):
    return (a.astype(jnp.float32) + b.astype(jnp.float32)).astype(a.dtype)


def local(query_rows, key_rows, value_rows, view_frame, control_row, control_gate, out_grad):
    queries, keys, values = query_rows[0, 0], key_rows[0, 0], value_rows[0, 0]
    tokens, width = queries.shape
    half = width // 2
    ranks = lax.axis_size("seq")
    reach = 2 * (tokens * ranks // 32)
    hops = (reach + tokens - 1) // tokens
    group, rank = lax.axis_index("grp"), lax.axis_index("seq")
    send = lambda block, route: lax.ppermute(block, "grp", route)

    tag = view_frame[0, 0]
    code = tag + 8 * (tag // FRAMES) + 16
    marks = jnp.stack((code, control_row[0, 0] % tokens)).astype(jnp.float32)
    code, rows = marks[:1], marks[1:]
    most = min(tokens, reach)
    even = rank % 2 == 0
    sent_a, sent_b = pack_grads(out_grad[0, 0], marks, queries, keys, values)
    code, sent_a, sent_b = lax.optimization_barrier((code, sent_a, sent_b))
    got_a, got_b = send(sent_a, SWAP_X), send(sent_b, SWAP_Y)
    end_one, end_two = pack_ends(keys, values, code, most)
    code, end_one, end_two = lax.optimization_barrier((code, end_one, end_two))
    own = [attend_middle(queries, keys, values, code, reach)] if tokens > 2 * reach else []
    gate = whole_gate(control_gate)[None]
    halos = [paired(end_one, "seq", 0), paired(end_two, "seq", 1)]
    for hop in range(2, hops + 1):
        count = min(tokens, reach - (hop - 1) * tokens)
        tail, head = jnp.where(even, end_one, end_two), jnp.where(even, end_two, end_one)
        halos.append(shifted(tail[most - count :], "seq", hop))
        halos.append(shifted(head[:count], "seq", -hop))
    sizes = [piece.shape[0] for piece in own] + [min(tokens, 2 * reach)]
    sums = [
        *pair_sums(0, gate, rows, sent_a, got_a, sizes),
        *pair_sums(1, gate, rows, sent_b, got_b, sizes),
    ]
    count = len(sizes)

    def outgoing(piece, sum_a, sum_b):
        to_a = jnp.where(group == 0, piece[:, :half], jnp.where(group == 1, sum_a, sum_b))
        to_b = jnp.where(group == 0, piece[:, half:], jnp.where(group == 2, sum_b, sum_a))
        return to_a, to_b

    going = [outgoing(own[0], sums[0], sums[count])] if own else []
    code, *ready = lax.optimization_barrier((code, *sums, *(going[0] if going else ())))
    sums = ready[: 2 * count]
    if going:
        going = [ready[2 * count :]]
    own.append(attend_edges(queries, keys, values, code, halos, reach))

    going.append(outgoing(own[-1], sums[count - 1], sums[2 * count - 1]))
    spots = [piece_spots(tokens, reach, n) for n in range(count)]
    order = [
        own[n][at : at + size] for top, size, n, at in sorted(
            (top, size, n, at) for n in range(count) for top, size, at in spots[n]
        )
    ]
    block_out = jnp.concatenate(order, axis=0)
    branch_grad, first_row = None, 0
    picks = (rows[0][:, None] == jnp.arange(tokens)).astype(jnp.bfloat16) if count == 1 else None
    for n, (piece, sum_a, sum_b) in enumerate(zip(own, sums[:count], sums[count:])):
        piece_a, piece_b = piece[:, :half], piece[:, half:]
        one, two = send(going[n][0], ROUND_A), send(going[n][1], ROUND_B)
        total_a = added(sum_a, jnp.where(group == 1, two, one))
        total_b = added(sum_b, jnp.where(group == 2, one, two))
        held_a = jnp.where(group == 0, piece_a, one)
        held_b = jnp.where(group == 0, piece_b, two)
        across = send(jnp.where((group == 0) | (group == 2), held_b, total_a), SWAP_X)
        down = send(jnp.where(group <= 1, held_a, total_b), SWAP_Y)
        branch_a = jnp.where(group <= 1, held_a, down)
        branch_b = jnp.where((group == 0) | (group == 2), held_b, across)
        totals = (
            jnp.where((group == 0) | (group == 2), across, total_a),
            jnp.where(group <= 1, down, total_b),
        )
        if n < count - 1:
            branch_grad, block_out, picks = relay_first(
                rows, gate, (branch_a, branch_b), block_out, totals, spots[n], spots[n + 1]
            )
            first_row = piece.shape[0]
            continue
        base, block_out = block_out, None
        ends = ((held_a, down, total_b), (held_b, across, total_a))
        for part in (1, 0):
            held, got, total = ends[part]
            branch_grad, block_out = relay_last(
                picks, gate, held, got, base, total, part, first_row, branch_grad, block_out
            )
    return (block_out[None, None], branch_grad[None])


def solution(mesh):
    placed = (
        P("rep", "grp", "seq", None),
        P("rep", "grp", "seq", None),
        P("rep", "grp", "seq", None),
        P("rep", "grp", "seq"),
        P("rep", "grp", "seq"),
        P("rep"),
        P("rep", "grp", "seq", None),
    )
    return jax.shard_map(
        local,
        mesh=mesh,
        in_specs=placed,
        out_specs=(P("rep", "grp", "seq", None), P("rep", "seq", None)),
        check_vma=False,
    )
```

```python
import functools
import math

import jax
import jax.numpy as jnp
from jax import lax
from jax.experimental import pallas as pl
from jax.experimental.pallas import tpu as pltpu
from jax.sharding import PartitionSpec as P

HEADS = 32
DH = 80
FRAMES = 20
LANES = 128
VMEM_LIMIT = 32 * 1024 * 1024
PACK_LIMIT = 53 * 1024 * 1024


def shifted(block, axis, distance):
    devices = range(lax.axis_size(axis))
    route = [(i - distance, i) for i in devices if i - distance in devices]
    return lax.ppermute(block, axis, route)


def paired(block, axis, first):
    size = lax.axis_size(axis)
    route = []
    for i in range(size):
        other = i + 1 if (i - first) % 2 == 0 else i - 1
        if 0 <= other < size:
            route.append((i, other))
    return lax.ppermute(block, axis, route)


def lane_windows(heads):
    windows = []
    for head in range(heads):
        first, last = head * DH, (head + 1) * DH
        if windows and last <= windows[-1][0] + 2 * LANES:
            windows[-1][1].append(head)
        else:
            windows.append((first // LANES * LANES, [head]))
    out = []
    for start, members in windows:
        start = min(start, heads * DH - 2 * LANES)
        out.append((start, members))
    return out


def head_masks(rows, period):
    masks = {}
    for start, members in lane_windows(period // DH):
        lane = lax.broadcasted_iota(jnp.int32, (rows, 2 * LANES), 1) + start
        for h in members:
            inside = (lane >= h * DH) & (lane < (h + 1) * DH)
            masks[h] = jnp.where(inside, 1.0, 0.0).astype(jnp.bfloat16)
    return masks


def period_scores(base, query, keys, masks, period):
    scores = []
    for start, members in lane_windows(period // DH):
        lanes = slice(base + start, base + start + 2 * LANES)
        part = query(lanes)
        stacked = jnp.concatenate([part * masks[h] for h in members], axis=0)
        scores.append(
            [
                lax.dot_general(
                    stacked, key(lanes), (((1,), (1,)), ((), ())), preferred_element_type=jnp.float32
                )
                for key in keys
            ]
        )
    return scores


def mixed_period(base, scores, sets, period):
    rows = sets[0][0].shape[0]
    factor = math.log2(math.e) / math.sqrt(DH)
    windows = lane_windows(period // DH)
    weights = []
    for parts, (start, members) in zip(scores, windows):
        parts = [
            part.reshape(len(members), rows, -1) + bias[None]
            for part, (bias, value) in zip(parts, sets)
        ]
        largest = row_max(parts)
        weights.append(
            [
                jnp.exp2((part - largest) * factor).astype(jnp.bfloat16).reshape(len(members) * rows, -1)
                for part in parts
            ]
        )
    tiles = {}
    for parts, (start, members) in zip(weights, windows):
        lanes = slice(base + start, base + start + 2 * LANES)
        mixed = sum(
            jnp.dot(part, value(lanes), preferred_element_type=jnp.float32)
            for part, (bias, value) in zip(parts, sets)
        )
        totals = sum(
            jnp.dot(part, jnp.ones((part.shape[1], LANES), part.dtype), preferred_element_type=jnp.float32)
            for part in parts
        )
        scale = 1.0 / totals
        for n, h in enumerate(members):
            for t in range(2):
                low = start + t * LANES
                if h * DH >= low + LANES or (h + 1) * DH <= low:
                    continue
                mine = slice(n * rows, (n + 1) * rows)
                piece = mixed[mine, t * LANES : (t + 1) * LANES] * scale[mine]
                if low in tiles:
                    lane = lax.broadcasted_iota(jnp.int32, (rows, LANES), 1) + low
                    tiles[low] = jnp.where(lane >= h * DH, piece, tiles[low])
                else:
                    tiles[low] = piece
    return {low: tile.astype(jnp.bfloat16) for low, tile in tiles.items()}


def row_max(parts):
    if all(part.shape == parts[0].shape for part in parts):
        return jnp.max(functools.reduce(jnp.maximum, parts), axis=-1, keepdims=True)
    return functools.reduce(jnp.maximum, [jnp.max(part, axis=-1, keepdims=True) for part in parts])


def columns(row):
    return jnp.broadcast_to(row, (LANES, row.shape[1])).T


def link_bias(mine, theirs):
    return jnp.where(jnp.abs(mine[:, :1] - theirs.T[: mine.shape[0]]) <= 1.5, 0.0, -1e30)


def store_period(base, tiles, out_ref):
    for low, tile in tiles.items():
        out_ref[:, base + low : base + low + LANES] = tile


def ends_kernel(k_ref, v_ref, code_ref, *end_refs):
    even = lax.axis_index("seq") % 2 == 0
    tokens, width = k_ref.shape
    code = columns(code_ref[...])
    for n, ref in enumerate(end_refs):
        most = ref.shape[0]
        tail = even if n == 0 else jnp.logical_not(even)
        first = pl.multiple_of(jnp.where(tail, tokens - most, 0), most)
        ref[:, :width] = k_ref[pl.ds(first, most), :]
        ref[:, width : 2 * width] = v_ref[pl.ds(first, most), :]
        here = jnp.where(tail, code[tokens - most :], code[:most])
        ref[:, 2 * width :] = here.astype(jnp.bfloat16)


def middle_kernel(reach, q_ref, k_ref, v_ref, code_ref, out_ref):
    rows = out_ref.shape[0]
    code = columns(code_ref[...])
    bias = link_bias(code[reach : reach + rows], code)
    period = math.lcm(DH, LANES)
    masks = head_masks(rows, period)
    query = lambda lanes: q_ref[reach : reach + rows, lanes]
    for base in range(0, out_ref.shape[1], period):
        scores = period_scores(base, query, [lambda lanes: k_ref[:, lanes]], masks, period)
        sets = [(bias, lambda lanes: v_ref[:, lanes])]
        store_period(base, mixed_period(base, scores, sets, period), out_ref)


def sides_kernel(reach, q_ref, k_ref, v_ref, code_ref, two_ref, one_ref, *refs):
    out_ref, keys, values, codes = refs
    tokens, width = q_ref.shape
    near = 2 * reach
    code = columns(code_ref[...])
    even = lax.axis_index("seq") % 2 == 0
    period = math.lcm(DH, LANES)
    masks = head_masks(reach, period)
    blocks = []
    for side, first in ((0, 0), (1, tokens - near)):
        own = slice(first, first + near)
        use_two = even if side == 0 else jnp.logical_not(even)
        halo = jnp.where(use_two, two_ref[...], one_ref[...])
        keys[side, :near] = k_ref[own]
        values[side, :near] = v_ref[own]
        codes[side, :near] = code[own]
        keys[side, near : near + reach] = halo[:, :width]
        values[side, near : near + reach] = halo[:, width : 2 * width]
        codes[side, near : near + reach] = halo[:, 2 * width :].astype(jnp.float32)
        spare = keys.shape[1] - near - reach
        if spare:
            for ref in (keys, values, codes):
                ref[side, near + reach :] = jnp.zeros((spare, ref.shape[2]), ref.dtype)
        top = side * (tokens - reach)
        blocks.append((side, top, link_bias(code[top : top + reach], codes[side])))
    for base in range(0, width, period):
        scores = []
        for side, top, bias in blocks:
            query = lambda lanes: q_ref[top : top + reach, lanes]
            key = lambda lanes: keys[side, :, lanes]
            scores.append(period_scores(base, query, [key], masks, period))
        for (side, top, bias), part in zip(blocks, scores):
            sets = [(bias, lambda lanes: values[side, :, lanes])]
            tiles = mixed_period(base, part, sets, period)
            store_period(base, tiles, out_ref.at[side * reach : (side + 1) * reach])


def edge_kernel(reach, q_ref, k_ref, v_ref, code_ref, *refs):
    halos = refs[:-4]
    out_ref, keys, values, codes = refs[-4:]
    width = q_ref.shape[1]
    code = columns(code_ref[...])
    at = 0
    for piece in halos:
        rows = piece.shape[0]
        keys[at : at + rows] = piece[:, :width]
        values[at : at + rows] = piece[:, width : 2 * width]
        codes[at : at + rows] = piece[:, 2 * width :].astype(jnp.float32)
        at += rows
    if at < keys.shape[0]:
        for ref in (keys, values, codes):
            ref[at:] = jnp.zeros((ref.shape[0] - at, ref.shape[1]), ref.dtype)
    period = math.lcm(DH, LANES)
    masks = head_masks(q_ref.shape[0], period)
    query = lambda lanes: q_ref[:, lanes]
    pair = [lambda lanes: k_ref[:, lanes], lambda lanes: keys[:, lanes]]
    sets = [
        (link_bias(code, code), lambda lanes: v_ref[:, lanes]),
        (link_bias(code, codes[...]), lambda lanes: values[:, lanes]),
    ]
    for base in range(0, width, period):
        scores = period_scores(base, query, pair, masks, period)
        store_period(base, mixed_period(base, scores, sets, period), out_ref)


def attend_cost(tokens, span, width):
    return pl.CostEstimate(
        flops=HEADS * tokens * span * 2 * LANES * 4,
        bytes_accessed=12 * tokens * width,
        transcendentals=HEADS * tokens * span,
    )


VMEM = pl.BlockSpec(memory_space=pltpu.VMEM)
PARAMS = pltpu.CompilerParams(vmem_limit_bytes=VMEM_LIMIT)


def pack_ends(keys, values, code, most):
    width = keys.shape[1]
    ends = jax.ShapeDtypeStruct((most, 2 * width + LANES), jnp.bfloat16)
    return pl.pallas_call(
        ends_kernel,
        in_specs=[VMEM] * 3,
        out_specs=[VMEM] * 2,
        out_shape=[ends, ends],
        compiler_params=PARAMS,
        cost_estimate=pl.CostEstimate(flops=0, bytes_accessed=16 * most * width, transcendentals=0),
        name="pack_ends",
    )(keys, values, code)


def attend_middle(queries, keys, values, code, reach):
    tokens, width = queries.shape
    return pl.pallas_call(
        functools.partial(middle_kernel, reach),
        in_specs=[VMEM] * 4,
        out_specs=VMEM,
        out_shape=jax.ShapeDtypeStruct((tokens - 2 * reach, width), jnp.bfloat16),
        compiler_params=PARAMS,
        cost_estimate=attend_cost(tokens - 2 * reach, tokens, width),
        name="attend_middle",
    )(queries, keys, values, code)


def attend_edges(queries, keys, values, code, halos, reach):
    tokens, width = queries.shape
    rows = min(tokens, 2 * reach)
    if tokens > 2 * reach:
        kernel = sides_kernel
        held = (2, -(-3 * reach // LANES) * LANES)
    else:
        kernel = edge_kernel
        held = (-(-2 * reach // LANES) * LANES,)
    operands = [queries, keys, values, code, *halos]
    return pl.pallas_call(
        functools.partial(kernel, reach),
        in_specs=[VMEM] * len(operands),
        out_specs=VMEM,
        out_shape=jax.ShapeDtypeStruct((rows, width), jnp.bfloat16),
        scratch_shapes=[
            pltpu.VMEM((*held, width), jnp.bfloat16),
            pltpu.VMEM((*held, width), jnp.bfloat16),
            pltpu.VMEM((*held, LANES), jnp.float32),
        ],
        compiler_params=PARAMS,
        cost_estimate=attend_cost(rows, LANES, width),
        name="attend_edges",
    )(*operands)


def pack_grads_kernel(grad_ref, mark_ref, *refs):
    first_ref, second_ref, sems = refs[-3:]
    half = grad_ref.shape[1] // 2
    copies = []
    for n, ref in enumerate((first_ref, second_ref)):
        copies.append(
            pltpu.make_async_copy(
                grad_ref.at[:, pl.ds(n * half, half)], ref.at[:, pl.ds(0, half)], sems.at[n]
            )
        )
    for copy in copies:
        copy.start()
    place = columns(mark_ref[1:2]).astype(jnp.bfloat16)
    for ref in (first_ref, second_ref):
        ref[:, half:] = place
    for copy in copies:
        copy.wait()


def pack_grads(grads, marks, *others):
    tokens, width = grads.shape
    far = pl.BlockSpec(memory_space=pltpu.HBM)
    return pl.pallas_call(
        pack_grads_kernel,
        in_specs=[far, VMEM] + [far] * len(others),
        out_specs=[VMEM] * 2,
        out_shape=[jax.ShapeDtypeStruct((tokens, width // 2 + LANES), jnp.bfloat16)] * 2,
        scratch_shapes=[pltpu.SemaphoreType.DMA((2,))],
        compiler_params=pltpu.CompilerParams(vmem_limit_bytes=PACK_LIMIT),
        cost_estimate=pl.CostEstimate(flops=0, bytes_accessed=4 * tokens * width, transcendentals=0),
        name="pack_grads",
    )(grads, marks, *others)


def selector(row):
    tokens = row.shape[1]
    wanted = lax.broadcasted_iota(jnp.int32, (tokens, tokens), 0).astype(jnp.float32)
    return jnp.where(wanted == row, 1.0, 0.0)


def sums_kernel(part, sizes, gate_ref, row_ref, mine_ref, theirs_ref, *out_refs):
    half = gate_ref.shape[1] // 2
    place = theirs_ref[:, half:].astype(jnp.float32).T[:1]
    picks = [selector(row).astype(jnp.bfloat16) for row in (row_ref[...], place)]
    theirs = theirs_ref[:, :half]
    summed = jnp.dot(
        jnp.concatenate(picks, axis=1),
        jnp.concatenate((mine_ref[:, :half], theirs), axis=0),
        preferred_element_type=jnp.float32,
    )
    own = jnp.where(lax.axis_index("grp") == part + 1, 1.0, 0.0)
    term = gate_ref[:, part * half : (part + 1) * half] * summed + own * theirs.astype(jnp.float32)
    term = term.astype(jnp.bfloat16)
    at = 0
    for ref, size in zip(out_refs, sizes):
        ref[...] = term[at : at + size]
        at += size


def pair_sums(part, gate, rows, mine, theirs, sizes):
    tokens, half = mine.shape[0], gate.shape[1] // 2
    return pl.pallas_call(
        functools.partial(sums_kernel, part, sizes),
        in_specs=[VMEM] * 4,
        out_specs=[VMEM] * len(sizes),
        out_shape=[jax.ShapeDtypeStruct((size, half), jnp.bfloat16) for size in sizes],
        compiler_params=PARAMS,
        cost_estimate=pl.CostEstimate(
            flops=4 * tokens * tokens * half, bytes_accessed=6 * tokens * half, transcendentals=0
        ),
        name="pair_sums",
    )(gate, rows, mine, theirs)


def piece_spots(tokens, reach, piece):
    if tokens <= 2 * reach:
        return [(0, tokens, 0)]
    if piece == 0:
        return [(reach, tokens - 2 * reach, 0)]
    return [(0, reach, 0), (tokens - reach, reach, reach)]


def picked(spots, row_ref):
    picks = selector(row_ref[...]).T.astype(jnp.bfloat16)
    return jnp.concatenate([picks[:, top : top + size] for top, size, at in spots], axis=1)


def relay_first_kernel(
    spots, later, row_ref, gate_ref, a_ref, b_ref, base_ref, c_ref, d_ref, grad_ref, out_ref, picks_ref, sems
):
    half = a_ref.shape[1]
    copies = []
    for n, ref in enumerate((c_ref, d_ref)):
        to = grad_ref.at[pl.ds(0, ref.shape[0]), pl.ds(n * half, half)]
        copies.append(pltpu.make_async_copy(ref, to, sems.at[n]))
    for copy in copies:
        copy.start()
    picks = picked(spots, row_ref)
    for n, ref in enumerate((a_ref, b_ref)):
        lanes = slice(n * half, (n + 1) * half)
        relayed = jnp.dot(picks, ref[...], preferred_element_type=jnp.float32)
        out_ref[:, lanes] = base_ref[:, lanes].astype(jnp.float32) + gate_ref[:, lanes] * relayed
    picks_ref[...] = picked(later, row_ref)
    for copy in copies:
        copy.wait()


def relay_first(rows, gate, branch, base, totals, spots, later):
    tokens, width = base.shape
    return pl.pallas_call(
        functools.partial(relay_first_kernel, spots, later),
        in_specs=[VMEM] * 7,
        out_specs=[pl.BlockSpec(memory_space=pltpu.HBM), VMEM, VMEM],
        out_shape=[
            jax.ShapeDtypeStruct((tokens, width), jnp.bfloat16),
            jax.ShapeDtypeStruct((tokens, width), jnp.float32),
            jax.ShapeDtypeStruct((tokens, sum(size for top, size, at in later)), jnp.bfloat16),
        ],
        scratch_shapes=[pltpu.SemaphoreType.DMA((2,))],
        compiler_params=PARAMS,
        cost_estimate=pl.CostEstimate(
            flops=2 * tokens * tokens * width, bytes_accessed=24 * tokens * width, transcendentals=0
        ),
        name="relay_first",
    )(rows, gate, *branch, base, *totals)


def relay_last_kernel(
    part, chunks, first_row, picks_ref, gate_ref, held_ref, got_ref, base_ref, total_ref, *refs
):
    grad_ref, out_ref, staged, summed, sems, grad_sem = refs[-6:]
    half = held_ref.shape[1]
    other = 1 - part
    group = lax.axis_index("grp")
    holds = group <= 1 if part == 0 else group % 2 == 0
    summed[...] = jnp.where(holds, got_ref[...], total_ref[...])
    to = grad_ref.at[pl.ds(first_row, total_ref.shape[0]), pl.ds(other * half, half)]
    copies = [pltpu.make_async_copy(summed, to, grad_sem)]
    copies[0].start()
    step = half // chunks
    for c in range(chunks):
        mine = slice(c * step, (c + 1) * step)
        lanes = slice(part * half + c * step, part * half + (c + 1) * step)
        branch = jnp.where(holds, held_ref[:, mine], got_ref[:, mine])
        relayed = jnp.dot(picks_ref[...], branch, preferred_element_type=jnp.float32)
        total = base_ref[:, lanes].astype(jnp.float32) + gate_ref[:, lanes] * relayed
        staged[:, mine] = total.astype(staged.dtype)
        copies.append(
            pltpu.make_async_copy(
                staged.at[:, pl.ds(c * step, step)],
                out_ref.at[:, pl.ds(part * half + c * step, step)],
                sems.at[c],
            )
        )
        copies[-1].start()
    for copy in copies:
        copy.wait()


def relay_last(picks, gate, held, got, base, total, part, first_row, grads, out):
    tokens, width = base.shape
    chunks = 2 if width // 2 % (2 * LANES) == 0 else 1
    far = pl.BlockSpec(memory_space=pltpu.HBM)
    operands = [picks, gate, held, got, base, total]
    aliases = {}
    for n, buffer in enumerate((grads, out)):
        if buffer is not None:
            aliases[len(operands)] = n
            operands.append(buffer)
    return pl.pallas_call(
        functools.partial(relay_last_kernel, part, chunks, first_row),
        in_specs=[VMEM] * 6 + [far] * len(aliases),
        out_specs=[far] * 2,
        out_shape=[jax.ShapeDtypeStruct((tokens, width), jnp.bfloat16)] * 2,
        input_output_aliases=aliases,
        scratch_shapes=[
            pltpu.VMEM((tokens, width // 2), jnp.bfloat16),
            pltpu.VMEM(total.shape, jnp.bfloat16),
            pltpu.SemaphoreType.DMA((chunks,)),
            pltpu.SemaphoreType.DMA,
        ],
        compiler_params=PARAMS,
        cost_estimate=pl.CostEstimate(
            flops=tokens * tokens * width, bytes_accessed=6 * tokens * width, transcendentals=0
        ),
        name="relay_last",
    )(*operands)


def whole_gate(gate):
    ranks = lax.axis_size("rep")
    if ranks != 2:
        return lax.all_gather(gate, "rep", axis=0, tiled=True)
    other = lax.ppermute(gate, "rep", [(0, 1), (1, 0)])
    first = lax.axis_index("rep") == 0
    return jnp.concatenate([jnp.where(first, gate, other), jnp.where(first, other, gate)])


SWAP_X, SWAP_Y = [(0, 1), (1, 0), (2, 3), (3, 2)], [(0, 2), (2, 0), (1, 3), (3, 1)]
ROUND_A, ROUND_B = [(0, 1), (1, 3), (3, 2), (2, 0)], [(0, 2), (2, 3), (3, 1), (1, 0)]


def added(a, b):
    return (a.astype(jnp.float32) + b.astype(jnp.float32)).astype(a.dtype)


def local(query_rows, key_rows, value_rows, view_frame, control_row, control_gate, out_grad):
    queries, keys, values = query_rows[0, 0], key_rows[0, 0], value_rows[0, 0]
    tokens, width = queries.shape
    half = width // 2
    ranks = lax.axis_size("seq")
    reach = 2 * (tokens * ranks // 32)
    hops = (reach + tokens - 1) // tokens
    group, rank = lax.axis_index("grp"), lax.axis_index("seq")
    send = lambda block, route: lax.ppermute(block, "grp", route)

    tag = view_frame[0, 0]
    code = tag + 8 * (tag // FRAMES) + 16
    marks = jnp.stack((code, control_row[0, 0] % tokens)).astype(jnp.float32)
    code, rows = marks[:1], marks[1:]
    most = min(tokens, reach)
    even = rank % 2 == 0
    sent_a, sent_b = pack_grads(out_grad[0, 0], marks, queries, keys, values)
    code, sent_a, sent_b = lax.optimization_barrier((code, sent_a, sent_b))
    got_a, got_b = send(sent_a, SWAP_X), send(sent_b, SWAP_Y)
    end_one, end_two = pack_ends(keys, values, code, most)
    code, end_one, end_two = lax.optimization_barrier((code, end_one, end_two))
    own = [attend_middle(queries, keys, values, code, reach)] if tokens > 2 * reach else []
    gate = whole_gate(control_gate)[None]
    inner = paired(end_two, "seq", 1)
    halos = [inner, paired(end_one, "seq", 0)]
    for hop in range(2, hops + 1):
        count = min(tokens, reach - (hop - 1) * tokens)
        tail, head = jnp.where(even, end_one, end_two), jnp.where(even, end_two, end_one)
        halos.append(shifted(tail[most - count :], "seq", hop))
        halos.append(shifted(head[:count], "seq", -hop))
    sizes = [piece.shape[0] for piece in own] + [min(tokens, 2 * reach)]
    sums = [
        *pair_sums(0, gate, rows, sent_a, got_a, sizes),
        *pair_sums(1, gate, rows, sent_b, got_b, sizes),
    ]
    count = len(sizes)

    def outgoing(piece, sum_a, sum_b):
        to_a = jnp.where(group == 0, piece[:, :half], jnp.where(group == 1, sum_a, sum_b))
        to_b = jnp.where(group == 0, piece[:, half:], jnp.where(group == 2, sum_b, sum_a))
        return to_a, to_b

    going = [outgoing(own[0], sums[0], sums[count])] if own else []
    code, *ready = lax.optimization_barrier((code, *sums, *(going[0] if going else ())))
    sums = ready[: 2 * count]
    if going:
        going = [ready[2 * count :]]
    own.append(attend_edges(queries, keys, values, code, halos, reach))

    going.append(outgoing(own[-1], sums[count - 1], sums[2 * count - 1]))
    spots = [piece_spots(tokens, reach, n) for n in range(count)]
    order = [
        own[n][at : at + size] for top, size, n, at in sorted(
            (top, size, n, at) for n in range(count) for top, size, at in spots[n]
        )
    ]
    block_out = jnp.concatenate(order, axis=0)
    branch_grad, first_row = None, 0
    picks = (rows[0][:, None] == jnp.arange(tokens)).astype(jnp.bfloat16) if count == 1 else None
    for n, (piece, sum_a, sum_b) in enumerate(zip(own, sums[:count], sums[count:])):
        piece_a, piece_b = piece[:, :half], piece[:, half:]
        one, two = send(going[n][0], ROUND_A), send(going[n][1], ROUND_B)
        total_a = added(sum_a, jnp.where(group == 1, two, one))
        total_b = added(sum_b, jnp.where(group == 2, one, two))
        held_a = jnp.where(group == 0, piece_a, one)
        held_b = jnp.where(group == 0, piece_b, two)
        across = send(jnp.where((group == 0) | (group == 2), held_b, total_a), SWAP_X)
        down = send(jnp.where(group <= 1, held_a, total_b), SWAP_Y)
        branch_a = jnp.where(group <= 1, held_a, down)
        branch_b = jnp.where((group == 0) | (group == 2), held_b, across)
        totals = (
            jnp.where((group == 0) | (group == 2), across, total_a),
            jnp.where(group <= 1, down, total_b),
        )
        if n < count - 1:
            branch_grad, block_out, picks = relay_first(
                rows, gate, (branch_a, branch_b), block_out, totals, spots[n], spots[n + 1]
            )
            first_row = piece.shape[0]
            continue
        base, block_out = block_out, None
        ends = ((held_a, down, total_b), (held_b, across, total_a))
        for part in (1, 0):
            held, got, total = ends[part]
            branch_grad, block_out = relay_last(
                picks, gate, held, got, base, total, part, first_row, branch_grad, block_out
            )
    return (block_out[None, None], branch_grad[None])


def solution(mesh):
    placed = (
        P("rep", "grp", "seq", None),
        P("rep", "grp", "seq", None),
        P("rep", "grp", "seq", None),
        P("rep", "grp", "seq"),
        P("rep", "grp", "seq"),
        P("rep"),
        P("rep", "grp", "seq", None),
    )
    return jax.shard_map(
        local,
        mesh=mesh,
        in_specs=placed,
        out_specs=(P("rep", "grp", "seq", None), P("rep", "seq", None)),
        check_vma=False,
    )
```

```python
import functools
import math

import jax
import jax.numpy as jnp
from jax import lax
from jax.experimental import pallas as pl
from jax.experimental.pallas import tpu as pltpu
from jax.sharding import PartitionSpec as P

HEADS = 32
DH = 80
FRAMES = 20
LANES = 128
VMEM_LIMIT = 32 * 1024 * 1024
PACK_LIMIT = 53 * 1024 * 1024


def shifted(block, axis, distance):
    devices = range(lax.axis_size(axis))
    route = [(i - distance, i) for i in devices if i - distance in devices]
    return lax.ppermute(block, axis, route)


def paired(block, axis, first):
    size = lax.axis_size(axis)
    route = []
    for i in range(size):
        other = i + 1 if (i - first) % 2 == 0 else i - 1
        if 0 <= other < size:
            route.append((i, other))
    return lax.ppermute(block, axis, route)


def lane_windows(heads):
    windows = []
    for head in range(heads):
        first, last = head * DH, (head + 1) * DH
        if windows and last <= windows[-1][0] + 2 * LANES:
            windows[-1][1].append(head)
        else:
            windows.append((first // LANES * LANES, [head]))
    out = []
    for start, members in windows:
        start = min(start, heads * DH - 2 * LANES)
        out.append((start, members))
    return out


def head_masks(rows, period):
    masks = {}
    for start, members in lane_windows(period // DH):
        lane = lax.broadcasted_iota(jnp.int32, (rows, 2 * LANES), 1) + start
        for h in members:
            inside = (lane >= h * DH) & (lane < (h + 1) * DH)
            masks[h] = jnp.where(inside, 1.0, 0.0).astype(jnp.bfloat16)
    return masks


def period_scores(base, query, keys, masks, period):
    scores = []
    for start, members in lane_windows(period // DH):
        lanes = slice(base + start, base + start + 2 * LANES)
        part = query(lanes)
        stacked = jnp.concatenate([part * masks[h] for h in members], axis=0)
        scores.append(
            [
                lax.dot_general(
                    stacked, key(lanes), (((1,), (1,)), ((), ())), preferred_element_type=jnp.float32
                )
                for key in keys
            ]
        )
    return scores


def mixed_period(base, scores, sets, period):
    rows = sets[0][0].shape[0]
    factor = math.log2(math.e) / math.sqrt(DH)
    windows = lane_windows(period // DH)
    weights = []
    for parts, (start, members) in zip(scores, windows):
        parts = [
            part.reshape(len(members), rows, -1) + bias[None]
            for part, (bias, value) in zip(parts, sets)
        ]
        largest = row_max(parts)
        weights.append(
            [
                jnp.exp2((part - largest) * factor).astype(jnp.bfloat16).reshape(len(members) * rows, -1)
                for part in parts
            ]
        )
    tiles = {}
    for parts, (start, members) in zip(weights, windows):
        lanes = slice(base + start, base + start + 2 * LANES)
        mixed = sum(
            jnp.dot(part, value(lanes), preferred_element_type=jnp.float32)
            for part, (bias, value) in zip(parts, sets)
        )
        totals = sum(
            jnp.dot(part, jnp.ones((part.shape[1], LANES), part.dtype), preferred_element_type=jnp.float32)
            for part in parts
        )
        scale = 1.0 / totals
        for n, h in enumerate(members):
            for t in range(2):
                low = start + t * LANES
                if h * DH >= low + LANES or (h + 1) * DH <= low:
                    continue
                mine = slice(n * rows, (n + 1) * rows)
                piece = mixed[mine, t * LANES : (t + 1) * LANES] * scale[mine]
                if low in tiles:
                    lane = lax.broadcasted_iota(jnp.int32, (rows, LANES), 1) + low
                    tiles[low] = jnp.where(lane >= h * DH, piece, tiles[low])
                else:
                    tiles[low] = piece
    return {low: tile.astype(jnp.bfloat16) for low, tile in tiles.items()}


def row_max(parts):
    if all(part.shape == parts[0].shape for part in parts):
        return jnp.max(functools.reduce(jnp.maximum, parts), axis=-1, keepdims=True)
    return functools.reduce(jnp.maximum, [jnp.max(part, axis=-1, keepdims=True) for part in parts])


def columns(row):
    return jnp.broadcast_to(row, (LANES, row.shape[1])).T


def link_bias(mine, theirs):
    return jnp.where(jnp.abs(mine[:, :1] - theirs.T[: mine.shape[0]]) <= 1.5, 0.0, -1e30)


def store_period(base, tiles, out_ref):
    for low, tile in tiles.items():
        out_ref[:, base + low : base + low + LANES] = tile


def ends_kernel(k_ref, v_ref, code_ref, *end_refs):
    even = lax.axis_index("seq") % 2 == 0
    tokens, width = k_ref.shape
    code = columns(code_ref[...])
    for n, ref in enumerate(end_refs):
        most = ref.shape[0]
        tail = even if n == 0 else jnp.logical_not(even)
        first = pl.multiple_of(jnp.where(tail, tokens - most, 0), most)
        ref[:, :width] = k_ref[pl.ds(first, most), :]
        ref[:, width : 2 * width] = v_ref[pl.ds(first, most), :]
        here = jnp.where(tail, code[tokens - most :], code[:most])
        ref[:, 2 * width :] = here.astype(jnp.bfloat16)


def middle_kernel(reach, q_ref, k_ref, v_ref, code_ref, out_ref):
    rows = out_ref.shape[0]
    code = columns(code_ref[...])
    bias = link_bias(code[reach : reach + rows], code)
    period = math.lcm(DH, LANES)
    masks = head_masks(rows, period)
    query = lambda lanes: q_ref[reach : reach + rows, lanes]
    for base in range(0, out_ref.shape[1], period):
        scores = period_scores(base, query, [lambda lanes: k_ref[:, lanes]], masks, period)
        sets = [(bias, lambda lanes: v_ref[:, lanes])]
        store_period(base, mixed_period(base, scores, sets, period), out_ref)


def sides_kernel(reach, q_ref, k_ref, v_ref, code_ref, one_ref, two_ref, *refs):
    out_ref, keys, values, codes, one, two, sems = refs
    copies = [
        pltpu.make_async_copy(one_ref, one, sems.at[0]),
        pltpu.make_async_copy(two_ref, two, sems.at[1]),
    ]
    for copy in copies:
        copy.start()
    tokens, width = q_ref.shape
    near = 2 * reach
    code = columns(code_ref[...])
    even = lax.axis_index("seq") % 2 == 0
    period = math.lcm(DH, LANES)
    masks = head_masks(reach, period)
    spare = keys.shape[1] - near - reach
    sides = ((0, 0, 0), (1, tokens - near, tokens - reach))
    for side, first, top in sides:
        own = slice(first, first + near)
        keys[side, :near] = k_ref[own]
        values[side, :near] = v_ref[own]
        codes[side, :near] = code[own]
        if spare:
            for ref in (keys, values, codes):
                ref[side, near + reach :] = jnp.zeros((spare, ref.shape[2]), ref.dtype)
    for copy in copies:
        copy.wait()
    blocks = []
    for side, first, top in sides:
        use_two = even if side == 0 else jnp.logical_not(even)
        halo = jnp.where(use_two, two[...], one[...])
        keys[side, near : near + reach] = halo[:, :width]
        values[side, near : near + reach] = halo[:, width : 2 * width]
        codes[side, near : near + reach] = halo[:, 2 * width :].astype(jnp.float32)
        blocks.append((side, top, link_bias(code[top : top + reach], codes[side])))
    for base in range(0, width, period):
        scores = []
        for side, top, bias in blocks:
            query = lambda lanes: q_ref[top : top + reach, lanes]
            key = lambda lanes: keys[side, :, lanes]
            scores.append(period_scores(base, query, [key], masks, period))
        for (side, top, bias), part in zip(blocks, scores):
            sets = [(bias, lambda lanes: values[side, :, lanes])]
            tiles = mixed_period(base, part, sets, period)
            store_period(base, tiles, out_ref.at[side * reach : (side + 1) * reach])


def edge_kernel(reach, q_ref, k_ref, v_ref, code_ref, *refs):
    halos = refs[:-4]
    out_ref, keys, values, codes = refs[-4:]
    width = q_ref.shape[1]
    code = columns(code_ref[...])
    at = 0
    for piece in halos:
        rows = piece.shape[0]
        keys[at : at + rows] = piece[:, :width]
        values[at : at + rows] = piece[:, width : 2 * width]
        codes[at : at + rows] = piece[:, 2 * width :].astype(jnp.float32)
        at += rows
    if at < keys.shape[0]:
        for ref in (keys, values, codes):
            ref[at:] = jnp.zeros((ref.shape[0] - at, ref.shape[1]), ref.dtype)
    period = math.lcm(DH, LANES)
    masks = head_masks(q_ref.shape[0], period)
    query = lambda lanes: q_ref[:, lanes]
    pair = [lambda lanes: k_ref[:, lanes], lambda lanes: keys[:, lanes]]
    sets = [
        (link_bias(code, code), lambda lanes: v_ref[:, lanes]),
        (link_bias(code, codes[...]), lambda lanes: values[:, lanes]),
    ]
    for base in range(0, width, period):
        scores = period_scores(base, query, pair, masks, period)
        store_period(base, mixed_period(base, scores, sets, period), out_ref)


def attend_cost(tokens, span, width):
    return pl.CostEstimate(
        flops=HEADS * tokens * span * 2 * LANES * 4,
        bytes_accessed=12 * tokens * width,
        transcendentals=HEADS * tokens * span,
    )


VMEM = pl.BlockSpec(memory_space=pltpu.VMEM)
PARAMS = pltpu.CompilerParams(vmem_limit_bytes=VMEM_LIMIT)


def pack_ends(keys, values, code, most):
    width = keys.shape[1]
    ends = jax.ShapeDtypeStruct((most, 2 * width + LANES), jnp.bfloat16)
    return pl.pallas_call(
        ends_kernel,
        in_specs=[VMEM] * 3,
        out_specs=[VMEM] * 2,
        out_shape=[ends, ends],
        compiler_params=PARAMS,
        cost_estimate=pl.CostEstimate(flops=0, bytes_accessed=16 * most * width, transcendentals=0),
        name="pack_ends",
    )(keys, values, code)


def attend_middle(queries, keys, values, code, reach):
    tokens, width = queries.shape
    return pl.pallas_call(
        functools.partial(middle_kernel, reach),
        in_specs=[VMEM] * 4,
        out_specs=VMEM,
        out_shape=jax.ShapeDtypeStruct((tokens - 2 * reach, width), jnp.bfloat16),
        compiler_params=PARAMS,
        cost_estimate=attend_cost(tokens - 2 * reach, tokens, width),
        name="attend_middle",
    )(queries, keys, values, code)


def attend_edges(queries, keys, values, code, halos, reach):
    tokens, width = queries.shape
    rows = min(tokens, 2 * reach)
    if tokens > 2 * reach:
        kernel = sides_kernel
        held = (2, -(-3 * reach // LANES) * LANES)
    else:
        kernel = edge_kernel
        held = (-(-2 * reach // LANES) * LANES,)
    operands = [queries, keys, values, code, *halos]
    far = pl.BlockSpec(memory_space=pltpu.HBM)
    landing = [pltpu.VMEM(halo.shape, jnp.bfloat16) for halo in halos[:2]]
    landing.append(pltpu.SemaphoreType.DMA((2,)))
    return pl.pallas_call(
        functools.partial(kernel, reach),
        in_specs=[VMEM] * 4 + [VMEM if kernel is edge_kernel else far] * len(halos),
        out_specs=VMEM,
        out_shape=jax.ShapeDtypeStruct((rows, width), jnp.bfloat16),
        scratch_shapes=[
            pltpu.VMEM((*held, width), jnp.bfloat16),
            pltpu.VMEM((*held, width), jnp.bfloat16),
            pltpu.VMEM((*held, LANES), jnp.float32),
        ]
        + (landing if kernel is sides_kernel else []),
        compiler_params=PARAMS,
        cost_estimate=attend_cost(rows, LANES, width),
        name="attend_edges",
    )(*operands)


def pack_grads_kernel(grad_ref, mark_ref, *refs):
    first_ref, second_ref, sems = refs[-3:]
    half = grad_ref.shape[1] // 2
    copies = []
    for n, ref in enumerate((first_ref, second_ref)):
        copies.append(
            pltpu.make_async_copy(
                grad_ref.at[:, pl.ds(n * half, half)], ref.at[:, pl.ds(0, half)], sems.at[n]
            )
        )
    for copy in copies:
        copy.start()
    place = columns(mark_ref[1:2]).astype(jnp.bfloat16)
    for ref in (first_ref, second_ref):
        ref[:, half:] = place
    for copy in copies:
        copy.wait()


def pack_grads(grads, marks, *others):
    tokens, width = grads.shape
    far = pl.BlockSpec(memory_space=pltpu.HBM)
    return pl.pallas_call(
        pack_grads_kernel,
        in_specs=[far, VMEM] + [far] * len(others),
        out_specs=[VMEM] * 2,
        out_shape=[jax.ShapeDtypeStruct((tokens, width // 2 + LANES), jnp.bfloat16)] * 2,
        scratch_shapes=[pltpu.SemaphoreType.DMA((2,))],
        compiler_params=pltpu.CompilerParams(vmem_limit_bytes=PACK_LIMIT),
        cost_estimate=pl.CostEstimate(flops=0, bytes_accessed=4 * tokens * width, transcendentals=0),
        name="pack_grads",
    )(grads, marks, *others)


def selector(row):
    tokens = row.shape[1]
    wanted = lax.broadcasted_iota(jnp.int32, (tokens, tokens), 0).astype(jnp.float32)
    return jnp.where(wanted == row, 1.0, 0.0)


def sums_kernel(part, sizes, gate_ref, row_ref, mine_ref, theirs_ref, *out_refs):
    half = gate_ref.shape[1] // 2
    place = theirs_ref[:, half:].astype(jnp.float32).T[:1]
    picks = [selector(row).astype(jnp.bfloat16) for row in (row_ref[...], place)]
    theirs = theirs_ref[:, :half]
    summed = jnp.dot(
        jnp.concatenate(picks, axis=1),
        jnp.concatenate((mine_ref[:, :half], theirs), axis=0),
        preferred_element_type=jnp.float32,
    )
    own = jnp.where(lax.axis_index("grp") == part + 1, 1.0, 0.0)
    term = gate_ref[:, part * half : (part + 1) * half] * summed + own * theirs.astype(jnp.float32)
    term = term.astype(jnp.bfloat16)
    at = 0
    for ref, size in zip(out_refs, sizes):
        ref[...] = term[at : at + size]
        at += size


def pair_sums(part, gate, rows, mine, theirs, sizes):
    tokens, half = mine.shape[0], gate.shape[1] // 2
    return pl.pallas_call(
        functools.partial(sums_kernel, part, sizes),
        in_specs=[VMEM] * 4,
        out_specs=[VMEM] * len(sizes),
        out_shape=[jax.ShapeDtypeStruct((size, half), jnp.bfloat16) for size in sizes],
        compiler_params=PARAMS,
        cost_estimate=pl.CostEstimate(
            flops=4 * tokens * tokens * half, bytes_accessed=6 * tokens * half, transcendentals=0
        ),
        name="pair_sums",
    )(gate, rows, mine, theirs)


def piece_spots(tokens, reach, piece):
    if tokens <= 2 * reach:
        return [(0, tokens, 0)]
    if piece == 0:
        return [(reach, tokens - 2 * reach, 0)]
    return [(0, reach, 0), (tokens - reach, reach, reach)]


def picked(spots, row_ref):
    picks = selector(row_ref[...]).T.astype(jnp.bfloat16)
    return jnp.concatenate([picks[:, top : top + size] for top, size, at in spots], axis=1)


def relay_first_kernel(
    spots, later, row_ref, gate_ref, a_ref, b_ref, base_ref, c_ref, d_ref, grad_ref, out_ref, picks_ref, sems
):
    half = a_ref.shape[1]
    copies = []
    for n, ref in enumerate((c_ref, d_ref)):
        to = grad_ref.at[pl.ds(0, ref.shape[0]), pl.ds(n * half, half)]
        copies.append(pltpu.make_async_copy(ref, to, sems.at[n]))
    for copy in copies:
        copy.start()
    picks = picked(spots, row_ref)
    for n, ref in enumerate((a_ref, b_ref)):
        lanes = slice(n * half, (n + 1) * half)
        relayed = jnp.dot(picks, ref[...], preferred_element_type=jnp.float32)
        out_ref[:, lanes] = base_ref[:, lanes].astype(jnp.float32) + gate_ref[:, lanes] * relayed
    picks_ref[...] = picked(later, row_ref)
    for copy in copies:
        copy.wait()


def relay_first(rows, gate, branch, base, totals, spots, later):
    tokens, width = base.shape
    return pl.pallas_call(
        functools.partial(relay_first_kernel, spots, later),
        in_specs=[VMEM] * 7,
        out_specs=[pl.BlockSpec(memory_space=pltpu.HBM), VMEM, VMEM],
        out_shape=[
            jax.ShapeDtypeStruct((tokens, width), jnp.bfloat16),
            jax.ShapeDtypeStruct((tokens, width), jnp.float32),
            jax.ShapeDtypeStruct((tokens, sum(size for top, size, at in later)), jnp.bfloat16),
        ],
        scratch_shapes=[pltpu.SemaphoreType.DMA((2,))],
        compiler_params=PARAMS,
        cost_estimate=pl.CostEstimate(
            flops=2 * tokens * tokens * width, bytes_accessed=24 * tokens * width, transcendentals=0
        ),
        name="relay_first",
    )(rows, gate, *branch, base, *totals)


def relay_last_kernel(
    part, chunks, first_row, picks_ref, gate_ref, held_ref, got_ref, base_ref, total_ref, *refs
):
    grad_ref, out_ref, staged, summed, sems, grad_sem = refs[-6:]
    half = held_ref.shape[1]
    other = 1 - part
    group = lax.axis_index("grp")
    holds = group <= 1 if part == 0 else group % 2 == 0
    summed[...] = jnp.where(holds, got_ref[...], total_ref[...])
    to = grad_ref.at[pl.ds(first_row, total_ref.shape[0]), pl.ds(other * half, half)]
    copies = [pltpu.make_async_copy(summed, to, grad_sem)]
    copies[0].start()
    step = half // chunks
    for c in range(chunks):
        mine = slice(c * step, (c + 1) * step)
        lanes = slice(part * half + c * step, part * half + (c + 1) * step)
        branch = jnp.where(holds, held_ref[:, mine], got_ref[:, mine])
        relayed = jnp.dot(picks_ref[...], branch, preferred_element_type=jnp.float32)
        total = base_ref[:, lanes].astype(jnp.float32) + gate_ref[:, lanes] * relayed
        staged[:, mine] = total.astype(staged.dtype)
        copies.append(
            pltpu.make_async_copy(
                staged.at[:, pl.ds(c * step, step)],
                out_ref.at[:, pl.ds(part * half + c * step, step)],
                sems.at[c],
            )
        )
        copies[-1].start()
    for copy in copies:
        copy.wait()


def relay_last(picks, gate, held, got, base, total, part, first_row, grads, out):
    tokens, width = base.shape
    chunks = 2 if width // 2 % (2 * LANES) == 0 else 1
    far = pl.BlockSpec(memory_space=pltpu.HBM)
    operands = [picks, gate, held, got, base, total]
    aliases = {}
    for n, buffer in enumerate((grads, out)):
        if buffer is not None:
            aliases[len(operands)] = n
            operands.append(buffer)
    return pl.pallas_call(
        functools.partial(relay_last_kernel, part, chunks, first_row),
        in_specs=[VMEM] * 6 + [far] * len(aliases),
        out_specs=[far] * 2,
        out_shape=[jax.ShapeDtypeStruct((tokens, width), jnp.bfloat16)] * 2,
        input_output_aliases=aliases,
        scratch_shapes=[
            pltpu.VMEM((tokens, width // 2), jnp.bfloat16),
            pltpu.VMEM(total.shape, jnp.bfloat16),
            pltpu.SemaphoreType.DMA((chunks,)),
            pltpu.SemaphoreType.DMA,
        ],
        compiler_params=PARAMS,
        cost_estimate=pl.CostEstimate(
            flops=tokens * tokens * width, bytes_accessed=6 * tokens * width, transcendentals=0
        ),
        name="relay_last",
    )(*operands)


def whole_gate(gate):
    ranks = lax.axis_size("rep")
    if ranks != 2:
        return lax.all_gather(gate, "rep", axis=0, tiled=True)
    other = lax.ppermute(gate, "rep", [(0, 1), (1, 0)])
    first = lax.axis_index("rep") == 0
    return jnp.concatenate([jnp.where(first, gate, other), jnp.where(first, other, gate)])


SWAP_X, SWAP_Y = [(0, 1), (1, 0), (2, 3), (3, 2)], [(0, 2), (2, 0), (1, 3), (3, 1)]
ROUND_A, ROUND_B = [(0, 1), (1, 3), (3, 2), (2, 0)], [(0, 2), (2, 3), (3, 1), (1, 0)]


def added(a, b):
    return (a.astype(jnp.float32) + b.astype(jnp.float32)).astype(a.dtype)


def local(query_rows, key_rows, value_rows, view_frame, control_row, control_gate, out_grad):
    queries, keys, values = query_rows[0, 0], key_rows[0, 0], value_rows[0, 0]
    tokens, width = queries.shape
    half = width // 2
    ranks = lax.axis_size("seq")
    reach = 2 * (tokens * ranks // 32)
    hops = (reach + tokens - 1) // tokens
    group, rank = lax.axis_index("grp"), lax.axis_index("seq")
    send = lambda block, route: lax.ppermute(block, "grp", route)

    tag = view_frame[0, 0]
    code = tag + 8 * (tag // FRAMES) + 16
    marks = jnp.stack((code, control_row[0, 0] % tokens)).astype(jnp.float32)
    code, rows = marks[:1], marks[1:]
    most = min(tokens, reach)
    even = rank % 2 == 0
    sent_a, sent_b = pack_grads(out_grad[0, 0], marks, queries, keys, values)
    code, sent_a, sent_b = lax.optimization_barrier((code, sent_a, sent_b))
    got_a, got_b = send(sent_a, SWAP_X), send(sent_b, SWAP_Y)
    end_one, end_two = pack_ends(keys, values, code, most)
    code, end_one, end_two = lax.optimization_barrier((code, end_one, end_two))
    own = [attend_middle(queries, keys, values, code, reach)] if tokens > 2 * reach else []
    gate = whole_gate(control_gate)[None]
    halos = [paired(end_one, "seq", 0), paired(end_two, "seq", 1)]
    for hop in range(2, hops + 1):
        count = min(tokens, reach - (hop - 1) * tokens)
        tail, head = jnp.where(even, end_one, end_two), jnp.where(even, end_two, end_one)
        halos.append(shifted(tail[most - count :], "seq", hop))
        halos.append(shifted(head[:count], "seq", -hop))
    sizes = [piece.shape[0] for piece in own] + [min(tokens, 2 * reach)]
    sums = [
        *pair_sums(0, gate, rows, sent_a, got_a, sizes),
        *pair_sums(1, gate, rows, sent_b, got_b, sizes),
    ]
    count = len(sizes)

    def outgoing(piece, sum_a, sum_b):
        to_a = jnp.where(group == 0, piece[:, :half], jnp.where(group == 1, sum_a, sum_b))
        to_b = jnp.where(group == 0, piece[:, half:], jnp.where(group == 2, sum_b, sum_a))
        return to_a, to_b

    going = [outgoing(own[0], sums[0], sums[count])] if own else []
    code, *ready = lax.optimization_barrier((code, *sums, *(going[0] if going else ())))
    sums = ready[: 2 * count]
    if going:
        going = [ready[2 * count :]]
    own.append(attend_edges(queries, keys, values, code, halos, reach))

    going.append(outgoing(own[-1], sums[count - 1], sums[2 * count - 1]))
    spots = [piece_spots(tokens, reach, n) for n in range(count)]
    order = [
        own[n][at : at + size] for top, size, n, at in sorted(
            (top, size, n, at) for n in range(count) for top, size, at in spots[n]
        )
    ]
    block_out = jnp.concatenate(order, axis=0)
    branch_grad, first_row = None, 0
    picks = (rows[0][:, None] == jnp.arange(tokens)).astype(jnp.bfloat16) if count == 1 else None
    for n, (piece, sum_a, sum_b) in enumerate(zip(own, sums[:count], sums[count:])):
        piece_a, piece_b = piece[:, :half], piece[:, half:]
        one, two = send(going[n][0], ROUND_A), send(going[n][1], ROUND_B)
        total_a = added(sum_a, jnp.where(group == 1, two, one))
        total_b = added(sum_b, jnp.where(group == 2, one, two))
        held_a = jnp.where(group == 0, piece_a, one)
        held_b = jnp.where(group == 0, piece_b, two)
        across = send(jnp.where((group == 0) | (group == 2), held_b, total_a), SWAP_X)
        down = send(jnp.where(group <= 1, held_a, total_b), SWAP_Y)
        branch_a = jnp.where(group <= 1, held_a, down)
        branch_b = jnp.where((group == 0) | (group == 2), held_b, across)
        totals = (
            jnp.where((group == 0) | (group == 2), across, total_a),
            jnp.where(group <= 1, down, total_b),
        )
        if n < count - 1:
            branch_grad, block_out, picks = relay_first(
                rows, gate, (branch_a, branch_b), block_out, totals, spots[n], spots[n + 1]
            )
            first_row = piece.shape[0]
            continue
        base, block_out = block_out, None
        ends = ((held_a, down, total_b), (held_b, across, total_a))
        for part in (1, 0):
            held, got, total = ends[part]
            branch_grad, block_out = relay_last(
                picks, gate, held, got, base, total, part, first_row, branch_grad, block_out
            )
    return (block_out[None, None], branch_grad[None])


def solution(mesh):
    placed = (
        P("rep", "grp", "seq", None),
        P("rep", "grp", "seq", None),
        P("rep", "grp", "seq", None),
        P("rep", "grp", "seq"),
        P("rep", "grp", "seq"),
        P("rep"),
        P("rep", "grp", "seq", None),
    )
    return jax.shard_map(
        local,
        mesh=mesh,
        in_specs=placed,
        out_specs=(P("rep", "grp", "seq", None), P("rep", "seq", None)),
        check_vma=False,
    )
```

```python
import functools
import math

import jax
import jax.numpy as jnp
from jax import lax
from jax.experimental import pallas as pl
from jax.experimental.pallas import tpu as pltpu
from jax.sharding import PartitionSpec as P

HEADS = 32
DH = 80
FRAMES = 20
LANES = 128
VMEM_LIMIT = 32 * 1024 * 1024
PACK_LIMIT = 53 * 1024 * 1024


def shifted(block, axis, distance):
    devices = range(lax.axis_size(axis))
    route = [(i - distance, i) for i in devices if i - distance in devices]
    return lax.ppermute(block, axis, route)


def paired(block, axis, first):
    size = lax.axis_size(axis)
    route = []
    for i in range(size):
        other = i + 1 if (i - first) % 2 == 0 else i - 1
        if 0 <= other < size:
            route.append((i, other))
    return lax.ppermute(block, axis, route)


def lane_windows(heads):
    windows = []
    for head in range(heads):
        first, last = head * DH, (head + 1) * DH
        if windows and last <= windows[-1][0] + 2 * LANES:
            windows[-1][1].append(head)
        else:
            windows.append((first // LANES * LANES, [head]))
    out = []
    for start, members in windows:
        start = min(start, heads * DH - 2 * LANES)
        out.append((start, members))
    return out


def head_masks(rows, period):
    masks = {}
    for start, members in lane_windows(period // DH):
        lane = lax.broadcasted_iota(jnp.int32, (rows, 2 * LANES), 1) + start
        for h in members:
            inside = (lane >= h * DH) & (lane < (h + 1) * DH)
            masks[h] = jnp.where(inside, 1.0, 0.0).astype(jnp.bfloat16)
    return masks


def period_scores(base, query, keys, masks, period):
    scores = []
    for start, members in lane_windows(period // DH):
        lanes = slice(base + start, base + start + 2 * LANES)
        part = query(lanes)
        stacked = jnp.concatenate([part * masks[h] for h in members], axis=0)
        scores.append(
            [
                lax.dot_general(
                    stacked, key(lanes), (((1,), (1,)), ((), ())), preferred_element_type=jnp.float32
                )
                for key in keys
            ]
        )
    return scores


def mixed_period(base, scores, sets, period):
    rows = sets[0][0].shape[0]
    factor = math.log2(math.e) / math.sqrt(DH)
    windows = lane_windows(period // DH)
    weights = []
    for parts, (start, members) in zip(scores, windows):
        parts = [
            part.reshape(len(members), rows, -1) + bias[None]
            for part, (bias, value) in zip(parts, sets)
        ]
        largest = row_max(parts)
        weights.append(
            [
                jnp.exp2((part - largest) * factor).astype(jnp.bfloat16).reshape(len(members) * rows, -1)
                for part in parts
            ]
        )
    totals = 0.0
    for n in range(len(sets)):
        part = jnp.concatenate([parts[n] for parts in weights], axis=0)
        ones = jnp.ones((part.shape[1], LANES), part.dtype)
        totals += jnp.dot(part, ones, preferred_element_type=jnp.float32)
    scales = 1.0 / totals
    tiles = {}
    for parts, (start, members) in zip(weights, windows):
        lanes = slice(base + start, base + start + 2 * LANES)
        mixed = sum(
            jnp.dot(part, value(lanes), preferred_element_type=jnp.float32)
            for part, (bias, value) in zip(parts, sets)
        )
        scale = scales[members[0] * rows : (members[-1] + 1) * rows]
        for n, h in enumerate(members):
            for t in range(2):
                low = start + t * LANES
                if h * DH >= low + LANES or (h + 1) * DH <= low:
                    continue
                mine = slice(n * rows, (n + 1) * rows)
                piece = mixed[mine, t * LANES : (t + 1) * LANES] * scale[mine]
                if low in tiles:
                    lane = lax.broadcasted_iota(jnp.int32, (rows, LANES), 1) + low
                    tiles[low] = jnp.where(lane >= h * DH, piece, tiles[low])
                else:
                    tiles[low] = piece
    return {low: tile.astype(jnp.bfloat16) for low, tile in tiles.items()}


def row_max(parts):
    if all(part.shape == parts[0].shape for part in parts):
        return jnp.max(functools.reduce(jnp.maximum, parts), axis=-1, keepdims=True)
    return functools.reduce(jnp.maximum, [jnp.max(part, axis=-1, keepdims=True) for part in parts])


def columns(row):
    return jnp.broadcast_to(row, (LANES, row.shape[1])).T


def link_bias(mine, theirs):
    return jnp.where(jnp.abs(mine[:, :1] - theirs.T[: mine.shape[0]]) <= 1.5, 0.0, -1e30)


def store_period(base, tiles, out_ref):
    for low, tile in tiles.items():
        out_ref[:, base + low : base + low + LANES] = tile


def ends_kernel(k_ref, v_ref, code_ref, *end_refs):
    even = lax.axis_index("seq") % 2 == 0
    tokens, width = k_ref.shape
    code = columns(code_ref[...])
    for n, ref in enumerate(end_refs):
        most = ref.shape[0]
        tail = even if n == 0 else jnp.logical_not(even)
        first = pl.multiple_of(jnp.where(tail, tokens - most, 0), most)
        ref[:, :width] = k_ref[pl.ds(first, most), :]
        ref[:, width : 2 * width] = v_ref[pl.ds(first, most), :]
        here = jnp.where(tail, code[tokens - most :], code[:most])
        ref[:, 2 * width :] = here.astype(jnp.bfloat16)


def middle_kernel(reach, q_ref, k_ref, v_ref, code_ref, out_ref):
    rows = out_ref.shape[0]
    code = columns(code_ref[...])
    bias = link_bias(code[reach : reach + rows], code)
    period = math.lcm(DH, LANES)
    masks = head_masks(rows, period)
    query = lambda lanes: q_ref[reach : reach + rows, lanes]
    for base in range(0, out_ref.shape[1], period):
        scores = period_scores(base, query, [lambda lanes: k_ref[:, lanes]], masks, period)
        sets = [(bias, lambda lanes: v_ref[:, lanes])]
        store_period(base, mixed_period(base, scores, sets, period), out_ref)


def sides_kernel(reach, q_ref, k_ref, v_ref, code_ref, one_ref, two_ref, *refs):
    out_ref, keys, values, codes = refs
    tokens, width = q_ref.shape
    near = 2 * reach
    code = columns(code_ref[...])
    even = lax.axis_index("seq") % 2 == 0
    period = math.lcm(DH, LANES)
    masks = head_masks(reach, period)
    blocks = []
    for side, first in ((0, 0), (1, tokens - near)):
        own = slice(first, first + near)
        use_two = even if side == 0 else jnp.logical_not(even)
        halo = jnp.where(use_two, two_ref[...], one_ref[...])
        keys[side, :near] = k_ref[own]
        values[side, :near] = v_ref[own]
        codes[side, :near] = code[own]
        keys[side, near : near + reach] = halo[:, :width]
        values[side, near : near + reach] = halo[:, width : 2 * width]
        codes[side, near : near + reach] = halo[:, 2 * width :].astype(jnp.float32)
        spare = keys.shape[1] - near - reach
        if spare:
            for ref in (keys, values, codes):
                ref[side, near + reach :] = jnp.zeros((spare, ref.shape[2]), ref.dtype)
        top = side * (tokens - reach)
        blocks.append((side, top, link_bias(code[top : top + reach], codes[side])))
    for base in range(0, width, period):
        scores = []
        for side, top, bias in blocks:
            query = lambda lanes: q_ref[top : top + reach, lanes]
            key = lambda lanes: keys[side, :, lanes]
            scores.append(period_scores(base, query, [key], masks, period))
        for (side, top, bias), part in zip(blocks, scores):
            sets = [(bias, lambda lanes: values[side, :, lanes])]
            tiles = mixed_period(base, part, sets, period)
            store_period(base, tiles, out_ref.at[side * reach : (side + 1) * reach])


def edge_kernel(reach, q_ref, k_ref, v_ref, code_ref, *refs):
    halos = refs[:-4]
    out_ref, keys, values, codes = refs[-4:]
    width = q_ref.shape[1]
    code = columns(code_ref[...])
    at = 0
    for piece in halos:
        rows = piece.shape[0]
        keys[at : at + rows] = piece[:, :width]
        values[at : at + rows] = piece[:, width : 2 * width]
        codes[at : at + rows] = piece[:, 2 * width :].astype(jnp.float32)
        at += rows
    if at < keys.shape[0]:
        for ref in (keys, values, codes):
            ref[at:] = jnp.zeros((ref.shape[0] - at, ref.shape[1]), ref.dtype)
    period = math.lcm(DH, LANES)
    masks = head_masks(q_ref.shape[0], period)
    query = lambda lanes: q_ref[:, lanes]
    pair = [lambda lanes: k_ref[:, lanes], lambda lanes: keys[:, lanes]]
    sets = [
        (link_bias(code, code), lambda lanes: v_ref[:, lanes]),
        (link_bias(code, codes[...]), lambda lanes: values[:, lanes]),
    ]
    for base in range(0, width, period):
        scores = period_scores(base, query, pair, masks, period)
        store_period(base, mixed_period(base, scores, sets, period), out_ref)


def attend_cost(tokens, span, width):
    return pl.CostEstimate(
        flops=HEADS * tokens * span * 2 * LANES * 4,
        bytes_accessed=12 * tokens * width,
        transcendentals=HEADS * tokens * span,
    )


VMEM = pl.BlockSpec(memory_space=pltpu.VMEM)
PARAMS = pltpu.CompilerParams(vmem_limit_bytes=VMEM_LIMIT)


def pack_ends(keys, values, code, most):
    width = keys.shape[1]
    ends = jax.ShapeDtypeStruct((most, 2 * width + LANES), jnp.bfloat16)
    return pl.pallas_call(
        ends_kernel,
        in_specs=[VMEM] * 3,
        out_specs=[VMEM] * 2,
        out_shape=[ends, ends],
        compiler_params=PARAMS,
        cost_estimate=pl.CostEstimate(flops=0, bytes_accessed=16 * most * width, transcendentals=0),
        name="pack_ends",
    )(keys, values, code)


def attend_middle(queries, keys, values, code, reach):
    tokens, width = queries.shape
    return pl.pallas_call(
        functools.partial(middle_kernel, reach),
        in_specs=[VMEM] * 4,
        out_specs=VMEM,
        out_shape=jax.ShapeDtypeStruct((tokens - 2 * reach, width), jnp.bfloat16),
        compiler_params=PARAMS,
        cost_estimate=attend_cost(tokens - 2 * reach, tokens, width),
        name="attend_middle",
    )(queries, keys, values, code)


def attend_edges(queries, keys, values, code, halos, reach):
    tokens, width = queries.shape
    rows = min(tokens, 2 * reach)
    if tokens > 2 * reach:
        kernel = sides_kernel
        held = (2, -(-3 * reach // LANES) * LANES)
    else:
        kernel = edge_kernel
        held = (-(-2 * reach // LANES) * LANES,)
    operands = [queries, keys, values, code, *halos]
    return pl.pallas_call(
        functools.partial(kernel, reach),
        in_specs=[VMEM] * len(operands),
        out_specs=VMEM,
        out_shape=jax.ShapeDtypeStruct((rows, width), jnp.bfloat16),
        scratch_shapes=[
            pltpu.VMEM((*held, width), jnp.bfloat16),
            pltpu.VMEM((*held, width), jnp.bfloat16),
            pltpu.VMEM((*held, LANES), jnp.float32),
        ],
        compiler_params=PARAMS,
        cost_estimate=attend_cost(rows, LANES, width),
        name="attend_edges",
    )(*operands)


def pack_grads_kernel(grad_ref, mark_ref, *refs):
    first_ref, second_ref, sems = refs[-3:]
    half = grad_ref.shape[1] // 2
    copies = []
    for n, ref in enumerate((first_ref, second_ref)):
        copies.append(
            pltpu.make_async_copy(
                grad_ref.at[:, pl.ds(n * half, half)], ref.at[:, pl.ds(0, half)], sems.at[n]
            )
        )
    for copy in copies:
        copy.start()
    place = columns(mark_ref[1:2]).astype(jnp.bfloat16)
    for ref in (first_ref, second_ref):
        ref[:, half:] = place
    for copy in copies:
        copy.wait()


def pack_grads(grads, marks, *others):
    tokens, width = grads.shape
    far = pl.BlockSpec(memory_space=pltpu.HBM)
    return pl.pallas_call(
        pack_grads_kernel,
        in_specs=[far, VMEM] + [far] * len(others),
        out_specs=[VMEM] * 2,
        out_shape=[jax.ShapeDtypeStruct((tokens, width // 2 + LANES), jnp.bfloat16)] * 2,
        scratch_shapes=[pltpu.SemaphoreType.DMA((2,))],
        compiler_params=pltpu.CompilerParams(vmem_limit_bytes=PACK_LIMIT),
        cost_estimate=pl.CostEstimate(flops=0, bytes_accessed=4 * tokens * width, transcendentals=0),
        name="pack_grads",
    )(grads, marks, *others)


def selector(row):
    tokens = row.shape[1]
    wanted = lax.broadcasted_iota(jnp.int32, (tokens, tokens), 0).astype(jnp.float32)
    return jnp.where(wanted == row, 1.0, 0.0)


def sums_kernel(part, sizes, gate_ref, row_ref, mine_ref, theirs_ref, *out_refs):
    half = gate_ref.shape[1] // 2
    place = theirs_ref[:, half:].astype(jnp.float32).T[:1]
    picks = [selector(row).astype(jnp.bfloat16) for row in (row_ref[...], place)]
    theirs = theirs_ref[:, :half]
    summed = jnp.dot(
        jnp.concatenate(picks, axis=1),
        jnp.concatenate((mine_ref[:, :half], theirs), axis=0),
        preferred_element_type=jnp.float32,
    )
    own = jnp.where(lax.axis_index("grp") == part + 1, 1.0, 0.0)
    term = gate_ref[:, part * half : (part + 1) * half] * summed + own * theirs.astype(jnp.float32)
    term = term.astype(jnp.bfloat16)
    at = 0
    for ref, size in zip(out_refs, sizes):
        ref[...] = term[at : at + size]
        at += size


def pair_sums(part, gate, rows, mine, theirs, sizes):
    tokens, half = mine.shape[0], gate.shape[1] // 2
    return pl.pallas_call(
        functools.partial(sums_kernel, part, sizes),
        in_specs=[VMEM] * 4,
        out_specs=[VMEM] * len(sizes),
        out_shape=[jax.ShapeDtypeStruct((size, half), jnp.bfloat16) for size in sizes],
        compiler_params=PARAMS,
        cost_estimate=pl.CostEstimate(
            flops=4 * tokens * tokens * half, bytes_accessed=6 * tokens * half, transcendentals=0
        ),
        name="pair_sums",
    )(gate, rows, mine, theirs)


def piece_spots(tokens, reach, piece):
    if tokens <= 2 * reach:
        return [(0, tokens, 0)]
    if piece == 0:
        return [(reach, tokens - 2 * reach, 0)]
    return [(0, reach, 0), (tokens - reach, reach, reach)]


def picked(spots, row_ref):
    picks = selector(row_ref[...]).T.astype(jnp.bfloat16)
    return jnp.concatenate([picks[:, top : top + size] for top, size, at in spots], axis=1)


def relay_first_kernel(
    spots, later, row_ref, gate_ref, a_ref, b_ref, base_ref, c_ref, d_ref, grad_ref, out_ref, picks_ref, sems
):
    half = a_ref.shape[1]
    copies = []
    for n, ref in enumerate((c_ref, d_ref)):
        to = grad_ref.at[pl.ds(0, ref.shape[0]), pl.ds(n * half, half)]
        copies.append(pltpu.make_async_copy(ref, to, sems.at[n]))
    for copy in copies:
        copy.start()
    picks = picked(spots, row_ref)
    for n, ref in enumerate((a_ref, b_ref)):
        lanes = slice(n * half, (n + 1) * half)
        relayed = jnp.dot(picks, ref[...], preferred_element_type=jnp.float32)
        out_ref[:, lanes] = base_ref[:, lanes].astype(jnp.float32) + gate_ref[:, lanes] * relayed
    picks_ref[...] = picked(later, row_ref)
    for copy in copies:
        copy.wait()


def relay_first(rows, gate, branch, base, totals, spots, later):
    tokens, width = base.shape
    return pl.pallas_call(
        functools.partial(relay_first_kernel, spots, later),
        in_specs=[VMEM] * 7,
        out_specs=[pl.BlockSpec(memory_space=pltpu.HBM), VMEM, VMEM],
        out_shape=[
            jax.ShapeDtypeStruct((tokens, width), jnp.bfloat16),
            jax.ShapeDtypeStruct((tokens, width), jnp.float32),
            jax.ShapeDtypeStruct((tokens, sum(size for top, size, at in later)), jnp.bfloat16),
        ],
        scratch_shapes=[pltpu.SemaphoreType.DMA((2,))],
        compiler_params=PARAMS,
        cost_estimate=pl.CostEstimate(
            flops=2 * tokens * tokens * width, bytes_accessed=24 * tokens * width, transcendentals=0
        ),
        name="relay_first",
    )(rows, gate, *branch, base, *totals)


def relay_last_kernel(
    part, chunks, first_row, picks_ref, gate_ref, held_ref, got_ref, base_ref, total_ref, *refs
):
    grad_ref, out_ref, staged, summed, sems, grad_sem = refs[-6:]
    half = held_ref.shape[1]
    other = 1 - part
    group = lax.axis_index("grp")
    holds = group <= 1 if part == 0 else group % 2 == 0
    summed[...] = jnp.where(holds, got_ref[...], total_ref[...])
    to = grad_ref.at[pl.ds(first_row, total_ref.shape[0]), pl.ds(other * half, half)]
    copies = [pltpu.make_async_copy(summed, to, grad_sem)]
    copies[0].start()
    step = half // chunks
    for c in range(chunks):
        mine = slice(c * step, (c + 1) * step)
        lanes = slice(part * half + c * step, part * half + (c + 1) * step)
        branch = jnp.where(holds, held_ref[:, mine], got_ref[:, mine])
        relayed = jnp.dot(picks_ref[...], branch, preferred_element_type=jnp.float32)
        total = base_ref[:, lanes].astype(jnp.float32) + gate_ref[:, lanes] * relayed
        staged[:, mine] = total.astype(staged.dtype)
        copies.append(
            pltpu.make_async_copy(
                staged.at[:, pl.ds(c * step, step)],
                out_ref.at[:, pl.ds(part * half + c * step, step)],
                sems.at[c],
            )
        )
        copies[-1].start()
    for copy in copies:
        copy.wait()


def relay_last(picks, gate, held, got, base, total, part, first_row, grads, out):
    tokens, width = base.shape
    chunks = 2 if width // 2 % (2 * LANES) == 0 else 1
    far = pl.BlockSpec(memory_space=pltpu.HBM)
    operands = [picks, gate, held, got, base, total]
    aliases = {}
    for n, buffer in enumerate((grads, out)):
        if buffer is not None:
            aliases[len(operands)] = n
            operands.append(buffer)
    return pl.pallas_call(
        functools.partial(relay_last_kernel, part, chunks, first_row),
        in_specs=[VMEM] * 6 + [far] * len(aliases),
        out_specs=[far] * 2,
        out_shape=[jax.ShapeDtypeStruct((tokens, width), jnp.bfloat16)] * 2,
        input_output_aliases=aliases,
        scratch_shapes=[
            pltpu.VMEM((tokens, width // 2), jnp.bfloat16),
            pltpu.VMEM(total.shape, jnp.bfloat16),
            pltpu.SemaphoreType.DMA((chunks,)),
            pltpu.SemaphoreType.DMA,
        ],
        compiler_params=PARAMS,
        cost_estimate=pl.CostEstimate(
            flops=tokens * tokens * width, bytes_accessed=6 * tokens * width, transcendentals=0
        ),
        name="relay_last",
    )(*operands)


def whole_gate(gate):
    ranks = lax.axis_size("rep")
    if ranks != 2:
        return lax.all_gather(gate, "rep", axis=0, tiled=True)
    other = lax.ppermute(gate, "rep", [(0, 1), (1, 0)])
    first = lax.axis_index("rep") == 0
    return jnp.concatenate([jnp.where(first, gate, other), jnp.where(first, other, gate)])


SWAP_X, SWAP_Y = [(0, 1), (1, 0), (2, 3), (3, 2)], [(0, 2), (2, 0), (1, 3), (3, 1)]
ROUND_A, ROUND_B = [(0, 1), (1, 3), (3, 2), (2, 0)], [(0, 2), (2, 3), (3, 1), (1, 0)]


def added(a, b):
    return (a.astype(jnp.float32) + b.astype(jnp.float32)).astype(a.dtype)


def local(query_rows, key_rows, value_rows, view_frame, control_row, control_gate, out_grad):
    queries, keys, values = query_rows[0, 0], key_rows[0, 0], value_rows[0, 0]
    tokens, width = queries.shape
    half = width // 2
    ranks = lax.axis_size("seq")
    reach = 2 * (tokens * ranks // 32)
    hops = (reach + tokens - 1) // tokens
    group, rank = lax.axis_index("grp"), lax.axis_index("seq")
    send = lambda block, route: lax.ppermute(block, "grp", route)

    tag = view_frame[0, 0]
    code = tag + 8 * (tag // FRAMES) + 16
    marks = jnp.stack((code, control_row[0, 0] % tokens)).astype(jnp.float32)
    code, rows = marks[:1], marks[1:]
    most = min(tokens, reach)
    even = rank % 2 == 0
    sent_a, sent_b = pack_grads(out_grad[0, 0], marks, queries, keys, values)
    code, sent_a, sent_b = lax.optimization_barrier((code, sent_a, sent_b))
    got_a, got_b = send(sent_a, SWAP_X), send(sent_b, SWAP_Y)
    end_one, end_two = pack_ends(keys, values, code, most)
    code, end_one, end_two = lax.optimization_barrier((code, end_one, end_two))
    own = [attend_middle(queries, keys, values, code, reach)] if tokens > 2 * reach else []
    gate = whole_gate(control_gate)[None]
    halos = [paired(end_one, "seq", 0), paired(end_two, "seq", 1)]
    for hop in range(2, hops + 1):
        count = min(tokens, reach - (hop - 1) * tokens)
        tail, head = jnp.where(even, end_one, end_two), jnp.where(even, end_two, end_one)
        halos.append(shifted(tail[most - count :], "seq", hop))
        halos.append(shifted(head[:count], "seq", -hop))
    sizes = [piece.shape[0] for piece in own] + [min(tokens, 2 * reach)]
    sums = [
        *pair_sums(0, gate, rows, sent_a, got_a, sizes),
        *pair_sums(1, gate, rows, sent_b, got_b, sizes),
    ]
    count = len(sizes)

    def outgoing(piece, sum_a, sum_b):
        to_a = jnp.where(group == 0, piece[:, :half], jnp.where(group == 1, sum_a, sum_b))
        to_b = jnp.where(group == 0, piece[:, half:], jnp.where(group == 2, sum_b, sum_a))
        return to_a, to_b

    going = [outgoing(own[0], sums[0], sums[count])] if own else []
    code, *ready = lax.optimization_barrier((code, *sums, *(going[0] if going else ())))
    sums = ready[: 2 * count]
    if going:
        going = [ready[2 * count :]]
    own.append(attend_edges(queries, keys, values, code, halos, reach))

    going.append(outgoing(own[-1], sums[count - 1], sums[2 * count - 1]))
    spots = [piece_spots(tokens, reach, n) for n in range(count)]
    order = [
        own[n][at : at + size] for top, size, n, at in sorted(
            (top, size, n, at) for n in range(count) for top, size, at in spots[n]
        )
    ]
    block_out = jnp.concatenate(order, axis=0)
    branch_grad, first_row = None, 0
    picks = (rows[0][:, None] == jnp.arange(tokens)).astype(jnp.bfloat16) if count == 1 else None
    for n, (piece, sum_a, sum_b) in enumerate(zip(own, sums[:count], sums[count:])):
        piece_a, piece_b = piece[:, :half], piece[:, half:]
        one, two = send(going[n][0], ROUND_A), send(going[n][1], ROUND_B)
        total_a = added(sum_a, jnp.where(group == 1, two, one))
        total_b = added(sum_b, jnp.where(group == 2, one, two))
        held_a = jnp.where(group == 0, piece_a, one)
        held_b = jnp.where(group == 0, piece_b, two)
        across = send(jnp.where((group == 0) | (group == 2), held_b, total_a), SWAP_X)
        down = send(jnp.where(group <= 1, held_a, total_b), SWAP_Y)
        branch_a = jnp.where(group <= 1, held_a, down)
        branch_b = jnp.where((group == 0) | (group == 2), held_b, across)
        totals = (
            jnp.where((group == 0) | (group == 2), across, total_a),
            jnp.where(group <= 1, down, total_b),
        )
        if n < count - 1:
            branch_grad, block_out, picks = relay_first(
                rows, gate, (branch_a, branch_b), block_out, totals, spots[n], spots[n + 1]
            )
            first_row = piece.shape[0]
            continue
        base, block_out = block_out, None
        ends = ((held_a, down, total_b), (held_b, across, total_a))
        for part in (1, 0):
            held, got, total = ends[part]
            branch_grad, block_out = relay_last(
                picks, gate, held, got, base, total, part, first_row, branch_grad, block_out
            )
    return (block_out[None, None], branch_grad[None])


def solution(mesh):
    placed = (
        P("rep", "grp", "seq", None),
        P("rep", "grp", "seq", None),
        P("rep", "grp", "seq", None),
        P("rep", "grp", "seq"),
        P("rep", "grp", "seq"),
        P("rep"),
        P("rep", "grp", "seq", None),
    )
    return jax.shard_map(
        local,
        mesh=mesh,
        in_specs=placed,
        out_specs=(P("rep", "grp", "seq", None), P("rep", "seq", None)),
        check_vma=False,
    )
```

```python
import functools
import math

import jax
import jax.numpy as jnp
from jax import lax
from jax.experimental import pallas as pl
from jax.experimental.pallas import tpu as pltpu
from jax.sharding import PartitionSpec as P

HEADS = 32
DH = 80
FRAMES = 20
LANES = 128
VMEM_LIMIT = 32 * 1024 * 1024
PACK_LIMIT = 53 * 1024 * 1024


def shifted(block, axis, distance):
    devices = range(lax.axis_size(axis))
    route = [(i - distance, i) for i in devices if i - distance in devices]
    return lax.ppermute(block, axis, route)


def paired(block, first):
    size, ranks = lax.axis_size("seq"), lax.axis_size("rep")
    route = []
    for i in range(size):
        other = i + 1 if (i - first) % 2 == 0 else i - 1
        for rank in range(ranks):
            if 0 <= other < size:
                route.append((i * ranks + rank, other * ranks + rank))
            elif rank ^ 1 < ranks:
                route.append((i * ranks + rank, i * ranks + (rank ^ 1)))
    return lax.ppermute(block, ("seq", "rep"), route)


def neighbours_there(ranks):
    rank = lax.axis_index("seq")
    return jnp.where(rank > 0, 1.0, 0.0), jnp.where(rank < ranks - 1, 1.0, 0.0)


def lane_windows(heads):
    windows = []
    for head in range(heads):
        first, last = head * DH, (head + 1) * DH
        if windows and last <= windows[-1][0] + 2 * LANES:
            windows[-1][1].append(head)
        else:
            windows.append((first // LANES * LANES, [head]))
    out = []
    for start, members in windows:
        start = min(start, heads * DH - 2 * LANES)
        out.append((start, members))
    return out


def head_masks(rows, period):
    masks = {}
    for start, members in lane_windows(period // DH):
        lane = lax.broadcasted_iota(jnp.int32, (rows, 2 * LANES), 1) + start
        for h in members:
            inside = (lane >= h * DH) & (lane < (h + 1) * DH)
            masks[h] = jnp.where(inside, 1.0, 0.0).astype(jnp.bfloat16)
    return masks


def period_scores(base, query, keys, masks, period):
    scores = []
    for start, members in lane_windows(period // DH):
        lanes = slice(base + start, base + start + 2 * LANES)
        part = query(lanes)
        stacked = jnp.concatenate([part * masks[h] for h in members], axis=0)
        scores.append(
            [
                lax.dot_general(
                    stacked, key(lanes), (((1,), (1,)), ((), ())), preferred_element_type=jnp.float32
                )
                for key in keys
            ]
        )
    return scores


def mixed_period(base, scores, sets, period):
    rows = sets[0][0].shape[0]
    factor = math.log2(math.e) / math.sqrt(DH)
    windows = lane_windows(period // DH)
    weights = []
    for parts, (start, members) in zip(scores, windows):
        parts = [
            part.reshape(len(members), rows, -1) + bias[None]
            for part, (bias, value) in zip(parts, sets)
        ]
        largest = row_max(parts)
        weights.append(
            [
                jnp.exp2((part - largest) * factor).astype(jnp.bfloat16).reshape(len(members) * rows, -1)
                for part in parts
            ]
        )
    tiles = {}
    for parts, (start, members) in zip(weights, windows):
        lanes = slice(base + start, base + start + 2 * LANES)
        mixed = sum(
            jnp.dot(part, value(lanes), preferred_element_type=jnp.float32)
            for part, (bias, value) in zip(parts, sets)
        )
        totals = sum(
            jnp.dot(part, jnp.ones((part.shape[1], LANES), part.dtype), preferred_element_type=jnp.float32)
            for part in parts
        )
        scale = 1.0 / totals
        for n, h in enumerate(members):
            for t in range(2):
                low = start + t * LANES
                if h * DH >= low + LANES or (h + 1) * DH <= low:
                    continue
                mine = slice(n * rows, (n + 1) * rows)
                piece = mixed[mine, t * LANES : (t + 1) * LANES] * scale[mine]
                if low in tiles:
                    lane = lax.broadcasted_iota(jnp.int32, (rows, LANES), 1) + low
                    tiles[low] = jnp.where(lane >= h * DH, piece, tiles[low])
                else:
                    tiles[low] = piece
    return {low: tile.astype(jnp.bfloat16) for low, tile in tiles.items()}


def row_max(parts):
    if all(part.shape == parts[0].shape for part in parts):
        return jnp.max(functools.reduce(jnp.maximum, parts), axis=-1, keepdims=True)
    return functools.reduce(jnp.maximum, [jnp.max(part, axis=-1, keepdims=True) for part in parts])


def columns(row):
    return jnp.broadcast_to(row, (LANES, row.shape[1])).T


def link_bias(mine, theirs):
    return jnp.where(jnp.abs(mine[:, :1] - theirs.T[: mine.shape[0]]) <= 1.5, 0.0, -1e30)


def store_period(base, tiles, out_ref):
    for low, tile in tiles.items():
        out_ref[:, base + low : base + low + LANES] = tile


def ends_kernel(k_ref, v_ref, code_ref, *end_refs):
    even = lax.axis_index("seq") % 2 == 0
    tokens, width = k_ref.shape
    code = columns(code_ref[...])
    for n, ref in enumerate(end_refs):
        most = ref.shape[0]
        tail = even if n == 0 else jnp.logical_not(even)
        first = pl.multiple_of(jnp.where(tail, tokens - most, 0), most)
        ref[:, :width] = k_ref[pl.ds(first, most), :]
        ref[:, width : 2 * width] = v_ref[pl.ds(first, most), :]
        here = jnp.where(tail, code[tokens - most :], code[:most])
        ref[:, 2 * width :] = here.astype(jnp.bfloat16)


def middle_kernel(reach, q_ref, k_ref, v_ref, code_ref, out_ref):
    rows = out_ref.shape[0]
    code = columns(code_ref[...])
    bias = link_bias(code[reach : reach + rows], code)
    period = math.lcm(DH, LANES)
    masks = head_masks(rows, period)
    query = lambda lanes: q_ref[reach : reach + rows, lanes]
    for base in range(0, out_ref.shape[1], period):
        scores = period_scores(base, query, [lambda lanes: k_ref[:, lanes]], masks, period)
        sets = [(bias, lambda lanes: v_ref[:, lanes])]
        store_period(base, mixed_period(base, scores, sets, period), out_ref)


def sides_kernel(reach, ranks, q_ref, k_ref, v_ref, code_ref, one_ref, two_ref, *refs):
    there = neighbours_there(ranks)
    out_ref, keys, values, codes = refs
    tokens, width = q_ref.shape
    near = 2 * reach
    code = columns(code_ref[...])
    even = lax.axis_index("seq") % 2 == 0
    period = math.lcm(DH, LANES)
    masks = head_masks(reach, period)
    blocks = []
    for side, first in ((0, 0), (1, tokens - near)):
        own = slice(first, first + near)
        use_two = even if side == 0 else jnp.logical_not(even)
        halo = jnp.where(use_two, two_ref[...], one_ref[...])
        keys[side, :near] = k_ref[own]
        values[side, :near] = v_ref[own]
        codes[side, :near] = code[own]
        keys[side, near : near + reach] = halo[:, :width]
        values[side, near : near + reach] = halo[:, width : 2 * width]
        codes[side, near : near + reach] = halo[:, 2 * width :].astype(jnp.float32) * there[side]
        spare = keys.shape[1] - near - reach
        if spare:
            for ref in (keys, values, codes):
                ref[side, near + reach :] = jnp.zeros((spare, ref.shape[2]), ref.dtype)
        top = side * (tokens - reach)
        blocks.append((side, top, link_bias(code[top : top + reach], codes[side])))
    for base in range(0, width, period):
        scores = []
        for side, top, bias in blocks:
            query = lambda lanes: q_ref[top : top + reach, lanes]
            key = lambda lanes: keys[side, :, lanes]
            scores.append(period_scores(base, query, [key], masks, period))
        for (side, top, bias), part in zip(blocks, scores):
            sets = [(bias, lambda lanes: values[side, :, lanes])]
            tiles = mixed_period(base, part, sets, period)
            store_period(base, tiles, out_ref.at[side * reach : (side + 1) * reach])


def edge_kernel(reach, ranks, q_ref, k_ref, v_ref, code_ref, *refs):
    below, above = neighbours_there(ranks)
    even = lax.axis_index("seq") % 2 == 0
    there = [jnp.where(even, above, below), jnp.where(even, below, above)]
    halos = refs[:-4]
    out_ref, keys, values, codes = refs[-4:]
    width = q_ref.shape[1]
    code = columns(code_ref[...])
    at = 0
    for n, piece in enumerate(halos):
        rows = piece.shape[0]
        known = there[n] if n < 2 else 1.0
        keys[at : at + rows] = piece[:, :width]
        values[at : at + rows] = piece[:, width : 2 * width]
        codes[at : at + rows] = piece[:, 2 * width :].astype(jnp.float32) * known
        at += rows
    if at < keys.shape[0]:
        for ref in (keys, values, codes):
            ref[at:] = jnp.zeros((ref.shape[0] - at, ref.shape[1]), ref.dtype)
    period = math.lcm(DH, LANES)
    masks = head_masks(q_ref.shape[0], period)
    query = lambda lanes: q_ref[:, lanes]
    pair = [lambda lanes: k_ref[:, lanes], lambda lanes: keys[:, lanes]]
    sets = [
        (link_bias(code, code), lambda lanes: v_ref[:, lanes]),
        (link_bias(code, codes[...]), lambda lanes: values[:, lanes]),
    ]
    for base in range(0, width, period):
        scores = period_scores(base, query, pair, masks, period)
        store_period(base, mixed_period(base, scores, sets, period), out_ref)


def attend_cost(tokens, span, width):
    return pl.CostEstimate(
        flops=HEADS * tokens * span * 2 * LANES * 4,
        bytes_accessed=12 * tokens * width,
        transcendentals=HEADS * tokens * span,
    )


VMEM = pl.BlockSpec(memory_space=pltpu.VMEM)
PARAMS = pltpu.CompilerParams(vmem_limit_bytes=VMEM_LIMIT)


def pack_ends(keys, values, code, most):
    width = keys.shape[1]
    ends = jax.ShapeDtypeStruct((most, 2 * width + LANES), jnp.bfloat16)
    return pl.pallas_call(
        ends_kernel,
        in_specs=[VMEM] * 3,
        out_specs=[VMEM] * 2,
        out_shape=[ends, ends],
        compiler_params=PARAMS,
        cost_estimate=pl.CostEstimate(flops=0, bytes_accessed=16 * most * width, transcendentals=0),
        name="pack_ends",
    )(keys, values, code)


def attend_middle(queries, keys, values, code, reach):
    tokens, width = queries.shape
    return pl.pallas_call(
        functools.partial(middle_kernel, reach),
        in_specs=[VMEM] * 4,
        out_specs=VMEM,
        out_shape=jax.ShapeDtypeStruct((tokens - 2 * reach, width), jnp.bfloat16),
        compiler_params=PARAMS,
        cost_estimate=attend_cost(tokens - 2 * reach, tokens, width),
        name="attend_middle",
    )(queries, keys, values, code)


def attend_edges(queries, keys, values, code, halos, reach):
    tokens, width = queries.shape
    rows = min(tokens, 2 * reach)
    if tokens > 2 * reach:
        kernel = sides_kernel
        held = (2, -(-3 * reach // LANES) * LANES)
    else:
        kernel = edge_kernel
        held = (-(-2 * reach // LANES) * LANES,)
    operands = [queries, keys, values, code, *halos]
    return pl.pallas_call(
        functools.partial(kernel, reach, lax.axis_size("seq")),
        in_specs=[VMEM] * len(operands),
        out_specs=VMEM,
        out_shape=jax.ShapeDtypeStruct((rows, width), jnp.bfloat16),
        scratch_shapes=[
            pltpu.VMEM((*held, width), jnp.bfloat16),
            pltpu.VMEM((*held, width), jnp.bfloat16),
            pltpu.VMEM((*held, LANES), jnp.float32),
        ],
        compiler_params=PARAMS,
        cost_estimate=attend_cost(rows, LANES, width),
        name="attend_edges",
    )(*operands)


def pack_grads_kernel(grad_ref, mark_ref, *refs):
    first_ref, second_ref, sems = refs[-3:]
    half = grad_ref.shape[1] // 2
    copies = []
    for n, ref in enumerate((first_ref, second_ref)):
        copies.append(
            pltpu.make_async_copy(
                grad_ref.at[:, pl.ds(n * half, half)], ref.at[:, pl.ds(0, half)], sems.at[n]
            )
        )
    for copy in copies:
        copy.start()
    place = columns(mark_ref[1:2]).astype(jnp.bfloat16)
    for ref in (first_ref, second_ref):
        ref[:, half:] = place
    for copy in copies:
        copy.wait()


def pack_grads(grads, marks, *others):
    tokens, width = grads.shape
    far = pl.BlockSpec(memory_space=pltpu.HBM)
    return pl.pallas_call(
        pack_grads_kernel,
        in_specs=[far, VMEM] + [far] * len(others),
        out_specs=[VMEM] * 2,
        out_shape=[jax.ShapeDtypeStruct((tokens, width // 2 + LANES), jnp.bfloat16)] * 2,
        scratch_shapes=[pltpu.SemaphoreType.DMA((2,))],
        compiler_params=pltpu.CompilerParams(vmem_limit_bytes=PACK_LIMIT),
        cost_estimate=pl.CostEstimate(flops=0, bytes_accessed=4 * tokens * width, transcendentals=0),
        name="pack_grads",
    )(grads, marks, *others)


def selector(row):
    tokens = row.shape[1]
    wanted = lax.broadcasted_iota(jnp.int32, (tokens, tokens), 0).astype(jnp.float32)
    return jnp.where(wanted == row, 1.0, 0.0)


def sums_kernel(part, sizes, gate_ref, row_ref, mine_ref, theirs_ref, *out_refs):
    half = gate_ref.shape[1] // 2
    place = theirs_ref[:, half:].astype(jnp.float32).T[:1]
    picks = [selector(row).astype(jnp.bfloat16) for row in (row_ref[...], place)]
    theirs = theirs_ref[:, :half]
    summed = jnp.dot(
        jnp.concatenate(picks, axis=1),
        jnp.concatenate((mine_ref[:, :half], theirs), axis=0),
        preferred_element_type=jnp.float32,
    )
    own = jnp.where(lax.axis_index("grp") == part + 1, 1.0, 0.0)
    term = gate_ref[:, part * half : (part + 1) * half] * summed + own * theirs.astype(jnp.float32)
    term = term.astype(jnp.bfloat16)
    at = 0
    for ref, size in zip(out_refs, sizes):
        ref[...] = term[at : at + size]
        at += size


def pair_sums(part, gate, rows, mine, theirs, sizes):
    tokens, half = mine.shape[0], gate.shape[1] // 2
    return pl.pallas_call(
        functools.partial(sums_kernel, part, sizes),
        in_specs=[VMEM] * 4,
        out_specs=[VMEM] * len(sizes),
        out_shape=[jax.ShapeDtypeStruct((size, half), jnp.bfloat16) for size in sizes],
        compiler_params=PARAMS,
        cost_estimate=pl.CostEstimate(
            flops=4 * tokens * tokens * half, bytes_accessed=6 * tokens * half, transcendentals=0
        ),
        name="pair_sums",
    )(gate, rows, mine, theirs)


def piece_spots(tokens, reach, piece):
    if tokens <= 2 * reach:
        return [(0, tokens, 0)]
    if piece == 0:
        return [(reach, tokens - 2 * reach, 0)]
    return [(0, reach, 0), (tokens - reach, reach, reach)]


def picked(spots, row_ref):
    picks = selector(row_ref[...]).T.astype(jnp.bfloat16)
    return jnp.concatenate([picks[:, top : top + size] for top, size, at in spots], axis=1)


def relay_first_kernel(
    spots, later, row_ref, gate_ref, a_ref, b_ref, base_ref, c_ref, d_ref, grad_ref, out_ref, picks_ref, sems
):
    half = a_ref.shape[1]
    copies = []
    for n, ref in enumerate((c_ref, d_ref)):
        to = grad_ref.at[pl.ds(0, ref.shape[0]), pl.ds(n * half, half)]
        copies.append(pltpu.make_async_copy(ref, to, sems.at[n]))
    for copy in copies:
        copy.start()
    picks = picked(spots, row_ref)
    for n, ref in enumerate((a_ref, b_ref)):
        lanes = slice(n * half, (n + 1) * half)
        relayed = jnp.dot(picks, ref[...], preferred_element_type=jnp.float32)
        out_ref[:, lanes] = base_ref[:, lanes].astype(jnp.float32) + gate_ref[:, lanes] * relayed
    picks_ref[...] = picked(later, row_ref)
    for copy in copies:
        copy.wait()


def relay_first(rows, gate, branch, base, totals, spots, later):
    tokens, width = base.shape
    return pl.pallas_call(
        functools.partial(relay_first_kernel, spots, later),
        in_specs=[VMEM] * 7,
        out_specs=[pl.BlockSpec(memory_space=pltpu.HBM), VMEM, VMEM],
        out_shape=[
            jax.ShapeDtypeStruct((tokens, width), jnp.bfloat16),
            jax.ShapeDtypeStruct((tokens, width), jnp.float32),
            jax.ShapeDtypeStruct((tokens, sum(size for top, size, at in later)), jnp.bfloat16),
        ],
        scratch_shapes=[pltpu.SemaphoreType.DMA((2,))],
        compiler_params=PARAMS,
        cost_estimate=pl.CostEstimate(
            flops=2 * tokens * tokens * width, bytes_accessed=24 * tokens * width, transcendentals=0
        ),
        name="relay_first",
    )(rows, gate, *branch, base, *totals)


def relay_last_kernel(
    part, chunks, first_row, picks_ref, gate_ref, held_ref, got_ref, base_ref, total_ref, *refs
):
    grad_ref, out_ref, staged, summed, sems, grad_sem = refs[-6:]
    half = held_ref.shape[1]
    other = 1 - part
    group = lax.axis_index("grp")
    holds = group <= 1 if part == 0 else group % 2 == 0
    summed[...] = jnp.where(holds, got_ref[...], total_ref[...])
    to = grad_ref.at[pl.ds(first_row, total_ref.shape[0]), pl.ds(other * half, half)]
    copies = [pltpu.make_async_copy(summed, to, grad_sem)]
    copies[0].start()
    step = half // chunks
    for c in range(chunks):
        mine = slice(c * step, (c + 1) * step)
        lanes = slice(part * half + c * step, part * half + (c + 1) * step)
        branch = jnp.where(holds, held_ref[:, mine], got_ref[:, mine])
        relayed = jnp.dot(picks_ref[...], branch, preferred_element_type=jnp.float32)
        total = base_ref[:, lanes].astype(jnp.float32) + gate_ref[:, lanes] * relayed
        staged[:, mine] = total.astype(staged.dtype)
        copies.append(
            pltpu.make_async_copy(
                staged.at[:, pl.ds(c * step, step)],
                out_ref.at[:, pl.ds(part * half + c * step, step)],
                sems.at[c],
            )
        )
        copies[-1].start()
    for copy in copies:
        copy.wait()


def relay_last(picks, gate, held, got, base, total, part, first_row, grads, out):
    tokens, width = base.shape
    chunks = 2 if width // 2 % (2 * LANES) == 0 else 1
    far = pl.BlockSpec(memory_space=pltpu.HBM)
    operands = [picks, gate, held, got, base, total]
    aliases = {}
    for n, buffer in enumerate((grads, out)):
        if buffer is not None:
            aliases[len(operands)] = n
            operands.append(buffer)
    return pl.pallas_call(
        functools.partial(relay_last_kernel, part, chunks, first_row),
        in_specs=[VMEM] * 6 + [far] * len(aliases),
        out_specs=[far] * 2,
        out_shape=[jax.ShapeDtypeStruct((tokens, width), jnp.bfloat16)] * 2,
        input_output_aliases=aliases,
        scratch_shapes=[
            pltpu.VMEM((tokens, width // 2), jnp.bfloat16),
            pltpu.VMEM(total.shape, jnp.bfloat16),
            pltpu.SemaphoreType.DMA((chunks,)),
            pltpu.SemaphoreType.DMA,
        ],
        compiler_params=PARAMS,
        cost_estimate=pl.CostEstimate(
            flops=tokens * tokens * width, bytes_accessed=6 * tokens * width, transcendentals=0
        ),
        name="relay_last",
    )(*operands)


def whole_gate(gate):
    ranks = lax.axis_size("rep")
    if ranks != 2:
        return lax.all_gather(gate, "rep", axis=0, tiled=True)
    other = lax.ppermute(gate, "rep", [(0, 1), (1, 0)])
    first = lax.axis_index("rep") == 0
    return jnp.concatenate([jnp.where(first, gate, other), jnp.where(first, other, gate)])


SWAP_X, SWAP_Y = [(0, 1), (1, 0), (2, 3), (3, 2)], [(0, 2), (2, 0), (1, 3), (3, 1)]
ROUND_A, ROUND_B = [(0, 1), (1, 3), (3, 2), (2, 0)], [(0, 2), (2, 3), (3, 1), (1, 0)]


def added(a, b):
    return (a.astype(jnp.float32) + b.astype(jnp.float32)).astype(a.dtype)


def local(query_rows, key_rows, value_rows, view_frame, control_row, control_gate, out_grad):
    queries, keys, values = query_rows[0, 0], key_rows[0, 0], value_rows[0, 0]
    tokens, width = queries.shape
    half = width // 2
    ranks = lax.axis_size("seq")
    reach = 2 * (tokens * ranks // 32)
    hops = (reach + tokens - 1) // tokens
    group, rank = lax.axis_index("grp"), lax.axis_index("seq")
    send = lambda block, route: lax.ppermute(block, "grp", route)

    tag = view_frame[0, 0]
    code = tag + 8 * (tag // FRAMES) + 16
    marks = jnp.stack((code, control_row[0, 0] % tokens)).astype(jnp.float32)
    code, rows = marks[:1], marks[1:]
    most = min(tokens, reach)
    even = rank % 2 == 0
    sent_a, sent_b = pack_grads(out_grad[0, 0], marks, queries, keys, values)
    code, sent_a, sent_b = lax.optimization_barrier((code, sent_a, sent_b))
    got_a, got_b = send(sent_a, SWAP_X), send(sent_b, SWAP_Y)
    end_one, end_two = pack_ends(keys, values, code, most)
    code, end_one, end_two = lax.optimization_barrier((code, end_one, end_two))
    own = [attend_middle(queries, keys, values, code, reach)] if tokens > 2 * reach else []
    gate = whole_gate(control_gate)[None]
    halos = [paired(end_one, 0), paired(end_two, 1)]
    for hop in range(2, hops + 1):
        count = min(tokens, reach - (hop - 1) * tokens)
        tail, head = jnp.where(even, end_one, end_two), jnp.where(even, end_two, end_one)
        halos.append(shifted(tail[most - count :], "seq", hop))
        halos.append(shifted(head[:count], "seq", -hop))
    sizes = [piece.shape[0] for piece in own] + [min(tokens, 2 * reach)]
    sums = [
        *pair_sums(0, gate, rows, sent_a, got_a, sizes),
        *pair_sums(1, gate, rows, sent_b, got_b, sizes),
    ]
    count = len(sizes)

    def outgoing(piece, sum_a, sum_b):
        to_a = jnp.where(group == 0, piece[:, :half], jnp.where(group == 1, sum_a, sum_b))
        to_b = jnp.where(group == 0, piece[:, half:], jnp.where(group == 2, sum_b, sum_a))
        return to_a, to_b

    going = [outgoing(own[0], sums[0], sums[count])] if own else []
    code, *ready = lax.optimization_barrier((code, *sums, *(going[0] if going else ())))
    sums = ready[: 2 * count]
    if going:
        going = [ready[2 * count :]]
    own.append(attend_edges(queries, keys, values, code, halos, reach))

    going.append(outgoing(own[-1], sums[count - 1], sums[2 * count - 1]))
    spots = [piece_spots(tokens, reach, n) for n in range(count)]
    order = [
        own[n][at : at + size] for top, size, n, at in sorted(
            (top, size, n, at) for n in range(count) for top, size, at in spots[n]
        )
    ]
    block_out = jnp.concatenate(order, axis=0)
    branch_grad, first_row = None, 0
    picks = (rows[0][:, None] == jnp.arange(tokens)).astype(jnp.bfloat16) if count == 1 else None
    for n, (piece, sum_a, sum_b) in enumerate(zip(own, sums[:count], sums[count:])):
        piece_a, piece_b = piece[:, :half], piece[:, half:]
        one, two = send(going[n][0], ROUND_A), send(going[n][1], ROUND_B)
        total_a = added(sum_a, jnp.where(group == 1, two, one))
        total_b = added(sum_b, jnp.where(group == 2, one, two))
        held_a = jnp.where(group == 0, piece_a, one)
        held_b = jnp.where(group == 0, piece_b, two)
        across = send(jnp.where((group == 0) | (group == 2), held_b, total_a), SWAP_X)
        down = send(jnp.where(group <= 1, held_a, total_b), SWAP_Y)
        branch_a = jnp.where(group <= 1, held_a, down)
        branch_b = jnp.where((group == 0) | (group == 2), held_b, across)
        totals = (
            jnp.where((group == 0) | (group == 2), across, total_a),
            jnp.where(group <= 1, down, total_b),
        )
        if n < count - 1:
            branch_grad, block_out, picks = relay_first(
                rows, gate, (branch_a, branch_b), block_out, totals, spots[n], spots[n + 1]
            )
            first_row = piece.shape[0]
            continue
        base, block_out = block_out, None
        ends = ((held_a, down, total_b), (held_b, across, total_a))
        for part in (1, 0):
            held, got, total = ends[part]
            branch_grad, block_out = relay_last(
                picks, gate, held, got, base, total, part, first_row, branch_grad, block_out
            )
    return (block_out[None, None], branch_grad[None])


def solution(mesh):
    placed = (
        P("rep", "grp", "seq", None),
        P("rep", "grp", "seq", None),
        P("rep", "grp", "seq", None),
        P("rep", "grp", "seq"),
        P("rep", "grp", "seq"),
        P("rep"),
        P("rep", "grp", "seq", None),
    )
    return jax.shard_map(
        local,
        mesh=mesh,
        in_specs=placed,
        out_specs=(P("rep", "grp", "seq", None), P("rep", "seq", None)),
        check_vma=False,
    )
```

```python
import functools
import math

import jax
import jax.numpy as jnp
from jax import lax
from jax.experimental import pallas as pl
from jax.experimental.pallas import tpu as pltpu
from jax.sharding import PartitionSpec as P

HEADS = 32
DH = 80
FRAMES = 20
LANES = 128
VMEM_LIMIT = 32 * 1024 * 1024
PACK_LIMIT = 53 * 1024 * 1024


def shifted(block, axis, distance):
    devices = range(lax.axis_size(axis))
    route = [(i - distance, i) for i in devices if i - distance in devices]
    return lax.ppermute(block, axis, route)


def paired(block, first):
    size, ranks = lax.axis_size("seq"), lax.axis_size("rep")
    route = []
    for i in range(size):
        other = i + 1 if (i - first) % 2 == 0 else i - 1
        for rank in range(ranks):
            if 0 <= other < size:
                route.append((i * ranks + rank, other * ranks + rank))
            elif rank ^ 1 < ranks:
                route.append((i * ranks + rank, i * ranks + (rank ^ 1)))
    return lax.ppermute(block, ("seq", "rep"), route)


def neighbours_there(ranks):
    rank = lax.axis_index("seq")
    return jnp.where(rank > 0, 1.0, 0.0), jnp.where(rank < ranks - 1, 1.0, 0.0)


def lane_windows(heads):
    windows = []
    for head in range(heads):
        first, last = head * DH, (head + 1) * DH
        if windows and last <= windows[-1][0] + 2 * LANES:
            windows[-1][1].append(head)
        else:
            windows.append((first // LANES * LANES, [head]))
    out = []
    for start, members in windows:
        start = min(start, heads * DH - 2 * LANES)
        out.append((start, members))
    return out


def head_masks(rows, period):
    masks = {}
    for start, members in lane_windows(period // DH):
        lane = lax.broadcasted_iota(jnp.int32, (rows, 2 * LANES), 1) + start
        for h in members:
            inside = (lane >= h * DH) & (lane < (h + 1) * DH)
            masks[h] = jnp.where(inside, 1.0, 0.0).astype(jnp.bfloat16)
    return masks


def period_scores(base, query, keys, masks, period):
    scores = []
    for start, members in lane_windows(period // DH):
        lanes = slice(base + start, base + start + 2 * LANES)
        part = query(lanes)
        stacked = jnp.concatenate([part * masks[h] for h in members], axis=0)
        scores.append(
            [
                lax.dot_general(
                    stacked, key(lanes), (((1,), (1,)), ((), ())), preferred_element_type=jnp.float32
                )
                for key in keys
            ]
        )
    return scores


def mixed_period(base, scores, sets, period):
    rows = sets[0][0].shape[0]
    factor = math.log2(math.e) / math.sqrt(DH)
    windows = lane_windows(period // DH)
    weights = []
    for parts, (start, members) in zip(scores, windows):
        parts = [
            part.reshape(len(members), rows, -1) + bias[None]
            for part, (bias, value) in zip(parts, sets)
        ]
        largest = row_max(parts)
        weights.append(
            [
                jnp.exp2((part - largest) * factor).astype(jnp.bfloat16).reshape(len(members) * rows, -1)
                for part in parts
            ]
        )
    tiles = {}
    for parts, (start, members) in zip(weights, windows):
        lanes = slice(base + start, base + start + 2 * LANES)
        mixed = sum(
            jnp.dot(part, value(lanes), preferred_element_type=jnp.float32)
            for part, (bias, value) in zip(parts, sets)
        )
        totals = sum(
            jnp.dot(part, jnp.ones((part.shape[1], LANES), part.dtype), preferred_element_type=jnp.float32)
            for part in parts
        )
        scale = 1.0 / totals
        for n, h in enumerate(members):
            for t in range(2):
                low = start + t * LANES
                if h * DH >= low + LANES or (h + 1) * DH <= low:
                    continue
                mine = slice(n * rows, (n + 1) * rows)
                piece = mixed[mine, t * LANES : (t + 1) * LANES] * scale[mine]
                if low in tiles:
                    lane = lax.broadcasted_iota(jnp.int32, (rows, LANES), 1) + low
                    tiles[low] = jnp.where(lane >= h * DH, piece, tiles[low])
                else:
                    tiles[low] = piece
    return {low: tile.astype(jnp.bfloat16) for low, tile in tiles.items()}


def row_max(parts):
    if all(part.shape == parts[0].shape for part in parts):
        return jnp.max(functools.reduce(jnp.maximum, parts), axis=-1, keepdims=True)
    return functools.reduce(jnp.maximum, [jnp.max(part, axis=-1, keepdims=True) for part in parts])


def columns(row):
    return jnp.broadcast_to(row, (LANES, row.shape[1])).T


def link_bias(mine, theirs):
    return jnp.where(jnp.abs(mine[:, :1] - theirs.T[: mine.shape[0]]) <= 1.5, 0.0, -1e30)


def store_period(base, tiles, out_ref):
    for low, tile in tiles.items():
        out_ref[:, base + low : base + low + LANES] = tile


def ends_kernel(k_ref, v_ref, code_ref, *end_refs):
    even = lax.axis_index("seq") % 2 == 0
    tokens, width = k_ref.shape
    code = columns(code_ref[...])
    for n, ref in enumerate(end_refs):
        most = ref.shape[0]
        tail = even if n == 0 else jnp.logical_not(even)
        first = pl.multiple_of(jnp.where(tail, tokens - most, 0), most)
        ref[:, :width] = k_ref[pl.ds(first, most), :]
        ref[:, width : 2 * width] = v_ref[pl.ds(first, most), :]
        here = jnp.where(tail, code[tokens - most :], code[:most])
        ref[:, 2 * width :] = here.astype(jnp.bfloat16)


def middle_kernel(reach, q_ref, k_ref, v_ref, code_ref, out_ref):
    rows = out_ref.shape[0]
    code = columns(code_ref[...])
    bias = link_bias(code[reach : reach + rows], code)
    period = math.lcm(DH, LANES)
    masks = head_masks(rows, period)
    query = lambda lanes: q_ref[reach : reach + rows, lanes]
    for base in range(0, out_ref.shape[1], period):
        scores = period_scores(base, query, [lambda lanes: k_ref[:, lanes]], masks, period)
        sets = [(bias, lambda lanes: v_ref[:, lanes])]
        store_period(base, mixed_period(base, scores, sets, period), out_ref)


def sides_kernel(reach, ranks, q_ref, k_ref, v_ref, code_ref, one_ref, two_ref, *refs):
    there = neighbours_there(ranks)
    out_ref, keys, values, codes = refs
    tokens, width = q_ref.shape
    near = 2 * reach
    code = columns(code_ref[...])
    even = lax.axis_index("seq") % 2 == 0
    period = math.lcm(DH, LANES)
    masks = head_masks(reach, period)
    blocks = []
    for side, first in ((0, 0), (1, tokens - near)):
        own = slice(first, first + near)
        use_two = even if side == 0 else jnp.logical_not(even)
        halo = jnp.where(use_two, two_ref[...], one_ref[...])
        keys[side, :near] = k_ref[own]
        values[side, :near] = v_ref[own]
        codes[side, :near] = code[own]
        keys[side, near : near + reach] = halo[:, :width]
        values[side, near : near + reach] = halo[:, width : 2 * width]
        codes[side, near : near + reach] = halo[:, 2 * width :].astype(jnp.float32) * there[side]
        spare = keys.shape[1] - near - reach
        if spare:
            for ref in (keys, values, codes):
                ref[side, near + reach :] = jnp.zeros((spare, ref.shape[2]), ref.dtype)
        top = side * (tokens - reach)
        blocks.append((side, top, link_bias(code[top : top + reach], codes[side])))
    for base in range(0, width, period):
        scores = []
        for side, top, bias in blocks:
            query = lambda lanes: q_ref[top : top + reach, lanes]
            key = lambda lanes: keys[side, :, lanes]
            scores.append(period_scores(base, query, [key], masks, period))
        for (side, top, bias), part in zip(blocks, scores):
            sets = [(bias, lambda lanes: values[side, :, lanes])]
            tiles = mixed_period(base, part, sets, period)
            store_period(base, tiles, out_ref.at[side * reach : (side + 1) * reach])


def edge_kernel(reach, ranks, q_ref, k_ref, v_ref, code_ref, *refs):
    below, above = neighbours_there(ranks)
    even = lax.axis_index("seq") % 2 == 0
    there = [jnp.where(even, above, below), jnp.where(even, below, above)]
    halos = refs[:-4]
    out_ref, keys, values, codes = refs[-4:]
    width = q_ref.shape[1]
    code = columns(code_ref[...])
    at = 0
    for n, piece in enumerate(halos):
        rows = piece.shape[0]
        known = there[n] if n < 2 else 1.0
        keys[at : at + rows] = piece[:, :width]
        values[at : at + rows] = piece[:, width : 2 * width]
        codes[at : at + rows] = piece[:, 2 * width :].astype(jnp.float32) * known
        at += rows
    if at < keys.shape[0]:
        for ref in (keys, values, codes):
            ref[at:] = jnp.zeros((ref.shape[0] - at, ref.shape[1]), ref.dtype)
    period = math.lcm(DH, LANES)
    masks = head_masks(q_ref.shape[0], period)
    query = lambda lanes: q_ref[:, lanes]
    pair = [lambda lanes: k_ref[:, lanes], lambda lanes: keys[:, lanes]]
    sets = [
        (link_bias(code, code), lambda lanes: v_ref[:, lanes]),
        (link_bias(code, codes[...]), lambda lanes: values[:, lanes]),
    ]
    for base in range(0, width, period):
        scores = period_scores(base, query, pair, masks, period)
        store_period(base, mixed_period(base, scores, sets, period), out_ref)


def attend_cost(tokens, span, width):
    return pl.CostEstimate(
        flops=HEADS * tokens * span * 2 * LANES * 4,
        bytes_accessed=12 * tokens * width,
        transcendentals=HEADS * tokens * span,
    )


VMEM = pl.BlockSpec(memory_space=pltpu.VMEM)
PARAMS = pltpu.CompilerParams(vmem_limit_bytes=VMEM_LIMIT)


def pack_ends(keys, values, code, most):
    width = keys.shape[1]
    ends = jax.ShapeDtypeStruct((most, 2 * width + LANES), jnp.bfloat16)
    return pl.pallas_call(
        ends_kernel,
        in_specs=[VMEM] * 3,
        out_specs=[VMEM] * 2,
        out_shape=[ends, ends],
        compiler_params=PARAMS,
        cost_estimate=pl.CostEstimate(flops=0, bytes_accessed=16 * most * width, transcendentals=0),
        name="pack_ends",
    )(keys, values, code)


def attend_middle(queries, keys, values, code, reach):
    tokens, width = queries.shape
    return pl.pallas_call(
        functools.partial(middle_kernel, reach),
        in_specs=[VMEM] * 4,
        out_specs=VMEM,
        out_shape=jax.ShapeDtypeStruct((tokens - 2 * reach, width), jnp.bfloat16),
        compiler_params=PARAMS,
        cost_estimate=attend_cost(tokens - 2 * reach, tokens, width),
        name="attend_middle",
    )(queries, keys, values, code)


def attend_edges(queries, keys, values, code, halos, reach):
    tokens, width = queries.shape
    rows = min(tokens, 2 * reach)
    if tokens > 2 * reach:
        kernel = sides_kernel
        held = (2, -(-3 * reach // LANES) * LANES)
    else:
        kernel = edge_kernel
        held = (-(-2 * reach // LANES) * LANES,)
    operands = [queries, keys, values, code, *halos]
    return pl.pallas_call(
        functools.partial(kernel, reach, lax.axis_size("seq")),
        in_specs=[VMEM] * len(operands),
        out_specs=VMEM,
        out_shape=jax.ShapeDtypeStruct((rows, width), jnp.bfloat16),
        scratch_shapes=[
            pltpu.VMEM((*held, width), jnp.bfloat16),
            pltpu.VMEM((*held, width), jnp.bfloat16),
            pltpu.VMEM((*held, LANES), jnp.float32),
        ],
        compiler_params=PARAMS,
        cost_estimate=attend_cost(rows, LANES, width),
        name="attend_edges",
    )(*operands)


def pack_grads_kernel(grad_ref, mark_ref, *refs):
    first_ref, second_ref, sems = refs[-3:]
    half = grad_ref.shape[1] // 2
    copies = []
    for n, ref in enumerate((first_ref, second_ref)):
        copies.append(
            pltpu.make_async_copy(
                grad_ref.at[:, pl.ds(n * half, half)], ref.at[:, pl.ds(0, half)], sems.at[n]
            )
        )
    for copy in copies:
        copy.start()
    place = columns(mark_ref[1:2]).astype(jnp.bfloat16)
    for ref in (first_ref, second_ref):
        ref[:, half:] = place
    for copy in copies:
        copy.wait()


def pack_grads(grads, marks, *others):
    tokens, width = grads.shape
    far = pl.BlockSpec(memory_space=pltpu.HBM)
    return pl.pallas_call(
        pack_grads_kernel,
        in_specs=[far, VMEM] + [far] * len(others),
        out_specs=[VMEM] * 2,
        out_shape=[jax.ShapeDtypeStruct((tokens, width // 2 + LANES), jnp.bfloat16)] * 2,
        scratch_shapes=[pltpu.SemaphoreType.DMA((2,))],
        compiler_params=pltpu.CompilerParams(vmem_limit_bytes=PACK_LIMIT),
        cost_estimate=pl.CostEstimate(flops=0, bytes_accessed=4 * tokens * width, transcendentals=0),
        name="pack_grads",
    )(grads, marks, *others)


def selector(row):
    tokens = row.shape[1]
    wanted = lax.broadcasted_iota(jnp.int32, (tokens, tokens), 0).astype(jnp.float32)
    return jnp.where(wanted == row, 1.0, 0.0)


def sums_kernel(part, sizes, gate_ref, row_ref, mine_ref, theirs_ref, *out_refs):
    half = gate_ref.shape[1] // 2
    place = theirs_ref[:, half:].astype(jnp.float32).T[:1]
    picks = [selector(row).astype(jnp.bfloat16) for row in (row_ref[...], place)]
    theirs = theirs_ref[:, :half]
    summed = jnp.dot(
        jnp.concatenate(picks, axis=1),
        jnp.concatenate((mine_ref[:, :half], theirs), axis=0),
        preferred_element_type=jnp.float32,
    )
    own = jnp.where(lax.axis_index("grp") == part + 1, 1.0, 0.0)
    term = gate_ref[:, part * half : (part + 1) * half] * summed + own * theirs.astype(jnp.float32)
    term = term.astype(jnp.bfloat16)
    at = 0
    for ref, size in zip(out_refs, sizes):
        ref[...] = term[at : at + size]
        at += size


def pair_sums(part, gate, rows, mine, theirs, sizes):
    tokens, half = mine.shape[0], gate.shape[1] // 2
    return pl.pallas_call(
        functools.partial(sums_kernel, part, sizes),
        in_specs=[VMEM] * 4,
        out_specs=[VMEM] * len(sizes),
        out_shape=[jax.ShapeDtypeStruct((size, half), jnp.bfloat16) for size in sizes],
        compiler_params=PARAMS,
        cost_estimate=pl.CostEstimate(
            flops=4 * tokens * tokens * half, bytes_accessed=6 * tokens * half, transcendentals=0
        ),
        name="pair_sums",
    )(gate, rows, mine, theirs)


def piece_spots(tokens, reach, piece):
    if tokens <= 2 * reach:
        return [(0, tokens, 0)]
    if piece == 0:
        return [(reach, tokens - 2 * reach, 0)]
    return [(0, reach, 0), (tokens - reach, reach, reach)]


def picked(spots, row_ref):
    picks = selector(row_ref[...]).T.astype(jnp.bfloat16)
    return jnp.concatenate([picks[:, top : top + size] for top, size, at in spots], axis=1)


def relay_first_kernel(
    spots, later, row_ref, gate_ref, a_ref, b_ref, base_ref, c_ref, d_ref, grad_ref, out_ref, picks_ref, sems
):
    half = a_ref.shape[1]
    copies = []
    for n, ref in enumerate((c_ref, d_ref)):
        to = grad_ref.at[pl.ds(0, ref.shape[0]), pl.ds(n * half, half)]
        copies.append(pltpu.make_async_copy(ref, to, sems.at[n]))
    for copy in copies:
        copy.start()
    picks = picked(spots, row_ref)
    for n, ref in enumerate((a_ref, b_ref)):
        lanes = slice(n * half, (n + 1) * half)
        relayed = jnp.dot(picks, ref[...], preferred_element_type=jnp.float32)
        out_ref[:, lanes] = base_ref[:, lanes].astype(jnp.float32) + gate_ref[:, lanes] * relayed
    picks_ref[...] = picked(later, row_ref)
    for copy in copies:
        copy.wait()


def relay_first(rows, gate, branch, base, totals, spots, later):
    tokens, width = base.shape
    return pl.pallas_call(
        functools.partial(relay_first_kernel, spots, later),
        in_specs=[VMEM] * 7,
        out_specs=[pl.BlockSpec(memory_space=pltpu.HBM), VMEM, VMEM],
        out_shape=[
            jax.ShapeDtypeStruct((tokens, width), jnp.bfloat16),
            jax.ShapeDtypeStruct((tokens, width), jnp.float32),
            jax.ShapeDtypeStruct((tokens, sum(size for top, size, at in later)), jnp.bfloat16),
        ],
        scratch_shapes=[pltpu.SemaphoreType.DMA((2,))],
        compiler_params=PARAMS,
        cost_estimate=pl.CostEstimate(
            flops=2 * tokens * tokens * width, bytes_accessed=24 * tokens * width, transcendentals=0
        ),
        name="relay_first",
    )(rows, gate, *branch, base, *totals)


def relay_last_kernel(chunks, first_row, picks_ref, gate_ref, base_ref, *refs):
    halves = (refs[:3], refs[3:6])
    grad_ref, out_ref, staged, summed, sems, grad_sems = refs[-6:]
    half = refs[0].shape[1]
    rows = refs[0].shape[0]
    group = lax.axis_index("grp")
    holds = (group <= 1, group % 2 == 0)
    copies = []
    for part in (1, 0):
        held_ref, got_ref, total_ref = halves[part]
        other = 1 - part
        summed[other] = jnp.where(holds[part], got_ref[...], total_ref[...])
        to = grad_ref.at[pl.ds(first_row, rows), pl.ds(other * half, half)]
        copies.append(pltpu.make_async_copy(summed.at[other], to, grad_sems.at[other]))
        copies[-1].start()
    step = half // chunks
    for part in (1, 0):
        held_ref, got_ref, total_ref = halves[part]
        for c in range(chunks):
            mine = slice(c * step, (c + 1) * step)
            first = part * half + c * step
            lanes = slice(first, first + step)
            branch = jnp.where(holds[part], held_ref[:, mine], got_ref[:, mine])
            relayed = jnp.dot(picks_ref[...], branch, preferred_element_type=jnp.float32)
            total = base_ref[:, lanes].astype(jnp.float32) + gate_ref[:, lanes] * relayed
            staged[:, lanes] = total.astype(staged.dtype)
            copies.append(
                pltpu.make_async_copy(
                    staged.at[:, pl.ds(first, step)],
                    out_ref.at[:, pl.ds(first, step)],
                    sems.at[part * chunks + c],
                )
            )
            copies[-1].start()
    for copy in copies:
        copy.wait()


def relay_last(picks, gate, base, halves, first_row, grads):
    tokens, width = base.shape
    chunks = 2 if width // 2 % (2 * LANES) == 0 else 1
    far = pl.BlockSpec(memory_space=pltpu.HBM)
    operands = [picks, gate, base, *halves[0], *halves[1]]
    known = len(operands)
    aliases = {}
    if grads is not None:
        aliases[known] = 0
        operands.append(grads)
    return pl.pallas_call(
        functools.partial(relay_last_kernel, chunks, first_row),
        in_specs=[VMEM] * known + [far] * len(aliases),
        out_specs=[far] * 2,
        out_shape=[jax.ShapeDtypeStruct((tokens, width), jnp.bfloat16)] * 2,
        input_output_aliases=aliases,
        scratch_shapes=[
            pltpu.VMEM((tokens, width), jnp.bfloat16),
            pltpu.VMEM((2, *halves[0][0].shape), jnp.bfloat16),
            pltpu.SemaphoreType.DMA((2 * chunks,)),
            pltpu.SemaphoreType.DMA((2,)),
        ],
        compiler_params=PARAMS,
        cost_estimate=pl.CostEstimate(
            flops=2 * tokens * tokens * width, bytes_accessed=12 * tokens * width, transcendentals=0
        ),
        name="relay_last",
    )(*operands)


def whole_gate(gate):
    ranks = lax.axis_size("rep")
    if ranks != 2:
        return lax.all_gather(gate, "rep", axis=0, tiled=True)
    other = lax.ppermute(gate, "rep", [(0, 1), (1, 0)])
    first = lax.axis_index("rep") == 0
    return jnp.concatenate([jnp.where(first, gate, other), jnp.where(first, other, gate)])


SWAP_X, SWAP_Y = [(0, 1), (1, 0), (2, 3), (3, 2)], [(0, 2), (2, 0), (1, 3), (3, 1)]
ROUND_A, ROUND_B = [(0, 1), (1, 3), (3, 2), (2, 0)], [(0, 2), (2, 3), (3, 1), (1, 0)]


def added(a, b):
    return (a.astype(jnp.float32) + b.astype(jnp.float32)).astype(a.dtype)


def local(query_rows, key_rows, value_rows, view_frame, control_row, control_gate, out_grad):
    queries, keys, values = query_rows[0, 0], key_rows[0, 0], value_rows[0, 0]
    tokens, width = queries.shape
    half = width // 2
    ranks = lax.axis_size("seq")
    reach = 2 * (tokens * ranks // 32)
    hops = (reach + tokens - 1) // tokens
    group, rank = lax.axis_index("grp"), lax.axis_index("seq")
    send = lambda block, route: lax.ppermute(block, "grp", route)

    tag = view_frame[0, 0]
    code = tag + 8 * (tag // FRAMES) + 16
    marks = jnp.stack((code, control_row[0, 0] % tokens)).astype(jnp.float32)
    code, rows = marks[:1], marks[1:]
    most = min(tokens, reach)
    even = rank % 2 == 0
    sent_a, sent_b = pack_grads(out_grad[0, 0], marks, queries, keys, values)
    code, sent_a, sent_b = lax.optimization_barrier((code, sent_a, sent_b))
    got_a, got_b = send(sent_a, SWAP_X), send(sent_b, SWAP_Y)
    end_one, end_two = pack_ends(keys, values, code, most)
    code, end_one, end_two = lax.optimization_barrier((code, end_one, end_two))
    own = [attend_middle(queries, keys, values, code, reach)] if tokens > 2 * reach else []
    gate = whole_gate(control_gate)[None]
    halos = [paired(end_one, 0), paired(end_two, 1)]
    for hop in range(2, hops + 1):
        count = min(tokens, reach - (hop - 1) * tokens)
        tail, head = jnp.where(even, end_one, end_two), jnp.where(even, end_two, end_one)
        halos.append(shifted(tail[most - count :], "seq", hop))
        halos.append(shifted(head[:count], "seq", -hop))
    sizes = [piece.shape[0] for piece in own] + [min(tokens, 2 * reach)]
    sums = [
        *pair_sums(0, gate, rows, sent_a, got_a, sizes),
        *pair_sums(1, gate, rows, sent_b, got_b, sizes),
    ]
    count = len(sizes)

    def outgoing(piece, sum_a, sum_b):
        to_a = jnp.where(group == 0, piece[:, :half], jnp.where(group == 1, sum_a, sum_b))
        to_b = jnp.where(group == 0, piece[:, half:], jnp.where(group == 2, sum_b, sum_a))
        return to_a, to_b

    going = [outgoing(own[0], sums[0], sums[count])] if own else []
    code, *ready = lax.optimization_barrier((code, *sums, *(going[0] if going else ())))
    sums = ready[: 2 * count]
    if going:
        going = [ready[2 * count :]]
    own.append(attend_edges(queries, keys, values, code, halos, reach))

    going.append(outgoing(own[-1], sums[count - 1], sums[2 * count - 1]))
    spots = [piece_spots(tokens, reach, n) for n in range(count)]
    order = [
        own[n][at : at + size] for top, size, n, at in sorted(
            (top, size, n, at) for n in range(count) for top, size, at in spots[n]
        )
    ]
    block_out = jnp.concatenate(order, axis=0)
    branch_grad, first_row = None, 0
    picks = (rows[0][:, None] == jnp.arange(tokens)).astype(jnp.bfloat16) if count == 1 else None
    for n, (piece, sum_a, sum_b) in enumerate(zip(own, sums[:count], sums[count:])):
        piece_a, piece_b = piece[:, :half], piece[:, half:]
        one, two = send(going[n][0], ROUND_A), send(going[n][1], ROUND_B)
        total_a = added(sum_a, jnp.where(group == 1, two, one))
        total_b = added(sum_b, jnp.where(group == 2, one, two))
        held_a = jnp.where(group == 0, piece_a, one)
        held_b = jnp.where(group == 0, piece_b, two)
        across = send(jnp.where((group == 0) | (group == 2), held_b, total_a), SWAP_X)
        down = send(jnp.where(group <= 1, held_a, total_b), SWAP_Y)
        branch_a = jnp.where(group <= 1, held_a, down)
        branch_b = jnp.where((group == 0) | (group == 2), held_b, across)
        totals = (
            jnp.where((group == 0) | (group == 2), across, total_a),
            jnp.where(group <= 1, down, total_b),
        )
        if n < count - 1:
            branch_grad, block_out, picks = relay_first(
                rows, gate, (branch_a, branch_b), block_out, totals, spots[n], spots[n + 1]
            )
            first_row = piece.shape[0]
            continue
        halves = ((held_a, down, total_b), (held_b, across, total_a))
        branch_grad, block_out = relay_last(picks, gate, block_out, halves, first_row, branch_grad)
    return (block_out[None, None], branch_grad[None])


def solution(mesh):
    placed = (
        P("rep", "grp", "seq", None),
        P("rep", "grp", "seq", None),
        P("rep", "grp", "seq", None),
        P("rep", "grp", "seq"),
        P("rep", "grp", "seq"),
        P("rep"),
        P("rep", "grp", "seq", None),
    )
    return jax.shard_map(
        local,
        mesh=mesh,
        in_specs=placed,
        out_specs=(P("rep", "grp", "seq", None), P("rep", "seq", None)),
        check_vma=False,
    )
```

```python
import functools
import math

import jax
import jax.numpy as jnp
from jax import lax
from jax.experimental import pallas as pl
from jax.experimental.pallas import tpu as pltpu
from jax.sharding import PartitionSpec as P

HEADS = 32
DH = 80
FRAMES = 20
LANES = 128
VMEM_LIMIT = 32 * 1024 * 1024
PACK_LIMIT = 53 * 1024 * 1024


def shifted(block, axis, distance):
    devices = range(lax.axis_size(axis))
    route = [(i - distance, i) for i in devices if i - distance in devices]
    return lax.ppermute(block, axis, route)


def paired(block, first):
    size, ranks = lax.axis_size("seq"), lax.axis_size("rep")
    route = []
    for i in range(size):
        other = i + 1 if (i - first) % 2 == 0 else i - 1
        for rank in range(ranks):
            if 0 <= other < size:
                route.append((i * ranks + rank, other * ranks + rank))
            elif rank ^ 1 < ranks:
                route.append((i * ranks + rank, i * ranks + (rank ^ 1)))
    return lax.ppermute(block, ("seq", "rep"), route)


def neighbours_there(ranks):
    rank = lax.axis_index("seq")
    return jnp.where(rank > 0, 1.0, 0.0), jnp.where(rank < ranks - 1, 1.0, 0.0)


def lane_windows(heads):
    windows = []
    for head in range(heads):
        first, last = head * DH, (head + 1) * DH
        if windows and last <= windows[-1][0] + 2 * LANES:
            windows[-1][1].append(head)
        else:
            windows.append((first // LANES * LANES, [head]))
    out = []
    for start, members in windows:
        start = min(start, heads * DH - 2 * LANES)
        out.append((start, members))
    return out


def head_masks(rows, period):
    masks = {}
    for start, members in lane_windows(period // DH):
        lane = lax.broadcasted_iota(jnp.int32, (rows, 2 * LANES), 1) + start
        for h in members:
            inside = (lane >= h * DH) & (lane < (h + 1) * DH)
            masks[h] = jnp.where(inside, 1.0, 0.0).astype(jnp.bfloat16)
    return masks


def period_scores(base, query, keys, masks, period):
    scores = []
    for start, members in lane_windows(period // DH):
        lanes = slice(base + start, base + start + 2 * LANES)
        part = query(lanes)
        stacked = jnp.concatenate([part * masks[h] for h in members], axis=0)
        scores.append(
            [
                lax.dot_general(
                    stacked, key(lanes), (((1,), (1,)), ((), ())), preferred_element_type=jnp.float32
                )
                for key in keys
            ]
        )
    return scores


def mixed_period(base, scores, sets, period):
    rows = sets[0][0].shape[0]
    factor = math.log2(math.e) / math.sqrt(DH)
    windows = lane_windows(period // DH)
    weights = []
    for parts, (start, members) in zip(scores, windows):
        parts = [
            part.reshape(len(members), rows, -1) + bias[None]
            for part, (bias, value) in zip(parts, sets)
        ]
        largest = row_max(parts)
        weights.append(
            [
                jnp.exp2((part - largest) * factor).astype(jnp.bfloat16).reshape(len(members) * rows, -1)
                for part in parts
            ]
        )
    tiles = {}
    for parts, (start, members) in zip(weights, windows):
        lanes = slice(base + start, base + start + 2 * LANES)
        mixed = sum(
            jnp.dot(part, value(lanes), preferred_element_type=jnp.float32)
            for part, (bias, value) in zip(parts, sets)
        )
        totals = sum(
            jnp.dot(part, jnp.ones((part.shape[1], LANES), part.dtype), preferred_element_type=jnp.float32)
            for part in parts
        )
        scale = 1.0 / totals
        for n, h in enumerate(members):
            for t in range(2):
                low = start + t * LANES
                if h * DH >= low + LANES or (h + 1) * DH <= low:
                    continue
                mine = slice(n * rows, (n + 1) * rows)
                piece = mixed[mine, t * LANES : (t + 1) * LANES] * scale[mine]
                if low in tiles:
                    lane = lax.broadcasted_iota(jnp.int32, (rows, LANES), 1) + low
                    tiles[low] = jnp.where(lane >= h * DH, piece, tiles[low])
                else:
                    tiles[low] = piece
    return {low: tile.astype(jnp.bfloat16) for low, tile in tiles.items()}


def row_max(parts):
    if all(part.shape == parts[0].shape for part in parts):
        return jnp.max(functools.reduce(jnp.maximum, parts), axis=-1, keepdims=True)
    return functools.reduce(jnp.maximum, [jnp.max(part, axis=-1, keepdims=True) for part in parts])


def columns(row):
    return jnp.broadcast_to(row, (LANES, row.shape[1])).T


def link_bias(mine, theirs):
    return jnp.where(jnp.abs(mine[:, :1] - theirs.T[: mine.shape[0]]) <= 1.5, 0.0, -1e30)


def store_period(base, tiles, out_ref):
    for low, tile in tiles.items():
        out_ref[:, base + low : base + low + LANES] = tile


def ends_kernel(k_ref, v_ref, code_ref, *end_refs):
    even = lax.axis_index("seq") % 2 == 0
    tokens, width = k_ref.shape
    code = columns(code_ref[...])
    for n, ref in enumerate(end_refs):
        most = ref.shape[0]
        tail = even if n == 0 else jnp.logical_not(even)
        first = pl.multiple_of(jnp.where(tail, tokens - most, 0), most)
        ref[:, :width] = k_ref[pl.ds(first, most), :]
        ref[:, width : 2 * width] = v_ref[pl.ds(first, most), :]
        here = jnp.where(tail, code[tokens - most :], code[:most])
        ref[:, 2 * width :] = here.astype(jnp.bfloat16)


def middle_kernel(reach, q_ref, k_ref, v_ref, code_ref, out_ref):
    rows = out_ref.shape[0]
    code = columns(code_ref[...])
    bias = link_bias(code[reach : reach + rows], code)
    period = math.lcm(DH, LANES)
    masks = head_masks(rows, period)
    query = lambda lanes: q_ref[reach : reach + rows, lanes]
    for base in range(0, out_ref.shape[1], period):
        scores = period_scores(base, query, [lambda lanes: k_ref[:, lanes]], masks, period)
        sets = [(bias, lambda lanes: v_ref[:, lanes])]
        store_period(base, mixed_period(base, scores, sets, period), out_ref)


def sides_kernel(reach, ranks, q_ref, k_ref, v_ref, code_ref, one_ref, two_ref, *refs):
    there = neighbours_there(ranks)
    out_ref, keys, values, codes = refs
    tokens, width = q_ref.shape
    near = 2 * reach
    code = columns(code_ref[...])
    even = lax.axis_index("seq") % 2 == 0
    period = math.lcm(DH, LANES)
    masks = head_masks(reach, period)
    blocks = []
    for side, first in ((0, 0), (1, tokens - near)):
        own = slice(first, first + near)
        use_two = even if side == 0 else jnp.logical_not(even)
        halo = jnp.where(use_two, two_ref[...], one_ref[...])
        keys[side, :near] = k_ref[own]
        values[side, :near] = v_ref[own]
        codes[side, :near] = code[own]
        keys[side, near : near + reach] = halo[:, :width]
        values[side, near : near + reach] = halo[:, width : 2 * width]
        codes[side, near : near + reach] = halo[:, 2 * width :].astype(jnp.float32) * there[side]
        spare = keys.shape[1] - near - reach
        if spare:
            for ref in (keys, values, codes):
                ref[side, near + reach :] = jnp.zeros((spare, ref.shape[2]), ref.dtype)
        top = side * (tokens - reach)
        blocks.append((side, top, link_bias(code[top : top + reach], codes[side])))
    for base in range(0, width, period):
        scores = []
        for side, top, bias in blocks:
            query = lambda lanes: q_ref[top : top + reach, lanes]
            key = lambda lanes: keys[side, :, lanes]
            scores.append(period_scores(base, query, [key], masks, period))
        for (side, top, bias), part in zip(blocks, scores):
            sets = [(bias, lambda lanes: values[side, :, lanes])]
            tiles = mixed_period(base, part, sets, period)
            store_period(base, tiles, out_ref.at[side * reach : (side + 1) * reach])


def edge_kernel(reach, ranks, q_ref, k_ref, v_ref, code_ref, *refs):
    below, above = neighbours_there(ranks)
    even = lax.axis_index("seq") % 2 == 0
    there = [jnp.where(even, above, below), jnp.where(even, below, above)]
    halos = refs[:-4]
    out_ref, keys, values, codes = refs[-4:]
    width = q_ref.shape[1]
    code = columns(code_ref[...])
    at = 0
    for n, piece in enumerate(halos):
        rows = piece.shape[0]
        known = there[n] if n < 2 else 1.0
        keys[at : at + rows] = piece[:, :width]
        values[at : at + rows] = piece[:, width : 2 * width]
        codes[at : at + rows] = piece[:, 2 * width :].astype(jnp.float32) * known
        at += rows
    if at < keys.shape[0]:
        for ref in (keys, values, codes):
            ref[at:] = jnp.zeros((ref.shape[0] - at, ref.shape[1]), ref.dtype)
    period = math.lcm(DH, LANES)
    masks = head_masks(q_ref.shape[0], period)
    query = lambda lanes: q_ref[:, lanes]
    pair = [lambda lanes: k_ref[:, lanes], lambda lanes: keys[:, lanes]]
    sets = [
        (link_bias(code, code), lambda lanes: v_ref[:, lanes]),
        (link_bias(code, codes[...]), lambda lanes: values[:, lanes]),
    ]
    for base in range(0, width, period):
        scores = period_scores(base, query, pair, masks, period)
        store_period(base, mixed_period(base, scores, sets, period), out_ref)


def attend_cost(tokens, span, width):
    return pl.CostEstimate(
        flops=HEADS * tokens * span * 2 * LANES * 4,
        bytes_accessed=12 * tokens * width,
        transcendentals=HEADS * tokens * span,
    )


VMEM = pl.BlockSpec(memory_space=pltpu.VMEM)
PARAMS = pltpu.CompilerParams(vmem_limit_bytes=VMEM_LIMIT)


def pack_ends(keys, values, code, most):
    width = keys.shape[1]
    ends = jax.ShapeDtypeStruct((most, 2 * width + LANES), jnp.bfloat16)
    return pl.pallas_call(
        ends_kernel,
        in_specs=[VMEM] * 3,
        out_specs=[VMEM] * 2,
        out_shape=[ends, ends],
        compiler_params=PARAMS,
        cost_estimate=pl.CostEstimate(flops=0, bytes_accessed=16 * most * width, transcendentals=0),
        name="pack_ends",
    )(keys, values, code)


def attend_middle(queries, keys, values, code, reach):
    tokens, width = queries.shape
    return pl.pallas_call(
        functools.partial(middle_kernel, reach),
        in_specs=[VMEM] * 4,
        out_specs=VMEM,
        out_shape=jax.ShapeDtypeStruct((tokens - 2 * reach, width), jnp.bfloat16),
        compiler_params=PARAMS,
        cost_estimate=attend_cost(tokens - 2 * reach, tokens, width),
        name="attend_middle",
    )(queries, keys, values, code)


def attend_edges(queries, keys, values, code, halos, reach):
    tokens, width = queries.shape
    rows = min(tokens, 2 * reach)
    if tokens > 2 * reach:
        kernel = sides_kernel
        held = (2, -(-3 * reach // LANES) * LANES)
    else:
        kernel = edge_kernel
        held = (-(-2 * reach // LANES) * LANES,)
    operands = [queries, keys, values, code, *halos]
    return pl.pallas_call(
        functools.partial(kernel, reach, lax.axis_size("seq")),
        in_specs=[VMEM] * len(operands),
        out_specs=VMEM,
        out_shape=jax.ShapeDtypeStruct((rows, width), jnp.bfloat16),
        scratch_shapes=[
            pltpu.VMEM((*held, width), jnp.bfloat16),
            pltpu.VMEM((*held, width), jnp.bfloat16),
            pltpu.VMEM((*held, LANES), jnp.float32),
        ],
        compiler_params=PARAMS,
        cost_estimate=attend_cost(rows, LANES, width),
        name="attend_edges",
    )(*operands)


def pack_grads_kernel(grad_ref, mark_ref, *refs):
    first_ref, second_ref, sems = refs[-3:]
    half = grad_ref.shape[1] // 2
    copies = []
    for n, ref in enumerate((first_ref, second_ref)):
        copies.append(
            pltpu.make_async_copy(
                grad_ref.at[:, pl.ds(n * half, half)], ref.at[:, pl.ds(0, half)], sems.at[n]
            )
        )
    for copy in copies:
        copy.start()
    place = columns(mark_ref[1:2]).astype(jnp.bfloat16)
    for ref in (first_ref, second_ref):
        ref[:, half:] = place
    for copy in copies:
        copy.wait()


def pack_grads(grads, marks, *others):
    tokens, width = grads.shape
    far = pl.BlockSpec(memory_space=pltpu.HBM)
    return pl.pallas_call(
        pack_grads_kernel,
        in_specs=[far, VMEM] + [far] * len(others),
        out_specs=[VMEM] * 2,
        out_shape=[jax.ShapeDtypeStruct((tokens, width // 2 + LANES), jnp.bfloat16)] * 2,
        scratch_shapes=[pltpu.SemaphoreType.DMA((2,))],
        compiler_params=pltpu.CompilerParams(vmem_limit_bytes=PACK_LIMIT),
        cost_estimate=pl.CostEstimate(flops=0, bytes_accessed=4 * tokens * width, transcendentals=0),
        name="pack_grads",
    )(grads, marks, *others)


def selector(row):
    tokens = row.shape[1]
    wanted = lax.broadcasted_iota(jnp.int32, (tokens, tokens), 0).astype(jnp.float32)
    return jnp.where(wanted == row, 1.0, 0.0)


def sums_kernel(part, sizes, gate_ref, row_ref, mine_ref, theirs_ref, *out_refs):
    half = gate_ref.shape[1] // 2
    place = theirs_ref[:, half:].astype(jnp.float32).T[:1]
    picks = [selector(row).astype(jnp.bfloat16) for row in (row_ref[...], place)]
    theirs = theirs_ref[:, :half]
    summed = jnp.dot(
        jnp.concatenate(picks, axis=1),
        jnp.concatenate((mine_ref[:, :half], theirs), axis=0),
        preferred_element_type=jnp.float32,
    )
    own = jnp.where(lax.axis_index("grp") == part + 1, 1.0, 0.0)
    term = gate_ref[:, part * half : (part + 1) * half] * summed + own * theirs.astype(jnp.float32)
    term = term.astype(jnp.bfloat16)
    at = 0
    for ref, size in zip(out_refs, sizes):
        ref[...] = term[at : at + size]
        at += size


def pair_sums(part, gate, rows, mine, theirs, sizes):
    tokens, half = mine.shape[0], gate.shape[1] // 2
    return pl.pallas_call(
        functools.partial(sums_kernel, part, sizes),
        in_specs=[VMEM] * 4,
        out_specs=[VMEM] * len(sizes),
        out_shape=[jax.ShapeDtypeStruct((size, half), jnp.bfloat16) for size in sizes],
        compiler_params=PARAMS,
        cost_estimate=pl.CostEstimate(
            flops=4 * tokens * tokens * half, bytes_accessed=6 * tokens * half, transcendentals=0
        ),
        name="pair_sums",
    )(gate, rows, mine, theirs)


def piece_spots(tokens, reach, piece):
    if tokens <= 2 * reach:
        return [(0, tokens, 0)]
    if piece == 0:
        return [(reach, tokens - 2 * reach, 0)]
    return [(0, reach, 0), (tokens - reach, reach, reach)]


def picked(spots, row_ref):
    picks = selector(row_ref[...]).T.astype(jnp.bfloat16)
    return jnp.concatenate([picks[:, top : top + size] for top, size, at in spots], axis=1)


def relay_first_kernel(
    spots, later, row_ref, gate_ref, a_ref, b_ref, base_ref, c_ref, d_ref, grad_ref, out_ref, picks_ref, sems
):
    half = a_ref.shape[1]
    copies = []
    for n, ref in enumerate((c_ref, d_ref)):
        to = grad_ref.at[pl.ds(0, ref.shape[0]), pl.ds(n * half, half)]
        copies.append(pltpu.make_async_copy(ref, to, sems.at[n]))
    for copy in copies:
        copy.start()
    picks = picked(spots, row_ref)
    for n, ref in enumerate((a_ref, b_ref)):
        lanes = slice(n * half, (n + 1) * half)
        relayed = jnp.dot(picks, ref[...], preferred_element_type=jnp.float32)
        out_ref[:, lanes] = base_ref[:, lanes].astype(jnp.float32) + gate_ref[:, lanes] * relayed
    picks_ref[...] = picked(later, row_ref)
    for copy in copies:
        copy.wait()


def relay_first(rows, gate, branch, base, totals, spots, later):
    tokens, width = base.shape
    return pl.pallas_call(
        functools.partial(relay_first_kernel, spots, later),
        in_specs=[VMEM] * 7,
        out_specs=[pl.BlockSpec(memory_space=pltpu.HBM), VMEM, VMEM],
        out_shape=[
            jax.ShapeDtypeStruct((tokens, width), jnp.bfloat16),
            jax.ShapeDtypeStruct((tokens, width), jnp.float32),
            jax.ShapeDtypeStruct((tokens, sum(size for top, size, at in later)), jnp.bfloat16),
        ],
        scratch_shapes=[pltpu.SemaphoreType.DMA((2,))],
        compiler_params=PARAMS,
        cost_estimate=pl.CostEstimate(
            flops=2 * tokens * tokens * width, bytes_accessed=24 * tokens * width, transcendentals=0
        ),
        name="relay_first",
    )(rows, gate, *branch, base, *totals)


def relay_last_kernel(
    part, chunks, first_row, picks_ref, gate_ref, held_ref, got_ref, base_ref, total_ref, *refs
):
    grad_ref, out_ref, staged, summed, sems, grad_sem = refs[-6:]
    half = held_ref.shape[1]
    other = 1 - part
    group = lax.axis_index("grp")
    holds = group <= 1 if part == 0 else group % 2 == 0
    summed[...] = jnp.where(holds, got_ref[...], total_ref[...])
    to = grad_ref.at[pl.ds(first_row, total_ref.shape[0]), pl.ds(other * half, half)]
    copies = [pltpu.make_async_copy(summed, to, grad_sem)]
    copies[0].start()
    step = half // chunks
    for c in range(chunks):
        mine = slice(c * step, (c + 1) * step)
        lanes = slice(part * half + c * step, part * half + (c + 1) * step)
        branch = jnp.where(holds, held_ref[:, mine], got_ref[:, mine])
        relayed = jnp.dot(picks_ref[...], branch, preferred_element_type=jnp.float32)
        total = base_ref[:, lanes].astype(jnp.float32) + gate_ref[:, lanes] * relayed
        staged[:, mine] = total.astype(staged.dtype)
        copies.append(
            pltpu.make_async_copy(
                staged.at[:, pl.ds(c * step, step)],
                out_ref.at[:, pl.ds(part * half + c * step, step)],
                sems.at[c],
            )
        )
        copies[-1].start()
    for copy in copies:
        copy.wait()


def relay_last(picks, gate, held, got, base, total, part, first_row, grads, out):
    tokens, width = base.shape
    chunks = 2 if width // 2 % (2 * LANES) == 0 else 1
    far = pl.BlockSpec(memory_space=pltpu.HBM)
    operands = [picks, gate, held, got, base, total]
    aliases = {}
    for n, buffer in enumerate((grads, out)):
        if buffer is not None:
            aliases[len(operands)] = n
            operands.append(buffer)
    return pl.pallas_call(
        functools.partial(relay_last_kernel, part, chunks, first_row),
        in_specs=[VMEM] * 6 + [far] * len(aliases),
        out_specs=[far] * 2,
        out_shape=[jax.ShapeDtypeStruct((tokens, width), jnp.bfloat16)] * 2,
        input_output_aliases=aliases,
        scratch_shapes=[
            pltpu.VMEM((tokens, width // 2), jnp.bfloat16),
            pltpu.VMEM(total.shape, jnp.bfloat16),
            pltpu.SemaphoreType.DMA((chunks,)),
            pltpu.SemaphoreType.DMA,
        ],
        compiler_params=PARAMS,
        cost_estimate=pl.CostEstimate(
            flops=tokens * tokens * width, bytes_accessed=6 * tokens * width, transcendentals=0
        ),
        name="relay_last",
    )(*operands)


def whole_gate(gate):
    ranks = lax.axis_size("rep")
    if ranks != 2:
        return lax.all_gather(gate, "rep", axis=0, tiled=True)
    other = lax.ppermute(gate, "rep", [(0, 1), (1, 0)])
    first = lax.axis_index("rep") == 0
    return jnp.concatenate([jnp.where(first, gate, other), jnp.where(first, other, gate)])


SWAP_X, SWAP_Y = [(0, 1), (1, 0), (2, 3), (3, 2)], [(0, 2), (2, 0), (1, 3), (3, 1)]
ROUND_A, ROUND_B = [(0, 1), (1, 3), (3, 2), (2, 0)], [(0, 2), (2, 3), (3, 1), (1, 0)]


def sent_both(to_a, to_b, route_a, route_b):
    ranks = lax.axis_size("rep")
    odd = lax.axis_index("rep") % 2 == 1

    def mixed(block, even_route, odd_route):
        route = []
        for rank in range(ranks):
            for source, target in odd_route if rank % 2 else even_route:
                route.append((source * ranks + rank, target * ranks + rank))
        return lax.ppermute(block, ("grp", "rep"), route)

    first = mixed(jnp.where(odd, to_b, to_a), route_a, route_b)
    second = mixed(jnp.where(odd, to_a, to_b), route_b, route_a)
    return jnp.where(odd, second, first), jnp.where(odd, first, second)


def added(a, b):
    return (a.astype(jnp.float32) + b.astype(jnp.float32)).astype(a.dtype)


def local(query_rows, key_rows, value_rows, view_frame, control_row, control_gate, out_grad):
    queries, keys, values = query_rows[0, 0], key_rows[0, 0], value_rows[0, 0]
    tokens, width = queries.shape
    half = width // 2
    ranks = lax.axis_size("seq")
    reach = 2 * (tokens * ranks // 32)
    hops = (reach + tokens - 1) // tokens
    group, rank = lax.axis_index("grp"), lax.axis_index("seq")
    send = lambda block, route: lax.ppermute(block, "grp", route)

    tag = view_frame[0, 0]
    code = tag + 8 * (tag // FRAMES) + 16
    marks = jnp.stack((code, control_row[0, 0] % tokens)).astype(jnp.float32)
    code, rows = marks[:1], marks[1:]
    most = min(tokens, reach)
    even = rank % 2 == 0
    sent_a, sent_b = pack_grads(out_grad[0, 0], marks, queries, keys, values)
    code, sent_a, sent_b = lax.optimization_barrier((code, sent_a, sent_b))
    got_a, got_b = send(sent_a, SWAP_X), send(sent_b, SWAP_Y)
    end_one, end_two = pack_ends(keys, values, code, most)
    code, end_one, end_two = lax.optimization_barrier((code, end_one, end_two))
    own = [attend_middle(queries, keys, values, code, reach)] if tokens > 2 * reach else []
    gate = whole_gate(control_gate)[None]
    halos = [paired(end_one, 0), paired(end_two, 1)]
    for hop in range(2, hops + 1):
        count = min(tokens, reach - (hop - 1) * tokens)
        tail, head = jnp.where(even, end_one, end_two), jnp.where(even, end_two, end_one)
        halos.append(shifted(tail[most - count :], "seq", hop))
        halos.append(shifted(head[:count], "seq", -hop))
    sizes = [piece.shape[0] for piece in own] + [min(tokens, 2 * reach)]
    sums = [
        *pair_sums(0, gate, rows, sent_a, got_a, sizes),
        *pair_sums(1, gate, rows, sent_b, got_b, sizes),
    ]
    count = len(sizes)

    def outgoing(piece, sum_a, sum_b):
        to_a = jnp.where(group == 0, piece[:, :half], jnp.where(group == 1, sum_a, sum_b))
        to_b = jnp.where(group == 0, piece[:, half:], jnp.where(group == 2, sum_b, sum_a))
        return to_a, to_b

    going = [outgoing(own[0], sums[0], sums[count])] if own else []
    code, *ready = lax.optimization_barrier((code, *sums, *(going[0] if going else ())))
    sums = ready[: 2 * count]
    if going:
        going = [ready[2 * count :]]
    own.append(attend_edges(queries, keys, values, code, halos, reach))

    going.append(outgoing(own[-1], sums[count - 1], sums[2 * count - 1]))
    spots = [piece_spots(tokens, reach, n) for n in range(count)]
    order = [
        own[n][at : at + size] for top, size, n, at in sorted(
            (top, size, n, at) for n in range(count) for top, size, at in spots[n]
        )
    ]
    block_out = jnp.concatenate(order, axis=0)
    branch_grad, first_row = None, 0
    picks = (rows[0][:, None] == jnp.arange(tokens)).astype(jnp.bfloat16) if count == 1 else None
    for n, (piece, sum_a, sum_b) in enumerate(zip(own, sums[:count], sums[count:])):
        piece_a, piece_b = piece[:, :half], piece[:, half:]
        one, two = sent_both(*going[n], ROUND_A, ROUND_B)
        total_a = added(sum_a, jnp.where(group == 1, two, one))
        total_b = added(sum_b, jnp.where(group == 2, one, two))
        held_a = jnp.where(group == 0, piece_a, one)
        held_b = jnp.where(group == 0, piece_b, two)
        to_across = jnp.where((group == 0) | (group == 2), held_b, total_a)
        to_down = jnp.where(group <= 1, held_a, total_b)
        if n < count - 1:
            across, down = sent_both(to_across, to_down, SWAP_X, SWAP_Y)
        else:
            across, down = send(to_across, SWAP_X), send(to_down, SWAP_Y)
        branch_a = jnp.where(group <= 1, held_a, down)
        branch_b = jnp.where((group == 0) | (group == 2), held_b, across)
        totals = (
            jnp.where((group == 0) | (group == 2), across, total_a),
            jnp.where(group <= 1, down, total_b),
        )
        if n < count - 1:
            branch_grad, block_out, picks = relay_first(
                rows, gate, (branch_a, branch_b), block_out, totals, spots[n], spots[n + 1]
            )
            first_row = piece.shape[0]
            continue
        base, block_out = block_out, None
        ends = ((held_a, down, total_b), (held_b, across, total_a))
        for part in (1, 0):
            held, got, total = ends[part]
            branch_grad, block_out = relay_last(
                picks, gate, held, got, base, total, part, first_row, branch_grad, block_out
            )
    return (block_out[None, None], branch_grad[None])


def solution(mesh):
    placed = (
        P("rep", "grp", "seq", None),
        P("rep", "grp", "seq", None),
        P("rep", "grp", "seq", None),
        P("rep", "grp", "seq"),
        P("rep", "grp", "seq"),
        P("rep"),
        P("rep", "grp", "seq", None),
    )
    return jax.shard_map(
        local,
        mesh=mesh,
        in_specs=placed,
        out_specs=(P("rep", "grp", "seq", None), P("rep", "seq", None)),
        check_vma=False,
    )
```

```python
import functools
import math

import jax
import jax.numpy as jnp
from jax import lax
from jax.experimental import pallas as pl
from jax.experimental.pallas import tpu as pltpu
from jax.sharding import PartitionSpec as P

HEADS = 32
DH = 80
FRAMES = 20
LANES = 128
VMEM_LIMIT = 32 * 1024 * 1024
PACK_LIMIT = 53 * 1024 * 1024


def shifted(block, axis, distance):
    devices = range(lax.axis_size(axis))
    route = [(i - distance, i) for i in devices if i - distance in devices]
    return lax.ppermute(block, axis, route)


def paired(block, first):
    size, ranks = lax.axis_size("seq"), lax.axis_size("rep")
    route = []
    for i in range(size):
        other = i + 1 if (i - first) % 2 == 0 else i - 1
        for rank in range(ranks):
            if 0 <= other < size:
                route.append((i * ranks + rank, other * ranks + rank))
            elif rank ^ 1 < ranks:
                route.append((i * ranks + rank, i * ranks + (rank ^ 1)))
    return lax.ppermute(block, ("seq", "rep"), route)


def neighbours_there(ranks):
    rank = lax.axis_index("seq")
    return jnp.where(rank > 0, 1.0, 0.0), jnp.where(rank < ranks - 1, 1.0, 0.0)


def lane_windows(heads):
    windows = []
    for head in range(heads):
        first, last = head * DH, (head + 1) * DH
        if windows and last <= windows[-1][0] + 2 * LANES:
            windows[-1][1].append(head)
        else:
            windows.append((first // LANES * LANES, [head]))
    out = []
    for start, members in windows:
        start = min(start, heads * DH - 2 * LANES)
        out.append((start, members))
    return out


def head_masks(rows, period):
    masks = {}
    for start, members in lane_windows(period // DH):
        lane = lax.broadcasted_iota(jnp.int32, (rows, 2 * LANES), 1) + start
        for h in members:
            inside = (lane >= h * DH) & (lane < (h + 1) * DH)
            masks[h] = jnp.where(inside, 1.0, 0.0).astype(jnp.bfloat16)
    return masks


def period_scores(base, query, keys, masks, period):
    scores = []
    for start, members in lane_windows(period // DH):
        lanes = slice(base + start, base + start + 2 * LANES)
        part = query(lanes)
        stacked = jnp.concatenate([part * masks[h] for h in members], axis=0)
        scores.append(
            [
                lax.dot_general(
                    stacked, key(lanes), (((1,), (1,)), ((), ())), preferred_element_type=jnp.float32
                )
                for key in keys
            ]
        )
    return scores


def mixed_period(base, scores, sets, period):
    rows = sets[0][0].shape[0]
    factor = math.log2(math.e) / math.sqrt(DH)
    windows = lane_windows(period // DH)
    weights = []
    for parts, (start, members) in zip(scores, windows):
        parts = [
            part.reshape(len(members), rows, -1) + bias[None]
            for part, (bias, value) in zip(parts, sets)
        ]
        largest = row_max(parts)
        weights.append(
            [
                jnp.exp2((part - largest) * factor).astype(jnp.bfloat16).reshape(len(members) * rows, -1)
                for part in parts
            ]
        )
    tiles = {}
    for parts, (start, members) in zip(weights, windows):
        lanes = slice(base + start, base + start + 2 * LANES)
        mixed = sum(
            jnp.dot(part, value(lanes), preferred_element_type=jnp.float32)
            for part, (bias, value) in zip(parts, sets)
        )
        totals = sum(
            jnp.dot(part, jnp.ones((part.shape[1], LANES), part.dtype), preferred_element_type=jnp.float32)
            for part in parts
        )
        scale = 1.0 / totals
        for n, h in enumerate(members):
            for t in range(2):
                low = start + t * LANES
                if h * DH >= low + LANES or (h + 1) * DH <= low:
                    continue
                mine = slice(n * rows, (n + 1) * rows)
                piece = mixed[mine, t * LANES : (t + 1) * LANES] * scale[mine]
                if low in tiles:
                    lane = lax.broadcasted_iota(jnp.int32, (rows, LANES), 1) + low
                    tiles[low] = jnp.where(lane >= h * DH, piece, tiles[low])
                else:
                    tiles[low] = piece
    return {low: tile.astype(jnp.bfloat16) for low, tile in tiles.items()}


def row_max(parts):
    if all(part.shape == parts[0].shape for part in parts):
        return jnp.max(functools.reduce(jnp.maximum, parts), axis=-1, keepdims=True)
    return functools.reduce(jnp.maximum, [jnp.max(part, axis=-1, keepdims=True) for part in parts])


def columns(row):
    return jnp.broadcast_to(row, (LANES, row.shape[1])).T


def link_bias(mine, theirs):
    return jnp.where(jnp.abs(mine[:, :1] - theirs.T[: mine.shape[0]]) <= 1.5, 0.0, -1e30)


def store_period(base, tiles, out_ref):
    for low, tile in tiles.items():
        out_ref[:, base + low : base + low + LANES] = tile


def ends_kernel(k_ref, v_ref, code_ref, *end_refs):
    even = lax.axis_index("seq") % 2 == 0
    tokens, width = k_ref.shape
    code = columns(code_ref[...])
    for n, ref in enumerate(end_refs):
        most = ref.shape[0]
        tail = even if n == 0 else jnp.logical_not(even)
        first = pl.multiple_of(jnp.where(tail, tokens - most, 0), most)
        ref[:, :width] = k_ref[pl.ds(first, most), :]
        ref[:, width : 2 * width] = v_ref[pl.ds(first, most), :]
        here = jnp.where(tail, code[tokens - most :], code[:most])
        ref[:, 2 * width :] = here.astype(jnp.bfloat16)


def middle_kernel(reach, q_ref, k_ref, v_ref, code_ref, out_ref):
    rows = out_ref.shape[0]
    code = columns(code_ref[...])
    bias = link_bias(code[reach : reach + rows], code)
    period = math.lcm(DH, LANES)
    masks = head_masks(rows, period)
    query = lambda lanes: q_ref[reach : reach + rows, lanes]
    for base in range(0, out_ref.shape[1], period):
        scores = period_scores(base, query, [lambda lanes: k_ref[:, lanes]], masks, period)
        sets = [(bias, lambda lanes: v_ref[:, lanes])]
        store_period(base, mixed_period(base, scores, sets, period), out_ref)


def sides_kernel(reach, ranks, q_ref, k_ref, v_ref, code_ref, one_ref, two_ref, *refs):
    there = neighbours_there(ranks)
    out_ref, keys, values, codes = refs
    tokens, width = q_ref.shape
    near = 2 * reach
    code = columns(code_ref[...])
    even = lax.axis_index("seq") % 2 == 0
    period = math.lcm(DH, LANES)
    masks = head_masks(reach, period)
    blocks = []
    for side, first in ((0, 0), (1, tokens - near)):
        own = slice(first, first + near)
        use_two = even if side == 0 else jnp.logical_not(even)
        halo = jnp.where(use_two, two_ref[...], one_ref[...])
        keys[side, :near] = k_ref[own]
        values[side, :near] = v_ref[own]
        codes[side, :near] = code[own]
        keys[side, near : near + reach] = halo[:, :width]
        values[side, near : near + reach] = halo[:, width : 2 * width]
        codes[side, near : near + reach] = halo[:, 2 * width :].astype(jnp.float32) * there[side]
        spare = keys.shape[1] - near - reach
        if spare:
            for ref in (keys, values, codes):
                ref[side, near + reach :] = jnp.zeros((spare, ref.shape[2]), ref.dtype)
        top = side * (tokens - reach)
        blocks.append((side, top, link_bias(code[top : top + reach], codes[side])))
    for base in range(0, width, period):
        scores = []
        for side, top, bias in blocks:
            query = lambda lanes: q_ref[top : top + reach, lanes]
            key = lambda lanes: keys[side, :, lanes]
            scores.append(period_scores(base, query, [key], masks, period))
        for (side, top, bias), part in zip(blocks, scores):
            sets = [(bias, lambda lanes: values[side, :, lanes])]
            tiles = mixed_period(base, part, sets, period)
            store_period(base, tiles, out_ref.at[side * reach : (side + 1) * reach])


def edge_kernel(reach, ranks, q_ref, k_ref, v_ref, code_ref, *refs):
    below, above = neighbours_there(ranks)
    even = lax.axis_index("seq") % 2 == 0
    there = [jnp.where(even, above, below), jnp.where(even, below, above)]
    halos = refs[:-4]
    out_ref, keys, values, codes = refs[-4:]
    width = q_ref.shape[1]
    code = columns(code_ref[...])
    at = 0
    for n, piece in enumerate(halos):
        rows = piece.shape[0]
        known = there[n] if n < 2 else 1.0
        keys[at : at + rows] = piece[:, :width]
        values[at : at + rows] = piece[:, width : 2 * width]
        codes[at : at + rows] = piece[:, 2 * width :].astype(jnp.float32) * known
        at += rows
    if at < keys.shape[0]:
        for ref in (keys, values, codes):
            ref[at:] = jnp.zeros((ref.shape[0] - at, ref.shape[1]), ref.dtype)
    period = math.lcm(DH, LANES)
    masks = head_masks(q_ref.shape[0], period)
    query = lambda lanes: q_ref[:, lanes]
    pair = [lambda lanes: k_ref[:, lanes], lambda lanes: keys[:, lanes]]
    sets = [
        (link_bias(code, code), lambda lanes: v_ref[:, lanes]),
        (link_bias(code, codes[...]), lambda lanes: values[:, lanes]),
    ]
    for base in range(0, width, period):
        scores = period_scores(base, query, pair, masks, period)
        store_period(base, mixed_period(base, scores, sets, period), out_ref)


def attend_cost(tokens, span, width):
    return pl.CostEstimate(
        flops=HEADS * tokens * span * 2 * LANES * 4,
        bytes_accessed=12 * tokens * width,
        transcendentals=HEADS * tokens * span,
    )


VMEM = pl.BlockSpec(memory_space=pltpu.VMEM)
PARAMS = pltpu.CompilerParams(vmem_limit_bytes=VMEM_LIMIT)


def pack_ends(keys, values, code, most):
    width = keys.shape[1]
    ends = jax.ShapeDtypeStruct((most, 2 * width + LANES), jnp.bfloat16)
    return pl.pallas_call(
        ends_kernel,
        in_specs=[VMEM] * 3,
        out_specs=[VMEM] * 2,
        out_shape=[ends, ends],
        compiler_params=PARAMS,
        cost_estimate=pl.CostEstimate(flops=0, bytes_accessed=16 * most * width, transcendentals=0),
        name="pack_ends",
    )(keys, values, code)


def attend_middle(queries, keys, values, code, reach):
    tokens, width = queries.shape
    return pl.pallas_call(
        functools.partial(middle_kernel, reach),
        in_specs=[VMEM] * 4,
        out_specs=VMEM,
        out_shape=jax.ShapeDtypeStruct((tokens - 2 * reach, width), jnp.bfloat16),
        compiler_params=PARAMS,
        cost_estimate=attend_cost(tokens - 2 * reach, tokens, width),
        name="attend_middle",
    )(queries, keys, values, code)


def attend_edges(queries, keys, values, code, halos, reach):
    tokens, width = queries.shape
    rows = min(tokens, 2 * reach)
    if tokens > 2 * reach:
        kernel = sides_kernel
        held = (2, -(-3 * reach // LANES) * LANES)
    else:
        kernel = edge_kernel
        held = (-(-2 * reach // LANES) * LANES,)
    operands = [queries, keys, values, code, *halos]
    return pl.pallas_call(
        functools.partial(kernel, reach, lax.axis_size("seq")),
        in_specs=[VMEM] * len(operands),
        out_specs=VMEM,
        out_shape=jax.ShapeDtypeStruct((rows, width), jnp.bfloat16),
        scratch_shapes=[
            pltpu.VMEM((*held, width), jnp.bfloat16),
            pltpu.VMEM((*held, width), jnp.bfloat16),
            pltpu.VMEM((*held, LANES), jnp.float32),
        ],
        compiler_params=PARAMS,
        cost_estimate=attend_cost(rows, LANES, width),
        name="attend_edges",
    )(*operands)


def pack_grads_kernel(grad_ref, mark_ref, *refs):
    first_ref, second_ref, sems = refs[-3:]
    half = grad_ref.shape[1] // 2
    copies = []
    for n, ref in enumerate((first_ref, second_ref)):
        copies.append(
            pltpu.make_async_copy(
                grad_ref.at[:, pl.ds(n * half, half)], ref.at[:, pl.ds(0, half)], sems.at[n]
            )
        )
    for copy in copies:
        copy.start()
    place = columns(mark_ref[1:2]).astype(jnp.bfloat16)
    for ref in (first_ref, second_ref):
        ref[:, half:] = place
    for copy in copies:
        copy.wait()


def pack_grads(grads, marks, *others):
    tokens, width = grads.shape
    far = pl.BlockSpec(memory_space=pltpu.HBM)
    return pl.pallas_call(
        pack_grads_kernel,
        in_specs=[far, VMEM] + [far] * len(others),
        out_specs=[VMEM] * 2,
        out_shape=[jax.ShapeDtypeStruct((tokens, width // 2 + LANES), jnp.bfloat16)] * 2,
        scratch_shapes=[pltpu.SemaphoreType.DMA((2,))],
        compiler_params=pltpu.CompilerParams(vmem_limit_bytes=PACK_LIMIT),
        cost_estimate=pl.CostEstimate(flops=0, bytes_accessed=4 * tokens * width, transcendentals=0),
        name="pack_grads",
    )(grads, marks, *others)


def selector(row):
    tokens = row.shape[1]
    wanted = lax.broadcasted_iota(jnp.int32, (tokens, tokens), 0).astype(jnp.float32)
    return jnp.where(wanted == row, 1.0, 0.0)


def sums_kernel(part, sizes, gate_ref, row_ref, mine_ref, theirs_ref, *out_refs):
    half = gate_ref.shape[1] // 2
    place = theirs_ref[:, half:].astype(jnp.float32).T[:1]
    picks = [selector(row).astype(jnp.bfloat16) for row in (row_ref[...], place)]
    theirs = theirs_ref[:, :half]
    summed = jnp.dot(
        jnp.concatenate(picks, axis=1),
        jnp.concatenate((mine_ref[:, :half], theirs), axis=0),
        preferred_element_type=jnp.float32,
    )
    own = jnp.where(lax.axis_index("grp") == part + 1, 1.0, 0.0)
    term = gate_ref[:, part * half : (part + 1) * half] * summed + own * theirs.astype(jnp.float32)
    term = term.astype(jnp.bfloat16)
    at = 0
    for ref, size in zip(out_refs, sizes):
        ref[...] = term[at : at + size]
        at += size


def pair_sums(part, gate, rows, mine, theirs, sizes):
    tokens, half = mine.shape[0], gate.shape[1] // 2
    return pl.pallas_call(
        functools.partial(sums_kernel, part, sizes),
        in_specs=[VMEM] * 4,
        out_specs=[VMEM] * len(sizes),
        out_shape=[jax.ShapeDtypeStruct((size, half), jnp.bfloat16) for size in sizes],
        compiler_params=PARAMS,
        cost_estimate=pl.CostEstimate(
            flops=4 * tokens * tokens * half, bytes_accessed=6 * tokens * half, transcendentals=0
        ),
        name="pair_sums",
    )(gate, rows, mine, theirs)


def piece_spots(tokens, reach, piece):
    if tokens <= 2 * reach:
        return [(0, tokens, 0)]
    if piece == 0:
        return [(reach, tokens - 2 * reach, 0)]
    return [(0, reach, 0), (tokens - reach, reach, reach)]


def picked(spots, row_ref):
    picks = selector(row_ref[...]).T.astype(jnp.bfloat16)
    return jnp.concatenate([picks[:, top : top + size] for top, size, at in spots], axis=1)


def relay_first_kernel(
    spots, later, row_ref, gate_ref, a_ref, b_ref, base_ref, c_ref, d_ref, grad_ref, out_ref, picks_ref, sems
):
    half = a_ref.shape[1]
    copies = []
    for n, ref in enumerate((c_ref, d_ref)):
        to = grad_ref.at[pl.ds(0, ref.shape[0]), pl.ds(n * half, half)]
        copies.append(pltpu.make_async_copy(ref, to, sems.at[n]))
    for copy in copies:
        copy.start()
    picks = picked(spots, row_ref)
    for n, ref in enumerate((a_ref, b_ref)):
        lanes = slice(n * half, (n + 1) * half)
        relayed = jnp.dot(picks, ref[...], preferred_element_type=jnp.float32)
        out_ref[:, lanes] = base_ref[:, lanes].astype(jnp.float32) + gate_ref[:, lanes] * relayed
    picks_ref[...] = picked(later, row_ref)
    for copy in copies:
        copy.wait()


def relay_first(rows, gate, branch, base, totals, spots, later):
    tokens, width = base.shape
    return pl.pallas_call(
        functools.partial(relay_first_kernel, spots, later),
        in_specs=[VMEM] * 7,
        out_specs=[pl.BlockSpec(memory_space=pltpu.HBM), VMEM, VMEM],
        out_shape=[
            jax.ShapeDtypeStruct((tokens, width), jnp.bfloat16),
            jax.ShapeDtypeStruct((tokens, width), jnp.float32),
            jax.ShapeDtypeStruct((tokens, sum(size for top, size, at in later)), jnp.bfloat16),
        ],
        scratch_shapes=[pltpu.SemaphoreType.DMA((2,))],
        compiler_params=PARAMS,
        cost_estimate=pl.CostEstimate(
            flops=2 * tokens * tokens * width, bytes_accessed=24 * tokens * width, transcendentals=0
        ),
        name="relay_first",
    )(rows, gate, *branch, base, *totals)


def relay_last_kernel(chunks, first_row, picks_ref, gate_ref, base_ref, *refs):
    halves = (refs[:3], refs[3:6])
    grad_ref, out_ref, staged, summed, sems, grad_sems = refs[-6:]
    half = refs[0].shape[1]
    rows = refs[0].shape[0]
    group = lax.axis_index("grp")
    holds = (group <= 1, group % 2 == 0)
    copies = []
    for part in (1, 0):
        held_ref, got_ref, total_ref = halves[part]
        other = 1 - part
        summed[other] = jnp.where(holds[part], got_ref[...], total_ref[...])
        to = grad_ref.at[pl.ds(first_row, rows), pl.ds(other * half, half)]
        copies.append(pltpu.make_async_copy(summed.at[other], to, grad_sems.at[other]))
        copies[-1].start()
    step = half // chunks
    for part in (1, 0):
        held_ref, got_ref, total_ref = halves[part]
        for c in range(chunks):
            mine = slice(c * step, (c + 1) * step)
            first = part * half + c * step
            lanes = slice(first, first + step)
            branch = jnp.where(holds[part], held_ref[:, mine], got_ref[:, mine])
            relayed = jnp.dot(picks_ref[...], branch, preferred_element_type=jnp.float32)
            total = base_ref[:, lanes].astype(jnp.float32) + gate_ref[:, lanes] * relayed
            staged[:, lanes] = total.astype(staged.dtype)
            copies.append(
                pltpu.make_async_copy(
                    staged.at[:, pl.ds(first, step)],
                    out_ref.at[:, pl.ds(first, step)],
                    sems.at[part * chunks + c],
                )
            )
            copies[-1].start()
    for copy in copies:
        copy.wait()


def relay_last(picks, gate, base, halves, first_row, grads):
    tokens, width = base.shape
    chunks = 2 if width // 2 % (2 * LANES) == 0 else 1
    far = pl.BlockSpec(memory_space=pltpu.HBM)
    operands = [picks, gate, base, *halves[0], *halves[1]]
    known = len(operands)
    aliases = {}
    if grads is not None:
        aliases[known] = 0
        operands.append(grads)
    return pl.pallas_call(
        functools.partial(relay_last_kernel, chunks, first_row),
        in_specs=[VMEM] * known + [far] * len(aliases),
        out_specs=[far] * 2,
        out_shape=[jax.ShapeDtypeStruct((tokens, width), jnp.bfloat16)] * 2,
        input_output_aliases=aliases,
        scratch_shapes=[
            pltpu.VMEM((tokens, width), jnp.bfloat16),
            pltpu.VMEM((2, *halves[0][0].shape), jnp.bfloat16),
            pltpu.SemaphoreType.DMA((2 * chunks,)),
            pltpu.SemaphoreType.DMA((2,)),
        ],
        compiler_params=PARAMS,
        cost_estimate=pl.CostEstimate(
            flops=2 * tokens * tokens * width, bytes_accessed=12 * tokens * width, transcendentals=0
        ),
        name="relay_last",
    )(*operands)


def whole_gate(gate):
    ranks = lax.axis_size("rep")
    if ranks != 2:
        return lax.all_gather(gate, "rep", axis=0, tiled=True)
    other = lax.ppermute(gate, "rep", [(0, 1), (1, 0)])
    first = lax.axis_index("rep") == 0
    return jnp.concatenate([jnp.where(first, gate, other), jnp.where(first, other, gate)])


SWAP_X, SWAP_Y = [(0, 1), (1, 0), (2, 3), (3, 2)], [(0, 2), (2, 0), (1, 3), (3, 1)]
ROUND_A, ROUND_B = [(0, 1), (1, 3), (3, 2), (2, 0)], [(0, 2), (2, 3), (3, 1), (1, 0)]


def sent_both(to_a, to_b, route_a, route_b):
    ranks = lax.axis_size("rep")
    odd = lax.axis_index("rep") % 2 == 1

    def mixed(block, even_route, odd_route):
        route = []
        for rank in range(ranks):
            for source, target in odd_route if rank % 2 else even_route:
                route.append((source * ranks + rank, target * ranks + rank))
        return lax.ppermute(block, ("grp", "rep"), route)

    first = mixed(jnp.where(odd, to_b, to_a), route_a, route_b)
    second = mixed(jnp.where(odd, to_a, to_b), route_b, route_a)
    return jnp.where(odd, second, first), jnp.where(odd, first, second)


def added(a, b):
    return (a.astype(jnp.float32) + b.astype(jnp.float32)).astype(a.dtype)


def local(query_rows, key_rows, value_rows, view_frame, control_row, control_gate, out_grad):
    queries, keys, values = query_rows[0, 0], key_rows[0, 0], value_rows[0, 0]
    tokens, width = queries.shape
    half = width // 2
    ranks = lax.axis_size("seq")
    reach = 2 * (tokens * ranks // 32)
    hops = (reach + tokens - 1) // tokens
    group, rank = lax.axis_index("grp"), lax.axis_index("seq")
    send = lambda block, route: lax.ppermute(block, "grp", route)

    tag = view_frame[0, 0]
    code = tag + 8 * (tag // FRAMES) + 16
    marks = jnp.stack((code, control_row[0, 0] % tokens)).astype(jnp.float32)
    code, rows = marks[:1], marks[1:]
    most = min(tokens, reach)
    even = rank % 2 == 0
    sent_a, sent_b = pack_grads(out_grad[0, 0], marks, queries, keys, values)
    code, sent_a, sent_b = lax.optimization_barrier((code, sent_a, sent_b))
    got_a, got_b = send(sent_a, SWAP_X), send(sent_b, SWAP_Y)
    end_one, end_two = pack_ends(keys, values, code, most)
    code, end_one, end_two = lax.optimization_barrier((code, end_one, end_two))
    own = [attend_middle(queries, keys, values, code, reach)] if tokens > 2 * reach else []
    gate = whole_gate(control_gate)[None]
    halos = [paired(end_one, 0), paired(end_two, 1)]
    for hop in range(2, hops + 1):
        count = min(tokens, reach - (hop - 1) * tokens)
        tail, head = jnp.where(even, end_one, end_two), jnp.where(even, end_two, end_one)
        halos.append(shifted(tail[most - count :], "seq", hop))
        halos.append(shifted(head[:count], "seq", -hop))
    sizes = [piece.shape[0] for piece in own] + [min(tokens, 2 * reach)]
    sums = [
        *pair_sums(0, gate, rows, sent_a, got_a, sizes),
        *pair_sums(1, gate, rows, sent_b, got_b, sizes),
    ]
    count = len(sizes)

    def outgoing(piece, sum_a, sum_b):
        to_a = jnp.where(group == 0, piece[:, :half], jnp.where(group == 1, sum_a, sum_b))
        to_b = jnp.where(group == 0, piece[:, half:], jnp.where(group == 2, sum_b, sum_a))
        return to_a, to_b

    going = [outgoing(own[0], sums[0], sums[count])] if own else []
    code, *ready = lax.optimization_barrier((code, *sums, *(going[0] if going else ())))
    sums = ready[: 2 * count]
    if going:
        going = [ready[2 * count :]]
    own.append(attend_edges(queries, keys, values, code, halos, reach))

    going.append(outgoing(own[-1], sums[count - 1], sums[2 * count - 1]))
    spots = [piece_spots(tokens, reach, n) for n in range(count)]
    order = [
        own[n][at : at + size] for top, size, n, at in sorted(
            (top, size, n, at) for n in range(count) for top, size, at in spots[n]
        )
    ]
    block_out = jnp.concatenate(order, axis=0)
    branch_grad, first_row = None, 0
    picks = (rows[0][:, None] == jnp.arange(tokens)).astype(jnp.bfloat16) if count == 1 else None
    for n, (piece, sum_a, sum_b) in enumerate(zip(own, sums[:count], sums[count:])):
        piece_a, piece_b = piece[:, :half], piece[:, half:]
        one, two = sent_both(*going[n], ROUND_A, ROUND_B)
        total_a = added(sum_a, jnp.where(group == 1, two, one))
        total_b = added(sum_b, jnp.where(group == 2, one, two))
        held_a = jnp.where(group == 0, piece_a, one)
        held_b = jnp.where(group == 0, piece_b, two)
        to_across = jnp.where((group == 0) | (group == 2), held_b, total_a)
        to_down = jnp.where(group <= 1, held_a, total_b)
        across, down = sent_both(to_across, to_down, SWAP_X, SWAP_Y)
        branch_a = jnp.where(group <= 1, held_a, down)
        branch_b = jnp.where((group == 0) | (group == 2), held_b, across)
        totals = (
            jnp.where((group == 0) | (group == 2), across, total_a),
            jnp.where(group <= 1, down, total_b),
        )
        if n < count - 1:
            branch_grad, block_out, picks = relay_first(
                rows, gate, (branch_a, branch_b), block_out, totals, spots[n], spots[n + 1]
            )
            first_row = piece.shape[0]
            continue
        halves = ((held_a, down, total_b), (held_b, across, total_a))
        branch_grad, block_out = relay_last(picks, gate, block_out, halves, first_row, branch_grad)
    return (block_out[None, None], branch_grad[None])


def solution(mesh):
    placed = (
        P("rep", "grp", "seq", None),
        P("rep", "grp", "seq", None),
        P("rep", "grp", "seq", None),
        P("rep", "grp", "seq"),
        P("rep", "grp", "seq"),
        P("rep"),
        P("rep", "grp", "seq", None),
    )
    return jax.shard_map(
        local,
        mesh=mesh,
        in_specs=placed,
        out_specs=(P("rep", "grp", "seq", None), P("rep", "seq", None)),
        check_vma=False,
    )
```

```python
import functools
import math

import jax
import jax.numpy as jnp
from jax import lax
from jax.experimental import pallas as pl
from jax.experimental.pallas import tpu as pltpu
from jax.sharding import PartitionSpec as P

HEADS = 32
DH = 80
FRAMES = 20
LANES = 128
VMEM_LIMIT = 32 * 1024 * 1024
PACK_LIMIT = 53 * 1024 * 1024


def shifted(block, axis, distance):
    devices = range(lax.axis_size(axis))
    route = [(i - distance, i) for i in devices if i - distance in devices]
    return lax.ppermute(block, axis, route)


def paired(block, first):
    size, ranks = lax.axis_size("seq"), lax.axis_size("rep")
    route = []
    for i in range(size):
        other = i + 1 if (i - first) % 2 == 0 else i - 1
        for rank in range(ranks):
            if 0 <= other < size:
                route.append((i * ranks + rank, other * ranks + rank))
            elif rank ^ 1 < ranks:
                route.append((i * ranks + rank, i * ranks + (rank ^ 1)))
    return lax.ppermute(block, ("seq", "rep"), route)


def neighbours_there(ranks):
    rank = lax.axis_index("seq")
    return jnp.where(rank > 0, 1.0, 0.0), jnp.where(rank < ranks - 1, 1.0, 0.0)


def lane_windows(heads):
    windows = []
    for head in range(heads):
        first, last = head * DH, (head + 1) * DH
        if windows and last <= windows[-1][0] + 2 * LANES:
            windows[-1][1].append(head)
        else:
            windows.append((first // LANES * LANES, [head]))
    out = []
    for start, members in windows:
        start = min(start, heads * DH - 2 * LANES)
        out.append((start, members))
    return out


def head_masks(rows, period):
    masks = {}
    for start, members in lane_windows(period // DH):
        lane = lax.broadcasted_iota(jnp.int32, (rows, 2 * LANES), 1) + start
        for h in members:
            inside = (lane >= h * DH) & (lane < (h + 1) * DH)
            masks[h] = jnp.where(inside, 1.0, 0.0).astype(jnp.bfloat16)
    return masks


def period_scores(base, query, keys, masks, period):
    scores = []
    for start, members in lane_windows(period // DH):
        lanes = slice(base + start, base + start + 2 * LANES)
        part = query(lanes)
        stacked = jnp.concatenate([part * masks[h] for h in members], axis=0)
        scores.append(
            [
                lax.dot_general(
                    stacked, key(lanes), (((1,), (1,)), ((), ())), preferred_element_type=jnp.float32
                )
                for key in keys
            ]
        )
    return scores


def mixed_period(base, scores, sets, period):
    rows = sets[0][0].shape[0]
    factor = math.log2(math.e) / math.sqrt(DH)
    windows = lane_windows(period // DH)
    weights = []
    for parts, (start, members) in zip(scores, windows):
        parts = [
            part.reshape(len(members), rows, -1) + bias[None]
            for part, (bias, value) in zip(parts, sets)
        ]
        largest = row_max(parts)
        weights.append(
            [
                jnp.exp2((part - largest) * factor).astype(jnp.bfloat16).reshape(len(members) * rows, -1)
                for part in parts
            ]
        )
    tiles = {}
    for parts, (start, members) in zip(weights, windows):
        lanes = slice(base + start, base + start + 2 * LANES)
        mixed = sum(
            jnp.dot(part, value(lanes), preferred_element_type=jnp.float32)
            for part, (bias, value) in zip(parts, sets)
        )
        totals = sum(
            jnp.dot(part, jnp.ones((part.shape[1], LANES), part.dtype), preferred_element_type=jnp.float32)
            for part in parts
        )
        scale = 1.0 / totals
        for n, h in enumerate(members):
            for t in range(2):
                low = start + t * LANES
                if h * DH >= low + LANES or (h + 1) * DH <= low:
                    continue
                mine = slice(n * rows, (n + 1) * rows)
                piece = mixed[mine, t * LANES : (t + 1) * LANES] * scale[mine]
                if low in tiles:
                    lane = lax.broadcasted_iota(jnp.int32, (rows, LANES), 1) + low
                    tiles[low] = jnp.where(lane >= h * DH, piece, tiles[low])
                else:
                    tiles[low] = piece
    return {low: tile.astype(jnp.bfloat16) for low, tile in tiles.items()}


def row_max(parts):
    if all(part.shape == parts[0].shape for part in parts):
        return jnp.max(functools.reduce(jnp.maximum, parts), axis=-1, keepdims=True)
    return functools.reduce(jnp.maximum, [jnp.max(part, axis=-1, keepdims=True) for part in parts])


def columns(row):
    return jnp.broadcast_to(row, (LANES, row.shape[1])).T


def link_bias(mine, theirs):
    return jnp.where(jnp.abs(mine[:, :1] - theirs.T[: mine.shape[0]]) <= 1.5, 0.0, -1e30)


def store_period(base, tiles, out_ref):
    for low, tile in tiles.items():
        out_ref[:, base + low : base + low + LANES] = tile


def ends_kernel(k_ref, v_ref, code_ref, *end_refs):
    even = lax.axis_index("seq") % 2 == 0
    tokens, width = k_ref.shape
    code = columns(code_ref[...])
    for n, ref in enumerate(end_refs):
        most = ref.shape[0]
        tail = even if n == 0 else jnp.logical_not(even)
        first = pl.multiple_of(jnp.where(tail, tokens - most, 0), most)
        ref[:, :width] = k_ref[pl.ds(first, most), :]
        ref[:, width : 2 * width] = v_ref[pl.ds(first, most), :]
        here = jnp.where(tail, code[tokens - most :], code[:most])
        ref[:, 2 * width :] = here.astype(jnp.bfloat16)


def middle_kernel(reach, q_ref, k_ref, v_ref, code_ref, out_ref):
    rows = out_ref.shape[0]
    code = columns(code_ref[...])
    bias = link_bias(code[reach : reach + rows], code)
    period = math.lcm(DH, LANES)
    masks = head_masks(rows, period)
    query = lambda lanes: q_ref[reach : reach + rows, lanes]
    for base in range(0, out_ref.shape[1], period):
        scores = period_scores(base, query, [lambda lanes: k_ref[:, lanes]], masks, period)
        sets = [(bias, lambda lanes: v_ref[:, lanes])]
        store_period(base, mixed_period(base, scores, sets, period), out_ref)


def sides_kernel(reach, ranks, q_ref, k_ref, v_ref, code_ref, one_ref, two_ref, *refs):
    there = neighbours_there(ranks)
    out_ref, keys, values, codes = refs
    tokens, width = q_ref.shape
    near = 2 * reach
    code = columns(code_ref[...])
    even = lax.axis_index("seq") % 2 == 0
    period = math.lcm(DH, LANES)
    masks = head_masks(reach, period)
    blocks = []
    for side, first in ((0, 0), (1, tokens - near)):
        own = slice(first, first + near)
        use_two = even if side == 0 else jnp.logical_not(even)
        halo = jnp.where(use_two, two_ref[...], one_ref[...])
        keys[side, :near] = k_ref[own]
        values[side, :near] = v_ref[own]
        codes[side, :near] = code[own]
        keys[side, near : near + reach] = halo[:, :width]
        values[side, near : near + reach] = halo[:, width : 2 * width]
        codes[side, near : near + reach] = halo[:, 2 * width :].astype(jnp.float32) * there[side]
        spare = keys.shape[1] - near - reach
        if spare:
            for ref in (keys, values, codes):
                ref[side, near + reach :] = jnp.zeros((spare, ref.shape[2]), ref.dtype)
        top = side * (tokens - reach)
        blocks.append((side, top, link_bias(code[top : top + reach], codes[side])))
    for base in range(0, width, period):
        scores = []
        for side, top, bias in blocks:
            query = lambda lanes: q_ref[top : top + reach, lanes]
            key = lambda lanes: keys[side, :, lanes]
            scores.append(period_scores(base, query, [key], masks, period))
        for (side, top, bias), part in zip(blocks, scores):
            sets = [(bias, lambda lanes: values[side, :, lanes])]
            tiles = mixed_period(base, part, sets, period)
            store_period(base, tiles, out_ref.at[side * reach : (side + 1) * reach])


def edge_kernel(reach, ranks, q_ref, k_ref, v_ref, code_ref, *refs):
    below, above = neighbours_there(ranks)
    even = lax.axis_index("seq") % 2 == 0
    there = [jnp.where(even, above, below), jnp.where(even, below, above)]
    halos = refs[:-4]
    out_ref, keys, values, codes = refs[-4:]
    width = q_ref.shape[1]
    code = columns(code_ref[...])
    at = 0
    for n, piece in enumerate(halos):
        rows = piece.shape[0]
        known = there[n] if n < 2 else 1.0
        keys[at : at + rows] = piece[:, :width]
        values[at : at + rows] = piece[:, width : 2 * width]
        codes[at : at + rows] = piece[:, 2 * width :].astype(jnp.float32) * known
        at += rows
    if at < keys.shape[0]:
        for ref in (keys, values, codes):
            ref[at:] = jnp.zeros((ref.shape[0] - at, ref.shape[1]), ref.dtype)
    period = math.lcm(DH, LANES)
    masks = head_masks(q_ref.shape[0], period)
    query = lambda lanes: q_ref[:, lanes]
    pair = [lambda lanes: k_ref[:, lanes], lambda lanes: keys[:, lanes]]
    sets = [
        (link_bias(code, code), lambda lanes: v_ref[:, lanes]),
        (link_bias(code, codes[...]), lambda lanes: values[:, lanes]),
    ]
    for base in range(0, width, period):
        scores = period_scores(base, query, pair, masks, period)
        store_period(base, mixed_period(base, scores, sets, period), out_ref)


def attend_cost(tokens, span, width):
    return pl.CostEstimate(
        flops=HEADS * tokens * span * 2 * LANES * 4,
        bytes_accessed=12 * tokens * width,
        transcendentals=HEADS * tokens * span,
    )


VMEM = pl.BlockSpec(memory_space=pltpu.VMEM)
PARAMS = pltpu.CompilerParams(vmem_limit_bytes=VMEM_LIMIT)


def pack_ends(keys, values, code, most):
    width = keys.shape[1]
    ends = jax.ShapeDtypeStruct((most, 2 * width + LANES), jnp.bfloat16)
    return pl.pallas_call(
        ends_kernel,
        in_specs=[VMEM] * 3,
        out_specs=[VMEM] * 2,
        out_shape=[ends, ends],
        compiler_params=PARAMS,
        cost_estimate=pl.CostEstimate(flops=0, bytes_accessed=16 * most * width, transcendentals=0),
        name="pack_ends",
    )(keys, values, code)


def attend_middle(queries, keys, values, code, reach):
    tokens, width = queries.shape
    return pl.pallas_call(
        functools.partial(middle_kernel, reach),
        in_specs=[VMEM] * 4,
        out_specs=VMEM,
        out_shape=jax.ShapeDtypeStruct((tokens - 2 * reach, width), jnp.bfloat16),
        compiler_params=PARAMS,
        cost_estimate=attend_cost(tokens - 2 * reach, tokens, width),
        name="attend_middle",
    )(queries, keys, values, code)


def attend_edges(queries, keys, values, code, halos, reach):
    tokens, width = queries.shape
    rows = min(tokens, 2 * reach)
    if tokens > 2 * reach:
        kernel = sides_kernel
        held = (2, -(-3 * reach // LANES) * LANES)
    else:
        kernel = edge_kernel
        held = (-(-2 * reach // LANES) * LANES,)
    operands = [queries, keys, values, code, *halos]
    return pl.pallas_call(
        functools.partial(kernel, reach, lax.axis_size("seq")),
        in_specs=[VMEM] * len(operands),
        out_specs=VMEM,
        out_shape=jax.ShapeDtypeStruct((rows, width), jnp.bfloat16),
        scratch_shapes=[
            pltpu.VMEM((*held, width), jnp.bfloat16),
            pltpu.VMEM((*held, width), jnp.bfloat16),
            pltpu.VMEM((*held, LANES), jnp.float32),
        ],
        compiler_params=PARAMS,
        cost_estimate=attend_cost(rows, LANES, width),
        name="attend_edges",
    )(*operands)


def pack_grads_kernel(grad_ref, mark_ref, *refs):
    first_ref, second_ref, sems = refs[-3:]
    half = grad_ref.shape[1] // 2
    copies = []
    for n, ref in enumerate((first_ref, second_ref)):
        copies.append(
            pltpu.make_async_copy(
                grad_ref.at[:, pl.ds(n * half, half)], ref.at[:, pl.ds(0, half)], sems.at[n]
            )
        )
    for copy in copies:
        copy.start()
    place = columns(mark_ref[1:2]).astype(jnp.bfloat16)
    for ref in (first_ref, second_ref):
        ref[:, half:] = place
    for copy in copies:
        copy.wait()


def pack_grads(grads, marks, *others):
    tokens, width = grads.shape
    far = pl.BlockSpec(memory_space=pltpu.HBM)
    return pl.pallas_call(
        pack_grads_kernel,
        in_specs=[far, VMEM] + [far] * len(others),
        out_specs=[VMEM] * 2,
        out_shape=[jax.ShapeDtypeStruct((tokens, width // 2 + LANES), jnp.bfloat16)] * 2,
        scratch_shapes=[pltpu.SemaphoreType.DMA((2,))],
        compiler_params=pltpu.CompilerParams(vmem_limit_bytes=PACK_LIMIT),
        cost_estimate=pl.CostEstimate(flops=0, bytes_accessed=4 * tokens * width, transcendentals=0),
        name="pack_grads",
    )(grads, marks, *others)


def selector(row):
    tokens = row.shape[1]
    wanted = lax.broadcasted_iota(jnp.int32, (tokens, tokens), 0).astype(jnp.float32)
    return jnp.where(wanted == row, 1.0, 0.0)


def sums_kernel(part, sizes, gate_ref, row_ref, mine_ref, theirs_ref, *out_refs):
    half = gate_ref.shape[1] // 2
    place = theirs_ref[:, half:].astype(jnp.float32).T[:1]
    picks = [selector(row).astype(jnp.bfloat16) for row in (row_ref[...], place)]
    theirs = theirs_ref[:, :half]
    summed = jnp.dot(
        jnp.concatenate(picks, axis=1),
        jnp.concatenate((mine_ref[:, :half], theirs), axis=0),
        preferred_element_type=jnp.float32,
    )
    own = jnp.where(lax.axis_index("grp") == part + 1, 1.0, 0.0)
    term = gate_ref[:, part * half : (part + 1) * half] * summed + own * theirs.astype(jnp.float32)
    term = term.astype(jnp.bfloat16)
    at = 0
    for ref, size in zip(out_refs, sizes):
        ref[...] = term[at : at + size]
        at += size


def pair_sums(part, gate, rows, mine, theirs, sizes):
    tokens, half = mine.shape[0], gate.shape[1] // 2
    return pl.pallas_call(
        functools.partial(sums_kernel, part, sizes),
        in_specs=[VMEM] * 4,
        out_specs=[VMEM] * len(sizes),
        out_shape=[jax.ShapeDtypeStruct((size, half), jnp.bfloat16) for size in sizes],
        compiler_params=PARAMS,
        cost_estimate=pl.CostEstimate(
            flops=4 * tokens * tokens * half, bytes_accessed=6 * tokens * half, transcendentals=0
        ),
        name="pair_sums",
    )(gate, rows, mine, theirs)


def piece_spots(tokens, reach, piece):
    if tokens <= 2 * reach:
        return [(0, tokens, 0)]
    if piece == 0:
        return [(reach, tokens - 2 * reach, 0)]
    return [(0, reach, 0), (tokens - reach, reach, reach)]


def picked(spots, row_ref):
    picks = selector(row_ref[...]).T.astype(jnp.bfloat16)
    return jnp.concatenate([picks[:, top : top + size] for top, size, at in spots], axis=1)


def relay_first_kernel(
    spots, later, row_ref, gate_ref, a_ref, b_ref, base_ref, c_ref, d_ref, grad_ref, out_ref, picks_ref, sems
):
    half = a_ref.shape[1]
    copies = []
    for n, ref in enumerate((c_ref, d_ref)):
        to = grad_ref.at[pl.ds(0, ref.shape[0]), pl.ds(n * half, half)]
        copies.append(pltpu.make_async_copy(ref, to, sems.at[n]))
    for copy in copies:
        copy.start()
    picks = picked(spots, row_ref)
    for n, ref in enumerate((a_ref, b_ref)):
        lanes = slice(n * half, (n + 1) * half)
        relayed = jnp.dot(picks, ref[...], preferred_element_type=jnp.float32)
        out_ref[:, lanes] = base_ref[:, lanes].astype(jnp.float32) + gate_ref[:, lanes] * relayed
    picks_ref[...] = picked(later, row_ref)
    for copy in copies:
        copy.wait()


def relay_first(rows, gate, branch, base, totals, spots, later):
    tokens, width = base.shape
    return pl.pallas_call(
        functools.partial(relay_first_kernel, spots, later),
        in_specs=[VMEM] * 7,
        out_specs=[pl.BlockSpec(memory_space=pltpu.HBM), VMEM, VMEM],
        out_shape=[
            jax.ShapeDtypeStruct((tokens, width), jnp.bfloat16),
            jax.ShapeDtypeStruct((tokens, width), jnp.float32),
            jax.ShapeDtypeStruct((tokens, sum(size for top, size, at in later)), jnp.bfloat16),
        ],
        scratch_shapes=[pltpu.SemaphoreType.DMA((2,))],
        compiler_params=PARAMS,
        cost_estimate=pl.CostEstimate(
            flops=2 * tokens * tokens * width, bytes_accessed=24 * tokens * width, transcendentals=0
        ),
        name="relay_first",
    )(rows, gate, *branch, base, *totals)


def relay_last_kernel(
    part, chunks, first_row, picks_ref, gate_ref, held_ref, got_ref, base_ref, total_ref, *refs
):
    grad_ref, out_ref, staged, summed, sems, grad_sem = refs[-6:]
    half = held_ref.shape[1]
    other = 1 - part
    group = lax.axis_index("grp")
    holds = group <= 1 if part == 0 else group % 2 == 0
    summed[...] = jnp.where(holds, got_ref[...], total_ref[...])
    to = grad_ref.at[pl.ds(first_row, total_ref.shape[0]), pl.ds(other * half, half)]
    copies = [pltpu.make_async_copy(summed, to, grad_sem)]
    copies[0].start()
    step = half // chunks
    for c in range(chunks):
        mine = slice(c * step, (c + 1) * step)
        lanes = slice(part * half + c * step, part * half + (c + 1) * step)
        branch = jnp.where(holds, held_ref[:, mine], got_ref[:, mine])
        relayed = jnp.dot(picks_ref[...], branch, preferred_element_type=jnp.float32)
        total = base_ref[:, lanes].astype(jnp.float32) + gate_ref[:, lanes] * relayed
        staged[:, mine] = total.astype(staged.dtype)
        copies.append(
            pltpu.make_async_copy(
                staged.at[:, pl.ds(c * step, step)],
                out_ref.at[:, pl.ds(part * half + c * step, step)],
                sems.at[c],
            )
        )
        copies[-1].start()
    for copy in copies:
        copy.wait()


def relay_last(picks, gate, held, got, base, total, part, first_row, grads, out):
    tokens, width = base.shape
    chunks = 2 if width // 2 % (2 * LANES) == 0 else 1
    far = pl.BlockSpec(memory_space=pltpu.HBM)
    operands = [picks, gate, held, got, base, total]
    aliases = {}
    for n, buffer in enumerate((grads, out)):
        if buffer is not None:
            aliases[len(operands)] = n
            operands.append(buffer)
    return pl.pallas_call(
        functools.partial(relay_last_kernel, part, chunks, first_row),
        in_specs=[VMEM] * 6 + [far] * len(aliases),
        out_specs=[far] * 2,
        out_shape=[jax.ShapeDtypeStruct((tokens, width), jnp.bfloat16)] * 2,
        input_output_aliases=aliases,
        scratch_shapes=[
            pltpu.VMEM((tokens, width // 2), jnp.bfloat16),
            pltpu.VMEM(total.shape, jnp.bfloat16),
            pltpu.SemaphoreType.DMA((chunks,)),
            pltpu.SemaphoreType.DMA,
        ],
        compiler_params=PARAMS,
        cost_estimate=pl.CostEstimate(
            flops=tokens * tokens * width, bytes_accessed=6 * tokens * width, transcendentals=0
        ),
        name="relay_last",
    )(*operands)


def whole_gate(gate):
    ranks = lax.axis_size("rep")
    if ranks != 2:
        return lax.all_gather(gate, "rep", axis=0, tiled=True)
    other = lax.ppermute(gate, "rep", [(0, 1), (1, 0)])
    first = lax.axis_index("rep") == 0
    return jnp.concatenate([jnp.where(first, gate, other), jnp.where(first, other, gate)])


SWAP_X, SWAP_Y = [(0, 1), (1, 0), (2, 3), (3, 2)], [(0, 2), (2, 0), (1, 3), (3, 1)]
ROUND_A, ROUND_B = [(0, 1), (1, 3), (3, 2), (2, 0)], [(0, 2), (2, 3), (3, 1), (1, 0)]


def sent_both(to_a, to_b, route_a, route_b):
    ranks = lax.axis_size("rep")
    odd = lax.axis_index("rep") % 2 == 1

    def mixed(block, even_route, odd_route):
        route = []
        for rank in range(ranks):
            for source, target in odd_route if rank % 2 else even_route:
                route.append((source * ranks + rank, target * ranks + rank))
        return lax.ppermute(block, ("grp", "rep"), route)

    first = mixed(jnp.where(odd, to_b, to_a), route_a, route_b)
    second = mixed(jnp.where(odd, to_a, to_b), route_b, route_a)
    return jnp.where(odd, second, first), jnp.where(odd, first, second)


def added(a, b):
    return (a.astype(jnp.float32) + b.astype(jnp.float32)).astype(a.dtype)


def local(query_rows, key_rows, value_rows, view_frame, control_row, control_gate, out_grad):
    queries, keys, values = query_rows[0, 0], key_rows[0, 0], value_rows[0, 0]
    tokens, width = queries.shape
    half = width // 2
    ranks = lax.axis_size("seq")
    reach = 2 * (tokens * ranks // 32)
    hops = (reach + tokens - 1) // tokens
    group, rank = lax.axis_index("grp"), lax.axis_index("seq")
    send = lambda block, route: lax.ppermute(block, "grp", route)

    tag = view_frame[0, 0]
    code = tag + 8 * (tag // FRAMES) + 16
    marks = jnp.stack((code, control_row[0, 0] % tokens)).astype(jnp.float32)
    code, rows = marks[:1], marks[1:]
    most = min(tokens, reach)
    even = rank % 2 == 0
    sent_a, sent_b = pack_grads(out_grad[0, 0], marks, queries, keys, values)
    code, sent_a, sent_b = lax.optimization_barrier((code, sent_a, sent_b))
    got_a, got_b = send(sent_a, SWAP_X), send(sent_b, SWAP_Y)
    end_one, end_two = pack_ends(keys, values, code, most)
    code, end_one, end_two = lax.optimization_barrier((code, end_one, end_two))
    own = [attend_middle(queries, keys, values, code, reach)] if tokens > 2 * reach else []
    gate = whole_gate(control_gate)[None]
    halos = [paired(end_one, 0), paired(end_two, 1)]
    for hop in range(2, hops + 1):
        count = min(tokens, reach - (hop - 1) * tokens)
        tail, head = jnp.where(even, end_one, end_two), jnp.where(even, end_two, end_one)
        halos.append(shifted(tail[most - count :], "seq", hop))
        halos.append(shifted(head[:count], "seq", -hop))
    sizes = [piece.shape[0] for piece in own] + [min(tokens, 2 * reach)]
    sums = [
        *pair_sums(0, gate, rows, sent_a, got_a, sizes),
        *pair_sums(1, gate, rows, sent_b, got_b, sizes),
    ]
    count = len(sizes)

    def outgoing(piece, sum_a, sum_b):
        to_a = jnp.where(group == 0, piece[:, :half], jnp.where(group == 1, sum_a, sum_b))
        to_b = jnp.where(group == 0, piece[:, half:], jnp.where(group == 2, sum_b, sum_a))
        return to_a, to_b

    going = [outgoing(own[0], sums[0], sums[count])] if own else []
    code, *ready = lax.optimization_barrier((code, *sums, *(going[0] if going else ())))
    sums = ready[: 2 * count]
    if going:
        going = [ready[2 * count :]]
    own.append(attend_edges(queries, keys, values, code, halos, reach))

    going.append(outgoing(own[-1], sums[count - 1], sums[2 * count - 1]))
    spots = [piece_spots(tokens, reach, n) for n in range(count)]
    order = [
        own[n][at : at + size] for top, size, n, at in sorted(
            (top, size, n, at) for n in range(count) for top, size, at in spots[n]
        )
    ]
    block_out = jnp.concatenate(order, axis=0)
    branch_grad, first_row = None, 0
    picks = (rows[0][:, None] == jnp.arange(tokens)).astype(jnp.bfloat16) if count == 1 else None
    for n, (piece, sum_a, sum_b) in enumerate(zip(own, sums[:count], sums[count:])):
        piece_a, piece_b = piece[:, :half], piece[:, half:]
        one, two = sent_both(*going[n], ROUND_A, ROUND_B)
        total_a = added(sum_a, jnp.where(group == 1, two, one))
        total_b = added(sum_b, jnp.where(group == 2, one, two))
        held_a = jnp.where(group == 0, piece_a, one)
        held_b = jnp.where(group == 0, piece_b, two)
        to_across = jnp.where((group == 0) | (group == 2), held_b, total_a)
        to_down = jnp.where(group <= 1, held_a, total_b)
        across, down = send(to_across, SWAP_X), send(to_down, SWAP_Y)
        branch_a = jnp.where(group <= 1, held_a, down)
        branch_b = jnp.where((group == 0) | (group == 2), held_b, across)
        totals = (
            jnp.where((group == 0) | (group == 2), across, total_a),
            jnp.where(group <= 1, down, total_b),
        )
        if n < count - 1:
            branch_grad, block_out, picks = relay_first(
                rows, gate, (branch_a, branch_b), block_out, totals, spots[n], spots[n + 1]
            )
            first_row = piece.shape[0]
            continue
        base, block_out = block_out, None
        ends = ((held_a, down, total_b), (held_b, across, total_a))
        for part in (1, 0):
            held, got, total = ends[part]
            branch_grad, block_out = relay_last(
                picks, gate, held, got, base, total, part, first_row, branch_grad, block_out
            )
    return (block_out[None, None], branch_grad[None])


def solution(mesh):
    placed = (
        P("rep", "grp", "seq", None),
        P("rep", "grp", "seq", None),
        P("rep", "grp", "seq", None),
        P("rep", "grp", "seq"),
        P("rep", "grp", "seq"),
        P("rep"),
        P("rep", "grp", "seq", None),
    )
    return jax.shard_map(
        local,
        mesh=mesh,
        in_specs=placed,
        out_specs=(P("rep", "grp", "seq", None), P("rep", "seq", None)),
        check_vma=False,
    )
```
